32 devices in a mesh: dp: 4 (over x, core), ep: 2 (over y), cp: 4 (over z).
Axes of the slice: x: 2, y: 2, z: 4, core: 2. Of those that a mesh axis runs over, the one named last changes fastest.
Arguments:
- tokens: bfloat16 [1024, 16, 1024], P('cp', ('dp', 'ep')), may hold values from -6 to 6
- lengths: int32 [16], P(('dp', 'ep')), may hold values from 256 to 1024, as said below
- expert_ids: int32 [1024, 16, 2], P('cp', ('dp', 'ep')), may hold values from 0 to 3, as said below
- places: int32 [1024, 16, 2], P('cp', ('dp', 'ep')), may hold values from -1 to 319, as said below
- buckets: int32 [1024], replicated, may hold values from 0 to 31, as said below
- w_attn: bfloat16 [1024, 4096], replicated
- bias_table: float32 [16, 32], replicated, may hold values from -4 to 4
- norm1_gain: float32 [1024], replicated, may hold values from 0.5 to 1.5
- norm2_gain: float32 [1024], replicated, may hold values from 0.5 to 1.5
- w_router: bfloat16 [1024, 4], replicated, may hold values from -0.125 to 0.125
- w_gate: bfloat16 [4, 1024, 2816], P('ep'), may hold values from -0.1875 to 0.1875
- w_up: bfloat16 [4, 1024, 2816], P('ep'), may hold values from -0.1875 to 0.1875
- w_down: bfloat16 [4, 1024, 2816], P('ep'), may hold values from -1.25 to 1.25
- cotangent: bfloat16 [1024, 16, 1024], P('cp', ('dp', 'ep')), may hold values from -6 to 6
Outputs:
- mixed: bfloat16 [1024, 16, 1024], P('cp', ('dp', 'ep'))
- tokens_grad: bfloat16 [1024, 16, 1024], P('cp', ('dp', 'ep'))
- w_attn_grad: float32 [1024, 4096], P(None, ('dp', 'ep', 'cp'))
- bias_table_grad: float32 [16, 32], replicated
- norm1_gain_grad: float32 [1024], replicated
- norm2_gain_grad: float32 [1024], replicated
- w_router_grad: float32 [1024, 4], replicated
- w_gate_grad: float32 [4, 1024, 2816], P('ep', None, ('dp', 'cp'))
- w_up_grad: float32 [4, 1024, 2816], P('ep', None, ('dp', 'cp'))
- w_down_grad: float32 [4, 1024, 2816], P('ep', None, ('dp', 'cp'))
The draws below stay inside these ranges and needn't reach their ends.
Inputs may be any that keep to these rules, and one draw needn't show every extreme that they name: `lengths`: in each group of 2 slots held by one index of dp+ep, one slot has length 1024. `expert_ids`: the 2 experts of a token differ. -1 for padding positions and for choices beyond an expert's places; within the rows of one device the routed choices of one expert have distinct places. `buckets`: Non-decreasing in the distance, 0 at distance 0.
All inputs are finite; a program needn't handle non-finite values.
Results may differ from the reference program's by a relative error of at most 0.02.
Values may be sent and summed in bfloat16 or wider, within the bound.
A program may use at most 320 MiB of HBM per device.

```python
import math
import jax
import jax.numpy as jnp
from jax import lax

D = 1024
HEADS = 16
HD = 64
FF = 2816
NB = 32
TOPK = 2
GROUP_SEQS = 2
SPAN = 256
SEQ = 1024
SLOTS = 16
EXPERTS = 4
CAP = 320
N_CP = 4


def shared_routes(key):
    len_key = jax.random.fold_in(key, 101)
    pick_key, other_key = jax.random.split(len_key, 2)
    groups = SLOTS // GROUP_SEQS
    full_pick = jax.random.randint(pick_key, (groups,), 0, GROUP_SEQS)
    other = jax.random.randint(other_key, (groups, GROUP_SEQS), SEQ // 4, SEQ + 1)
    group_lengths = jnp.where(jnp.arange(GROUP_SEQS)[None, :] == full_pick[:, None], SEQ, other)
    lengths = group_lengths.reshape(SLOTS).astype(jnp.int32)
    exp_key = jax.random.fold_in(key, 202)
    hot_key, coin_key, first_key, second_key = jax.random.split(exp_key, 4)
    hot_expert = jax.random.randint(hot_key, (), 0, EXPERTS)
    coin = jax.random.randint(coin_key, (SEQ, SLOTS), 0, 4)
    first = jnp.where(coin == 0, hot_expert, jax.random.randint(first_key, (SEQ, SLOTS), 0, EXPERTS))
    second = (first + jax.random.randint(second_key, (SEQ, SLOTS), 1, EXPERTS)) % EXPERTS
    chosen = jnp.stack([first, second], axis=-1).astype(jnp.int32)
    valid = jnp.arange(SEQ)[:, None] < lengths[None, :]
    live = jnp.broadcast_to(valid[:, :, None], (SEQ, SLOTS, TOPK))
    blocks = SEQ // SPAN
    order = (blocks, SPAN, groups, GROUP_SEQS, TOPK)
    blocked = chosen.reshape(order).transpose(0, 2, 1, 3, 4).reshape(blocks, groups, SPAN * GROUP_SEQS * TOPK)
    blocked_live = live.reshape(order).transpose(0, 2, 1, 3, 4).reshape(blocks, groups, SPAN * GROUP_SEQS * TOPK)
    onehot = ((blocked[..., None] == jnp.arange(EXPERTS, dtype=jnp.int32)) & blocked_live[..., None]).astype(jnp.int32)
    ranks = jnp.cumsum(onehot, axis=2) - 1
    mine = jnp.sum(ranks * onehot, axis=-1)
    place = jnp.where(blocked_live & (mine < CAP), mine, -1)
    place = place.reshape(blocks, groups, SPAN, GROUP_SEQS, TOPK).transpose(0, 2, 1, 3, 4).reshape(SEQ, SLOTS, TOPK)
    return (lengths, chosen, place.astype(jnp.int32))


def draw_lengths(key, part):
    table = shared_routes(key)
    return table[0]


def draw_expert_ids(key, part):
    table = shared_routes(key)
    return table[1]


def draw_places(key, part):
    table = shared_routes(key)
    return table[2]


def draw_buckets(key, part):
    key = jax.random.fold_in(key, 4)
    distance = jnp.arange(SEQ, dtype=jnp.int32)
    shuffled = jax.random.permutation(key, SEQ - 1).astype(jnp.int32) + 1
    rise_points = shuffled[:NB - 1]
    bucket = jnp.sum((distance[:, None] >= rise_points[None, :]).astype(jnp.int32), axis=1)
    return bucket.astype(jnp.int32)


def draw_w_attn(key, part):
    key = jax.random.fold_in(key, 5)
    values = jnp.clip(jax.random.normal(key, (D, 4 * D), jnp.float32), -6.0, 6.0)
    column = jnp.arange(4 * D)
    factor = jnp.where(column < 3 * D, 1.0, 6.0) / jnp.sqrt(jnp.float32(D))
    return (values * factor[None, :]).astype(jnp.bfloat16)


def shard_levels(key, dims, cuts, low, largest):
    factor_of, own = 1.0, jax.random.fold_in(key, 6)
    for position, shards_of in cuts:
        draws = jnp.exp(jax.random.uniform(jax.random.fold_in(own, position), (shards_of,), jnp.float32, low / len(cuts), largest / len(cuts)))
        factor_of = factor_of * jnp.repeat(draws, dims[position] // shards_of).reshape([-1 if axis == position else 1 for axis in range(len(dims))])
    return factor_of


def centred(rng, extent, width, most, shards=(), kind=jnp.bfloat16):
    array = width * jax.random.normal(rng, extent, jnp.float32)
    if shards:
        array = array * shard_levels(rng, extent, shards, -0.22, 0.18)
    return jnp.clip(array, -most, most).astype(kind)


def setup_inputs(seed: int = 0) -> dict:
    arg_keys = jax.random.split(jax.random.key(seed), 15)
    return {
        "tokens": centred(arg_keys[0], (SEQ, SLOTS, D), 1.0, 6.0, ((0, 4), (1, 8))),
        "lengths": draw_lengths(jax.random.fold_in(arg_keys[14], 71), 0),
        "expert_ids": draw_expert_ids(jax.random.fold_in(arg_keys[14], 71), 0),
        "places": draw_places(jax.random.fold_in(arg_keys[14], 71), 0),
        "buckets": draw_buckets(jax.random.fold_in(arg_keys[14], 71), 0),
        "w_attn": draw_w_attn(jax.random.fold_in(arg_keys[14], 71), 0),
        "bias_table": centred(arg_keys[6], (HEADS, NB), 1.0, 4.0, (), jnp.float32),
        "norm1_gain": jnp.clip(1.0 + 0.1 * jax.random.normal(arg_keys[7], (D,), jnp.float32), 0.5, 1.5),
        "norm2_gain": jnp.clip(1.0 + 0.1 * jax.random.normal(arg_keys[8], (D,), jnp.float32), 0.5, 1.5),
        "w_router": centred(arg_keys[9], (D, EXPERTS), (2 * D) ** -0.5, 0.125),
        "w_gate": centred(arg_keys[10], (EXPERTS, D, FF), D ** -0.5, 0.1875, ((0, 2),)),
        "w_up": centred(arg_keys[11], (EXPERTS, D, FF), D ** -0.5, 0.1875, ((0, 2),)),
        "w_down": centred(arg_keys[12], (EXPERTS, D, FF), (max(1, FF // 128)) ** -0.5, 1.25, ((0, 2),)),
        "cotangent": centred(arg_keys[13], (SEQ, SLOTS, D), 1.0, 6.0, ((0, 4), (1, 8))),
    }


epsilon = 1e-06
masked_value = -1000000000.0

@jax.custom_vjp
def low(v):
    return lax.optimization_barrier(v.astype(jnp.bfloat16)).astype(jnp.float32)

@jax.custom_vjp
def low_back(v):
    return v

def low_keep(v):
    return (low(v), None)

def low_pass(kept, grad):
    return (grad,)

def back_keep(v):
    return (v, None)

def back_low(kept, grad):
    return (low(grad),)
low.defvjp(low_keep, low_pass)
low_back.defvjp(back_keep, back_low)

def matmul(form, left, right):
    return jnp.einsum(form, left, right, precision=lax.Precision.HIGHEST)

def gelu_tanh(values):
    return jax.nn.gelu(values, approximate=True)

def root_scale(values):
    return lax.rsqrt(lax.optimization_barrier(jnp.mean(values * values, axis=-1, keepdims=True)) + epsilon)

def reference(tokens, lengths, expert_ids, places, buckets, w_attn, bias_table, norm1_gain, norm2_gain, w_router, w_gate, w_up, w_down, cotangent):
    query_block = math.gcd(SEQ, 512)
    sources = SLOTS // GROUP_SEQS * N_CP
    slot_total = EXPERTS * sources * CAP
    head_scale = HD ** (-0.5)
    live_mask = (jnp.arange(SEQ, dtype=jnp.int32)[:, None] < lengths[None, :]).astype(jnp.float32)
    kept_mask = places >= 0
    source_id = (jnp.arange(SLOTS, dtype=jnp.int32) // GROUP_SEQS)[None, :] * N_CP + (jnp.arange(SEQ, dtype=jnp.int32) // SPAN)[:, None]
    target = jnp.where(kept_mask, expert_ids * (sources * CAP) + source_id[:, :, None] * CAP + places, slot_total).astype(jnp.int32)

    def forward(inputs, attn_weight, table, gain_first, gain_second, router_weight, gate_weight, up_weight, down_weight):
        normed_first = low(inputs * root_scale(inputs) * gain_first)
        qkv = low(low_back(matmul('tsd,de->tse', normed_first, attn_weight[:, :3 * D])))
        relative = table[:, buckets]
        key_pos = jnp.arange(SEQ, dtype=jnp.int32)

        def attend(seq_item):
            query_all, key_rows, value_rows, seq_length = seq_item
            query_all = query_all.reshape(SEQ // query_block, query_block, HEADS, HD)
            key_rows = key_rows.reshape(SEQ, HEADS, HD)
            value_rows = value_rows.reshape(SEQ, HEADS, HD)

            def block_out(block_item):
                query_rows, block_start = block_item
                query_pos = block_start + jnp.arange(query_block, dtype=jnp.int32)
                scores = low_back(matmul('qhd,khd->hqk', query_rows, key_rows) * head_scale)
                distance = query_pos[:, None] - key_pos[None, :]
                pair_bias = jnp.take(relative, jnp.clip(distance, 0, SEQ - 1), axis=1)
                allowed = (distance >= 0) & (key_pos[None, :] < seq_length)
                logits = jnp.where(allowed[None], scores + pair_bias, masked_value)
                weights = low(jax.nn.softmax(logits, axis=-1))
                return matmul('hqk,khd->qhd', weights, value_rows)
            block_starts = jnp.arange(SEQ // query_block, dtype=jnp.int32) * query_block
            outputs = lax.map(jax.checkpoint(block_out), (query_all, block_starts))
            return outputs.reshape(SEQ, D)
        per_slot = (qkv[..., :D].transpose(1, 0, 2), qkv[..., D:2 * D].transpose(1, 0, 2), qkv[..., 2 * D:].transpose(1, 0, 2), lengths)
        attended = lax.map(jax.checkpoint(attend), per_slot).transpose(1, 0, 2)
        attended = low(low_back(attended))
        projected = low_back(matmul('tsd,de->tse', attended, attn_weight[:, 3 * D:]))
        hidden = inputs + live_mask[:, :, None] * projected
        normed_second = low(hidden * root_scale(hidden) * gain_second)
        router_logits = low_back(matmul('tsd,de->tse', normed_second, router_weight))
        router_probs = jax.nn.softmax(router_logits, axis=-1)
        gate_values = jnp.take_along_axis(router_probs, expert_ids, axis=-1) * kept_mask.astype(jnp.float32)
        buffer = jnp.zeros((slot_total, D), jnp.float32)
        for assign in range(TOPK):
            buffer = buffer.at[target[:, :, assign].reshape(-1)].add(low_back(normed_second).reshape(-1, D), mode='drop')

        def expert_out(expert_item):
            rows_in, gate_w, up_w, down_w = expert_item
            gate_pre = low_back(matmul('rd,df->rf', rows_in, gate_w))
            up_pre = low_back(matmul('rd,df->rf', rows_in, up_w))
            inner_act = low(gelu_tanh(gate_pre) * up_pre)
            return low(low_back(matmul('rf,df->rd', inner_act, down_w)))
        produced = lax.map(jax.checkpoint(expert_out), (buffer.reshape(EXPERTS, sources * CAP, D), gate_weight, up_weight, down_weight)).reshape(slot_total, D)
        mixed = hidden
        for assign in range(TOPK):
            picked = jnp.take(produced, jnp.minimum(target[:, :, assign], slot_total - 1), axis=0)
            mixed = mixed + gate_values[:, :, assign, None] * picked
        return mixed
    float_args = (tokens.astype(jnp.float32), w_attn.astype(jnp.float32), bias_table, norm1_gain, norm2_gain, w_router.astype(jnp.float32), w_gate.astype(jnp.float32), w_up.astype(jnp.float32), w_down.astype(jnp.float32))
    mixed, pullback = jax.vjp(forward, *float_args)
    grads = pullback(cotangent.astype(jnp.float32))
    return (mixed.astype(jnp.bfloat16), grads[0].astype(jnp.bfloat16), grads[1], grads[2], grads[3], grads[4], grads[5], grads[6], grads[7], grads[8])
```

```python
import functools

import jax
import jax.numpy as jnp
from jax import lax
from jax.experimental import pallas as pl
from jax.experimental.pallas import tpu as pltpu
from jax.sharding import PartitionSpec as P

epsilon = 1e-06
masked_value = -1000000000.0


def gelu_tanh(values):
    return jax.nn.gelu(values, approximate=True)


def root_scale(values):
    return lax.rsqrt(jnp.mean(values * values, axis=-1, keepdims=True) + epsilon)


def norm_back(grad_in, values, scale_rows, gain_vector):
    scaled = grad_in * gain_vector
    inner_mean = jnp.mean(scaled * values, axis=-1, keepdims=True)
    return scale_rows * (scaled - values * scale_rows * scale_rows * inner_mean)


def block_logits(
    queries, key_rows, key_start, query_pos, lengths, table_step, rise_points, head_scale
):
    key_count = key_rows.shape[0]
    key_pos = key_start + jnp.arange(key_count, dtype=jnp.int32)
    scores = (
        jnp.einsum("qshd,kshd->shqk", queries, key_rows, preferred_element_type=jnp.float32)
        * head_scale
    )
    distance = query_pos[:, None] - key_pos[None, :]
    steps = (distance[:, :, None] >= rise_points[None, None, :]).astype(jnp.float32)
    pair_bias = jnp.einsum("hb,qkb->hqk", table_step, steps, precision=lax.Precision.HIGHEST)
    allowed = (distance >= 0)[None, :, :] & (key_pos[None, None, :] < lengths[:, None, None])
    logits = jnp.where(allowed[:, None], scores + pair_bias[None], masked_value)
    return (logits, steps)


def on_device(
    tokens,
    lengths,
    expert_ids,
    places,
    buckets,
    w_attn,
    bias_table,
    norm1_gain,
    norm2_gain,
    w_router,
    w_gate,
    w_up,
    w_down,
    cotangent,
):
    span_rows, pair_count, model_width = tokens.shape
    head_count, bucket_count = bias_table.shape
    head_size = model_width // head_count
    head_scale = head_size ** (-0.5)
    n_cp = lax.axis_size("cp")
    n_ep = lax.axis_size("ep")
    seq_len = span_rows * n_cp
    row_count = span_rows * pair_count
    top_count = expert_ids.shape[2]
    experts = w_router.shape[1]
    exp_dev = w_gate.shape[0]
    capacity = (5 * row_count * top_count + 4 * experts - 1) // (4 * experts)
    my_start = lax.axis_index("cp") * span_rows
    query_pos = my_start + jnp.arange(span_rows, dtype=jnp.int32)
    live_mask = (query_pos[:, None] < lengths[None, :]).astype(jnp.float32)
    inputs = tokens.astype(jnp.float32)
    scale_first = root_scale(inputs)
    normed_first = (inputs * scale_first * norm1_gain).astype(jnp.bfloat16)
    w_qkv = w_attn[:, : 3 * model_width]
    w_out = w_attn[:, 3 * model_width :]
    qkv = jnp.einsum("csd,de->cse", normed_first, w_qkv, preferred_element_type=jnp.float32).astype(
        jnp.bfloat16
    )
    queries = qkv[..., :model_width].reshape(span_rows, pair_count, head_count, head_size)
    keyval = qkv[..., model_width:]
    keyval_all = lax.all_gather(keyval, "cp", axis=0, tiled=True)
    bucket_ids = jnp.arange(bucket_count, dtype=jnp.int32)
    rise_points = jnp.sum((buckets[:, None] < bucket_ids[None, :]).astype(jnp.int32), axis=0)
    table_step = jnp.concatenate(
        [bias_table[:, :1], bias_table[:, 1:] - bias_table[:, :-1]], axis=1
    )
    block_starts = jnp.arange(n_cp, dtype=jnp.int32) * span_rows

    def split_kv(kv_block):
        key_rows = kv_block[..., :model_width].reshape(span_rows, pair_count, head_count, head_size)
        value_rows = kv_block[..., model_width:].reshape(
            span_rows, pair_count, head_count, head_size
        )
        return (key_rows, value_rows)

    kv_blocks = keyval_all.reshape(n_cp, span_rows, pair_count, 2 * model_width)

    def max_step(state_pair, block_item):
        row_peak, row_total = state_pair
        kv_block, block_start = block_item
        key_rows, value_rows = split_kv(kv_block)
        logits, steps = block_logits(
            queries, key_rows, block_start, query_pos, lengths, table_step, rise_points, head_scale
        )
        new_peak = jnp.maximum(row_peak, jnp.max(logits, axis=-1))
        row_total = row_total * jnp.exp(row_peak - new_peak) + jnp.sum(
            jnp.exp(logits - new_peak[..., None]), axis=-1
        )
        return ((new_peak, row_total), None)

    stat_shape = (pair_count, head_count, span_rows)
    (row_peak, row_total), unused = lax.scan(
        max_step,
        (jnp.full(stat_shape, masked_value, jnp.float32), jnp.zeros(stat_shape, jnp.float32)),
        (kv_blocks, block_starts),
    )
    log_total = row_peak + jnp.log(row_total)

    def value_step(running, block_item):
        kv_block, block_start = block_item
        key_rows, value_rows = split_kv(kv_block)
        logits, steps = block_logits(
            queries, key_rows, block_start, query_pos, lengths, table_step, rise_points, head_scale
        )
        weights = jnp.exp(logits - log_total[..., None]).astype(jnp.bfloat16)
        return (
            running
            + jnp.einsum(
                "shqk,kshd->qshd", weights, value_rows, preferred_element_type=jnp.float32
            ),
            None,
        )

    attended, unused = lax.scan(
        value_step,
        jnp.zeros((span_rows, pair_count, head_count, head_size), jnp.float32),
        (kv_blocks, block_starts),
    )
    attended = attended.reshape(span_rows, pair_count, model_width)
    attended_low = attended.astype(jnp.bfloat16)
    projected = jnp.einsum("csd,de->cse", attended_low, w_out, preferred_element_type=jnp.float32)
    hidden = inputs + live_mask[..., None] * projected
    scale_second = root_scale(hidden)
    normed_second = (hidden * scale_second * norm2_gain).astype(jnp.bfloat16)
    router_logits = jnp.einsum(
        "csd,de->cse", normed_second, w_router, preferred_element_type=jnp.float32
    )
    router_probs = jax.nn.softmax(router_logits, axis=-1)
    expert_hot = (expert_ids[..., None] == jnp.arange(experts, dtype=jnp.int32)).astype(jnp.float32)
    kept_mask = (places >= 0).astype(jnp.float32)
    gate_values = jnp.sum(expert_hot * router_probs[:, :, None, :], axis=-1) * kept_mask
    target = jnp.where(places >= 0, expert_ids * capacity + places, -1).reshape(
        row_count, top_count
    )
    slot_ids = jnp.arange(experts * capacity, dtype=jnp.int32)
    route_hot = (target[None, :, :] == slot_ids[:, None, None]).astype(jnp.bfloat16)
    dispatch = jnp.sum(route_hot, axis=2)
    sent_rows = jnp.dot(
        dispatch, normed_second.reshape(row_count, model_width), preferred_element_type=jnp.float32
    )
    sent_rows = sent_rows.astype(jnp.bfloat16).reshape(n_ep, exp_dev, capacity, model_width)
    arrived = lax.all_to_all(sent_rows, "ep", split_axis=0, concat_axis=0, tiled=True)
    gate_pre = jnp.einsum("secd,edf->secf", arrived, w_gate, preferred_element_type=jnp.float32)
    up_pre = jnp.einsum("secd,edf->secf", arrived, w_up, preferred_element_type=jnp.float32)
    active, gelu_pullback = jax.vjp(gelu_tanh, gate_pre)
    inner_act = (active * up_pre).astype(jnp.bfloat16)
    produced = jnp.einsum(
        "secf,edf->secd", inner_act, w_down, preferred_element_type=jnp.float32
    ).astype(jnp.bfloat16)
    returned = lax.all_to_all(produced, "ep", split_axis=0, concat_axis=0, tiled=True).reshape(
        experts * capacity, model_width
    )
    picked = jnp.einsum("jrk,jd->rkd", route_hot, returned, preferred_element_type=jnp.float32)
    gate_flat = gate_values.reshape(row_count, top_count)
    mixed = hidden.reshape(row_count, model_width) + jnp.sum(gate_flat[..., None] * picked, axis=1)
    mixed = mixed.reshape(span_rows, pair_count, model_width).astype(jnp.bfloat16)
    grad_out = cotangent.astype(jnp.float32).reshape(row_count, model_width)
    gate_grads = jnp.sum(grad_out[:, None, :] * picked, axis=-1)
    sent_back = (gate_flat[..., None] * grad_out[:, None, :]).astype(jnp.bfloat16)
    scattered = jnp.einsum("jrk,rkd->jd", route_hot, sent_back, preferred_element_type=jnp.float32)
    scattered = scattered.astype(jnp.bfloat16).reshape(n_ep, exp_dev, capacity, model_width)
    grad_produced = lax.all_to_all(scattered, "ep", split_axis=0, concat_axis=0, tiled=True)
    down_grad = jnp.einsum(
        "secd,secf->edf", grad_produced, inner_act, preferred_element_type=jnp.float32
    )
    grad_inner = jnp.einsum(
        "secd,edf->secf", grad_produced, w_down, preferred_element_type=jnp.float32
    )
    grad_gate_pre = gelu_pullback(grad_inner * up_pre)[0].astype(jnp.bfloat16)
    grad_up_pre = (grad_inner * active).astype(jnp.bfloat16)
    gate_grad = jnp.einsum(
        "secd,secf->edf", arrived, grad_gate_pre, preferred_element_type=jnp.float32
    )
    up_grad = jnp.einsum("secd,secf->edf", arrived, grad_up_pre, preferred_element_type=jnp.float32)
    grad_arrived = jnp.einsum(
        "secf,edf->secd", grad_gate_pre, w_gate, preferred_element_type=jnp.float32
    )
    grad_arrived = (
        grad_arrived
        + jnp.einsum("secf,edf->secd", grad_up_pre, w_up, preferred_element_type=jnp.float32)
    ).astype(jnp.bfloat16)
    grad_sent = lax.all_to_all(grad_arrived, "ep", split_axis=0, concat_axis=0, tiled=True).reshape(
        experts * capacity, model_width
    )
    grad_rows = jnp.einsum("jr,jd->rd", dispatch, grad_sent, preferred_element_type=jnp.float32)
    choice_grads = gate_grads.reshape(span_rows, pair_count, top_count) * kept_mask
    prob_grads = jnp.sum(expert_hot * choice_grads[..., None], axis=2)
    logit_grads = router_probs * (
        prob_grads - jnp.sum(router_probs * prob_grads, axis=-1, keepdims=True)
    )
    logit_grads = logit_grads.astype(jnp.bfloat16)
    router_grad = jnp.einsum(
        "csd,cse->de", normed_second, logit_grads, preferred_element_type=jnp.float32
    )
    grad_normed_second = grad_rows.reshape(span_rows, pair_count, model_width)
    grad_normed_second = grad_normed_second + jnp.einsum(
        "cse,de->csd", logit_grads, w_router, preferred_element_type=jnp.float32
    )
    gain_second_grad = jnp.sum(grad_normed_second * hidden * scale_second, axis=(0, 1))
    grad_hidden = grad_out.reshape(span_rows, pair_count, model_width) + norm_back(
        grad_normed_second, hidden, scale_second, norm2_gain
    )
    grad_proj = (live_mask[..., None] * grad_hidden).astype(jnp.bfloat16)
    out_grad = jnp.einsum(
        "csd,cse->de", attended_low, grad_proj, preferred_element_type=jnp.float32
    )
    grad_att = jnp.einsum(
        "cse,de->csd", grad_proj, w_out, preferred_element_type=jnp.float32
    ).astype(jnp.bfloat16)
    grad_att_heads = grad_att.reshape(span_rows, pair_count, head_count, head_size)
    row_terms = jnp.sum(
        grad_att_heads.astype(jnp.float32)
        * attended.reshape(span_rows, pair_count, head_count, head_size),
        axis=-1,
    )
    row_terms = row_terms.transpose(1, 2, 0)
    keyval_back = lax.all_gather(keyval, "cp", axis=0, tiled=True)
    back_blocks = keyval_back.reshape(n_cp, span_rows, pair_count, 2 * model_width)

    def pair_terms(
        query_rows, grad_rows_att, row_part, total_part, key_rows, value_rows, key_start, rows_pos
    ):
        logits, steps = block_logits(
            query_rows, key_rows, key_start, rows_pos, lengths, table_step, rise_points, head_scale
        )
        weights = jnp.exp(logits - total_part[..., None])
        weight_grads = jnp.einsum(
            "qshd,kshd->shqk", grad_rows_att, value_rows, preferred_element_type=jnp.float32
        )
        score_grads = weights * (weight_grads - row_part[..., None])
        return (weights, score_grads, steps)

    def query_side_step(state_pair, kv_block, block_start):
        query_grad, step_grad = state_pair
        key_rows, value_rows = split_kv(kv_block)
        weights, score_grads, steps = pair_terms(
            queries,
            grad_att_heads,
            row_terms,
            log_total,
            key_rows,
            value_rows,
            block_start,
            query_pos,
        )
        low_grads = score_grads.astype(jnp.bfloat16)
        query_grad = (
            query_grad
            + jnp.einsum("shqk,kshd->qshd", low_grads, key_rows, preferred_element_type=jnp.float32)
            * head_scale
        )
        step_grad = step_grad + jnp.einsum(
            "hqk,qkb->hb", jnp.sum(score_grads, axis=0), steps, precision=lax.Precision.HIGHEST
        )
        return ((query_grad, step_grad), weights, low_grads)

    start_state = (
        jnp.zeros((span_rows, pair_count, head_count, head_size), jnp.float32),
        jnp.zeros((head_count, bucket_count), jnp.float32),
    )

    def grad_step(state_pair, block_item):
        kv_block, block_start = block_item
        new_state, weights, low_grads = query_side_step(state_pair, kv_block, block_start)
        value_grad = jnp.einsum(
            "shqk,qshd->kshd",
            weights.astype(jnp.bfloat16),
            grad_att_heads,
            preferred_element_type=jnp.float32,
        )
        key_grad = (
            jnp.einsum("shqk,qshd->kshd", low_grads, queries, preferred_element_type=jnp.float32)
            * head_scale
        )
        block_grad = jnp.concatenate(
            [
                key_grad.reshape(span_rows, pair_count, model_width),
                value_grad.reshape(span_rows, pair_count, model_width),
            ],
            axis=-1,
        )
        return (new_state, block_grad)

    (query_grad, step_grad), kv_terms = lax.scan(
        grad_step, start_state, (back_blocks, block_starts)
    )
    kv_terms = kv_terms.reshape(seq_len, pair_count, 2 * model_width)
    keyval_grad = lax.psum_scatter(
        kv_terms.astype(jnp.bfloat16), "cp", scatter_dimension=0, tiled=True
    )
    table_grad = step_grad - jnp.concatenate(
        [step_grad[:, 1:], jnp.zeros((head_count, 1), jnp.float32)], axis=1
    )
    qkv_grad = jnp.concatenate(
        [query_grad.reshape(span_rows, pair_count, model_width).astype(jnp.bfloat16), keyval_grad],
        axis=-1,
    )
    qkv_weight_grad = jnp.einsum(
        "csd,cse->de", normed_first, qkv_grad, preferred_element_type=jnp.float32
    )
    grad_normed_first = jnp.einsum(
        "cse,de->csd", qkv_grad, w_qkv, preferred_element_type=jnp.float32
    )
    gain_first_grad = jnp.sum(grad_normed_first * inputs * scale_first, axis=(0, 1))
    tokens_grad = (
        grad_hidden + norm_back(grad_normed_first, inputs, scale_first, norm1_gain)
    ).astype(jnp.bfloat16)
    attn_term = jnp.concatenate([qkv_weight_grad, out_grad], axis=1)
    w_attn_grad = lax.psum_scatter(attn_term, ("dp", "ep", "cp"), scatter_dimension=1, tiled=True)
    router_sum, table_sum, gain_first_sum, gain_second_sum = lax.psum(
        (router_grad, table_grad, gain_first_grad, gain_second_grad), ("dp", "ep", "cp")
    )
    gate_sum, up_sum, down_sum = (
        lax.psum_scatter(
            gate_grad.astype(jnp.bfloat16), ("dp", "cp"), scatter_dimension=2, tiled=True
        ).astype(jnp.float32),
        lax.psum_scatter(
            up_grad.astype(jnp.bfloat16), ("dp", "cp"), scatter_dimension=2, tiled=True
        ).astype(jnp.float32),
        lax.psum_scatter(
            down_grad.astype(jnp.bfloat16), ("dp", "cp"), scatter_dimension=2, tiled=True
        ).astype(jnp.float32),
    )
    return (
        mixed,
        tokens_grad,
        w_attn_grad,
        table_sum,
        gain_first_sum,
        gain_second_sum,
        router_sum,
        gate_sum,
        up_sum,
        down_sum,
    )


minus_big = -1000000000.0
vmem_bytes = 56 * 1024 * 1024


def compiler_params():
    return pltpu.CompilerParams(vmem_limit_bytes=vmem_bytes)


def shear(values, leftward):
    rows, lanes = values.shape
    row_ids = lax.broadcasted_iota(jnp.int32, (rows, lanes), 0)
    bit = 1
    while bit < rows:
        amount = lanes - bit if leftward else bit
        moved = pltpu.roll(values, amount, 1)
        values = jnp.where((row_ids & bit) != 0, moved, values)
        bit *= 2
    return values


def bias_kernel(line_ref, bias_ref):
    rows, columns = bias_ref.shape[1], bias_ref.shape[2]
    lanes = rows + columns
    line = pltpu.roll(line_ref[0], lanes - (rows - 1), 1)
    full = jnp.broadcast_to(line, (rows, lanes))
    bias_ref[0] = shear(full, False)[:, :columns]


def make_bias(lines, span_rows):
    heads, _, lanes = lines.shape
    columns = lanes - span_rows
    return pl.pallas_call(
        bias_kernel,
        grid=(heads,),
        in_specs=[pl.BlockSpec((1, 1, lanes), lambda h: (h, 0, 0))],
        out_specs=pl.BlockSpec((1, span_rows, columns), lambda h: (h, 0, 0)),
        out_shape=jax.ShapeDtypeStruct((heads, span_rows, columns), jnp.float32),
        compiler_params=compiler_params(),
        name="bias_planes",
    )(lines)


def dot_nt(left, right):
    return lax.dot_general(
        left, right, (((1,), (1,)), ((), ())), preferred_element_type=jnp.float32
    )


def dot_tn(left, right):
    return lax.dot_general(
        left, right, (((0,), (0,)), ((), ())), preferred_element_type=jnp.float32
    )


def dot_nn(left, right):
    return jnp.dot(left, right, preferred_element_type=jnp.float32)


def key_masks(length, blocks, span_rows):
    masks = []
    for block in range(blocks):
        position = block * span_rows + lax.broadcasted_iota(jnp.int32, (1, span_rows), 1)
        masks.append(jnp.where(position < length, 0.0, minus_big))
    return masks


def forward_kernel(
    scale, head_size, meta_ref, q_ref, k_ref, v_ref, bias_ref, low_ref, full_ref, total_ref
):
    blocks, span_rows, lanes = q_ref.shape
    mine, length = meta_ref[0], meta_ref[1]
    lane = lax.broadcasted_iota(jnp.int32, (1, lanes), 1)
    masks = key_masks(length, blocks, span_rows)

    def place(block):
        return lax.rem(mine - block + blocks, blocks)

    for row in range(blocks):
        queries = q_ref[place(row)]
        totals = jnp.zeros((span_rows, lanes), jnp.float32)
        result = jnp.zeros((span_rows, lanes), jnp.float32)
        for half in range(lanes // head_size):
            own = lane // head_size == half
            head_q = queries * jnp.where(own, scale, 0.0).astype(jnp.bfloat16)
            head_v = jnp.where(own, 1.0, 0.0).astype(jnp.bfloat16)
            logits = []
            for column in range(row + 1):
                at = (blocks - 1 - row + column) * span_rows
                part = dot_nt(head_q, k_ref[place(column)])
                part = part + bias_ref[half, :, at : at + span_rows] + masks[column]
                logits.append(part)
            peak = jnp.max(logits[0], axis=1, keepdims=True)
            for part in logits[1:]:
                peak = jnp.maximum(peak, jnp.max(part, axis=1, keepdims=True))
            total = jnp.zeros((span_rows, 1), jnp.float32)
            mixed = jnp.zeros((span_rows, lanes), jnp.float32)
            for column in range(row + 1):
                weights = jnp.exp(logits[column] - peak)
                total = total + jnp.sum(weights, axis=1, keepdims=True)
                mixed = mixed + dot_nn(
                    weights.astype(jnp.bfloat16), v_ref[place(column)] * head_v
                )
            result = result + mixed / total
            totals = jnp.where(lane == half, peak + jnp.log(total), totals)
        low_ref[row] = result.astype(jnp.bfloat16)
        full_ref[row] = result
        total_ref[row] = totals


def attend_forward(meta, qkv, bias, scale, head_size):
    blocks, span_rows, width = qkv.shape
    pairs = width // (3 * 128)
    per_pair = bias.shape[0] // pairs

    def part(which):
        return pl.BlockSpec((blocks, span_rows, 128), lambda p, which=which: (0, 0, 3 * p + which))

    plain = pl.BlockSpec((blocks, span_rows, 128), lambda p: (0, 0, p))

    return pl.pallas_call(
        functools.partial(forward_kernel, scale, head_size),
        grid=(pairs,),
        in_specs=[
            pl.BlockSpec(memory_space=pltpu.SMEM),
            part(0),
            part(1),
            part(2),
            pl.BlockSpec((per_pair,) + bias.shape[1:], lambda p: (p, 0, 0)),
        ],
        out_specs=[plain, plain, plain],
        out_shape=[
            jax.ShapeDtypeStruct((blocks, span_rows, pairs * 128), jnp.bfloat16),
            jax.ShapeDtypeStruct((blocks, span_rows, pairs * 128), jnp.float32),
            jax.ShapeDtypeStruct((blocks, span_rows, pairs * 128), jnp.float32),
        ],
        compiler_params=compiler_params(),
        name="attend_forward",
    )(meta, qkv, qkv, qkv, bias)


def backward_kernel(
    scale,
    head_size,
    meta_ref,
    q_ref,
    k_ref,
    v_ref,
    bias_ref,
    grad_ref,
    full_ref,
    total_ref,
    sent_ref,
    ring_ref,
    line_ref,
    key_sum,
    value_sum,
    plane,
):
    blocks, span_rows, lanes = q_ref.shape
    mine, length = meta_ref[0], meta_ref[1]
    lane = lax.broadcasted_iota(jnp.int32, (1, lanes), 1)
    masks = key_masks(length, blocks, span_rows)
    halves = lanes // head_size

    def place(block):
        return lax.rem(mine - block + blocks, blocks)

    key_sum[...] = jnp.zeros_like(key_sum)
    value_sum[...] = jnp.zeros_like(value_sum)
    plane[...] = jnp.zeros_like(plane)
    for row in range(blocks):
        queries = q_ref[place(row)]
        grads = grad_ref[row]
        products = grads.astype(jnp.float32) * full_ref[row]
        totals = total_ref[row]
        query_sum = jnp.zeros((span_rows, lanes), jnp.float32)
        for half in range(halves):
            own = lane // head_size == half
            one = jnp.where(own, 1.0, 0.0).astype(jnp.bfloat16)
            head_q = queries * jnp.where(own, scale, 0.0).astype(jnp.bfloat16)
            head_g = grads * one
            delta = jnp.sum(jnp.where(own, products, 0.0), axis=1, keepdims=True)
            total = totals[:, half : half + 1]
            for column in range(row + 1):
                at = (blocks - 1 - row + column) * span_rows
                keys = k_ref[place(column)]
                logits = dot_nt(head_q, keys)
                logits = logits + bias_ref[half, :, at : at + span_rows] + masks[column]
                weights = jnp.exp(logits - total)
                weight_grads = dot_nt(head_g, v_ref[place(column)])
                score_grads = weights * (weight_grads - delta)
                plane[half, :, at : at + span_rows] += score_grads
                low_weights = weights.astype(jnp.bfloat16)
                low_grads = score_grads.astype(jnp.bfloat16)
                query_sum = query_sum + dot_nn(low_grads, keys * one)
                key_sum[column] += dot_tn(low_grads, head_q)
                value_sum[column] += dot_tn(low_weights, head_g)
        result = (query_sum * scale).astype(jnp.bfloat16)
        sent_ref[row, :, :lanes] = result
        ring_ref[place(row), :, :lanes] = result
    for row in range(blocks):
        result = key_sum[row].astype(jnp.bfloat16)
        sent_ref[row, :, lanes : 2 * lanes] = result
        ring_ref[place(row), :, lanes : 2 * lanes] = result
        result = value_sum[row].astype(jnp.bfloat16)
        sent_ref[row, :, 2 * lanes :] = result
        ring_ref[place(row), :, 2 * lanes :] = result
    for half in range(halves):
        full = jnp.concatenate(
            [plane[half], jnp.zeros((span_rows, span_rows), jnp.float32)], axis=1
        )
        summed = jnp.sum(shear(full, True), axis=0, keepdims=True)
        line_ref[half] = pltpu.roll(summed, span_rows - 1, 1)


def attend_backward(meta, qkv, bias, grads, full, totals, scale, head_size):
    blocks, span_rows, width = qkv.shape
    pairs = width // (3 * 128)
    per_pair = bias.shape[0] // pairs
    lanes = bias.shape[2] + span_rows

    def part(which):
        return pl.BlockSpec((blocks, span_rows, 128), lambda p, which=which: (0, 0, 3 * p + which))

    plain = pl.BlockSpec((blocks, span_rows, 128), lambda p: (0, 0, p))
    wide = pl.BlockSpec((blocks, span_rows, 384), lambda p: (0, 0, p))
    return pl.pallas_call(
        functools.partial(backward_kernel, scale, head_size),
        grid=(pairs,),
        in_specs=[
            pl.BlockSpec(memory_space=pltpu.SMEM),
            part(0),
            part(1),
            part(2),
            pl.BlockSpec((per_pair,) + bias.shape[1:], lambda p: (p, 0, 0)),
            plain,
            plain,
            plain,
        ],
        out_specs=[wide, wide, pl.BlockSpec((per_pair, 1, lanes), lambda p: (p, 0, 0))],
        out_shape=[
            jax.ShapeDtypeStruct(qkv.shape, jnp.bfloat16),
            jax.ShapeDtypeStruct(qkv.shape, jnp.bfloat16),
            jax.ShapeDtypeStruct((bias.shape[0], 1, lanes), jnp.float32),
        ],
        scratch_shapes=[
            pltpu.VMEM((blocks, span_rows, 128), jnp.float32),
            pltpu.VMEM((blocks, span_rows, 128), jnp.float32),
            pltpu.VMEM((per_pair,) + bias.shape[1:], jnp.float32),
        ],
        compiler_params=compiler_params(),
        name="attend_backward",
    )(meta, qkv, qkv, qkv, bias, grads, full, totals)


gelu_inner = 0.7978845608028654
gelu_cubic = 0.044715


def expert_kernel(
    experts,
    expert_ref,
    rows_ref,
    grads_ref,
    router_ref,
    gate_ref,
    up_ref,
    down_ref,
    back_ref,
    out_ref,
    weight_ref,
    total,
):
    step = pl.program_id(0)
    model_width = rows_ref.shape[1]
    pieces, _, piece, _ = weight_ref.shape
    rows, grads = rows_ref[...], grads_ref[...]
    lane = lax.broadcasted_iota(jnp.int32, (1, router_ref.shape[1]), 1)
    expert = expert_ref[0]
    router = jnp.where(lane < experts, dot_nn(rows, router_ref[...]), minus_big)
    router = jnp.exp(router - jnp.max(router, axis=1, keepdims=True))
    gates = jnp.sum(jnp.where(lane == expert, router, 0.0), axis=1, keepdims=True) / jnp.sum(
        router, axis=1, keepdims=True
    )
    gate_pre = dot_nn(rows, gate_ref[...])
    up_pre = dot_nn(rows, up_ref[...])
    square = gate_pre * gate_pre
    tanh = jnp.tanh(gelu_inner * gate_pre * (1.0 + gelu_cubic * square))
    half = 0.5 + 0.5 * tanh
    active = gate_pre * half
    slope = half + active * (1.0 - tanh) * (
        gelu_inner * (1.0 + 3.0 * gelu_cubic * square)
    )
    inner = active * up_pre
    low_inner = inner.astype(jnp.bfloat16)
    plain_grads = dot_nn(grads, down_ref[...])
    gate_grads = jnp.sum(plain_grads * low_inner.astype(jnp.float32), axis=1, keepdims=True)
    inner_grads = plain_grads * gates
    low_gate = (inner_grads * up_pre * slope).astype(jnp.bfloat16)
    low_up = (inner_grads * active).astype(jnp.bfloat16)
    gated = (inner * gates).astype(jnp.bfloat16)
    back = dot_nt(low_gate, gate_ref[...]) + dot_nt(low_up, up_ref[...])
    back_ref[:, :model_width] = back.astype(jnp.bfloat16)
    back_ref[:, model_width:] = jnp.where(lane == expert, gate_grads, 0.0).astype(jnp.bfloat16)
    out_ref[...] = (gates * dot_nt(low_inner, down_ref[...])).astype(jnp.bfloat16)

    @pl.when(step == 0)
    def _():
        total[...] = jnp.zeros_like(total)

    total[0] += dot_tn(low_gate, rows)
    total[1] += dot_tn(low_up, rows)
    total[2] += dot_tn(gated, grads)

    @pl.when(step == pl.num_programs(0) - 1)
    def _():
        for at in range(pieces):
            weight_ref[at] = total[:, at * piece : (at + 1) * piece].astype(jnp.bfloat16)


def run_expert(expert, rows, grads, router, gate_w, up_w, down_w, experts, pieces, tile):
    count, model_width = rows.shape
    hidden_units = gate_w.shape[1]
    whole = lambda shape: pl.BlockSpec(shape, lambda i: (0,) * len(shape))
    tiled = lambda width: pl.BlockSpec((tile, width), lambda i: (i, 0))
    grad_shape = (pieces, 3, hidden_units // pieces, model_width)
    return pl.pallas_call(
        functools.partial(expert_kernel, experts),
        grid=(count // tile,),
        in_specs=[
            pl.BlockSpec(memory_space=pltpu.SMEM),
            tiled(model_width),
            tiled(model_width),
            whole(router.shape),
            whole(gate_w.shape),
            whole(up_w.shape),
            whole(down_w.shape),
        ],
        out_specs=[tiled(model_width + 128), tiled(model_width), whole(grad_shape)],
        out_shape=[
            jax.ShapeDtypeStruct((count, model_width + 128), jnp.bfloat16),
            jax.ShapeDtypeStruct((count, model_width), jnp.bfloat16),
            jax.ShapeDtypeStruct(grad_shape, jnp.bfloat16),
        ],
        scratch_shapes=[pltpu.VMEM((3, hidden_units, model_width), jnp.float32)],
        compiler_params=compiler_params(),
        name="expert_rows",
    )(expert, rows, grads, router, gate_w, up_w, down_w)


def send(values, axis, pairs):
    return lax.ppermute(values, axis, pairs)


def fast_device(
    tokens,
    lengths,
    expert_ids,
    places,
    buckets,
    w_attn,
    bias_table,
    norm1_gain,
    norm2_gain,
    w_router,
    w_gate,
    w_up,
    w_down,
    cotangent,
):
    span_rows, slots, model_width = tokens.shape
    head_count, bucket_count = bias_table.shape
    head_size = model_width // head_count
    scale = head_size ** (-0.5)
    n_dp = lax.axis_size("dp")
    n_ep = lax.axis_size("ep")
    n_cp = lax.axis_size("cp")
    my_dp, my_ep, my_cp = (lax.axis_index(name) for name in ("dp", "ep", "cp"))
    seq_len = span_rows * n_cp
    rows = span_rows * slots
    top_count = expert_ids.shape[2]
    experts = w_router.shape[1]
    exp_dev = w_gate.shape[0]
    units = w_gate.shape[2] // n_dp
    piece = units // n_cp
    capacity = (5 * rows * top_count + 4 * experts - 1) // (4 * experts)
    groups = model_width // (128 * n_cp)
    own_width = 3 * groups * 128
    heads_own = head_count // n_cp
    over_core = [(i, i ^ 1) for i in range(n_dp)]
    over_x = [(i, i ^ 2) for i in range(n_dp)]
    over_y = [(i, i ^ 1) for i in range(n_ep)]
    ring = [(i, (i + 1) % n_cp) for i in range(n_cp)]
    f32, bf16 = jnp.float32, jnp.bfloat16

    slot_tokens = tokens.transpose(1, 0, 2).astype(f32)
    scale_first = root_scale(slot_tokens)
    normed_first = (slot_tokens * scale_first * norm1_gain).astype(bf16)

    def ring_gather(values):
        parts = [values]
        for _ in range(n_cp - 1):
            parts.append(send(parts[-1], "cp", ring))
        return jnp.stack(parts)

    normed_all = [ring_gather(normed_first[s]) for s in range(slots)]

    w_qkv = (
        w_attn[:, : 3 * model_width]
        .reshape(model_width, 3, groups, n_cp, 128)
        .transpose(0, 3, 2, 1, 4)
        .reshape(model_width, 3 * model_width)
    )
    w_own = lax.dynamic_slice(w_qkv, (0, my_cp * own_width), (model_width, own_width))
    w_out = (
        w_attn[:, 3 * model_width :]
        .reshape(groups, n_cp, 128, model_width)
        .transpose(1, 0, 2, 3)
        .reshape(model_width, model_width)
    )
    per_group = 128 // head_size
    own_heads = (
        jnp.arange(groups)[:, None] * (n_cp * per_group)
        + my_cp * per_group
        + jnp.arange(per_group)[None, :]
    ).reshape(heads_own)
    head_hot = (own_heads[:, None] == jnp.arange(head_count)[None, :]).astype(f32)
    bucket_hot = (buckets[:, None] == jnp.arange(bucket_count)[None, :]).astype(f32)
    exact = lax.Precision.HIGHEST
    own_table = jnp.dot(head_hot, bias_table, precision=exact)
    lines = jnp.einsum("hb,db->hd", own_table, bucket_hot[::-1], precision=exact)
    lines = jnp.concatenate([lines, jnp.full((heads_own, span_rows), minus_big, f32)], axis=1)
    bias = make_bias(lines[:, None, :], span_rows)

    def plane_gather(values):
        over = send(values, "dp", over_x)
        up = send(values, "ep", over_y)
        half = values.shape[0] // 2
        across = jnp.concatenate(
            [send(over[:half], "ep", over_y), send(up[half:], "dp", over_x)], axis=0
        )
        return [values, over, up, across]

    target = jnp.where(places >= 0, expert_ids * capacity + places, -1)
    target = target.transpose(2, 1, 0).reshape(top_count, rows)
    targets = plane_gather(target)
    row_ids = my_ep * (exp_dev * capacity) + jnp.arange(exp_dev * capacity, dtype=jnp.int32)

    def hot_rows(chosen):
        hot = jnp.zeros((exp_dev * capacity, rows), f32)
        for c in range(top_count):
            hot = hot + (row_ids[:, None] == chosen[c][None, :]).astype(f32)
        return hot.astype(bf16)

    hots = [hot_rows(chosen) for chosen in targets]

    def pick_rows(blocks):
        picked = [
            jnp.dot(hot, block, preferred_element_type=f32).astype(bf16)
            for hot, block in zip(hots, blocks)
        ]
        mine = jnp.stack(picked)
        theirs = send(mine, "dp", over_core)
        whole = jnp.stack([mine, theirs]).reshape(2 * len(blocks), exp_dev, capacity, model_width)
        return [whole[:, e].reshape(-1, model_width) for e in range(exp_dev)]

    low_out = cotangent.transpose(1, 0, 2)
    grad_out = low_out.astype(f32).reshape(rows, model_width)
    grad_picked = pick_rows(plane_gather(low_out.reshape(rows, model_width)))
    units_at = my_dp * units
    gate_own = lax.dynamic_slice_in_dim(w_gate, units_at, units, axis=2)
    up_own = lax.dynamic_slice_in_dim(w_up, units_at, units, axis=2)
    down_own = lax.dynamic_slice_in_dim(w_down, units_at, units, axis=2)
    router_wide = jnp.concatenate(
        [w_router, jnp.zeros((model_width, 128 - experts), w_router.dtype)], axis=1
    )

    metas = [jnp.stack([my_cp.astype(jnp.int32), lengths[s]]) for s in range(slots)]
    qkvs, fulls, totals, returned = [], [], [], []
    for s in range(slots):
        qkv = jnp.dot(
            normed_all[s].reshape(seq_len, model_width), w_own, preferred_element_type=f32
        )
        qkv = qkv.astype(bf16).reshape(n_cp, span_rows, own_width)
        low, full, total = attend_forward(metas[s], qkv, bias, scale, head_size)
        qkvs.append(qkv)
        fulls.append(full)
        totals.append(total)
        back = lax.all_to_all(low, "cp", split_axis=0, concat_axis=0, tiled=True)
        returned.append(back.transpose(1, 0, 2).reshape(span_rows, model_width))
    attended = jnp.concatenate(returned, axis=0)
    projected = jnp.dot(attended, w_out, preferred_element_type=f32)
    positions = my_cp * span_rows + jnp.arange(span_rows, dtype=jnp.int32)
    live = (positions[None, :] < lengths[:, None]).astype(f32).reshape(rows, 1)
    inputs = slot_tokens.reshape(rows, model_width)
    hidden = inputs + live * projected
    scale_second = root_scale(hidden)
    normed_second = (hidden * scale_second * norm2_gain).astype(bf16)
    router_logits = jnp.dot(normed_second, w_router, preferred_element_type=f32)
    router_probs = jax.nn.softmax(router_logits, axis=-1)

    rows_picked = pick_rows(plane_gather(normed_second))
    sources = len(hots)

    def combine(per_expert, e):
        mine, theirs = per_expert[: sources * capacity], per_expert[sources * capacity :]
        theirs = send(theirs, "dp", over_core)
        both = (mine.astype(f32) + theirs.astype(f32)).astype(bf16)
        both = both.reshape(sources, capacity, -1)
        at = e * capacity
        return [dot_tn(hots[k][at : at + capacity], both[k]) for k in range(sources)]

    def plane_sum(blocks):
        here, over, up, across = blocks
        half = rows // 2
        got = send(jnp.stack([over[:half], across[:half]]), "dp", over_x).astype(f32)
        first, next_first = here[:half] + got[0], up[:half] + got[1]
        got = send(jnp.stack([up[half:], across[half:]]), "ep", over_y).astype(f32)
        second, next_second = here[half:] + got[0], over[half:] + got[1]
        first = first + send(next_first.astype(bf16), "ep", over_y).astype(f32)
        second = second + send(next_second.astype(bf16), "dp", over_x).astype(f32)
        return jnp.concatenate([first, second], axis=0)

    back_parts, out_parts, weight_sums = [], [], []
    for e in range(exp_dev):
        expert = (my_ep * exp_dev + e).astype(jnp.int32).reshape(1)
        back, out, weight = run_expert(
            expert,
            rows_picked[e],
            grad_picked[e],
            router_wide,
            gate_own[e],
            up_own[e],
            down_own[e],
            experts,
            n_cp,
            2 * capacity,
        )
        weight_sums.append(lax.psum_scatter(weight, "cp", scatter_dimension=0, tiled=False))
        back_parts.append(combine(back, e))
        out_parts.append(combine(out, e))

    def merged(parts):
        return plane_sum(
            [sum(part[k] for part in parts).astype(bf16) for k in range(sources)]
        )

    back_rows = merged(back_parts)
    mixed = hidden + merged(out_parts)
    mixed = mixed.astype(bf16).reshape(slots, span_rows, model_width).transpose(1, 0, 2)

    prob_grads = back_rows[:, model_width : model_width + experts]
    logit_grads = router_probs * (
        prob_grads - jnp.sum(router_probs * prob_grads, axis=-1, keepdims=True)
    )
    logit_grads = logit_grads.astype(bf16)
    router_grad = dot_tn(normed_second, logit_grads)
    grad_normed_second = back_rows[:, :model_width] + dot_nt(logit_grads, w_router)
    gain_second_grad = jnp.sum(grad_normed_second * hidden * scale_second, axis=0)
    grad_hidden = grad_out + norm_back(grad_normed_second, hidden, scale_second, norm2_gain)
    grad_proj = (live * grad_hidden).astype(bf16)
    grad_att = dot_nt(grad_proj, w_out).astype(bf16)

    sents, rings = [], []
    line_grads = jnp.zeros((heads_own, seq_len + span_rows), f32)
    for s in range(slots):
        leaving = grad_att[s * span_rows : (s + 1) * span_rows]
        leaving = leaving.reshape(span_rows, n_cp, groups * 128).transpose(1, 0, 2)
        grads = lax.all_to_all(leaving, "cp", split_axis=0, concat_axis=0, tiled=True)
        sent, ringed, line = attend_backward(
            metas[s], qkvs[s], bias, grads, fulls[s], totals[s], scale, head_size
        )
        line_grads = line_grads + line[:, 0]
        rings.append(ringed.reshape(seq_len, own_width))
        sent = lax.all_to_all(sent, "cp", split_axis=0, concat_axis=0, tiled=True)
        sents.append(sent.transpose(1, 0, 2).reshape(span_rows, 3 * model_width))

    out_grad = dot_tn(attended, grad_proj).astype(bf16)
    out_grad = out_grad.reshape(n_cp, groups, 128, n_ep, n_cp, 128)
    out_grad = out_grad.transpose(4, 3, 1, 0, 2, 5).reshape(n_cp, n_ep, model_width, 128)
    out_grad = lax.psum_scatter(out_grad, "cp", scatter_dimension=0, tiled=False)
    qkv_grad = sum(
        dot_tn(normed_all[s].reshape(seq_len, model_width), rings[s]) for s in range(slots)
    )
    gain_first_grad = jnp.sum(qkv_grad * w_own.astype(f32), axis=1) / norm1_gain
    attn_term = qkv_grad.reshape(model_width, groups, 3, 128).transpose(2, 1, 0, 3)
    attn_term = jnp.concatenate(
        [attn_term.reshape(3 * groups, model_width, 128).astype(bf16), out_grad], axis=0
    )
    attn_sum = lax.psum_scatter(attn_term, ("dp", "ep"), scatter_dimension=0, tiled=False)
    distance_grads = line_grads[:, :seq_len][:, ::-1]
    table_grad = jnp.dot(distance_grads, bucket_hot, precision=exact)
    table_grad = jnp.einsum("hg,hb->gb", head_hot, table_grad, precision=exact)
    router_sum, table_sum, gain_first_sum, gain_second_sum = lax.psum(
        (router_grad, table_grad, gain_first_grad, gain_second_grad), ("dp", "ep", "cp")
    )

    grad_normed_first = dot_nt(jnp.concatenate(sents, axis=0), w_qkv)
    tokens_grad = grad_hidden + norm_back(
        grad_normed_first, inputs, scale_first.reshape(rows, 1), norm1_gain
    )
    tokens_grad = tokens_grad.astype(bf16).reshape(slots, span_rows, model_width).transpose(1, 0, 2)
    weight_all = jnp.stack(weight_sums)
    gate_sum, up_sum, down_sum = (
        weight_all[:, which].transpose(0, 2, 1).astype(f32) for which in range(3)
    )
    return (
        mixed,
        tokens_grad,
        attn_sum.astype(f32),
        table_sum,
        gain_first_sum,
        gain_second_sum,
        router_sum,
        gate_sum,
        up_sum,
        down_sum,
    )


def solution(mesh):
    placed = (
        P("cp", ("dp", "ep"), None),
        P(("dp", "ep")),
        P("cp", ("dp", "ep"), None),
        P("cp", ("dp", "ep"), None),
        P(),
        P(),
        P(),
        P(),
        P(),
        P(),
        P("ep", None, None),
        P("ep", None, None),
        P("ep", None, None),
        P("cp", ("dp", "ep"), None),
    )
    sizes = dict(mesh.shape)
    square = sizes["dp"] == 4 and sizes["ep"] == 2 and sizes["cp"] == 4
    return jax.shard_map(
        fast_device if square else on_device,
        mesh=mesh,
        in_specs=placed,
        out_specs=(
            P("cp", ("dp", "ep"), None),
            P("cp", ("dp", "ep"), None),
            P(None, ("dp", "ep", "cp")),
            P(),
            P(),
            P(),
            P(),
            P("ep", None, ("dp", "cp")),
            P("ep", None, ("dp", "cp")),
            P("ep", None, ("dp", "cp")),
        ),
        check_vma=False,
    )
```

```python
import functools

import jax
import jax.numpy as jnp
from jax import lax
from jax.experimental import pallas as pl
from jax.experimental.pallas import tpu as pltpu
from jax.sharding import PartitionSpec as P

epsilon = 1e-06
masked_value = -1000000000.0


def gelu_tanh(values):
    return jax.nn.gelu(values, approximate=True)


def root_scale(values):
    return lax.rsqrt(jnp.mean(values * values, axis=-1, keepdims=True) + epsilon)


def norm_back(grad_in, values, scale_rows, gain_vector):
    scaled = grad_in * gain_vector
    inner_mean = jnp.mean(scaled * values, axis=-1, keepdims=True)
    return scale_rows * (scaled - values * scale_rows * scale_rows * inner_mean)


def block_logits(
    queries, key_rows, key_start, query_pos, lengths, table_step, rise_points, head_scale
):
    key_count = key_rows.shape[0]
    key_pos = key_start + jnp.arange(key_count, dtype=jnp.int32)
    scores = (
        jnp.einsum("qshd,kshd->shqk", queries, key_rows, preferred_element_type=jnp.float32)
        * head_scale
    )
    distance = query_pos[:, None] - key_pos[None, :]
    steps = (distance[:, :, None] >= rise_points[None, None, :]).astype(jnp.float32)
    pair_bias = jnp.einsum("hb,qkb->hqk", table_step, steps, precision=lax.Precision.HIGHEST)
    allowed = (distance >= 0)[None, :, :] & (key_pos[None, None, :] < lengths[:, None, None])
    logits = jnp.where(allowed[:, None], scores + pair_bias[None], masked_value)
    return (logits, steps)


def on_device(
    tokens,
    lengths,
    expert_ids,
    places,
    buckets,
    w_attn,
    bias_table,
    norm1_gain,
    norm2_gain,
    w_router,
    w_gate,
    w_up,
    w_down,
    cotangent,
):
    span_rows, pair_count, model_width = tokens.shape
    head_count, bucket_count = bias_table.shape
    head_size = model_width // head_count
    head_scale = head_size ** (-0.5)
    n_cp = lax.axis_size("cp")
    n_ep = lax.axis_size("ep")
    seq_len = span_rows * n_cp
    row_count = span_rows * pair_count
    top_count = expert_ids.shape[2]
    experts = w_router.shape[1]
    exp_dev = w_gate.shape[0]
    capacity = (5 * row_count * top_count + 4 * experts - 1) // (4 * experts)
    my_start = lax.axis_index("cp") * span_rows
    query_pos = my_start + jnp.arange(span_rows, dtype=jnp.int32)
    live_mask = (query_pos[:, None] < lengths[None, :]).astype(jnp.float32)
    inputs = tokens.astype(jnp.float32)
    scale_first = root_scale(inputs)
    normed_first = (inputs * scale_first * norm1_gain).astype(jnp.bfloat16)
    w_qkv = w_attn[:, : 3 * model_width]
    w_out = w_attn[:, 3 * model_width :]
    qkv = jnp.einsum("csd,de->cse", normed_first, w_qkv, preferred_element_type=jnp.float32).astype(
        jnp.bfloat16
    )
    queries = qkv[..., :model_width].reshape(span_rows, pair_count, head_count, head_size)
    keyval = qkv[..., model_width:]
    keyval_all = lax.all_gather(keyval, "cp", axis=0, tiled=True)
    bucket_ids = jnp.arange(bucket_count, dtype=jnp.int32)
    rise_points = jnp.sum((buckets[:, None] < bucket_ids[None, :]).astype(jnp.int32), axis=0)
    table_step = jnp.concatenate(
        [bias_table[:, :1], bias_table[:, 1:] - bias_table[:, :-1]], axis=1
    )
    block_starts = jnp.arange(n_cp, dtype=jnp.int32) * span_rows

    def split_kv(kv_block):
        key_rows = kv_block[..., :model_width].reshape(span_rows, pair_count, head_count, head_size)
        value_rows = kv_block[..., model_width:].reshape(
            span_rows, pair_count, head_count, head_size
        )
        return (key_rows, value_rows)

    kv_blocks = keyval_all.reshape(n_cp, span_rows, pair_count, 2 * model_width)

    def max_step(state_pair, block_item):
        row_peak, row_total = state_pair
        kv_block, block_start = block_item
        key_rows, value_rows = split_kv(kv_block)
        logits, steps = block_logits(
            queries, key_rows, block_start, query_pos, lengths, table_step, rise_points, head_scale
        )
        new_peak = jnp.maximum(row_peak, jnp.max(logits, axis=-1))
        row_total = row_total * jnp.exp(row_peak - new_peak) + jnp.sum(
            jnp.exp(logits - new_peak[..., None]), axis=-1
        )
        return ((new_peak, row_total), None)

    stat_shape = (pair_count, head_count, span_rows)
    (row_peak, row_total), unused = lax.scan(
        max_step,
        (jnp.full(stat_shape, masked_value, jnp.float32), jnp.zeros(stat_shape, jnp.float32)),
        (kv_blocks, block_starts),
    )
    log_total = row_peak + jnp.log(row_total)

    def value_step(running, block_item):
        kv_block, block_start = block_item
        key_rows, value_rows = split_kv(kv_block)
        logits, steps = block_logits(
            queries, key_rows, block_start, query_pos, lengths, table_step, rise_points, head_scale
        )
        weights = jnp.exp(logits - log_total[..., None]).astype(jnp.bfloat16)
        return (
            running
            + jnp.einsum(
                "shqk,kshd->qshd", weights, value_rows, preferred_element_type=jnp.float32
            ),
            None,
        )

    attended, unused = lax.scan(
        value_step,
        jnp.zeros((span_rows, pair_count, head_count, head_size), jnp.float32),
        (kv_blocks, block_starts),
    )
    attended = attended.reshape(span_rows, pair_count, model_width)
    attended_low = attended.astype(jnp.bfloat16)
    projected = jnp.einsum("csd,de->cse", attended_low, w_out, preferred_element_type=jnp.float32)
    hidden = inputs + live_mask[..., None] * projected
    scale_second = root_scale(hidden)
    normed_second = (hidden * scale_second * norm2_gain).astype(jnp.bfloat16)
    router_logits = jnp.einsum(
        "csd,de->cse", normed_second, w_router, preferred_element_type=jnp.float32
    )
    router_probs = jax.nn.softmax(router_logits, axis=-1)
    expert_hot = (expert_ids[..., None] == jnp.arange(experts, dtype=jnp.int32)).astype(jnp.float32)
    kept_mask = (places >= 0).astype(jnp.float32)
    gate_values = jnp.sum(expert_hot * router_probs[:, :, None, :], axis=-1) * kept_mask
    target = jnp.where(places >= 0, expert_ids * capacity + places, -1).reshape(
        row_count, top_count
    )
    slot_ids = jnp.arange(experts * capacity, dtype=jnp.int32)
    route_hot = (target[None, :, :] == slot_ids[:, None, None]).astype(jnp.bfloat16)
    dispatch = jnp.sum(route_hot, axis=2)
    sent_rows = jnp.dot(
        dispatch, normed_second.reshape(row_count, model_width), preferred_element_type=jnp.float32
    )
    sent_rows = sent_rows.astype(jnp.bfloat16).reshape(n_ep, exp_dev, capacity, model_width)
    arrived = lax.all_to_all(sent_rows, "ep", split_axis=0, concat_axis=0, tiled=True)
    gate_pre = jnp.einsum("secd,edf->secf", arrived, w_gate, preferred_element_type=jnp.float32)
    up_pre = jnp.einsum("secd,edf->secf", arrived, w_up, preferred_element_type=jnp.float32)
    active, gelu_pullback = jax.vjp(gelu_tanh, gate_pre)
    inner_act = (active * up_pre).astype(jnp.bfloat16)
    produced = jnp.einsum(
        "secf,edf->secd", inner_act, w_down, preferred_element_type=jnp.float32
    ).astype(jnp.bfloat16)
    returned = lax.all_to_all(produced, "ep", split_axis=0, concat_axis=0, tiled=True).reshape(
        experts * capacity, model_width
    )
    picked = jnp.einsum("jrk,jd->rkd", route_hot, returned, preferred_element_type=jnp.float32)
    gate_flat = gate_values.reshape(row_count, top_count)
    mixed = hidden.reshape(row_count, model_width) + jnp.sum(gate_flat[..., None] * picked, axis=1)
    mixed = mixed.reshape(span_rows, pair_count, model_width).astype(jnp.bfloat16)
    grad_out = cotangent.astype(jnp.float32).reshape(row_count, model_width)
    gate_grads = jnp.sum(grad_out[:, None, :] * picked, axis=-1)
    sent_back = (gate_flat[..., None] * grad_out[:, None, :]).astype(jnp.bfloat16)
    scattered = jnp.einsum("jrk,rkd->jd", route_hot, sent_back, preferred_element_type=jnp.float32)
    scattered = scattered.astype(jnp.bfloat16).reshape(n_ep, exp_dev, capacity, model_width)
    grad_produced = lax.all_to_all(scattered, "ep", split_axis=0, concat_axis=0, tiled=True)
    down_grad = jnp.einsum(
        "secd,secf->edf", grad_produced, inner_act, preferred_element_type=jnp.float32
    )
    grad_inner = jnp.einsum(
        "secd,edf->secf", grad_produced, w_down, preferred_element_type=jnp.float32
    )
    grad_gate_pre = gelu_pullback(grad_inner * up_pre)[0].astype(jnp.bfloat16)
    grad_up_pre = (grad_inner * active).astype(jnp.bfloat16)
    gate_grad = jnp.einsum(
        "secd,secf->edf", arrived, grad_gate_pre, preferred_element_type=jnp.float32
    )
    up_grad = jnp.einsum("secd,secf->edf", arrived, grad_up_pre, preferred_element_type=jnp.float32)
    grad_arrived = jnp.einsum(
        "secf,edf->secd", grad_gate_pre, w_gate, preferred_element_type=jnp.float32
    )
    grad_arrived = (
        grad_arrived
        + jnp.einsum("secf,edf->secd", grad_up_pre, w_up, preferred_element_type=jnp.float32)
    ).astype(jnp.bfloat16)
    grad_sent = lax.all_to_all(grad_arrived, "ep", split_axis=0, concat_axis=0, tiled=True).reshape(
        experts * capacity, model_width
    )
    grad_rows = jnp.einsum("jr,jd->rd", dispatch, grad_sent, preferred_element_type=jnp.float32)
    choice_grads = gate_grads.reshape(span_rows, pair_count, top_count) * kept_mask
    prob_grads = jnp.sum(expert_hot * choice_grads[..., None], axis=2)
    logit_grads = router_probs * (
        prob_grads - jnp.sum(router_probs * prob_grads, axis=-1, keepdims=True)
    )
    logit_grads = logit_grads.astype(jnp.bfloat16)
    router_grad = jnp.einsum(
        "csd,cse->de", normed_second, logit_grads, preferred_element_type=jnp.float32
    )
    grad_normed_second = grad_rows.reshape(span_rows, pair_count, model_width)
    grad_normed_second = grad_normed_second + jnp.einsum(
        "cse,de->csd", logit_grads, w_router, preferred_element_type=jnp.float32
    )
    gain_second_grad = jnp.sum(grad_normed_second * hidden * scale_second, axis=(0, 1))
    grad_hidden = grad_out.reshape(span_rows, pair_count, model_width) + norm_back(
        grad_normed_second, hidden, scale_second, norm2_gain
    )
    grad_proj = (live_mask[..., None] * grad_hidden).astype(jnp.bfloat16)
    out_grad = jnp.einsum(
        "csd,cse->de", attended_low, grad_proj, preferred_element_type=jnp.float32
    )
    grad_att = jnp.einsum(
        "cse,de->csd", grad_proj, w_out, preferred_element_type=jnp.float32
    ).astype(jnp.bfloat16)
    grad_att_heads = grad_att.reshape(span_rows, pair_count, head_count, head_size)
    row_terms = jnp.sum(
        grad_att_heads.astype(jnp.float32)
        * attended.reshape(span_rows, pair_count, head_count, head_size),
        axis=-1,
    )
    row_terms = row_terms.transpose(1, 2, 0)
    keyval_back = lax.all_gather(keyval, "cp", axis=0, tiled=True)
    back_blocks = keyval_back.reshape(n_cp, span_rows, pair_count, 2 * model_width)

    def pair_terms(
        query_rows, grad_rows_att, row_part, total_part, key_rows, value_rows, key_start, rows_pos
    ):
        logits, steps = block_logits(
            query_rows, key_rows, key_start, rows_pos, lengths, table_step, rise_points, head_scale
        )
        weights = jnp.exp(logits - total_part[..., None])
        weight_grads = jnp.einsum(
            "qshd,kshd->shqk", grad_rows_att, value_rows, preferred_element_type=jnp.float32
        )
        score_grads = weights * (weight_grads - row_part[..., None])
        return (weights, score_grads, steps)

    def query_side_step(state_pair, kv_block, block_start):
        query_grad, step_grad = state_pair
        key_rows, value_rows = split_kv(kv_block)
        weights, score_grads, steps = pair_terms(
            queries,
            grad_att_heads,
            row_terms,
            log_total,
            key_rows,
            value_rows,
            block_start,
            query_pos,
        )
        low_grads = score_grads.astype(jnp.bfloat16)
        query_grad = (
            query_grad
            + jnp.einsum("shqk,kshd->qshd", low_grads, key_rows, preferred_element_type=jnp.float32)
            * head_scale
        )
        step_grad = step_grad + jnp.einsum(
            "hqk,qkb->hb", jnp.sum(score_grads, axis=0), steps, precision=lax.Precision.HIGHEST
        )
        return ((query_grad, step_grad), weights, low_grads)

    start_state = (
        jnp.zeros((span_rows, pair_count, head_count, head_size), jnp.float32),
        jnp.zeros((head_count, bucket_count), jnp.float32),
    )

    def grad_step(state_pair, block_item):
        kv_block, block_start = block_item
        new_state, weights, low_grads = query_side_step(state_pair, kv_block, block_start)
        value_grad = jnp.einsum(
            "shqk,qshd->kshd",
            weights.astype(jnp.bfloat16),
            grad_att_heads,
            preferred_element_type=jnp.float32,
        )
        key_grad = (
            jnp.einsum("shqk,qshd->kshd", low_grads, queries, preferred_element_type=jnp.float32)
            * head_scale
        )
        block_grad = jnp.concatenate(
            [
                key_grad.reshape(span_rows, pair_count, model_width),
                value_grad.reshape(span_rows, pair_count, model_width),
            ],
            axis=-1,
        )
        return (new_state, block_grad)

    (query_grad, step_grad), kv_terms = lax.scan(
        grad_step, start_state, (back_blocks, block_starts)
    )
    kv_terms = kv_terms.reshape(seq_len, pair_count, 2 * model_width)
    keyval_grad = lax.psum_scatter(
        kv_terms.astype(jnp.bfloat16), "cp", scatter_dimension=0, tiled=True
    )
    table_grad = step_grad - jnp.concatenate(
        [step_grad[:, 1:], jnp.zeros((head_count, 1), jnp.float32)], axis=1
    )
    qkv_grad = jnp.concatenate(
        [query_grad.reshape(span_rows, pair_count, model_width).astype(jnp.bfloat16), keyval_grad],
        axis=-1,
    )
    qkv_weight_grad = jnp.einsum(
        "csd,cse->de", normed_first, qkv_grad, preferred_element_type=jnp.float32
    )
    grad_normed_first = jnp.einsum(
        "cse,de->csd", qkv_grad, w_qkv, preferred_element_type=jnp.float32
    )
    gain_first_grad = jnp.sum(grad_normed_first * inputs * scale_first, axis=(0, 1))
    tokens_grad = (
        grad_hidden + norm_back(grad_normed_first, inputs, scale_first, norm1_gain)
    ).astype(jnp.bfloat16)
    attn_term = jnp.concatenate([qkv_weight_grad, out_grad], axis=1)
    w_attn_grad = lax.psum_scatter(attn_term, ("dp", "ep", "cp"), scatter_dimension=1, tiled=True)
    router_sum, table_sum, gain_first_sum, gain_second_sum = lax.psum(
        (router_grad, table_grad, gain_first_grad, gain_second_grad), ("dp", "ep", "cp")
    )
    gate_sum, up_sum, down_sum = (
        lax.psum_scatter(
            gate_grad.astype(jnp.bfloat16), ("dp", "cp"), scatter_dimension=2, tiled=True
        ).astype(jnp.float32),
        lax.psum_scatter(
            up_grad.astype(jnp.bfloat16), ("dp", "cp"), scatter_dimension=2, tiled=True
        ).astype(jnp.float32),
        lax.psum_scatter(
            down_grad.astype(jnp.bfloat16), ("dp", "cp"), scatter_dimension=2, tiled=True
        ).astype(jnp.float32),
    )
    return (
        mixed,
        tokens_grad,
        w_attn_grad,
        table_sum,
        gain_first_sum,
        gain_second_sum,
        router_sum,
        gate_sum,
        up_sum,
        down_sum,
    )


minus_big = -1000000000.0
vmem_bytes = 56 * 1024 * 1024


def cost(flops, moved):
    return pl.CostEstimate(flops=int(flops), bytes_accessed=int(moved), transcendentals=0)


def compiler_params():
    return pltpu.CompilerParams(vmem_limit_bytes=vmem_bytes)


def shear(values, leftward):
    rows, lanes = values.shape
    row_ids = lax.broadcasted_iota(jnp.int32, (rows, lanes), 0)
    bit = 1
    while bit < rows:
        amount = lanes - bit if leftward else bit
        moved = pltpu.roll(values, amount, 1)
        values = jnp.where((row_ids & bit) != 0, moved, values)
        bit *= 2
    return values


def dot_nt(left, right):
    return lax.dot_general(
        left, right, (((1,), (1,)), ((), ())), preferred_element_type=jnp.float32
    )


def dot_tn(left, right):
    return lax.dot_general(
        left, right, (((0,), (0,)), ((), ())), preferred_element_type=jnp.float32
    )


def dot_nn(left, right):
    return jnp.dot(left, right, preferred_element_type=jnp.float32)


def gather_kernel(normed_ref, weight_ref, line_ref, all_ref, qkv_ref, bias_ref, send_sem, recv_sem):
    slots, count, span_rows, _ = all_ref.shape
    mine = lax.axis_index("cp")
    right, left = lax.rem(mine + 1, count), lax.rem(mine + count - 1, count)
    barrier = pltpu.get_barrier_semaphore()
    for near in (left, right):
        pl.semaphore_signal(
            barrier, inc=1, device_id={"cp": near}, device_id_type=pl.DeviceIdType.MESH
        )
    pl.semaphore_wait(barrier, 2)

    def copy(slot, hop):
        return pltpu.make_async_remote_copy(
            src_ref=normed_ref.at[slot] if hop == 0 else all_ref.at[slot, hop],
            dst_ref=all_ref.at[slot, hop + 1],
            send_sem=send_sem.at[slot, hop],
            recv_sem=recv_sem.at[slot, hop],
            device_id={"cp": right},
            device_id_type=pl.DeviceIdType.MESH,
        )

    for slot in range(slots):
        copy(slot, 0).start()
    for slot in range(slots):
        rows = normed_ref[slot]
        all_ref[slot, 0] = rows
        qkv_ref[slot, 0] = dot_nn(rows, weight_ref[...]).astype(jnp.bfloat16)
    columns = bias_ref.shape[2]
    lanes = span_rows + columns
    for head in range(bias_ref.shape[0]):
        line = pltpu.roll(line_ref[head], lanes - (span_rows - 1), 1)
        full = jnp.broadcast_to(line, (span_rows, lanes))
        bias_ref[head] = shear(full, False)[:, :columns]
    for hop in range(1, count):
        for slot in range(slots):
            copy(slot, hop - 1).wait_recv()
            if hop < count - 1:
                copy(slot, hop).start()
            rows = all_ref[slot, hop]
            qkv_ref[slot, hop] = dot_nn(rows, weight_ref[...]).astype(jnp.bfloat16)
    for hop in range(count - 1):
        for slot in range(slots):
            copy(slot, hop).wait_send()


def gather_project(normed, weight, lines, count):
    slots, span_rows, model_width = normed.shape
    columns = lines.shape[2] - span_rows
    whole = pl.BlockSpec(memory_space=pltpu.VMEM)
    return pl.pallas_call(
        gather_kernel,
        in_specs=[whole] * 3,
        out_specs=[whole] * 3,
        out_shape=[
            jax.ShapeDtypeStruct((slots, count, span_rows, model_width), jnp.bfloat16),
            jax.ShapeDtypeStruct((slots, count, span_rows, weight.shape[1]), jnp.bfloat16),
            jax.ShapeDtypeStruct((lines.shape[0], span_rows, columns), jnp.float32),
        ],
        scratch_shapes=[
            pltpu.SemaphoreType.DMA((slots, count - 1)),
            pltpu.SemaphoreType.DMA((slots, count - 1)),
        ],
        cost_estimate=cost(60e9, 20e6),
        compiler_params=pltpu.CompilerParams(
            vmem_limit_bytes=vmem_bytes, collective_id=0, has_side_effects=True
        ),
        name="gather_project",
    )(normed, weight, lines)


def key_masks(length, blocks, span_rows):
    masks = []
    for block in range(blocks):
        position = block * span_rows + lax.broadcasted_iota(jnp.int32, (1, span_rows), 1)
        masks.append(jnp.where(position < length, 0.0, minus_big))
    return masks


def forward_kernel(
    scale, head_size, meta_ref, q_ref, k_ref, v_ref, bias_ref, low_ref, full_ref, total_ref
):
    _, blocks, span_rows, lanes = q_ref.shape
    mine, length = meta_ref[0], meta_ref[1]
    lane = lax.broadcasted_iota(jnp.int32, (1, lanes), 1)
    masks = key_masks(length, blocks, span_rows)

    def place(block):
        return lax.rem(mine - block + blocks, blocks)

    for row in range(blocks):
        queries = q_ref[0, place(row)]
        totals = jnp.zeros((span_rows, lanes), jnp.float32)
        result = jnp.zeros((span_rows, lanes), jnp.float32)
        for half in range(lanes // head_size):
            own = lane // head_size == half
            head_q = queries * jnp.where(own, scale, 0.0).astype(jnp.bfloat16)
            head_v = jnp.where(own, 1.0, 0.0).astype(jnp.bfloat16)
            logits = []
            for column in range(row + 1):
                at = (blocks - 1 - row + column) * span_rows
                part = dot_nt(head_q, k_ref[0, place(column)])
                part = part + bias_ref[half, :, at : at + span_rows] + masks[column]
                logits.append(part)
            peak = jnp.max(logits[0], axis=1, keepdims=True)
            for part in logits[1:]:
                peak = jnp.maximum(peak, jnp.max(part, axis=1, keepdims=True))
            total = jnp.zeros((span_rows, 1), jnp.float32)
            mixed = jnp.zeros((span_rows, lanes), jnp.float32)
            for column in range(row + 1):
                weights = jnp.exp(logits[column] - peak)
                total = total + jnp.sum(weights, axis=1, keepdims=True)
                mixed = mixed + dot_nn(
                    weights.astype(jnp.bfloat16), v_ref[0, place(column)] * head_v
                )
            result = result + mixed / total
            totals = jnp.where(lane == half, peak + jnp.log(total), totals)
        low_ref[place(row)] = result.astype(jnp.bfloat16)
        full_ref[row] = result
        total_ref[row] = totals


def attend_forward(meta, slot, qkv, bias, scale, head_size):
    _, blocks, span_rows, width = qkv.shape
    pairs = width // (3 * 128)
    per_pair = bias.shape[0] // pairs

    def part(which):
        return pl.BlockSpec((1, blocks, span_rows, 128), lambda p: (slot, 0, 0, 3 * p + which))

    plain = pl.BlockSpec((blocks, span_rows, 128), lambda p: (0, 0, p))

    return pl.pallas_call(
        functools.partial(forward_kernel, scale, head_size),
        grid=(pairs,),
        in_specs=[
            pl.BlockSpec(memory_space=pltpu.SMEM),
            part(0),
            part(1),
            part(2),
            pl.BlockSpec((per_pair,) + bias.shape[1:], lambda p: (p, 0, 0)),
        ],
        out_specs=[plain, plain, plain],
        out_shape=[
            jax.ShapeDtypeStruct((blocks, span_rows, pairs * 128), jnp.bfloat16),
            jax.ShapeDtypeStruct((blocks, span_rows, pairs * 128), jnp.float32),
            jax.ShapeDtypeStruct((blocks, span_rows, pairs * 128), jnp.float32),
        ],
        cost_estimate=cost(8e9, 8e6),
        compiler_params=compiler_params(),
        name="attend_forward",
    )(meta, qkv, qkv, qkv, bias)


def backward_kernel(
    scale,
    head_size,
    meta_ref,
    q_ref,
    k_ref,
    v_ref,
    bias_ref,
    grad_ref,
    full_ref,
    total_ref,
    ring_ref,
    line_ref,
    key_sum,
    value_sum,
    plane,
):
    _, blocks, span_rows, lanes = q_ref.shape
    mine, length = meta_ref[0], meta_ref[1]
    lane = lax.broadcasted_iota(jnp.int32, (1, lanes), 1)
    masks = key_masks(length, blocks, span_rows)
    halves = lanes // head_size

    def place(block):
        return lax.rem(mine - block + blocks, blocks)

    key_sum[...] = jnp.zeros_like(key_sum)
    value_sum[...] = jnp.zeros_like(value_sum)
    plane[...] = jnp.zeros_like(plane)
    for row in range(blocks):
        queries = q_ref[0, place(row)]
        grads = grad_ref[lax.rem(row - mine + blocks, blocks)]
        products = grads.astype(jnp.float32) * full_ref[row]
        totals = total_ref[row]
        query_sum = jnp.zeros((span_rows, lanes), jnp.float32)
        for half in range(halves):
            own = lane // head_size == half
            one = jnp.where(own, 1.0, 0.0).astype(jnp.bfloat16)
            head_q = queries * jnp.where(own, scale, 0.0).astype(jnp.bfloat16)
            head_g = grads * one
            delta = jnp.sum(jnp.where(own, products, 0.0), axis=1, keepdims=True)
            total = totals[:, half : half + 1]
            for column in range(row + 1):
                at = (blocks - 1 - row + column) * span_rows
                keys = k_ref[0, place(column)]
                logits = dot_nt(head_q, keys)
                logits = logits + bias_ref[half, :, at : at + span_rows] + masks[column]
                weights = jnp.exp(logits - total)
                weight_grads = dot_nt(head_g, v_ref[0, place(column)])
                score_grads = weights * (weight_grads - delta)
                plane[half, :, at : at + span_rows] += score_grads
                low_weights = weights.astype(jnp.bfloat16)
                low_grads = score_grads.astype(jnp.bfloat16)
                query_sum = query_sum + dot_nn(low_grads, keys * one)
                key_sum[column] += dot_tn(low_grads, head_q)
                value_sum[column] += dot_tn(low_weights, head_g)
        result = (query_sum * scale).astype(jnp.bfloat16)
        ring_ref[place(row), :, :lanes] = result
    for row in range(blocks):
        result = key_sum[row].astype(jnp.bfloat16)
        ring_ref[place(row), :, lanes : 2 * lanes] = result
        result = value_sum[row].astype(jnp.bfloat16)
        ring_ref[place(row), :, 2 * lanes :] = result
    for half in range(halves):
        full = jnp.concatenate(
            [plane[half], jnp.zeros((span_rows, span_rows), jnp.float32)], axis=1
        )
        summed = jnp.sum(shear(full, True), axis=0, keepdims=True)
        line_ref[half] = pltpu.roll(summed, span_rows - 1, 1)


def attend_backward(meta, slot, qkv, bias, grads, full, totals, scale, head_size):
    _, blocks, span_rows, width = qkv.shape
    pairs = width // (3 * 128)
    per_pair = bias.shape[0] // pairs
    lanes = bias.shape[2] + span_rows

    def part(which):
        return pl.BlockSpec((1, blocks, span_rows, 128), lambda p: (slot, 0, 0, 3 * p + which))

    plain = pl.BlockSpec((blocks, span_rows, 128), lambda p: (0, 0, p))
    wide = pl.BlockSpec((blocks, span_rows, 384), lambda p: (0, 0, p))
    return pl.pallas_call(
        functools.partial(backward_kernel, scale, head_size),
        grid=(pairs,),
        in_specs=[
            pl.BlockSpec(memory_space=pltpu.SMEM),
            part(0),
            part(1),
            part(2),
            pl.BlockSpec((per_pair,) + bias.shape[1:], lambda p: (p, 0, 0)),
            plain,
            plain,
            plain,
        ],
        out_specs=[wide, pl.BlockSpec((per_pair, 1, lanes), lambda p: (p, 0, 0))],
        out_shape=[
            jax.ShapeDtypeStruct(qkv.shape[1:], jnp.bfloat16),
            jax.ShapeDtypeStruct((bias.shape[0], 1, lanes), jnp.float32),
        ],
        scratch_shapes=[
            pltpu.VMEM((blocks, span_rows, 128), jnp.float32),
            pltpu.VMEM((blocks, span_rows, 128), jnp.float32),
            pltpu.VMEM((per_pair,) + bias.shape[1:], jnp.float32),
        ],
        cost_estimate=cost(20e9, 12e6),
        compiler_params=compiler_params(),
        name="attend_backward",
    )(meta, qkv, qkv, qkv, bias, grads, full, totals)


def own_rows(meta_ref, span_rows):
    position = meta_ref[0] * span_rows + lax.broadcasted_iota(jnp.int32, (span_rows, 1), 0)
    return jnp.where(position < meta_ref[1], 1.0, 0.0)


def router_of(rows, router_w, experts):
    lane = lax.broadcasted_iota(jnp.int32, (1, router_w.shape[1]), 1)
    logits = jnp.where(lane < experts, dot_nn(rows, router_w), minus_big)
    shares = jnp.exp(logits - jnp.max(logits, axis=1, keepdims=True))
    return shares / jnp.sum(shares, axis=1, keepdims=True)


def project_kernel(meta_ref, input_ref, gain_ref, weight_ref, *refs):
    attended_ref, hidden_ref, normed_ref = refs[-3:]
    parts = refs[:-3]
    count = len(parts)
    for j, part in enumerate(parts):
        owner = lax.rem(meta_ref[0] + j, count)
        for group in range(part.shape[1] // 128):
            at = pl.multiple_of((group * count + owner) * 128, 128)
            attended_ref[:, pl.ds(at, 128)] = part[:, group * 128 : (group + 1) * 128]
    projected = dot_nn(attended_ref[...], weight_ref[...])
    hidden = input_ref[...].astype(jnp.float32) + own_rows(meta_ref, projected.shape[0]) * projected
    hidden_ref[...] = hidden
    normed_ref[...] = (hidden * root_scale(hidden) * gain_ref[...]).astype(jnp.bfloat16)


def project_rows(meta, inputs, gain, w_attn, parts):
    span_rows, model_width = inputs.shape
    whole = pl.BlockSpec(memory_space=pltpu.VMEM)
    return pl.pallas_call(
        project_kernel,
        grid=(1,),
        in_specs=[
            pl.BlockSpec(memory_space=pltpu.SMEM),
            whole,
            whole,
            pl.BlockSpec((model_width, model_width), lambda i: (0, 3)),
        ]
        + [whole] * len(parts),
        out_specs=[whole] * 3,
        out_shape=[
            jax.ShapeDtypeStruct((span_rows, model_width), jnp.bfloat16),
            jax.ShapeDtypeStruct((span_rows, model_width), jnp.float32),
            jax.ShapeDtypeStruct((span_rows, model_width), jnp.bfloat16),
        ],
        cost_estimate=cost(2e9, 6e6),
        compiler_params=compiler_params(),
        name="project_rows",
    )(meta, inputs, gain, w_attn, *parts)


def hidden_kernel(
    experts,
    meta_ref,
    own_ref,
    first_ref,
    last_ref,
    grad_ref,
    hidden_ref,
    normed_ref,
    gain_ref,
    router_ref,
    weight_ref,
    *refs,
):
    hidden_grad_ref, proj_ref, router_grad_ref, gain_grad_ref = refs[:4]
    leaving, attended = refs[4:-1], refs[-1]
    count = len(leaving)
    span_rows, model_width = hidden_ref.shape
    back = (
        own_ref[...].astype(jnp.float32)
        + first_ref[...].astype(jnp.float32)
        + last_ref[...].astype(jnp.float32)
    )
    normed = normed_ref[...]
    probs = router_of(normed, router_ref[...], experts)
    shares = back[:, model_width:]
    logit_grads = probs * (shares - jnp.sum(probs * shares, axis=1, keepdims=True))
    logit_grads = logit_grads.astype(jnp.bfloat16)
    router_grad_ref[...] = dot_tn(normed, logit_grads)
    grads = back[:, :model_width] + dot_nt(logit_grads, router_ref[...])
    hidden = hidden_ref[...]
    scale_rows = root_scale(hidden)
    gain_grad_ref[...] = jnp.sum(grads * hidden * scale_rows, axis=0, keepdims=True)
    hidden_grads = grad_ref[...].astype(jnp.float32) + norm_back(
        grads, hidden, scale_rows, gain_ref[...]
    )
    hidden_grad_ref[...] = hidden_grads
    proj = (own_rows(meta_ref, span_rows) * hidden_grads).astype(jnp.bfloat16)
    proj_ref[...] = proj
    attended[...] = dot_nt(proj, weight_ref[...]).astype(jnp.bfloat16)
    for j, part in enumerate(leaving):
        owner = lax.rem(meta_ref[0] + (count - j), count)
        for group in range(part.shape[1] // 128):
            at = pl.multiple_of((group * count + owner) * 128, 128)
            part[:, group * 128 : (group + 1) * 128] = attended[:, pl.ds(at, 128)]


def hidden_back(meta, own, first, last, grads, hidden, normed, gain, router, w_attn, experts, count):
    span_rows, model_width = hidden.shape
    whole = pl.BlockSpec(memory_space=pltpu.VMEM)
    f32, bf16 = jnp.float32, jnp.bfloat16
    return pl.pallas_call(
        functools.partial(hidden_kernel, experts),
        grid=(1,),
        in_specs=[pl.BlockSpec(memory_space=pltpu.SMEM)]
        + [whole] * 8
        + [pl.BlockSpec((model_width, model_width), lambda i: (0, 3))],
        out_specs=[whole] * (4 + count),
        out_shape=[
            jax.ShapeDtypeStruct((span_rows, model_width), f32),
            jax.ShapeDtypeStruct((span_rows, model_width), bf16),
            jax.ShapeDtypeStruct((model_width, router.shape[1]), f32),
            jax.ShapeDtypeStruct((1, model_width), f32),
        ]
        + [jax.ShapeDtypeStruct((span_rows, model_width // count), bf16)] * count,
        scratch_shapes=[pltpu.VMEM((span_rows, model_width), bf16)],
        cost_estimate=cost(3e9, 8e6),
        compiler_params=compiler_params(),
        name="hidden_back",
    )(meta, own, first, last, grads, hidden, normed, gain, router, w_attn)


def token_kernel(meta_ref, input_ref, hidden_ref, gain_ref, weight_ref, *refs):
    parts, out_ref = refs[:-1], refs[-1]
    count = len(parts)
    model_width = input_ref.shape[1]
    total = None
    for j, part in enumerate(parts):
        owner = lax.rem(meta_ref[0] + j, count)
        pieces = []
        for group in range(part.shape[1] // 384):
            for which in range(3):
                at = which * model_width + (group * count + owner) * 128
                pieces.append(weight_ref[:, pl.ds(pl.multiple_of(at, 128), 128)])
        term = dot_nt(part[...], jnp.concatenate(pieces, axis=1))
        total = term if total is None else total + term
    inputs = input_ref[...].astype(jnp.float32)
    back = norm_back(total, inputs, root_scale(inputs), gain_ref[...])
    out_ref[...] = (hidden_ref[...] + back).astype(jnp.bfloat16)


def token_grads(meta, inputs, hidden_grads, gain, w_attn, parts):
    span_rows, model_width = inputs.shape
    whole = pl.BlockSpec(memory_space=pltpu.VMEM)
    return pl.pallas_call(
        token_kernel,
        grid=(1,),
        in_specs=[
            pl.BlockSpec(memory_space=pltpu.SMEM),
            whole,
            whole,
            whole,
            pl.BlockSpec((model_width, 3 * model_width), lambda i: (0, 0)),
        ]
        + [whole] * len(parts),
        out_specs=whole,
        out_shape=jax.ShapeDtypeStruct((span_rows, model_width), jnp.bfloat16),
        cost_estimate=cost(4e9, 8e6),
        compiler_params=compiler_params(),
        name="token_grads",
    )(meta, inputs, hidden_grads, gain, w_attn, *parts)


gelu_inner = 0.7978845608028654
gelu_cubic = 0.044715


def pick_kernel(base_ref, target_ref, *refs):
    out_ref = refs[-1]
    sources, experts, capacity, _ = out_ref.shape
    parts = (len(refs) - 1) // sources
    for source in range(sources):
        for expert in range(experts):
            picked = None
            for at in range(parts):
                part = refs[source * parts + at]
                span = part.shape[0]
                ids = lax.broadcasted_iota(jnp.int32, (capacity, span), 0)
                ids = ids + (base_ref[0] + expert * capacity)
                hot = jnp.zeros((capacity, span), jnp.float32)
                for choice in range(target_ref.shape[1]):
                    chosen = target_ref[source, choice : choice + 1, at * span : (at + 1) * span]
                    hot = hot + jnp.where(ids == chosen, 1.0, 0.0)
                term = dot_nn(hot.astype(jnp.bfloat16), part[...])
                picked = term if picked is None else picked + term
            out_ref[source, expert] = picked.astype(jnp.bfloat16)


def pick_rows(base, targets, blocks, experts, capacity):
    flat = [part for parts in blocks for part in parts]
    width = flat[0].shape[1]
    whole = pl.BlockSpec(memory_space=pltpu.VMEM)
    return pl.pallas_call(
        pick_kernel,
        in_specs=[pl.BlockSpec(memory_space=pltpu.SMEM)] + [whole] * (1 + len(flat)),
        out_specs=whole,
        out_shape=jax.ShapeDtypeStruct((len(blocks), experts, capacity, width), jnp.bfloat16),
        cost_estimate=cost(1.6e9 * len(blocks), 3e6 * len(blocks)),
        compiler_params=compiler_params(),
        name="pick_rows",
    )(base, targets, *flat)


def place_kernel(base_ref, target_ref, mine_ref, theirs_ref, *out_refs):
    sources, experts, capacity, _ = mine_ref.shape
    parts = len(out_refs) // sources
    span = out_refs[0].shape[0]
    for source in range(sources):
        both = [
            (
                mine_ref[source, expert].astype(jnp.float32)
                + theirs_ref[source, expert].astype(jnp.float32)
            ).astype(jnp.bfloat16)
            for expert in range(experts)
        ]
        for at in range(parts):
            total = None
            for expert in range(experts):
                ids = lax.broadcasted_iota(jnp.int32, (span, capacity), 1)
                ids = ids + (base_ref[0] + expert * capacity)
                hot = jnp.zeros((span, capacity), jnp.float32)
                for choice in range(target_ref.shape[2]):
                    chosen = target_ref[source, at * span : (at + 1) * span, choice : choice + 1]
                    hot = hot + jnp.where(ids == chosen, 1.0, 0.0)
                term = dot_nn(hot.astype(jnp.bfloat16), both[expert])
                total = term if total is None else total + term
            out_refs[source * parts + at][...] = total.astype(jnp.bfloat16)


def place_rows(base, targets, mine, theirs, parts):
    sources, experts, capacity, width = mine.shape
    span = targets.shape[1] // parts
    whole = pl.BlockSpec(memory_space=pltpu.VMEM)
    return pl.pallas_call(
        place_kernel,
        in_specs=[pl.BlockSpec(memory_space=pltpu.SMEM), whole, whole, whole],
        out_specs=[whole] * (sources * parts),
        out_shape=[jax.ShapeDtypeStruct((span, width), jnp.bfloat16)] * (sources * parts),
        cost_estimate=cost(1.6e9 * sources, 4e6 * sources),
        compiler_params=compiler_params(),
        name="place_rows",
    )(base, targets, mine, theirs)


def expert_kernel(
    experts,
    own_units,
    kept_count,
    first_ref,
    window_ref,
    rows_mine,
    rows_theirs,
    grads_mine,
    grads_theirs,
    router_ref,
    gate_ref,
    up_ref,
    down_ref,
    *refs,
):
    back_mine, back_theirs, out_mine, out_theirs = refs[kept_count : kept_count + 4]
    kept_rows, kept_grads, kept_gate, kept_up, kept_inner = refs[kept_count + 4 :]
    capacity, model_width = rows_mine.shape[2:]
    rows = jnp.concatenate([rows_mine[0, 0], rows_theirs[0, 0]], axis=0)
    grads = jnp.concatenate([grads_mine[0, 0], grads_theirs[0, 0]], axis=0)
    kept_rows[0, 0] = rows
    kept_grads[0, 0] = grads
    lane = lax.broadcasted_iota(jnp.int32, (1, router_ref.shape[1]), 1)
    expert = first_ref[0] + pl.program_id(0)
    probs = router_of(rows, router_ref[...], experts)
    gates = jnp.sum(jnp.where(lane == expert, probs, 0.0), axis=1, keepdims=True)
    unit = lax.broadcasted_iota(jnp.int32, (1, gate_ref.shape[2]), 1) - window_ref[1]
    own = jnp.logical_and(unit >= 0, unit < own_units)
    gate_w, up_w, down_w = gate_ref[0], up_ref[0], down_ref[0]
    gate_pre = dot_nn(rows, gate_w)
    up_pre = jnp.where(own, dot_nn(rows, up_w), 0.0)
    square = gate_pre * gate_pre
    tanh = jnp.tanh(gelu_inner * gate_pre * (1.0 + gelu_cubic * square))
    half = 0.5 + 0.5 * tanh
    active = gate_pre * half
    slope = half + active * (1.0 - tanh) * (gelu_inner * (1.0 + 3.0 * gelu_cubic * square))
    inner = active * up_pre
    low_inner = inner.astype(jnp.bfloat16)
    plain_grads = jnp.where(own, dot_nn(grads, down_w), 0.0)
    gate_grads = jnp.sum(plain_grads * low_inner.astype(jnp.float32), axis=1, keepdims=True)
    inner_grads = plain_grads * gates
    low_gate = (inner_grads * up_pre * slope).astype(jnp.bfloat16)
    low_up = (inner_grads * active).astype(jnp.bfloat16)
    kept_gate[0, 0] = low_gate
    kept_up[0, 0] = low_up
    kept_inner[0, 0] = (inner * gates).astype(jnp.bfloat16)
    back = (dot_nt(low_gate, gate_w) + dot_nt(low_up, up_w)).astype(jnp.bfloat16)
    shares = jnp.where(lane == expert, gate_grads, 0.0).astype(jnp.bfloat16)
    out = (gates * dot_nt(low_inner, down_w)).astype(jnp.bfloat16)
    for at, back_ref, out_ref in ((0, back_mine, out_mine), (1, back_theirs, out_theirs)):
        part = slice(at * capacity, (at + 1) * capacity)
        back_ref[0, 0, :, :model_width] = back[part]
        back_ref[0, 0, :, model_width:] = shares[part]
        out_ref[0, 0] = out[part]


def run_experts(
    first, window, mine, theirs, grads_mine, grads_theirs, router, weights, kept, at, total, experts, units
):
    sources, exp_dev, capacity, model_width = mine.shape
    wide_units = aligned_units(units)
    tile = 2 * capacity
    rows = pl.BlockSpec((1, 1, capacity, model_width), lambda e, k, f, w: (k, e, 0, 0))
    wide = pl.BlockSpec((1, 1, capacity, model_width + 128), lambda e, k, f, w: (k, e, 0, 0))
    weight = pl.BlockSpec(
        (pl.Element(1), pl.Element(model_width), pl.Element(wide_units)),
        lambda e, k, f, w: (e, 0, pl.multiple_of(w[0], 128)),
    )
    keep = lambda width: pl.BlockSpec((1, 1, tile, width), lambda e, k, f, w: (e, at + k, 0, 0))
    keep_widths = (model_width, model_width, wide_units, wide_units, wide_units)
    kept = list(kept)
    back_shape = jax.ShapeDtypeStruct((sources, exp_dev, capacity, model_width + 128), jnp.bfloat16)
    out_shape = jax.ShapeDtypeStruct((sources, exp_dev, capacity, model_width), jnp.bfloat16)
    got = pl.pallas_call(
        functools.partial(expert_kernel, experts, units, len(kept)),
        grid_spec=pltpu.PrefetchScalarGridSpec(
            num_scalar_prefetch=2,
            grid=(exp_dev, sources),
            in_specs=[
                rows,
                rows,
                rows,
                rows,
                pl.BlockSpec(router.shape, lambda e, k, f, w: (0, 0)),
                weight,
                weight,
                weight,
            ]
            + [pl.BlockSpec(memory_space=pl.ANY)] * len(kept),
            out_specs=[wide, wide, rows, rows] + [keep(width) for width in keep_widths],
        ),
        out_shape=[back_shape, back_shape, out_shape, out_shape]
        + [jax.ShapeDtypeStruct((exp_dev, total, tile, w), jnp.bfloat16) for w in keep_widths],
        input_output_aliases={10 + i: 4 + i for i in range(len(kept))},
        cost_estimate=cost(20e9 * sources, 8e6 * sources),
        compiler_params=compiler_params(),
        name="expert_rows",
    )(first, window, mine, theirs, grads_mine, grads_theirs, router, *weights, *kept)
    return got[:4], got[4:]


def aligned_units(units):
    return (units + 127) // 128 * 128


def weight_kernel(window_ref, rows_ref, grads_ref, gate_ref, up_ref, inner_ref, weight_ref, total):
    step = pl.program_id(0)
    pieces, _, piece, _ = weight_ref.shape

    @pl.when(step == 0)
    def _():
        total[...] = jnp.zeros_like(total)

    total[0] += dot_tn(gate_ref[0, 0], rows_ref[0, 0])
    total[1] += dot_tn(up_ref[0, 0], rows_ref[0, 0])
    total[2] += dot_tn(inner_ref[0, 0], grads_ref[0, 0])

    @pl.when(step == pl.num_programs(0) - 1)
    def _():
        skip = pl.multiple_of(window_ref[1], 64)
        for at in range(pieces):
            got = total[:, pl.ds(skip + at * piece, piece), :]
            weight_ref[at] = got.astype(jnp.bfloat16)


def weight_grads(window, kept, expert, pieces, units):
    _, tiles, tile, model_width = kept[0].shape
    wide_units = kept[2].shape[3]
    block = lambda a: pl.BlockSpec((1, 1) + a.shape[2:], lambda i: (expert, i, 0, 0))
    shape = (pieces, 3, units // pieces, model_width)
    return pl.pallas_call(
        weight_kernel,
        grid=(tiles,),
        in_specs=[pl.BlockSpec(memory_space=pltpu.SMEM)] + [block(a) for a in kept],
        out_specs=pl.BlockSpec(shape, lambda i: (0, 0, 0, 0)),
        out_shape=jax.ShapeDtypeStruct(shape, jnp.bfloat16),
        scratch_shapes=[pltpu.VMEM((3, wide_units, model_width), jnp.float32)],
        cost_estimate=cost(20e9, 20e6),
        compiler_params=compiler_params(),
        name="weight_grads",
    )(window, *kept)


def send(values, axis, pairs):
    return lax.ppermute(values, axis, pairs)


def after(values, *earlier):
    return lax.optimization_barrier((values, earlier))[0]


def fast_device(
    tokens,
    lengths,
    expert_ids,
    places,
    buckets,
    w_attn,
    bias_table,
    norm1_gain,
    norm2_gain,
    w_router,
    w_gate,
    w_up,
    w_down,
    cotangent,
):
    span_rows, slots, model_width = tokens.shape
    head_count, bucket_count = bias_table.shape
    head_size = model_width // head_count
    scale = head_size ** (-0.5)
    n_dp = lax.axis_size("dp")
    n_ep = lax.axis_size("ep")
    n_cp = lax.axis_size("cp")
    my_dp, my_ep, my_cp = (lax.axis_index(name) for name in ("dp", "ep", "cp"))
    seq_len = span_rows * n_cp
    rows = span_rows * slots
    top_count = expert_ids.shape[2]
    experts = w_router.shape[1]
    exp_dev = w_gate.shape[0]
    units = w_gate.shape[2] // n_dp
    capacity = (5 * rows * top_count + 4 * experts - 1) // (4 * experts)
    groups = model_width // (128 * n_cp)
    own_width = 3 * groups * 128
    heads_own = head_count // n_cp
    over_core = [(i, i ^ 1) for i in range(n_dp)]
    over_x = [(i, i ^ 2) for i in range(n_dp)]
    over_y = [(i, i ^ 1) for i in range(n_ep)]
    ring = [(i, (i + 1) % n_cp) for i in range(n_cp)]
    f32, bf16 = jnp.float32, jnp.bfloat16
    exact = lax.Precision.HIGHEST
    each = range(slots)

    low_in = [tokens[:, s] for s in each]
    inputs = jnp.stack(low_in).astype(f32)
    normed_first = (inputs * root_scale(inputs) * norm1_gain).astype(bf16)

    w_own = jnp.concatenate(
        [
            lax.dynamic_slice(
                w_attn,
                (0, which * model_width + (group * n_cp + my_cp) * 128),
                (model_width, 128),
            )
            for group in range(groups)
            for which in range(3)
        ],
        axis=1,
    )
    per_group = 128 // head_size
    own_heads = (
        jnp.arange(groups)[:, None] * (n_cp * per_group)
        + my_cp * per_group
        + jnp.arange(per_group)[None, :]
    ).reshape(heads_own)
    head_hot = (own_heads[:, None] == jnp.arange(head_count)[None, :]).astype(f32)
    bucket_hot = (buckets[:, None] == jnp.arange(bucket_count)[None, :]).astype(f32)
    own_table = jnp.dot(head_hot, bias_table, precision=exact)
    lines = jnp.einsum("hb,db->hd", own_table, bucket_hot[::-1], precision=exact)
    lines = jnp.concatenate([lines, jnp.full((heads_own, span_rows), minus_big, f32)], axis=1)
    normed_all, qkvs, bias = gather_project(normed_first, w_own, lines[:, None, :], n_cp)

    def plane_gather(parts):
        over = [send(part, "dp", over_x) for part in parts]
        up = [send(part, "ep", over_y) for part in parts]
        across = [send(over[0], "ep", over_y), send(up[1], "dp", over_x)]
        return [list(parts), over, up, across]

    target = jnp.where(places >= 0, expert_ids * capacity + places, -1)
    target_parts = plane_gather([target[:, s].T for s in each])
    target_rows = jnp.stack([jnp.concatenate(parts, axis=1) for parts in target_parts])
    target_columns = target_rows.transpose(0, 2, 1)
    base = (my_ep * (exp_dev * capacity)).astype(jnp.int32).reshape(1)
    group_at = ((0, 1), (1, 3), (3, 4))
    sources = target_rows.shape[0]
    target_groups = [
        (target_rows[low:high], target_columns[low:high]) for low, high in group_at
    ]

    def pick_group(at, blocks):
        low, high = group_at[at]
        mine = pick_rows(base, target_groups[at][0], blocks[low:high], exp_dev, capacity)
        return mine, send(mine, "dp", over_core)

    low_out = [cotangent[:, s] for s in each]
    grad_blocks = plane_gather(low_out)
    window_at = my_dp * units // 128 * 128
    window = jnp.stack([window_at, my_dp * units - window_at]).astype(jnp.int32)
    router_wide = jnp.concatenate(
        [w_router, jnp.zeros((model_width, 128 - experts), w_router.dtype)], axis=1
    )

    def deliver(blocks):
        return [blocks[0]] + [
            send(blocks[j], "cp", [(i, (i - j) % n_cp) for i in range(n_cp)])
            for j in range(1, n_cp)
        ]

    metas = [jnp.stack([my_cp.astype(jnp.int32), lengths[s]]) for s in each]
    gain_first, gain_second = norm1_gain[None, :], norm2_gain[None, :]
    fulls, totals, returned = [], [], []
    for s in each:
        if s:
            qkvs = after(qkvs, fulls[-1])
        low, full, total = attend_forward(metas[s], s, qkvs, bias, scale, head_size)
        fulls.append(full)
        totals.append(total)
        returned.append(deliver(low))
    grad_blocks = after(grad_blocks, fulls)
    grad_groups = [pick_group(at, grad_blocks) for at in range(len(group_at))]
    attended, hidden, normed_second = [], [], []
    for s in each:
        got = project_rows(metas[s], low_in[s], gain_second, w_attn, returned[s])
        attended.append(got[0])
        hidden.append(got[1])
        normed_second.append(got[2])

    first = (my_ep * exp_dev).astype(jnp.int32).reshape(1)
    row_blocks = plane_gather(normed_second)

    def experts_of(at, picked, kept):
        low, high = group_at[at]
        results, kept = run_experts(
            first,
            window,
            *picked,
            *grad_groups[at],
            router_wide,
            (w_gate, w_up, w_down),
            kept,
            low,
            sources,
            experts,
            units,
        )
        return results[:2], results[2:], kept

    def placed(at, pair):
        return place_rows(base, target_groups[at][1], *pair, slots)

    def over_cores(pair):
        return pair[0], send(pair[1], "dp", over_core)

    picked_own = pick_group(0, row_blocks)
    back_own, out_own, kept = experts_of(0, picked_own, ())
    row_blocks = after(row_blocks, kept)
    picked_near = pick_group(1, row_blocks)
    picked_far = pick_group(2, row_blocks)
    place_own = placed(0, over_cores(back_own))
    picked_near = after(picked_near, picked_far[0], place_own)
    back_near, out_near, kept = experts_of(1, picked_near, kept)
    back_far, out_far, kept = experts_of(2, picked_far, kept)
    pair_near = over_cores(back_near)
    pair_far = over_cores(back_far)
    place_near = placed(1, after(pair_near, kept))
    weight_part = weight_grads(window, after(kept, place_near), 0, n_cp, units)
    place_far = placed(2, after(pair_far, weight_part))
    weight_sums = []
    for e in range(exp_dev):
        if e:
            weight_part = weight_grads(window, after(kept, place_far, weight_part), e, n_cp, units)
        part = after(weight_part, weight_sums)
        weight_sums.append(lax.psum_scatter(part, "cp", scatter_dimension=0, tiled=False))

    def plane_sum(own, near, far, hold=None):
        (over, up), across = (near[:2], near[2:]), far
        got_first = send(over[0], "dp", over_x)
        got_second = send(up[1], "ep", over_y)
        far_first = send(across[0], "dp", over_x).astype(f32)
        far_second = send(across[1], "ep", over_y).astype(f32)
        if hold is not None:
            far_first, far_second = after((far_first, far_second), hold)
        next_first = (up[0].astype(f32) + far_first).astype(bf16)
        next_second = (over[1].astype(f32) + far_second).astype(bf16)
        last_first = send(next_first, "ep", over_y)
        last_second = send(next_second, "dp", over_x)
        return [(own[0], got_first, last_first), (own[1], got_second, last_second)]

    back_rows = plane_sum(place_own, place_near, place_far, weight_part)
    hidden_grads, proj_grads, leaving, router_parts, gain_parts = [], [], [], [], []
    for s in each:
        got = hidden_back(
            metas[s],
            *back_rows[s],
            low_out[s],
            hidden[s],
            normed_second[s],
            gain_second,
            router_wide,
            w_attn,
            experts,
            n_cp,
        )
        hidden_grads.append(got[0])
        proj_grads.append(got[1])
        router_parts.append(got[2])
        gain_parts.append(got[3])
        leaving.append(deliver(got[4:]))
    router_grad = sum(router_parts)[:, :experts]
    gain_second_grad = sum(gain_parts)[0]
    out_grad = sum(dot_tn(attended[s], proj_grads[s]) for s in each)

    out_grad = out_grad.astype(bf16).reshape(model_width, n_ep, n_cp, 128).transpose(2, 1, 0, 3)
    out_grad = after(out_grad, weight_sums)
    out_grad = lax.psum_scatter(out_grad, "cp", scatter_dimension=0, tiled=False)
    arriving = []
    line_grads, qkv_grad = 0.0, 0.0
    for s in each:
        grads = jnp.stack(leaving[s])
        ringed, line = attend_backward(
            metas[s], s, qkvs, bias, grads, fulls[s], totals[s], scale, head_size
        )
        line_grads = line_grads + line[:, 0]
        qkv_grad = qkv_grad + dot_tn(
            normed_all[s].reshape(seq_len, model_width), ringed.reshape(seq_len, own_width)
        )
        arriving.append(deliver(ringed))

    gain_first_grad = jnp.sum(qkv_grad * w_own.astype(f32), axis=1) / norm1_gain
    attn_term = qkv_grad.reshape(model_width, groups, 3, 128).transpose(2, 1, 0, 3)
    attn_term = jnp.concatenate(
        [attn_term.reshape(3 * groups, model_width, 128).astype(bf16), out_grad], axis=0
    )
    attn_sum = lax.psum_scatter(attn_term, ("dp", "ep"), scatter_dimension=0, tiled=False)
    distance_grads = line_grads[:, :seq_len][:, ::-1]
    table_grad = jnp.dot(distance_grads, bucket_hot, precision=exact)
    table_grad = jnp.einsum("hg,hb->gb", head_hot, table_grad, precision=exact)
    small = [router_grad.T, table_grad, gain_first_grad, gain_second_grad]
    total = jnp.concatenate([part.reshape(-1, 128) for part in small], axis=0)
    for axis, pairs in (("dp", over_core), ("dp", over_x), ("ep", over_y)):
        total = total + send(total, axis, pairs)
    step = 1
    while step < n_cp:
        total = total + send(total, "cp", [(i, i ^ step) for i in range(n_cp)])
        step *= 2
    total = total.reshape(-1)
    cuts = [0]
    for part in small:
        cuts.append(cuts[-1] + part.size)
    router_sum, table_sum, gain_first_sum, gain_second_sum = (
        total[cuts[i] : cuts[i + 1]].reshape(part.shape) for i, part in enumerate(small)
    )

    out_pairs = after([out_own, out_near, out_far], hidden_grads)
    out_rows = plane_sum(*(placed(at, over_cores(pair)) for at, pair in enumerate(out_pairs)))
    mixed = [
        (hidden[s] + sum(part.astype(f32) for part in out_rows[s])).astype(bf16) for s in each
    ]
    tokens_grad = [
        token_grads(metas[s], low_in[s], hidden_grads[s], gain_first, w_attn, arriving[s])
        for s in each
    ]
    weight_sum = jnp.stack(weight_sums)
    gate_sum, up_sum, down_sum = (
        weight_sum[:, which].transpose(0, 2, 1).astype(f32) for which in range(3)
    )
    return (
        jnp.stack(mixed, axis=1),
        jnp.stack(tokens_grad, axis=1),
        attn_sum.astype(f32),
        table_sum,
        gain_first_sum,
        gain_second_sum,
        router_sum.T,
        gate_sum,
        up_sum,
        down_sum,
    )


def solution(mesh):
    placed = (
        P("cp", ("dp", "ep"), None),
        P(("dp", "ep")),
        P("cp", ("dp", "ep"), None),
        P("cp", ("dp", "ep"), None),
        P(),
        P(),
        P(),
        P(),
        P(),
        P(),
        P("ep", None, None),
        P("ep", None, None),
        P("ep", None, None),
        P("cp", ("dp", "ep"), None),
    )
    sizes = dict(mesh.shape)
    square = sizes["dp"] == 4 and sizes["ep"] == 2 and sizes["cp"] == 4
    return jax.shard_map(
        fast_device if square else on_device,
        mesh=mesh,
        in_specs=placed,
        out_specs=(
            P("cp", ("dp", "ep"), None),
            P("cp", ("dp", "ep"), None),
            P(None, ("dp", "ep", "cp")),
            P(),
            P(),
            P(),
            P(),
            P("ep", None, ("dp", "cp")),
            P("ep", None, ("dp", "cp")),
            P("ep", None, ("dp", "cp")),
        ),
        check_vma=False,
    )
```

```python
import functools

import jax
import jax.numpy as jnp
from jax import lax
from jax.experimental import pallas as pl
from jax.experimental.pallas import tpu as pltpu
from jax.sharding import PartitionSpec as P

epsilon = 1e-06
masked_value = -1000000000.0


def gelu_tanh(values):
    return jax.nn.gelu(values, approximate=True)


def root_scale(values):
    return lax.rsqrt(jnp.mean(values * values, axis=-1, keepdims=True) + epsilon)


def norm_back(grad_in, values, scale_rows, gain_vector):
    scaled = grad_in * gain_vector
    inner_mean = jnp.mean(scaled * values, axis=-1, keepdims=True)
    return scale_rows * (scaled - values * scale_rows * scale_rows * inner_mean)


def block_logits(
    queries, key_rows, key_start, query_pos, lengths, table_step, rise_points, head_scale
):
    key_count = key_rows.shape[0]
    key_pos = key_start + jnp.arange(key_count, dtype=jnp.int32)
    scores = (
        jnp.einsum("qshd,kshd->shqk", queries, key_rows, preferred_element_type=jnp.float32)
        * head_scale
    )
    distance = query_pos[:, None] - key_pos[None, :]
    steps = (distance[:, :, None] >= rise_points[None, None, :]).astype(jnp.float32)
    pair_bias = jnp.einsum("hb,qkb->hqk", table_step, steps, precision=lax.Precision.HIGHEST)
    allowed = (distance >= 0)[None, :, :] & (key_pos[None, None, :] < lengths[:, None, None])
    logits = jnp.where(allowed[:, None], scores + pair_bias[None], masked_value)
    return (logits, steps)


def on_device(
    tokens,
    lengths,
    expert_ids,
    places,
    buckets,
    w_attn,
    bias_table,
    norm1_gain,
    norm2_gain,
    w_router,
    w_gate,
    w_up,
    w_down,
    cotangent,
):
    span_rows, pair_count, model_width = tokens.shape
    head_count, bucket_count = bias_table.shape
    head_size = model_width // head_count
    head_scale = head_size ** (-0.5)
    n_cp = lax.axis_size("cp")
    n_ep = lax.axis_size("ep")
    seq_len = span_rows * n_cp
    row_count = span_rows * pair_count
    top_count = expert_ids.shape[2]
    experts = w_router.shape[1]
    exp_dev = w_gate.shape[0]
    capacity = (5 * row_count * top_count + 4 * experts - 1) // (4 * experts)
    my_start = lax.axis_index("cp") * span_rows
    query_pos = my_start + jnp.arange(span_rows, dtype=jnp.int32)
    live_mask = (query_pos[:, None] < lengths[None, :]).astype(jnp.float32)
    inputs = tokens.astype(jnp.float32)
    scale_first = root_scale(inputs)
    normed_first = (inputs * scale_first * norm1_gain).astype(jnp.bfloat16)
    w_qkv = w_attn[:, : 3 * model_width]
    w_out = w_attn[:, 3 * model_width :]
    qkv = jnp.einsum("csd,de->cse", normed_first, w_qkv, preferred_element_type=jnp.float32).astype(
        jnp.bfloat16
    )
    queries = qkv[..., :model_width].reshape(span_rows, pair_count, head_count, head_size)
    keyval = qkv[..., model_width:]
    keyval_all = lax.all_gather(keyval, "cp", axis=0, tiled=True)
    bucket_ids = jnp.arange(bucket_count, dtype=jnp.int32)
    rise_points = jnp.sum((buckets[:, None] < bucket_ids[None, :]).astype(jnp.int32), axis=0)
    table_step = jnp.concatenate(
        [bias_table[:, :1], bias_table[:, 1:] - bias_table[:, :-1]], axis=1
    )
    block_starts = jnp.arange(n_cp, dtype=jnp.int32) * span_rows

    def split_kv(kv_block):
        key_rows = kv_block[..., :model_width].reshape(span_rows, pair_count, head_count, head_size)
        value_rows = kv_block[..., model_width:].reshape(
            span_rows, pair_count, head_count, head_size
        )
        return (key_rows, value_rows)

    kv_blocks = keyval_all.reshape(n_cp, span_rows, pair_count, 2 * model_width)

    def max_step(state_pair, block_item):
        row_peak, row_total = state_pair
        kv_block, block_start = block_item
        key_rows, value_rows = split_kv(kv_block)
        logits, steps = block_logits(
            queries, key_rows, block_start, query_pos, lengths, table_step, rise_points, head_scale
        )
        new_peak = jnp.maximum(row_peak, jnp.max(logits, axis=-1))
        row_total = row_total * jnp.exp(row_peak - new_peak) + jnp.sum(
            jnp.exp(logits - new_peak[..., None]), axis=-1
        )
        return ((new_peak, row_total), None)

    stat_shape = (pair_count, head_count, span_rows)
    (row_peak, row_total), unused = lax.scan(
        max_step,
        (jnp.full(stat_shape, masked_value, jnp.float32), jnp.zeros(stat_shape, jnp.float32)),
        (kv_blocks, block_starts),
    )
    log_total = row_peak + jnp.log(row_total)

    def value_step(running, block_item):
        kv_block, block_start = block_item
        key_rows, value_rows = split_kv(kv_block)
        logits, steps = block_logits(
            queries, key_rows, block_start, query_pos, lengths, table_step, rise_points, head_scale
        )
        weights = jnp.exp(logits - log_total[..., None]).astype(jnp.bfloat16)
        return (
            running
            + jnp.einsum(
                "shqk,kshd->qshd", weights, value_rows, preferred_element_type=jnp.float32
            ),
            None,
        )

    attended, unused = lax.scan(
        value_step,
        jnp.zeros((span_rows, pair_count, head_count, head_size), jnp.float32),
        (kv_blocks, block_starts),
    )
    attended = attended.reshape(span_rows, pair_count, model_width)
    attended_low = attended.astype(jnp.bfloat16)
    projected = jnp.einsum("csd,de->cse", attended_low, w_out, preferred_element_type=jnp.float32)
    hidden = inputs + live_mask[..., None] * projected
    scale_second = root_scale(hidden)
    normed_second = (hidden * scale_second * norm2_gain).astype(jnp.bfloat16)
    router_logits = jnp.einsum(
        "csd,de->cse", normed_second, w_router, preferred_element_type=jnp.float32
    )
    router_probs = jax.nn.softmax(router_logits, axis=-1)
    expert_hot = (expert_ids[..., None] == jnp.arange(experts, dtype=jnp.int32)).astype(jnp.float32)
    kept_mask = (places >= 0).astype(jnp.float32)
    gate_values = jnp.sum(expert_hot * router_probs[:, :, None, :], axis=-1) * kept_mask
    target = jnp.where(places >= 0, expert_ids * capacity + places, -1).reshape(
        row_count, top_count
    )
    slot_ids = jnp.arange(experts * capacity, dtype=jnp.int32)
    route_hot = (target[None, :, :] == slot_ids[:, None, None]).astype(jnp.bfloat16)
    dispatch = jnp.sum(route_hot, axis=2)
    sent_rows = jnp.dot(
        dispatch, normed_second.reshape(row_count, model_width), preferred_element_type=jnp.float32
    )
    sent_rows = sent_rows.astype(jnp.bfloat16).reshape(n_ep, exp_dev, capacity, model_width)
    arrived = lax.all_to_all(sent_rows, "ep", split_axis=0, concat_axis=0, tiled=True)
    gate_pre = jnp.einsum("secd,edf->secf", arrived, w_gate, preferred_element_type=jnp.float32)
    up_pre = jnp.einsum("secd,edf->secf", arrived, w_up, preferred_element_type=jnp.float32)
    active, gelu_pullback = jax.vjp(gelu_tanh, gate_pre)
    inner_act = (active * up_pre).astype(jnp.bfloat16)
    produced = jnp.einsum(
        "secf,edf->secd", inner_act, w_down, preferred_element_type=jnp.float32
    ).astype(jnp.bfloat16)
    returned = lax.all_to_all(produced, "ep", split_axis=0, concat_axis=0, tiled=True).reshape(
        experts * capacity, model_width
    )
    picked = jnp.einsum("jrk,jd->rkd", route_hot, returned, preferred_element_type=jnp.float32)
    gate_flat = gate_values.reshape(row_count, top_count)
    mixed = hidden.reshape(row_count, model_width) + jnp.sum(gate_flat[..., None] * picked, axis=1)
    mixed = mixed.reshape(span_rows, pair_count, model_width).astype(jnp.bfloat16)
    grad_out = cotangent.astype(jnp.float32).reshape(row_count, model_width)
    gate_grads = jnp.sum(grad_out[:, None, :] * picked, axis=-1)
    sent_back = (gate_flat[..., None] * grad_out[:, None, :]).astype(jnp.bfloat16)
    scattered = jnp.einsum("jrk,rkd->jd", route_hot, sent_back, preferred_element_type=jnp.float32)
    scattered = scattered.astype(jnp.bfloat16).reshape(n_ep, exp_dev, capacity, model_width)
    grad_produced = lax.all_to_all(scattered, "ep", split_axis=0, concat_axis=0, tiled=True)
    down_grad = jnp.einsum(
        "secd,secf->edf", grad_produced, inner_act, preferred_element_type=jnp.float32
    )
    grad_inner = jnp.einsum(
        "secd,edf->secf", grad_produced, w_down, preferred_element_type=jnp.float32
    )
    grad_gate_pre = gelu_pullback(grad_inner * up_pre)[0].astype(jnp.bfloat16)
    grad_up_pre = (grad_inner * active).astype(jnp.bfloat16)
    gate_grad = jnp.einsum(
        "secd,secf->edf", arrived, grad_gate_pre, preferred_element_type=jnp.float32
    )
    up_grad = jnp.einsum("secd,secf->edf", arrived, grad_up_pre, preferred_element_type=jnp.float32)
    grad_arrived = jnp.einsum(
        "secf,edf->secd", grad_gate_pre, w_gate, preferred_element_type=jnp.float32
    )
    grad_arrived = (
        grad_arrived
        + jnp.einsum("secf,edf->secd", grad_up_pre, w_up, preferred_element_type=jnp.float32)
    ).astype(jnp.bfloat16)
    grad_sent = lax.all_to_all(grad_arrived, "ep", split_axis=0, concat_axis=0, tiled=True).reshape(
        experts * capacity, model_width
    )
    grad_rows = jnp.einsum("jr,jd->rd", dispatch, grad_sent, preferred_element_type=jnp.float32)
    choice_grads = gate_grads.reshape(span_rows, pair_count, top_count) * kept_mask
    prob_grads = jnp.sum(expert_hot * choice_grads[..., None], axis=2)
    logit_grads = router_probs * (
        prob_grads - jnp.sum(router_probs * prob_grads, axis=-1, keepdims=True)
    )
    logit_grads = logit_grads.astype(jnp.bfloat16)
    router_grad = jnp.einsum(
        "csd,cse->de", normed_second, logit_grads, preferred_element_type=jnp.float32
    )
    grad_normed_second = grad_rows.reshape(span_rows, pair_count, model_width)
    grad_normed_second = grad_normed_second + jnp.einsum(
        "cse,de->csd", logit_grads, w_router, preferred_element_type=jnp.float32
    )
    gain_second_grad = jnp.sum(grad_normed_second * hidden * scale_second, axis=(0, 1))
    grad_hidden = grad_out.reshape(span_rows, pair_count, model_width) + norm_back(
        grad_normed_second, hidden, scale_second, norm2_gain
    )
    grad_proj = (live_mask[..., None] * grad_hidden).astype(jnp.bfloat16)
    out_grad = jnp.einsum(
        "csd,cse->de", attended_low, grad_proj, preferred_element_type=jnp.float32
    )
    grad_att = jnp.einsum(
        "cse,de->csd", grad_proj, w_out, preferred_element_type=jnp.float32
    ).astype(jnp.bfloat16)
    grad_att_heads = grad_att.reshape(span_rows, pair_count, head_count, head_size)
    row_terms = jnp.sum(
        grad_att_heads.astype(jnp.float32)
        * attended.reshape(span_rows, pair_count, head_count, head_size),
        axis=-1,
    )
    row_terms = row_terms.transpose(1, 2, 0)
    keyval_back = lax.all_gather(keyval, "cp", axis=0, tiled=True)
    back_blocks = keyval_back.reshape(n_cp, span_rows, pair_count, 2 * model_width)

    def pair_terms(
        query_rows, grad_rows_att, row_part, total_part, key_rows, value_rows, key_start, rows_pos
    ):
        logits, steps = block_logits(
            query_rows, key_rows, key_start, rows_pos, lengths, table_step, rise_points, head_scale
        )
        weights = jnp.exp(logits - total_part[..., None])
        weight_grads = jnp.einsum(
            "qshd,kshd->shqk", grad_rows_att, value_rows, preferred_element_type=jnp.float32
        )
        score_grads = weights * (weight_grads - row_part[..., None])
        return (weights, score_grads, steps)

    def query_side_step(state_pair, kv_block, block_start):
        query_grad, step_grad = state_pair
        key_rows, value_rows = split_kv(kv_block)
        weights, score_grads, steps = pair_terms(
            queries,
            grad_att_heads,
            row_terms,
            log_total,
            key_rows,
            value_rows,
            block_start,
            query_pos,
        )
        low_grads = score_grads.astype(jnp.bfloat16)
        query_grad = (
            query_grad
            + jnp.einsum("shqk,kshd->qshd", low_grads, key_rows, preferred_element_type=jnp.float32)
            * head_scale
        )
        step_grad = step_grad + jnp.einsum(
            "hqk,qkb->hb", jnp.sum(score_grads, axis=0), steps, precision=lax.Precision.HIGHEST
        )
        return ((query_grad, step_grad), weights, low_grads)

    start_state = (
        jnp.zeros((span_rows, pair_count, head_count, head_size), jnp.float32),
        jnp.zeros((head_count, bucket_count), jnp.float32),
    )

    def grad_step(state_pair, block_item):
        kv_block, block_start = block_item
        new_state, weights, low_grads = query_side_step(state_pair, kv_block, block_start)
        value_grad = jnp.einsum(
            "shqk,qshd->kshd",
            weights.astype(jnp.bfloat16),
            grad_att_heads,
            preferred_element_type=jnp.float32,
        )
        key_grad = (
            jnp.einsum("shqk,qshd->kshd", low_grads, queries, preferred_element_type=jnp.float32)
            * head_scale
        )
        block_grad = jnp.concatenate(
            [
                key_grad.reshape(span_rows, pair_count, model_width),
                value_grad.reshape(span_rows, pair_count, model_width),
            ],
            axis=-1,
        )
        return (new_state, block_grad)

    (query_grad, step_grad), kv_terms = lax.scan(
        grad_step, start_state, (back_blocks, block_starts)
    )
    kv_terms = kv_terms.reshape(seq_len, pair_count, 2 * model_width)
    keyval_grad = lax.psum_scatter(
        kv_terms.astype(jnp.bfloat16), "cp", scatter_dimension=0, tiled=True
    )
    table_grad = step_grad - jnp.concatenate(
        [step_grad[:, 1:], jnp.zeros((head_count, 1), jnp.float32)], axis=1
    )
    qkv_grad = jnp.concatenate(
        [query_grad.reshape(span_rows, pair_count, model_width).astype(jnp.bfloat16), keyval_grad],
        axis=-1,
    )
    qkv_weight_grad = jnp.einsum(
        "csd,cse->de", normed_first, qkv_grad, preferred_element_type=jnp.float32
    )
    grad_normed_first = jnp.einsum(
        "cse,de->csd", qkv_grad, w_qkv, preferred_element_type=jnp.float32
    )
    gain_first_grad = jnp.sum(grad_normed_first * inputs * scale_first, axis=(0, 1))
    tokens_grad = (
        grad_hidden + norm_back(grad_normed_first, inputs, scale_first, norm1_gain)
    ).astype(jnp.bfloat16)
    attn_term = jnp.concatenate([qkv_weight_grad, out_grad], axis=1)
    w_attn_grad = lax.psum_scatter(attn_term, ("dp", "ep", "cp"), scatter_dimension=1, tiled=True)
    router_sum, table_sum, gain_first_sum, gain_second_sum = lax.psum(
        (router_grad, table_grad, gain_first_grad, gain_second_grad), ("dp", "ep", "cp")
    )
    gate_sum, up_sum, down_sum = (
        lax.psum_scatter(
            gate_grad.astype(jnp.bfloat16), ("dp", "cp"), scatter_dimension=2, tiled=True
        ).astype(jnp.float32),
        lax.psum_scatter(
            up_grad.astype(jnp.bfloat16), ("dp", "cp"), scatter_dimension=2, tiled=True
        ).astype(jnp.float32),
        lax.psum_scatter(
            down_grad.astype(jnp.bfloat16), ("dp", "cp"), scatter_dimension=2, tiled=True
        ).astype(jnp.float32),
    )
    return (
        mixed,
        tokens_grad,
        w_attn_grad,
        table_sum,
        gain_first_sum,
        gain_second_sum,
        router_sum,
        gate_sum,
        up_sum,
        down_sum,
    )


minus_big = -1000000000.0
vmem_bytes = 56 * 1024 * 1024


cost_share = 0.05


def cost(flops, moved):
    return pl.CostEstimate(
        flops=int(flops * cost_share), bytes_accessed=int(moved * cost_share), transcendentals=0
    )


def held(kernel, at, count):
    def run(*refs):
        kernel(*refs[:at], *refs[at + count :])

    return run


def anywhere(arrays):
    return [pl.BlockSpec(memory_space=pl.ANY)] * len(arrays)


def compiler_params():
    return pltpu.CompilerParams(vmem_limit_bytes=vmem_bytes)


def shear(values, leftward):
    rows, lanes = values.shape
    row_ids = lax.broadcasted_iota(jnp.int32, (rows, lanes), 0)
    bit = 1
    while bit < rows:
        amount = lanes - bit if leftward else bit
        moved = pltpu.roll(values, amount, 1)
        values = jnp.where((row_ids & bit) != 0, moved, values)
        bit *= 2
    return values


def dot_nt(left, right):
    return lax.dot_general(
        left, right, (((1,), (1,)), ((), ())), preferred_element_type=jnp.float32
    )


def dot_tn(left, right):
    return lax.dot_general(
        left, right, (((0,), (0,)), ((), ())), preferred_element_type=jnp.float32
    )


def dot_nn(left, right):
    return jnp.dot(left, right, preferred_element_type=jnp.float32)


def gather_kernel(normed_ref, weight_ref, line_ref, all_ref, qkv_ref, bias_ref, send_sem, recv_sem):
    slots, count, span_rows, _ = all_ref.shape
    mine = lax.axis_index("cp")
    right, left = lax.rem(mine + 1, count), lax.rem(mine + count - 1, count)
    barrier = pltpu.get_barrier_semaphore()
    for near in (left, right):
        pl.semaphore_signal(
            barrier, inc=1, device_id={"cp": near}, device_id_type=pl.DeviceIdType.MESH
        )
    pl.semaphore_wait(barrier, 2)

    def copy(slot, hop):
        return pltpu.make_async_remote_copy(
            src_ref=normed_ref.at[slot] if hop == 0 else all_ref.at[slot, hop],
            dst_ref=all_ref.at[slot, hop + 1],
            send_sem=send_sem.at[slot, hop],
            recv_sem=recv_sem.at[slot, hop],
            device_id={"cp": right},
            device_id_type=pl.DeviceIdType.MESH,
        )

    for slot in range(slots):
        copy(slot, 0).start()
    for slot in range(slots):
        rows = normed_ref[slot]
        all_ref[slot, 0] = rows
        qkv_ref[slot, 0] = dot_nn(rows, weight_ref[...]).astype(jnp.bfloat16)
    columns = bias_ref.shape[2]
    lanes = span_rows + columns
    for head in range(bias_ref.shape[0]):
        line = pltpu.roll(line_ref[head], lanes - (span_rows - 1), 1)
        full = jnp.broadcast_to(line, (span_rows, lanes))
        bias_ref[head] = shear(full, False)[:, :columns]
    for hop in range(1, count):
        for slot in range(slots):
            copy(slot, hop - 1).wait_recv()
            if hop < count - 1:
                copy(slot, hop).start()
            rows = all_ref[slot, hop]
            qkv_ref[slot, hop] = dot_nn(rows, weight_ref[...]).astype(jnp.bfloat16)
    for hop in range(count - 1):
        for slot in range(slots):
            copy(slot, hop).wait_send()


def gather_project(normed, weight, lines, count):
    slots, span_rows, model_width = normed.shape
    columns = lines.shape[2] - span_rows
    whole = pl.BlockSpec(memory_space=pltpu.VMEM)
    return pl.pallas_call(
        gather_kernel,
        in_specs=[whole] * 3,
        out_specs=[whole] * 3,
        out_shape=[
            jax.ShapeDtypeStruct((slots, count, span_rows, model_width), jnp.bfloat16),
            jax.ShapeDtypeStruct((slots, count, span_rows, weight.shape[1]), jnp.bfloat16),
            jax.ShapeDtypeStruct((lines.shape[0], span_rows, columns), jnp.float32),
        ],
        scratch_shapes=[
            pltpu.SemaphoreType.DMA((slots, count - 1)),
            pltpu.SemaphoreType.DMA((slots, count - 1)),
        ],
        cost_estimate=cost(60e9, 20e6),
        compiler_params=pltpu.CompilerParams(
            vmem_limit_bytes=vmem_bytes, collective_id=0, has_side_effects=True
        ),
        name="gather_project",
    )(normed, weight, lines)


def key_masks(length, blocks, span_rows):
    masks = []
    for block in range(blocks):
        position = block * span_rows + lax.broadcasted_iota(jnp.int32, (1, span_rows), 1)
        masks.append(jnp.where(position < length, 0.0, minus_big))
    return masks


def forward_kernel(
    scale, head_size, meta_ref, q_ref, k_ref, v_ref, bias_ref, low_ref, full_ref, total_ref
):
    _, blocks, span_rows, lanes = q_ref.shape
    mine, length = meta_ref[0], meta_ref[1]
    lane = lax.broadcasted_iota(jnp.int32, (1, lanes), 1)
    masks = key_masks(length, blocks, span_rows)

    def place(block):
        return lax.rem(mine - block + blocks, blocks)

    for row in range(blocks):
        queries = q_ref[0, place(row)]
        totals = jnp.zeros((span_rows, lanes), jnp.float32)
        result = jnp.zeros((span_rows, lanes), jnp.float32)
        for half in range(lanes // head_size):
            own = lane // head_size == half
            head_q = queries * jnp.where(own, scale, 0.0).astype(jnp.bfloat16)
            head_v = jnp.where(own, 1.0, 0.0).astype(jnp.bfloat16)
            logits = []
            for column in range(row + 1):
                at = (blocks - 1 - row + column) * span_rows
                part = dot_nt(head_q, k_ref[0, place(column)])
                part = part + bias_ref[half, :, at : at + span_rows] + masks[column]
                logits.append(part)
            peak = jnp.max(logits[0], axis=1, keepdims=True)
            for part in logits[1:]:
                peak = jnp.maximum(peak, jnp.max(part, axis=1, keepdims=True))
            total = jnp.zeros((span_rows, 1), jnp.float32)
            mixed = jnp.zeros((span_rows, lanes), jnp.float32)
            for column in range(row + 1):
                weights = jnp.exp(logits[column] - peak)
                total = total + jnp.sum(weights, axis=1, keepdims=True)
                mixed = mixed + dot_nn(
                    weights.astype(jnp.bfloat16), v_ref[0, place(column)] * head_v
                )
            result = result + mixed / total
            totals = jnp.where(lane == half, peak + jnp.log(total), totals)
        low_ref[place(row)] = result.astype(jnp.bfloat16)
        full_ref[row] = result
        total_ref[row] = totals


def attend_forward(meta, slot, qkv, bias, scale, head_size):
    _, blocks, span_rows, width = qkv.shape
    pairs = width // (3 * 128)
    per_pair = bias.shape[0] // pairs

    def part(which):
        return pl.BlockSpec((1, blocks, span_rows, 128), lambda p: (slot, 0, 0, 3 * p + which))

    plain = pl.BlockSpec((blocks, span_rows, 128), lambda p: (0, 0, p))

    return pl.pallas_call(
        functools.partial(forward_kernel, scale, head_size),
        grid=(pairs,),
        in_specs=[
            pl.BlockSpec(memory_space=pltpu.SMEM),
            part(0),
            part(1),
            part(2),
            pl.BlockSpec((per_pair,) + bias.shape[1:], lambda p: (p, 0, 0)),
        ],
        out_specs=[plain, plain, plain],
        out_shape=[
            jax.ShapeDtypeStruct((blocks, span_rows, pairs * 128), jnp.bfloat16),
            jax.ShapeDtypeStruct((blocks, span_rows, pairs * 128), jnp.float32),
            jax.ShapeDtypeStruct((blocks, span_rows, pairs * 128), jnp.float32),
        ],
        cost_estimate=cost(8e9, 8e6),
        compiler_params=compiler_params(),
        name="attend_forward",
    )(meta, qkv, qkv, qkv, bias)


def backward_body(
    mine, length, scale, head_size, qkv_ref, bias_ref, grad_ref, full_ref, total_ref, ring_ref, line_ref, work,
    after_pair=None,
):
    key_sum, value_sum, plane = work
    blocks, span_rows, width = qkv_ref.shape
    lanes = 128
    lane = lax.broadcasted_iota(jnp.int32, (1, lanes), 1)
    masks = key_masks(length, blocks, span_rows)
    halves = lanes // head_size

    def place(block):
        return lax.rem(mine - block + blocks, blocks)

    def one_pair(pair, carry):
        wide = pl.multiple_of(pair * (3 * lanes), lanes)
        own_lanes = pl.ds(pl.multiple_of(pair * lanes, lanes), lanes)
        part = [pl.ds(pl.multiple_of(wide + which * lanes, lanes), lanes) for which in range(3)]
        key_sum[...] = jnp.zeros_like(key_sum)
        value_sum[...] = jnp.zeros_like(value_sum)
        plane[...] = jnp.zeros_like(plane)
        for row in range(blocks):
            queries = qkv_ref[place(row), :, part[0]]
            grads = grad_ref[lax.rem(row - mine + blocks, blocks), :, own_lanes]
            products = grads.astype(jnp.float32) * full_ref[row, :, own_lanes]
            totals = total_ref[row, :, own_lanes]
            query_sum = jnp.zeros((span_rows, lanes), jnp.float32)
            for half in range(halves):
                own = lane // head_size == half
                one = jnp.where(own, 1.0, 0.0).astype(jnp.bfloat16)
                head_q = queries * jnp.where(own, scale, 0.0).astype(jnp.bfloat16)
                head_g = grads * one
                delta = jnp.sum(jnp.where(own, products, 0.0), axis=1, keepdims=True)
                total = totals[:, half : half + 1]
                for column in range(row + 1):
                    at = (blocks - 1 - row + column) * span_rows
                    keys = qkv_ref[place(column), :, part[1]]
                    logits = dot_nt(head_q, keys)
                    bias = bias_ref[pair * halves + half, :, at : at + span_rows]
                    logits = logits + bias + masks[column]
                    weights = jnp.exp(logits - total)
                    weight_grads = dot_nt(head_g, qkv_ref[place(column), :, part[2]])
                    score_grads = weights * (weight_grads - delta)
                    plane[half, :, at : at + span_rows] += score_grads
                    low_weights = weights.astype(jnp.bfloat16)
                    low_grads = score_grads.astype(jnp.bfloat16)
                    query_sum = query_sum + dot_nn(low_grads, keys * one)
                    key_sum[column] += dot_tn(low_grads, head_q)
                    value_sum[column] += dot_tn(low_weights, head_g)
            ring_ref[place(row), :, part[0]] = (query_sum * scale).astype(jnp.bfloat16)
        for row in range(blocks):
            ring_ref[place(row), :, part[1]] = key_sum[row].astype(jnp.bfloat16)
            ring_ref[place(row), :, part[2]] = value_sum[row].astype(jnp.bfloat16)
        for half in range(halves):
            full = jnp.concatenate(
                [plane[half], jnp.zeros((span_rows, span_rows), jnp.float32)], axis=1
            )
            summed = jnp.sum(shear(full, True), axis=0, keepdims=True)
            line_ref[pair * halves + half] = pltpu.roll(summed, span_rows - 1, 1)
        if after_pair is not None:
            after_pair(pair)
        return carry

    lax.fori_loop(0, width // (3 * lanes), one_pair, 0)


def backward_work(blocks, span_rows, head_size):
    return [
        pltpu.VMEM((blocks, span_rows, 128), jnp.float32),
        pltpu.VMEM((blocks, span_rows, 128), jnp.float32),
        pltpu.VMEM((128 // head_size, span_rows, blocks * span_rows), jnp.float32),
    ]


def greet(*others):
    barrier = pltpu.get_barrier_semaphore()
    for other in others:
        pl.semaphore_signal(
            barrier, inc=1, device_id=other, device_id_type=pl.DeviceIdType.MESH
        )
    pl.semaphore_wait(barrier, len(others))


def push(source, target, send_sem, recv_sem, other):
    return pltpu.make_async_remote_copy(
        src_ref=source,
        dst_ref=target,
        send_sem=send_sem,
        recv_sem=recv_sem,
        device_id=other,
        device_id_type=pl.DeviceIdType.MESH,
    )


def ring_others(mine, count):
    return [{"cp": lax.rem(mine + j, count)} for j in range(1, count)]


def deliveries(source, target, sems, mine, count):
    return [
        push(
            source.at[j],
            target.at[j],
            sems.at[0, j],
            sems.at[1, j],
            {"cp": lax.rem(mine + (count - j), count)},
        )
        for j in range(1, count)
    ]


def remote_params(number):
    return pltpu.CompilerParams(
        vmem_limit_bytes=vmem_bytes, collective_id=number, has_side_effects=True
    )


def own_rows(block, length, span_rows):
    position = block * span_rows + lax.broadcasted_iota(jnp.int32, (span_rows, 1), 0)
    return jnp.where(position < length, 1.0, 0.0)


def router_of(rows, router_w, experts):
    lane = lax.broadcasted_iota(jnp.int32, (1, router_w.shape[1]), 1)
    logits = jnp.where(lane < experts, dot_nn(rows, router_w), minus_big)
    shares = jnp.exp(logits - jnp.max(logits, axis=1, keepdims=True))
    return shares / jnp.sum(shares, axis=1, keepdims=True)


def project_kernel(meta_ref, input_ref, gain_ref, weight_ref, *refs):
    attended_ref, hidden_ref, normed_ref = refs[-3:]
    parts = refs[:-3]
    count = len(parts)
    for j, part in enumerate(parts):
        owner = lax.rem(meta_ref[0] + j, count)
        for group in range(part.shape[1] // 128):
            at = pl.multiple_of((group * count + owner) * 128, 128)
            attended_ref[:, pl.ds(at, 128)] = part[:, group * 128 : (group + 1) * 128]
    projected = dot_nn(attended_ref[...], weight_ref[...])
    hidden = input_ref[...].astype(jnp.float32) + own_rows(meta_ref[0], meta_ref[1], projected.shape[0]) * projected
    hidden_ref[...] = hidden
    normed_ref[...] = (hidden * root_scale(hidden) * gain_ref[...]).astype(jnp.bfloat16)


def project_rows(meta, inputs, gain, w_attn, parts, waits=()):
    span_rows, model_width = inputs.shape
    whole = pl.BlockSpec(memory_space=pltpu.VMEM)
    return pl.pallas_call(
        held(project_kernel, 4 + len(parts), len(waits)),
        grid=(1,),
        in_specs=[
            pl.BlockSpec(memory_space=pltpu.SMEM),
            whole,
            whole,
            pl.BlockSpec((model_width, model_width), lambda i: (0, 3)),
        ]
        + [whole] * len(parts)
        + anywhere(waits),
        out_specs=[whole] * 3,
        out_shape=[
            jax.ShapeDtypeStruct((span_rows, model_width), jnp.bfloat16),
            jax.ShapeDtypeStruct((span_rows, model_width), jnp.float32),
            jax.ShapeDtypeStruct((span_rows, model_width), jnp.bfloat16),
        ],
        cost_estimate=cost(2e9, 6e6),
        compiler_params=compiler_params(),
        name="project_rows",
    )(meta, inputs, gain, w_attn, *parts, *waits)


def hidden_body(
    experts, mine, length, own, first, last, grad_ref, hidden_ref, normed_ref, gain_ref, router_ref, weight_ref,
    hidden_grad_ref, proj_ref, router_grad_ref, gain_grad_ref, leaving_ref, attended,
):
    count = leaving_ref.shape[0]
    span_rows, model_width = hidden_ref.shape
    back = own[...].astype(jnp.float32) + first[...].astype(jnp.float32)
    back = back + last[...].astype(jnp.float32)
    normed = normed_ref[...]
    probs = router_of(normed, router_ref[...], experts)
    shares = back[:, model_width:]
    logit_grads = probs * (shares - jnp.sum(probs * shares, axis=1, keepdims=True))
    logit_grads = logit_grads.astype(jnp.bfloat16)
    router_grad_ref[...] = dot_tn(normed, logit_grads)
    grads = back[:, :model_width] + dot_nt(logit_grads, router_ref[...])
    hidden = hidden_ref[...]
    scale_rows = root_scale(hidden)
    gain_grad_ref[...] = jnp.sum(grads * hidden * scale_rows, axis=0, keepdims=True)
    hidden_grads = grad_ref[...].astype(jnp.float32) + norm_back(
        grads, hidden, scale_rows, gain_ref[...]
    )
    hidden_grad_ref[...] = hidden_grads
    proj = (own_rows(mine, length, span_rows) * hidden_grads).astype(jnp.bfloat16)
    proj_ref[...] = proj
    attended[...] = dot_nt(proj, weight_ref[...]).astype(jnp.bfloat16)
    for j in range(count):
        owner = lax.rem(mine + (count - j), count)
        for group in range(leaving_ref.shape[2] // 128):
            at = pl.multiple_of((group * count + owner) * 128, 128)
            leaving_ref[j, :, group * 128 : (group + 1) * 128] = attended[:, pl.ds(at, 128)]


def hidden_kernel(
    experts, scale, head_size, slots, length_ref, gain_ref, router_ref, weight_ref, qkv_ref, bias_ref, full_ref, total_ref, *refs
):
    per_slot = [refs[6 * s : 6 * s + 6] for s in range(slots)]
    refs = refs[6 * slots :]
    outs = [refs[4 * s : 4 * s + 4] for s in range(slots)]
    ring_ref, line_ref, rest_ref, leaving, arriving, attended, sems = refs[4 * slots : 4 * slots + 7]
    work = refs[4 * slots + 7 :]
    count = qkv_ref.shape[1]
    mine = lax.axis_index("cp")
    greet(*ring_others(mine, count))
    copies = []
    for s in range(slots):
        hidden_body(
            experts, mine, length_ref[s], *per_slot[s], gain_ref, router_ref, weight_ref,
            *outs[s], leaving.at[s], attended,
        )
        target = arriving if s == 0 else rest_ref.at[s - 1]
        copies.append(deliveries(leaving.at[s], target, sems.at[s], mine, count))
        for copy in copies[s]:
            copy.start()
        target[0] = leaving[s, 0]
    for copy in copies[0]:
        copy.wait()
    backward_body(
        mine, length_ref[0], scale, head_size, qkv_ref.at[0], bias_ref, arriving, full_ref, total_ref,
        ring_ref, line_ref, work,
    )
    for copy in (copy for some in copies[1:] for copy in some):
        copy.wait()


def hidden_back(
    lengths, back_rows, grads, hidden, normed, gain, router, w_attn, experts, qkvs, bias, full, total, scale, head_size, waits=()
):
    slots, count, span_rows, own_width = qkvs.shape
    model_width = hidden[0].shape[1]
    heads = bias.shape[0]
    whole = pl.BlockSpec(memory_space=pltpu.VMEM)
    f32, bf16 = jnp.float32, jnp.bfloat16
    each = []
    for s in range(slots):
        each += [*back_rows[s], grads[s], hidden[s], normed[s]]
    own_shape = (count, span_rows, own_width // 3)
    got = pl.pallas_call(
        held(
            functools.partial(hidden_kernel, experts, scale, head_size, slots),
            8 + len(each),
            len(waits),
        ),
        grid=(1,),
        in_specs=[
            pl.BlockSpec(memory_space=pltpu.SMEM),
            whole,
            whole,
            pl.BlockSpec((model_width, model_width), lambda i: (0, 3)),
            pl.BlockSpec((1,) + qkvs.shape[1:], lambda i: (0, 0, 0, 0)),
        ]
        + [whole] * (3 + len(each))
        + anywhere(waits),
        out_specs=[whole] * (4 * slots + 3),
        out_shape=[
            jax.ShapeDtypeStruct((span_rows, model_width), f32),
            jax.ShapeDtypeStruct((span_rows, model_width), bf16),
            jax.ShapeDtypeStruct((model_width, router.shape[1]), f32),
            jax.ShapeDtypeStruct((1, model_width), f32),
        ]
        * slots
        + [
            jax.ShapeDtypeStruct(qkvs.shape[1:], bf16),
            jax.ShapeDtypeStruct((heads, 1, bias.shape[2] + span_rows), f32),
            jax.ShapeDtypeStruct((slots - 1,) + own_shape, bf16),
        ],
        scratch_shapes=[
            pltpu.VMEM((slots,) + own_shape, bf16),
            pltpu.VMEM(own_shape, bf16),
            pltpu.VMEM((span_rows, model_width), bf16),
            pltpu.SemaphoreType.DMA((slots, 2, count)),
        ]
        + backward_work(count, span_rows, head_size),
        cost_estimate=cost(20e9, 20e6),
        compiler_params=remote_params(1),
        name="hidden_back",
    )(lengths, gain, router, w_attn, qkvs, bias, full, total, *each, *waits)
    return [got[4 * s : 4 * s + 4] for s in range(slots)], got[4 * slots :]


def near_others(dp, ep):
    core, across = lax.rem(dp, 2), dp // 2
    return (
        {"dp": across * 2 + (1 - core)},
        {"dp": (1 - across) * 2 + core},
        {"ep": 1 - ep},
    )


def second_kernel(
    scale, head_size, slots, length_ref, former_ref, normed_ref, qkv_ref, bias_ref, grad_ref, full_ref, total_ref,
    *refs,
):
    attended, proj, refs = refs[:slots], refs[slots : 2 * slots], refs[2 * slots :]
    ring_ref, line_ref, arrived_ref, weight_ref, rows_ref = refs[:5]
    sums, low, got_core, got_x, got_y, leaving, coming, sems, near_sems, last_sems = refs[5:15]
    work = refs[15:]
    count = qkv_ref.shape[1]
    mine = lax.axis_index("cp")
    dp, ep = lax.axis_index("dp"), lax.axis_index("ep")
    core, across = lax.rem(dp, 2), dp // 2
    others = near_others(dp, ep)
    greet(*ring_others(mine, count), *others)
    copies = deliveries(former_ref, arrived_ref, sems, mine, count)
    for copy in copies:
        copy.start()
    arrived_ref[0] = former_ref[0]
    height = sums.shape[0] // 2
    sizes = (height, height // 2, height // 4)
    bits = (core, across, ep)
    landing = (got_core, got_x, got_y)
    total = None
    for s in range(slots):
        term = dot_tn(attended[s][...], proj[s][...])
        total = term if total is None else total + term
    sums[...] = total

    def low_part(stage):
        return low.at[stage, pl.ds(0, sizes[stage])]

    def stage_copy(stage):
        return push(
            low_part(stage), landing[stage], near_sems.at[0, stage], near_sems.at[1, stage], others[stage]
        )

    def start_of(stage):
        start = 0
        for former in range(stage):
            start = start + bits[former] * sizes[former]
        return start

    def begin(stage):
        at = start_of(stage) + (1 - bits[stage]) * sizes[stage]
        away = sums[pl.ds(pl.multiple_of(at, 128), sizes[stage]), :]
        low[stage, : sizes[stage]] = away.astype(jnp.bfloat16)
        stage_copy(stage).start()

    def finish(stage):
        stage_copy(stage).wait()
        at = pl.ds(pl.multiple_of(start_of(stage + 1), 128), sizes[stage])
        sums[at, :] = sums[at, :] + landing[stage][...].astype(jnp.float32)

    def after_pair(pair):
        for stage in range(2):

            @pl.when(pair == stage)
            def _():
                finish(stage)
                begin(stage + 1)

    begin(0)
    backward_body(
        mine, length_ref[1], scale, head_size, qkv_ref.at[0], bias_ref, grad_ref.at[0], full_ref, total_ref,
        ring_ref, line_ref, work, after_pair,
    )
    finish(2)
    at = pl.ds(pl.multiple_of(start_of(3), 128), sizes[2])
    groups = leaving.shape[2] // 128
    for j in range(count):
        owner = lax.rem(mine + (count - j), count)
        for group in range(groups):
            lanes = pl.ds(pl.multiple_of((group * count + owner) * 128, 128), 128)
            part = sums[at, lanes]
            leaving[j, :, group * 128 : (group + 1) * 128] = part.astype(jnp.bfloat16)
            if j == 0:
                rows_ref[:, group * 128 : (group + 1) * 128] = part
    last = deliveries(leaving, coming, last_sems, mine, count)
    for copy in last:
        copy.start()
    total = None
    for j in range(count):
        term = dot_tn(normed_ref[0, j], former_ref[j])
        total = term if total is None else total + term
    weight_ref[...] = total
    for copy in last:
        copy.wait()
    for j in range(1, count):
        rows_ref[...] = rows_ref[...] + coming[j].astype(jnp.float32)
    for copy in copies:
        copy.wait()


def second_back(
    lengths, former, normed_all, qkvs, bias, grads, full, total, attended, proj, scale, head_size, waits=()
):
    slots, count, span_rows, own_width = qkvs.shape
    model_width = normed_all.shape[3]
    whole = pl.BlockSpec(memory_space=pltpu.VMEM)
    slot = lambda a, s: pl.BlockSpec((1,) + a.shape[1:], lambda i: (s,) + (0,) * (len(a.shape) - 1))
    f32, bf16 = jnp.float32, jnp.bfloat16
    rows_shape = (model_width // 8, own_width // 3)
    return pl.pallas_call(
        held(
            functools.partial(second_kernel, scale, head_size, slots), 8 + 2 * slots, len(waits)
        ),
        grid=(1,),
        in_specs=[
            pl.BlockSpec(memory_space=pltpu.SMEM),
            whole,
            slot(normed_all, 0),
            slot(qkvs, 1),
            whole,
            whole,
            whole,
            whole,
        ]
        + [whole] * (2 * slots)
        + anywhere(waits),
        out_specs=[whole] * 5,
        out_shape=[
            jax.ShapeDtypeStruct(qkvs.shape[1:], bf16),
            jax.ShapeDtypeStruct((bias.shape[0], 1, bias.shape[2] + span_rows), f32),
            jax.ShapeDtypeStruct(qkvs.shape[1:], bf16),
            jax.ShapeDtypeStruct((model_width, own_width), f32),
            jax.ShapeDtypeStruct(rows_shape, f32),
        ],
        scratch_shapes=[
            pltpu.VMEM((model_width, model_width), f32),
            pltpu.VMEM((3, model_width // 2, model_width), bf16),
            pltpu.VMEM((model_width // 2, model_width), bf16),
            pltpu.VMEM((model_width // 4, model_width), bf16),
            pltpu.VMEM((model_width // 8, model_width), bf16),
            pltpu.VMEM((count,) + rows_shape, bf16),
            pltpu.VMEM((count,) + rows_shape, bf16),
            pltpu.SemaphoreType.DMA((2, count)),
            pltpu.SemaphoreType.DMA((2, 3)),
            pltpu.SemaphoreType.DMA((2, count)),
        ]
        + backward_work(count, span_rows, head_size),
        cost_estimate=cost(20e9, 20e6),
        compiler_params=remote_params(2),
        name="second_back",
    )(lengths, former, normed_all, qkvs, bias, grads, full, total, *attended, *proj, *waits)


def token_body(mine, input_ref, hidden_ref, gain_ref, weight_ref, parts_ref, own_ref, out_ref):
    count = parts_ref.shape[0]
    model_width = input_ref.shape[1]
    total = None
    for j in range(count):
        owner = lax.rem(mine + j, count)
        pieces = []
        for group in range(parts_ref.shape[2] // 384):
            for which in range(3):
                at = which * model_width + (group * count + owner) * 128
                pieces.append(weight_ref[:, pl.ds(pl.multiple_of(at, 128), 128)])
        part = own_ref[j] if j == 0 else parts_ref[j]
        term = dot_nt(part, jnp.concatenate(pieces, axis=1))
        total = term if total is None else total + term
    inputs = input_ref[...].astype(jnp.float32)
    back = norm_back(total, inputs, root_scale(inputs), gain_ref[...])
    out_ref[...] = (hidden_ref[...] + back).astype(jnp.bfloat16)


def final_kernel(
    slots, ring_ref, normed_ref, former_ref, own_w_ref, arrived_ref, blocks_ref, small_ref, gain_ref, weight_ref, *refs
):
    inputs, hiddens, refs = refs[:slots], refs[slots : 2 * slots], refs[2 * slots :]
    outs, refs = refs[:slots], refs[slots:]
    small_out, attn_out = refs[:2]
    coming, here, sum_blocks, low_blocks, small_now, small_in, sems, near_sems, small_sems = refs[2:11]
    got_core, got_x, got_y = refs[11:]
    count = ring_ref.shape[0]
    mine = lax.axis_index("cp")
    dp, ep = lax.axis_index("dp"), lax.axis_index("ep")
    core, across = lax.rem(dp, 2), dp // 2
    core_other, x_other, y_other = near_others(dp, ep)
    greet(*ring_others(mine, count), core_other, x_other, y_other)
    copies = deliveries(ring_ref, coming, sems, mine, count)
    for copy in copies:
        copy.start()

    total = former_ref[...]
    for j in range(count):
        total = total + dot_tn(normed_ref[0, j], ring_ref[j])
    ones = jnp.ones((8, total.shape[1]), jnp.float32)
    first_gain = lax.dot_general(
        ones,
        total * own_w_ref[...].astype(jnp.float32),
        (((1,), (1,)), ((), ())),
        precision=lax.Precision.HIGHEST,
        preferred_element_type=jnp.float32,
    )
    row = lax.broadcasted_iota(jnp.int32, small_ref.shape, 0)
    small_now[0] = jnp.where(row == 6, first_gain / gain_ref[...], small_ref[...])
    groups = total.shape[1] // 384
    for group in range(groups):
        for which in range(3):
            at = (group * 3 + which) * 128
            part = total[:, at : at + 128]
            sum_blocks[which % 2, which // 2, group] = part
            low_blocks[which % 2, which // 2, group] = part.astype(jnp.bfloat16)
        height = blocks_ref.shape[0]
        here_rows = pl.ds(pl.multiple_of((core * 4 + across * 2 + ep) * height, 128), height)
        part = blocks_ref[:, group * 128 : (group + 1) * 128]
        sum_blocks[1, 1, group] = jnp.zeros_like(sum_blocks[1, 1, group])
        low_blocks[1, 1, group] = jnp.zeros_like(low_blocks[1, 1, group])
        sum_blocks[1, 1, group, here_rows] = part
        low_blocks[1, 1, group, here_rows] = part.astype(jnp.bfloat16)
    first = push(low_blocks.at[1 - core], got_core, near_sems.at[0, 0], near_sems.at[1, 0], core_other)
    first.start()

    stages = [core_other, x_other, y_other]
    step = 1
    while step < count:
        flip = mine + step - 2 * step * lax.rem(mine // step, 2)
        stages.append({"cp": flip})
        step *= 2

    def small_push(at):
        return push(small_now.at[at], small_in.at[at], small_sems.at[0, at], small_sems.at[1, at], stages[at])

    small_push(0).start()
    token_body(mine, inputs[0], hiddens[0], gain_ref, weight_ref, arrived_ref, arrived_ref, outs[0])
    first.wait()
    here[...] = sum_blocks[core] + got_core[...].astype(jnp.float32)
    low_blocks[0, 0] = here[1 - across].astype(jnp.bfloat16)
    second = push(low_blocks.at[0, 0], got_x, near_sems.at[0, 1], near_sems.at[1, 1], x_other)
    second.start()
    for at in range(len(stages)):
        small_push(at).wait()
        now = small_now[at] + small_in[at]
        if at + 1 < len(stages):
            small_now[at + 1] = now
            small_push(at + 1).start()
        else:
            small_out[...] = now
        if at == 1:
            second.wait()
            sum_blocks[0, 0] = here[across] + got_x[...].astype(jnp.float32)
            low_blocks[0, 1, 0] = sum_blocks[0, 0, 1 - ep].astype(jnp.bfloat16)
            third = push(low_blocks.at[0, 1, 0], got_y, near_sems.at[0, 2], near_sems.at[1, 2], y_other)
            third.start()
    third.wait()
    attn_out[...] = sum_blocks[0, 0, ep] + got_y[...].astype(jnp.float32)
    for copy in copies:
        copy.wait()
    token_body(mine, inputs[1], hiddens[1], gain_ref, weight_ref, coming, ring_ref, outs[1])


def final_back(ring, normed_all, former, own_w, arrived, blocks, small, gain, w_attn, inputs, hiddens):
    count, span_rows, own_width = ring.shape
    slots = len(inputs)
    model_width = inputs[0].shape[1]
    groups = blocks.shape[1] // 128
    whole = pl.BlockSpec(memory_space=pltpu.VMEM)
    f32, bf16 = jnp.float32, jnp.bfloat16
    stages = 3 + (count - 1).bit_length()
    tile = (model_width, 128)
    return pl.pallas_call(
        functools.partial(final_kernel, slots),
        grid=(1,),
        in_specs=[
            whole,
            pl.BlockSpec((1,) + normed_all.shape[1:], lambda i: (1, 0, 0, 0)),
            whole,
            whole,
            whole,
            whole,
            whole,
            whole,
            pl.BlockSpec((model_width, 3 * model_width), lambda i: (0, 0)),
        ]
        + [whole] * (2 * slots),
        out_specs=[whole] * (slots + 2),
        out_shape=[jax.ShapeDtypeStruct((span_rows, model_width), bf16)] * slots
        + [jax.ShapeDtypeStruct(small.shape, f32), jax.ShapeDtypeStruct(tile, f32)],
        scratch_shapes=[
            pltpu.VMEM(ring.shape, bf16),
            pltpu.VMEM((2, groups) + tile, f32),
            pltpu.VMEM((2, 2, groups) + tile, f32),
            pltpu.VMEM((2, 2, groups) + tile, bf16),
            pltpu.VMEM((stages,) + small.shape, f32),
            pltpu.VMEM((stages,) + small.shape, f32),
            pltpu.SemaphoreType.DMA((2, count)),
            pltpu.SemaphoreType.DMA((2, 3)),
            pltpu.SemaphoreType.DMA((2, stages)),
            pltpu.VMEM((2, groups) + tile, bf16),
            pltpu.VMEM((groups,) + tile, bf16),
            pltpu.VMEM(tile, bf16),
        ],
        cost_estimate=cost(20e9, 20e6),
        compiler_params=remote_params(3),
        name="final_back",
    )(ring, normed_all, former, own_w, arrived, blocks, small, gain, w_attn, *inputs, *hiddens)


gelu_inner = 0.7978845608028654
gelu_cubic = 0.044715


def pick_kernel(base_ref, target_ref, *refs):
    out_ref = refs[-1]
    sources, experts, capacity, _ = out_ref.shape
    parts = (len(refs) - 1) // sources
    for source in range(sources):
        for expert in range(experts):
            picked = None
            for at in range(parts):
                part = refs[source * parts + at]
                span = part.shape[0]
                ids = lax.broadcasted_iota(jnp.int32, (capacity, span), 0)
                ids = ids + (base_ref[0] + expert * capacity)
                hot = jnp.zeros((capacity, span), jnp.float32)
                for choice in range(target_ref.shape[1]):
                    chosen = target_ref[source, choice : choice + 1, at * span : (at + 1) * span]
                    hot = hot + jnp.where(ids == chosen, 1.0, 0.0)
                term = dot_nn(hot.astype(jnp.bfloat16), part[...])
                picked = term if picked is None else picked + term
            out_ref[source, expert] = picked.astype(jnp.bfloat16)


def pick_rows(base, targets, blocks, experts, capacity, waits=()):
    flat = [part for parts in blocks for part in parts]
    width = flat[0].shape[1]
    whole = pl.BlockSpec(memory_space=pltpu.VMEM)
    return pl.pallas_call(
        held(pick_kernel, 2 + len(flat), len(waits)),
        in_specs=[pl.BlockSpec(memory_space=pltpu.SMEM)]
        + [whole] * (1 + len(flat))
        + anywhere(waits),
        out_specs=whole,
        out_shape=jax.ShapeDtypeStruct((len(blocks), experts, capacity, width), jnp.bfloat16),
        cost_estimate=cost(1.6e9 * len(blocks), 3e6 * len(blocks)),
        compiler_params=compiler_params(),
        name="pick_rows",
    )(base, targets, *flat, *waits)


def place_kernel(experts, base_ref, target_ref, *refs):
    pairs = [refs[2 * e : 2 * e + 2] for e in range(experts)]
    out_refs = refs[2 * experts :]
    sources, capacity, _ = pairs[0][0].shape
    parts = len(out_refs) // sources
    span = out_refs[0].shape[0]
    for source in range(sources):
        both = [
            (mine[source].astype(jnp.float32) + theirs[source].astype(jnp.float32)).astype(
                jnp.bfloat16
            )
            for mine, theirs in pairs
        ]
        for at in range(parts):
            total = None
            for expert in range(experts):
                ids = lax.broadcasted_iota(jnp.int32, (span, capacity), 1)
                ids = ids + (base_ref[0] + expert * capacity)
                hot = jnp.zeros((span, capacity), jnp.float32)
                for choice in range(target_ref.shape[2]):
                    chosen = target_ref[source, at * span : (at + 1) * span, choice : choice + 1]
                    hot = hot + jnp.where(ids == chosen, 1.0, 0.0)
                term = dot_nn(hot.astype(jnp.bfloat16), both[expert])
                total = term if total is None else total + term
            out_refs[source * parts + at][...] = total.astype(jnp.bfloat16)


def place_rows(base, targets, pairs, parts, waits=()):
    sources, capacity, width = pairs[0][0].shape
    span = targets.shape[1] // parts
    whole = pl.BlockSpec(memory_space=pltpu.VMEM)
    flat = [part for pair in pairs for part in pair]
    return pl.pallas_call(
        held(functools.partial(place_kernel, len(pairs)), 2 + len(flat), len(waits)),
        in_specs=[pl.BlockSpec(memory_space=pltpu.SMEM)]
        + [whole] * (1 + len(flat))
        + anywhere(waits),
        out_specs=[whole] * (sources * parts),
        out_shape=[jax.ShapeDtypeStruct((span, width), jnp.bfloat16)] * (sources * parts),
        cost_estimate=cost(1.6e9 * sources, 4e6 * sources),
        compiler_params=compiler_params(),
        name="place_rows",
    )(base, targets, *flat, *waits)


def expert_kernel(
    experts,
    own_units,
    kept_count,
    ends,
    first_ref,
    window_ref,
    *refs,
):
    given, refs = refs[: 4 * len(ends)], refs[4 * len(ends) :]
    router_ref, gate_ref, up_ref, down_ref = refs[:4]
    refs = refs[4 + kept_count :]
    back_mine, back_theirs, out_mine, out_theirs = refs[:4]
    kept_rows, kept_grads, kept_gate, kept_up, kept_inner = refs[4:]
    capacity, model_width = given[0].shape[2:]
    source = pl.program_id(1)

    def chosen(which):
        value = given[which][0, 0]
        for at in range(1, len(ends)):
            value = jnp.where(source < ends[at - 1], value, given[4 * at + which][0, 0])
        return value

    rows = jnp.concatenate([chosen(0), chosen(1)], axis=0)
    grads = jnp.concatenate([chosen(2), chosen(3)], axis=0)
    kept_rows[0, 0] = rows
    kept_grads[0, 0] = grads
    lane = lax.broadcasted_iota(jnp.int32, (1, router_ref.shape[1]), 1)
    expert = first_ref[0] + pl.program_id(0)
    probs = router_of(rows, router_ref[...], experts)
    gates = jnp.sum(jnp.where(lane == expert, probs, 0.0), axis=1, keepdims=True)
    unit = lax.broadcasted_iota(jnp.int32, (1, gate_ref.shape[2]), 1) - window_ref[1]
    own = jnp.logical_and(unit >= 0, unit < own_units)
    gate_w, up_w, down_w = gate_ref[0], up_ref[0], down_ref[0]
    gate_pre = dot_nn(rows, gate_w)
    up_pre = jnp.where(own, dot_nn(rows, up_w), 0.0)
    square = gate_pre * gate_pre
    tanh = jnp.tanh(gelu_inner * gate_pre * (1.0 + gelu_cubic * square))
    half = 0.5 + 0.5 * tanh
    active = gate_pre * half
    slope = half + active * (1.0 - tanh) * (gelu_inner * (1.0 + 3.0 * gelu_cubic * square))
    inner = active * up_pre
    low_inner = inner.astype(jnp.bfloat16)
    plain_grads = jnp.where(own, dot_nn(grads, down_w), 0.0)
    gate_grads = jnp.sum(plain_grads * low_inner.astype(jnp.float32), axis=1, keepdims=True)
    inner_grads = plain_grads * gates
    low_gate = (inner_grads * up_pre * slope).astype(jnp.bfloat16)
    low_up = (inner_grads * active).astype(jnp.bfloat16)
    kept_gate[0, 0] = low_gate
    kept_up[0, 0] = low_up
    kept_inner[0, 0] = (inner * gates).astype(jnp.bfloat16)
    back = (dot_nt(low_gate, gate_w) + dot_nt(low_up, up_w)).astype(jnp.bfloat16)
    shares = jnp.where(lane == expert, gate_grads, 0.0).astype(jnp.bfloat16)
    out = (gates * dot_nt(low_inner, down_w)).astype(jnp.bfloat16)
    for at, back_ref, out_ref in ((0, back_mine, out_mine), (1, back_theirs, out_theirs)):
        part = slice(at * capacity, (at + 1) * capacity)
        back_ref[0, 0, :, :model_width] = back[part]
        back_ref[0, 0, :, model_width:] = shares[part]
        out_ref[0, 0] = out[part]


def run_experts(first, window, given, router, weights, kept, at, total, experts, units, chosen):
    low, high = chosen
    _, exp_dev, capacity, model_width = given[0][0].shape
    sizes = [group[0].shape[0] for group in given]
    ends = [sum(sizes[: i + 1]) for i in range(len(sizes))]
    sources = ends[-1]
    wide_units = aligned_units(units)
    tile = 2 * capacity

    def rows_of(i):
        start, size = ends[i] - sizes[i], sizes[i]
        return pl.BlockSpec(
            (1, 1, capacity, model_width),
            lambda e, k, f, w: (jnp.clip(k - start, 0, size - 1), low + e, 0, 0),
        )

    out = lambda width: pl.BlockSpec((1, 1, capacity, width), lambda e, k, f, w: (e, k, 0, 0))
    wide, rows = out(model_width + 128), out(model_width)
    weight = pl.BlockSpec(
        (pl.Element(1), pl.Element(model_width), pl.Element(wide_units)),
        lambda e, k, f, w: (low + e, 0, pl.multiple_of(w[0], 128)),
    )
    keep = lambda width: pl.BlockSpec(
        (1, 1, tile, width), lambda e, k, f, w: (low + e, at + k, 0, 0)
    )
    keep_widths = (model_width, model_width, wide_units, wide_units, wide_units)
    kept = list(kept)
    flat = [part for group in given for part in group]
    out_of = lambda width: jax.ShapeDtypeStruct(
        (high - low, sources, capacity, width), jnp.bfloat16
    )
    back_shape, out_shape = out_of(model_width + 128), out_of(model_width)
    got = pl.pallas_call(
        functools.partial(expert_kernel, experts, units, len(kept), tuple(ends)),
        grid_spec=pltpu.PrefetchScalarGridSpec(
            num_scalar_prefetch=2,
            grid=(high - low, sources),
            in_specs=[rows_of(i) for i in range(len(given)) for _ in range(4)]
            + [
                pl.BlockSpec(router.shape, lambda e, k, f, w: (0, 0)),
                weight,
                weight,
                weight,
            ]
            + anywhere(kept),
            out_specs=[wide, wide, rows, rows] + [keep(width) for width in keep_widths],
        ),
        out_shape=[back_shape, back_shape, out_shape, out_shape]
        + [jax.ShapeDtypeStruct((exp_dev, total, tile, w), jnp.bfloat16) for w in keep_widths],
        input_output_aliases={6 + len(flat) + i: 4 + i for i in range(len(kept))},
        cost_estimate=cost(20e9 * sources, 8e6 * sources),
        compiler_params=compiler_params(),
        name="expert_rows",
    )(first + low, window, *flat, router, *weights, *kept)
    return got[:4], got[4:]


def aligned_units(units):
    return (units + 127) // 128 * 128


def weight_kernel(window_ref, rows_ref, grads_ref, gate_ref, up_ref, inner_ref, weight_ref, total):
    step = pl.program_id(0)
    pieces, _, piece, _ = weight_ref.shape

    @pl.when(step == 0)
    def _():
        total[...] = jnp.zeros_like(total)

    total[0] += dot_tn(gate_ref[0, 0], rows_ref[0, 0])
    total[1] += dot_tn(up_ref[0, 0], rows_ref[0, 0])
    total[2] += dot_tn(inner_ref[0, 0], grads_ref[0, 0])

    @pl.when(step == pl.num_programs(0) - 1)
    def _():
        skip = pl.multiple_of(window_ref[1], 64)
        for at in range(pieces):
            got = total[:, pl.ds(skip + at * piece, piece), :]
            weight_ref[at] = got.astype(jnp.bfloat16)


def weight_grads(window, kept, expert, pieces, units, waits=()):
    _, tiles, tile, model_width = kept[0].shape
    wide_units = kept[2].shape[3]
    block = lambda a: pl.BlockSpec((1, 1) + a.shape[2:], lambda i: (expert, i, 0, 0))
    shape = (pieces, 3, units // pieces, model_width)
    return pl.pallas_call(
        held(weight_kernel, 1 + len(kept), len(waits)),
        grid=(tiles,),
        in_specs=[pl.BlockSpec(memory_space=pltpu.SMEM)]
        + [block(a) for a in kept]
        + anywhere(waits),
        out_specs=pl.BlockSpec(shape, lambda i: (0, 0, 0, 0)),
        out_shape=jax.ShapeDtypeStruct(shape, jnp.bfloat16),
        scratch_shapes=[pltpu.VMEM((3, wide_units, model_width), jnp.float32)],
        cost_estimate=cost(20e9, 20e6),
        compiler_params=compiler_params(),
        name="weight_grads",
    )(window, *kept, *waits)


def send(values, axis, pairs):
    return lax.ppermute(values, axis, pairs)


def after(values, *earlier):
    return lax.optimization_barrier((values, earlier))[0]


def fast_device(
    tokens,
    lengths,
    expert_ids,
    places,
    buckets,
    w_attn,
    bias_table,
    norm1_gain,
    norm2_gain,
    w_router,
    w_gate,
    w_up,
    w_down,
    cotangent,
):
    span_rows, slots, model_width = tokens.shape
    head_count, bucket_count = bias_table.shape
    head_size = model_width // head_count
    scale = head_size ** (-0.5)
    n_dp = lax.axis_size("dp")
    n_ep = lax.axis_size("ep")
    n_cp = lax.axis_size("cp")
    my_dp, my_ep, my_cp = (lax.axis_index(name) for name in ("dp", "ep", "cp"))
    seq_len = span_rows * n_cp
    rows = span_rows * slots
    top_count = expert_ids.shape[2]
    experts = w_router.shape[1]
    exp_dev = w_gate.shape[0]
    units = w_gate.shape[2] // n_dp
    capacity = (5 * rows * top_count + 4 * experts - 1) // (4 * experts)
    groups = model_width // (128 * n_cp)
    own_width = 3 * groups * 128
    heads_own = head_count // n_cp
    over_core = [(i, i ^ 1) for i in range(n_dp)]
    over_x = [(i, i ^ 2) for i in range(n_dp)]
    over_y = [(i, i ^ 1) for i in range(n_ep)]
    ring = [(i, (i + 1) % n_cp) for i in range(n_cp)]
    f32, bf16 = jnp.float32, jnp.bfloat16
    exact = lax.Precision.HIGHEST
    each = range(slots)

    low_in = [tokens[:, s] for s in each]
    inputs = jnp.stack(low_in).astype(f32)
    normed_first = (inputs * root_scale(inputs) * norm1_gain).astype(bf16)

    w_own = jnp.concatenate(
        [
            lax.dynamic_slice(
                w_attn,
                (0, which * model_width + (group * n_cp + my_cp) * 128),
                (model_width, 128),
            )
            for group in range(groups)
            for which in range(3)
        ],
        axis=1,
    )
    per_group = 128 // head_size
    own_heads = (
        jnp.arange(groups)[:, None] * (n_cp * per_group)
        + my_cp * per_group
        + jnp.arange(per_group)[None, :]
    ).reshape(heads_own)
    head_hot = (own_heads[:, None] == jnp.arange(head_count)[None, :]).astype(f32)
    bucket_hot = (buckets[:, None] == jnp.arange(bucket_count)[None, :]).astype(f32)
    own_table = jnp.dot(head_hot, bias_table, precision=exact)
    lines = jnp.einsum("hb,db->hd", own_table, bucket_hot[::-1], precision=exact)
    lines = jnp.concatenate([lines, jnp.full((heads_own, span_rows), minus_big, f32)], axis=1)
    normed_all, qkvs, bias = gather_project(normed_first, w_own, lines[:, None, :], n_cp)

    def plane_gather(parts):
        over = [send(part, "dp", over_x) for part in parts]
        up = [send(part, "ep", over_y) for part in parts]
        across = [send(over[0], "ep", over_y), send(up[1], "dp", over_x)]
        return [list(parts), over, up, across]

    target = jnp.where(places >= 0, expert_ids * capacity + places, -1)
    target_parts = plane_gather([target[:, s].T for s in each])
    target_rows = jnp.stack([jnp.concatenate(parts, axis=1) for parts in target_parts])
    target_columns = target_rows.transpose(0, 2, 1)
    base = (my_ep * (exp_dev * capacity)).astype(jnp.int32).reshape(1)
    group_at = ((0, 1), (1, 3), (3, 4))
    sources = target_rows.shape[0]
    target_groups = [
        (target_rows[low:high], target_columns[low:high]) for low, high in group_at
    ]

    def pick_group(at, blocks, waits=()):
        low, high = group_at[at]
        mine = pick_rows(
            base, target_groups[at][0], blocks[low:high], exp_dev, capacity, waits
        )
        return mine, send(mine, "dp", over_core)

    low_out = [cotangent[:, s] for s in each]
    grad_blocks = plane_gather(low_out)
    window_at = my_dp * units // 128 * 128
    window = jnp.stack([window_at, my_dp * units - window_at]).astype(jnp.int32)
    router_wide = jnp.concatenate(
        [w_router, jnp.zeros((model_width, 128 - experts), w_router.dtype)], axis=1
    )

    def deliver(blocks):
        return [blocks[0]] + [
            send(blocks[j], "cp", [(i, (i - j) % n_cp) for i in range(n_cp)])
            for j in range(1, n_cp)
        ]

    metas = [jnp.stack([my_cp.astype(jnp.int32), lengths[s]]) for s in each]
    gain_first, gain_second = norm1_gain[None, :], norm2_gain[None, :]
    fulls, totals, returned = [], [], []
    for s in each:
        if s:
            qkvs = after(qkvs, fulls[-1])
        low, full, total = attend_forward(metas[s], s, qkvs, bias, scale, head_size)
        fulls.append(full)
        totals.append(total)
        returned.append(deliver(low))
    grad_groups = [pick_group(at, grad_blocks) for at in range(len(group_at))]
    attended, hidden, normed_second = [], [], []
    for s in each:
        got = project_rows(
            metas[s],
            low_in[s],
            gain_second,
            w_attn,
            returned[s],
            [group[0] for group in grad_groups],
        )
        attended.append(got[0])
        hidden.append(got[1])
        normed_second.append(got[2])

    first = (my_ep * exp_dev).astype(jnp.int32).reshape(1)
    row_blocks = plane_gather(normed_second)

    def experts_of(at, picked, kept, chosen):
        given = [(*picked[i], *grad_groups[at + i]) for i in range(len(picked))]
        return run_experts(
            first,
            window,
            given,
            router_wide,
            (w_gate, w_up, w_down),
            kept,
            group_at[at][0],
            sources,
            experts,
            units,
            chosen,
        )

    def over_cores(mine, theirs):
        return mine, send(theirs, "dp", over_core)

    def expert_pairs(mine, theirs):
        mine, theirs = over_cores(mine, theirs)
        return [(mine[e], theirs[e]) for e in range(mine.shape[0])]

    own_columns = target_columns[: group_at[0][1]]
    rest_columns = target_columns[group_at[0][1] :]
    picked_own = pick_group(0, row_blocks)
    own, kept = experts_of(0, [picked_own], (), (0, exp_dev))
    picked_rest = [pick_group(1, row_blocks, kept[:1]), pick_group(2, row_blocks, kept[:1])]
    place_own = place_rows(
        base, own_columns, expert_pairs(own[0], own[1]), slots, [part[0] for part in picked_rest]
    )
    back_pairs, out_pairs, weight_sums = [], [], []
    weight_part = None
    for e in range(exp_dev):
        rest, kept = experts_of(1, picked_rest, kept, (e, e + 1))
        back_pairs += expert_pairs(rest[0], rest[1])
        out_pairs += expert_pairs(rest[2], rest[3])
        if e + 1 < exp_dev:
            weight_part = weight_grads(window, kept, e, n_cp, units)
            weight_sums.append(
                lax.psum_scatter(weight_part, "cp", scatter_dimension=0, tiled=False)
            )
            kept = after(kept, weight_part)
    place_rest = place_rows(base, rest_columns, back_pairs, slots)
    weight_part = weight_grads(window, kept, exp_dev - 1, n_cp, units, place_rest[:1])
    weight_sums.append(lax.psum_scatter(weight_part, "cp", scatter_dimension=0, tiled=False))
    out_own = place_rows(
        base, own_columns, expert_pairs(own[2], own[3]), slots, [weight_part]
    )
    out_rest = place_rows(base, rest_columns, out_pairs, slots, [weight_part])

    def plane_sum(own, rest):
        over, up, across = (rest[i * slots : (i + 1) * slots] for i in range(3))
        got_first = send(over[0], "dp", over_x)
        got_second = send(up[1], "ep", over_y)
        far_first = send(across[0], "dp", over_x).astype(f32)
        far_second = send(across[1], "ep", over_y).astype(f32)
        next_first = (up[0].astype(f32) + far_first).astype(bf16)
        next_second = (over[1].astype(f32) + far_second).astype(bf16)
        last_first = send(next_first, "ep", over_y)
        last_second = send(next_second, "dp", over_x)
        return [(own[0], got_first, last_first), (own[1], got_second, last_second)]

    back_rows = plane_sum(place_own, place_rest)
    got, (ringed, line_first, grads_rest) = hidden_back(
        lengths,
        back_rows,
        low_out,
        hidden,
        normed_second,
        gain_second,
        router_wide,
        w_attn,
        experts,
        qkvs,
        bias,
        fulls[0],
        totals[0],
        scale,
        head_size,
        [out_own[0], out_rest[0]],
    )
    hidden_grads, proj_grads, router_parts, gain_parts = zip(*got)
    router_grad = sum(router_parts)[:, :experts].T
    ring_second, line_second, arrived, weight_first, out_grad = second_back(
        lengths,
        ringed,
        normed_all,
        qkvs,
        bias,
        grads_rest,
        fulls[1],
        totals[1],
        attended,
        proj_grads,
        scale,
        head_size,
        weight_sums[:1],
    )
    distance_grads = (line_first + line_second)[:, 0, :seq_len][:, ::-1]
    table_grad = jnp.dot(distance_grads, bucket_hot, precision=exact)
    table_grad = jnp.einsum("hg,hb->gb", head_hot, table_grad, precision=exact)
    table_row = jnp.pad(table_grad.reshape(1, -1), ((0, 0), (0, model_width - table_grad.size)))
    small = jnp.concatenate(
        [router_grad, sum(gain_parts), table_row, jnp.zeros((2, model_width), f32)], axis=0
    )
    *tokens_grad, small_sum, attn_sum = final_back(
        ring_second,
        normed_all,
        weight_first,
        w_own,
        arrived,
        out_grad,
        small,
        gain_first,
        w_attn,
        low_in,
        hidden_grads,
    )
    router_sum, gain_second_sum = small_sum[:experts], small_sum[experts]
    table_sum = small_sum[experts + 1, : table_grad.size].reshape(table_grad.shape)
    gain_first_sum = small_sum[experts + 2]

    out_rows = plane_sum(out_own, out_rest)
    mixed = [
        (hidden[s] + sum(part.astype(f32) for part in out_rows[s])).astype(bf16) for s in each
    ]
    weight_sum = jnp.stack(weight_sums)
    gate_sum, up_sum, down_sum = (
        weight_sum[:, which].transpose(0, 2, 1).astype(f32) for which in range(3)
    )
    return (
        jnp.stack(mixed, axis=1),
        jnp.stack(tokens_grad, axis=1),
        attn_sum,
        table_sum,
        gain_first_sum,
        gain_second_sum,
        router_sum.T,
        gate_sum,
        up_sum,
        down_sum,
    )


def solution(mesh):
    placed = (
        P("cp", ("dp", "ep"), None),
        P(("dp", "ep")),
        P("cp", ("dp", "ep"), None),
        P("cp", ("dp", "ep"), None),
        P(),
        P(),
        P(),
        P(),
        P(),
        P(),
        P("ep", None, None),
        P("ep", None, None),
        P("ep", None, None),
        P("cp", ("dp", "ep"), None),
    )
    sizes = dict(mesh.shape)
    square = sizes["dp"] == 4 and sizes["ep"] == 2 and sizes["cp"] == 4
    return jax.shard_map(
        fast_device if square else on_device,
        mesh=mesh,
        in_specs=placed,
        out_specs=(
            P("cp", ("dp", "ep"), None),
            P("cp", ("dp", "ep"), None),
            P(None, ("dp", "ep", "cp")),
            P(),
            P(),
            P(),
            P(),
            P("ep", None, ("dp", "cp")),
            P("ep", None, ("dp", "cp")),
            P("ep", None, ("dp", "cp")),
        ),
        check_vma=False,
    )
```

```python
import functools

import jax
import jax.numpy as jnp
from jax import lax
from jax.experimental import pallas as pl
from jax.experimental.pallas import tpu as pltpu
from jax.sharding import PartitionSpec as P

epsilon = 1e-06
masked_value = -1000000000.0


def gelu_tanh(values):
    return jax.nn.gelu(values, approximate=True)


def root_scale(values):
    return lax.rsqrt(jnp.mean(values * values, axis=-1, keepdims=True) + epsilon)


def norm_back(grad_in, values, scale_rows, gain_vector):
    scaled = grad_in * gain_vector
    inner_mean = jnp.mean(scaled * values, axis=-1, keepdims=True)
    return scale_rows * (scaled - values * scale_rows * scale_rows * inner_mean)


def block_logits(
    queries, key_rows, key_start, query_pos, lengths, table_step, rise_points, head_scale
):
    key_count = key_rows.shape[0]
    key_pos = key_start + jnp.arange(key_count, dtype=jnp.int32)
    scores = (
        jnp.einsum("qshd,kshd->shqk", queries, key_rows, preferred_element_type=jnp.float32)
        * head_scale
    )
    distance = query_pos[:, None] - key_pos[None, :]
    steps = (distance[:, :, None] >= rise_points[None, None, :]).astype(jnp.float32)
    pair_bias = jnp.einsum("hb,qkb->hqk", table_step, steps, precision=lax.Precision.HIGHEST)
    allowed = (distance >= 0)[None, :, :] & (key_pos[None, None, :] < lengths[:, None, None])
    logits = jnp.where(allowed[:, None], scores + pair_bias[None], masked_value)
    return (logits, steps)


def on_device(
    tokens,
    lengths,
    expert_ids,
    places,
    buckets,
    w_attn,
    bias_table,
    norm1_gain,
    norm2_gain,
    w_router,
    w_gate,
    w_up,
    w_down,
    cotangent,
):
    span_rows, pair_count, model_width = tokens.shape
    head_count, bucket_count = bias_table.shape
    head_size = model_width // head_count
    head_scale = head_size ** (-0.5)
    n_cp = lax.axis_size("cp")
    n_ep = lax.axis_size("ep")
    seq_len = span_rows * n_cp
    row_count = span_rows * pair_count
    top_count = expert_ids.shape[2]
    experts = w_router.shape[1]
    exp_dev = w_gate.shape[0]
    capacity = (5 * row_count * top_count + 4 * experts - 1) // (4 * experts)
    my_start = lax.axis_index("cp") * span_rows
    query_pos = my_start + jnp.arange(span_rows, dtype=jnp.int32)
    live_mask = (query_pos[:, None] < lengths[None, :]).astype(jnp.float32)
    inputs = tokens.astype(jnp.float32)
    scale_first = root_scale(inputs)
    normed_first = (inputs * scale_first * norm1_gain).astype(jnp.bfloat16)
    w_qkv = w_attn[:, : 3 * model_width]
    w_out = w_attn[:, 3 * model_width :]
    qkv = jnp.einsum("csd,de->cse", normed_first, w_qkv, preferred_element_type=jnp.float32).astype(
        jnp.bfloat16
    )
    queries = qkv[..., :model_width].reshape(span_rows, pair_count, head_count, head_size)
    keyval = qkv[..., model_width:]
    keyval_all = lax.all_gather(keyval, "cp", axis=0, tiled=True)
    bucket_ids = jnp.arange(bucket_count, dtype=jnp.int32)
    rise_points = jnp.sum((buckets[:, None] < bucket_ids[None, :]).astype(jnp.int32), axis=0)
    table_step = jnp.concatenate(
        [bias_table[:, :1], bias_table[:, 1:] - bias_table[:, :-1]], axis=1
    )
    block_starts = jnp.arange(n_cp, dtype=jnp.int32) * span_rows

    def split_kv(kv_block):
        key_rows = kv_block[..., :model_width].reshape(span_rows, pair_count, head_count, head_size)
        value_rows = kv_block[..., model_width:].reshape(
            span_rows, pair_count, head_count, head_size
        )
        return (key_rows, value_rows)

    kv_blocks = keyval_all.reshape(n_cp, span_rows, pair_count, 2 * model_width)

    def max_step(state_pair, block_item):
        row_peak, row_total = state_pair
        kv_block, block_start = block_item
        key_rows, value_rows = split_kv(kv_block)
        logits, steps = block_logits(
            queries, key_rows, block_start, query_pos, lengths, table_step, rise_points, head_scale
        )
        new_peak = jnp.maximum(row_peak, jnp.max(logits, axis=-1))
        row_total = row_total * jnp.exp(row_peak - new_peak) + jnp.sum(
            jnp.exp(logits - new_peak[..., None]), axis=-1
        )
        return ((new_peak, row_total), None)

    stat_shape = (pair_count, head_count, span_rows)
    (row_peak, row_total), unused = lax.scan(
        max_step,
        (jnp.full(stat_shape, masked_value, jnp.float32), jnp.zeros(stat_shape, jnp.float32)),
        (kv_blocks, block_starts),
    )
    log_total = row_peak + jnp.log(row_total)

    def value_step(running, block_item):
        kv_block, block_start = block_item
        key_rows, value_rows = split_kv(kv_block)
        logits, steps = block_logits(
            queries, key_rows, block_start, query_pos, lengths, table_step, rise_points, head_scale
        )
        weights = jnp.exp(logits - log_total[..., None]).astype(jnp.bfloat16)
        return (
            running
            + jnp.einsum(
                "shqk,kshd->qshd", weights, value_rows, preferred_element_type=jnp.float32
            ),
            None,
        )

    attended, unused = lax.scan(
        value_step,
        jnp.zeros((span_rows, pair_count, head_count, head_size), jnp.float32),
        (kv_blocks, block_starts),
    )
    attended = attended.reshape(span_rows, pair_count, model_width)
    attended_low = attended.astype(jnp.bfloat16)
    projected = jnp.einsum("csd,de->cse", attended_low, w_out, preferred_element_type=jnp.float32)
    hidden = inputs + live_mask[..., None] * projected
    scale_second = root_scale(hidden)
    normed_second = (hidden * scale_second * norm2_gain).astype(jnp.bfloat16)
    router_logits = jnp.einsum(
        "csd,de->cse", normed_second, w_router, preferred_element_type=jnp.float32
    )
    router_probs = jax.nn.softmax(router_logits, axis=-1)
    expert_hot = (expert_ids[..., None] == jnp.arange(experts, dtype=jnp.int32)).astype(jnp.float32)
    kept_mask = (places >= 0).astype(jnp.float32)
    gate_values = jnp.sum(expert_hot * router_probs[:, :, None, :], axis=-1) * kept_mask
    target = jnp.where(places >= 0, expert_ids * capacity + places, -1).reshape(
        row_count, top_count
    )
    slot_ids = jnp.arange(experts * capacity, dtype=jnp.int32)
    route_hot = (target[None, :, :] == slot_ids[:, None, None]).astype(jnp.bfloat16)
    dispatch = jnp.sum(route_hot, axis=2)
    sent_rows = jnp.dot(
        dispatch, normed_second.reshape(row_count, model_width), preferred_element_type=jnp.float32
    )
    sent_rows = sent_rows.astype(jnp.bfloat16).reshape(n_ep, exp_dev, capacity, model_width)
    arrived = lax.all_to_all(sent_rows, "ep", split_axis=0, concat_axis=0, tiled=True)
    gate_pre = jnp.einsum("secd,edf->secf", arrived, w_gate, preferred_element_type=jnp.float32)
    up_pre = jnp.einsum("secd,edf->secf", arrived, w_up, preferred_element_type=jnp.float32)
    active, gelu_pullback = jax.vjp(gelu_tanh, gate_pre)
    inner_act = (active * up_pre).astype(jnp.bfloat16)
    produced = jnp.einsum(
        "secf,edf->secd", inner_act, w_down, preferred_element_type=jnp.float32
    ).astype(jnp.bfloat16)
    returned = lax.all_to_all(produced, "ep", split_axis=0, concat_axis=0, tiled=True).reshape(
        experts * capacity, model_width
    )
    picked = jnp.einsum("jrk,jd->rkd", route_hot, returned, preferred_element_type=jnp.float32)
    gate_flat = gate_values.reshape(row_count, top_count)
    mixed = hidden.reshape(row_count, model_width) + jnp.sum(gate_flat[..., None] * picked, axis=1)
    mixed = mixed.reshape(span_rows, pair_count, model_width).astype(jnp.bfloat16)
    grad_out = cotangent.astype(jnp.float32).reshape(row_count, model_width)
    gate_grads = jnp.sum(grad_out[:, None, :] * picked, axis=-1)
    sent_back = (gate_flat[..., None] * grad_out[:, None, :]).astype(jnp.bfloat16)
    scattered = jnp.einsum("jrk,rkd->jd", route_hot, sent_back, preferred_element_type=jnp.float32)
    scattered = scattered.astype(jnp.bfloat16).reshape(n_ep, exp_dev, capacity, model_width)
    grad_produced = lax.all_to_all(scattered, "ep", split_axis=0, concat_axis=0, tiled=True)
    down_grad = jnp.einsum(
        "secd,secf->edf", grad_produced, inner_act, preferred_element_type=jnp.float32
    )
    grad_inner = jnp.einsum(
        "secd,edf->secf", grad_produced, w_down, preferred_element_type=jnp.float32
    )
    grad_gate_pre = gelu_pullback(grad_inner * up_pre)[0].astype(jnp.bfloat16)
    grad_up_pre = (grad_inner * active).astype(jnp.bfloat16)
    gate_grad = jnp.einsum(
        "secd,secf->edf", arrived, grad_gate_pre, preferred_element_type=jnp.float32
    )
    up_grad = jnp.einsum("secd,secf->edf", arrived, grad_up_pre, preferred_element_type=jnp.float32)
    grad_arrived = jnp.einsum(
        "secf,edf->secd", grad_gate_pre, w_gate, preferred_element_type=jnp.float32
    )
    grad_arrived = (
        grad_arrived
        + jnp.einsum("secf,edf->secd", grad_up_pre, w_up, preferred_element_type=jnp.float32)
    ).astype(jnp.bfloat16)
    grad_sent = lax.all_to_all(grad_arrived, "ep", split_axis=0, concat_axis=0, tiled=True).reshape(
        experts * capacity, model_width
    )
    grad_rows = jnp.einsum("jr,jd->rd", dispatch, grad_sent, preferred_element_type=jnp.float32)
    choice_grads = gate_grads.reshape(span_rows, pair_count, top_count) * kept_mask
    prob_grads = jnp.sum(expert_hot * choice_grads[..., None], axis=2)
    logit_grads = router_probs * (
        prob_grads - jnp.sum(router_probs * prob_grads, axis=-1, keepdims=True)
    )
    logit_grads = logit_grads.astype(jnp.bfloat16)
    router_grad = jnp.einsum(
        "csd,cse->de", normed_second, logit_grads, preferred_element_type=jnp.float32
    )
    grad_normed_second = grad_rows.reshape(span_rows, pair_count, model_width)
    grad_normed_second = grad_normed_second + jnp.einsum(
        "cse,de->csd", logit_grads, w_router, preferred_element_type=jnp.float32
    )
    gain_second_grad = jnp.sum(grad_normed_second * hidden * scale_second, axis=(0, 1))
    grad_hidden = grad_out.reshape(span_rows, pair_count, model_width) + norm_back(
        grad_normed_second, hidden, scale_second, norm2_gain
    )
    grad_proj = (live_mask[..., None] * grad_hidden).astype(jnp.bfloat16)
    out_grad = jnp.einsum(
        "csd,cse->de", attended_low, grad_proj, preferred_element_type=jnp.float32
    )
    grad_att = jnp.einsum(
        "cse,de->csd", grad_proj, w_out, preferred_element_type=jnp.float32
    ).astype(jnp.bfloat16)
    grad_att_heads = grad_att.reshape(span_rows, pair_count, head_count, head_size)
    row_terms = jnp.sum(
        grad_att_heads.astype(jnp.float32)
        * attended.reshape(span_rows, pair_count, head_count, head_size),
        axis=-1,
    )
    row_terms = row_terms.transpose(1, 2, 0)
    keyval_back = lax.all_gather(keyval, "cp", axis=0, tiled=True)
    back_blocks = keyval_back.reshape(n_cp, span_rows, pair_count, 2 * model_width)

    def pair_terms(
        query_rows, grad_rows_att, row_part, total_part, key_rows, value_rows, key_start, rows_pos
    ):
        logits, steps = block_logits(
            query_rows, key_rows, key_start, rows_pos, lengths, table_step, rise_points, head_scale
        )
        weights = jnp.exp(logits - total_part[..., None])
        weight_grads = jnp.einsum(
            "qshd,kshd->shqk", grad_rows_att, value_rows, preferred_element_type=jnp.float32
        )
        score_grads = weights * (weight_grads - row_part[..., None])
        return (weights, score_grads, steps)

    def query_side_step(state_pair, kv_block, block_start):
        query_grad, step_grad = state_pair
        key_rows, value_rows = split_kv(kv_block)
        weights, score_grads, steps = pair_terms(
            queries,
            grad_att_heads,
            row_terms,
            log_total,
            key_rows,
            value_rows,
            block_start,
            query_pos,
        )
        low_grads = score_grads.astype(jnp.bfloat16)
        query_grad = (
            query_grad
            + jnp.einsum("shqk,kshd->qshd", low_grads, key_rows, preferred_element_type=jnp.float32)
            * head_scale
        )
        step_grad = step_grad + jnp.einsum(
            "hqk,qkb->hb", jnp.sum(score_grads, axis=0), steps, precision=lax.Precision.HIGHEST
        )
        return ((query_grad, step_grad), weights, low_grads)

    start_state = (
        jnp.zeros((span_rows, pair_count, head_count, head_size), jnp.float32),
        jnp.zeros((head_count, bucket_count), jnp.float32),
    )

    def grad_step(state_pair, block_item):
        kv_block, block_start = block_item
        new_state, weights, low_grads = query_side_step(state_pair, kv_block, block_start)
        value_grad = jnp.einsum(
            "shqk,qshd->kshd",
            weights.astype(jnp.bfloat16),
            grad_att_heads,
            preferred_element_type=jnp.float32,
        )
        key_grad = (
            jnp.einsum("shqk,qshd->kshd", low_grads, queries, preferred_element_type=jnp.float32)
            * head_scale
        )
        block_grad = jnp.concatenate(
            [
                key_grad.reshape(span_rows, pair_count, model_width),
                value_grad.reshape(span_rows, pair_count, model_width),
            ],
            axis=-1,
        )
        return (new_state, block_grad)

    (query_grad, step_grad), kv_terms = lax.scan(
        grad_step, start_state, (back_blocks, block_starts)
    )
    kv_terms = kv_terms.reshape(seq_len, pair_count, 2 * model_width)
    keyval_grad = lax.psum_scatter(
        kv_terms.astype(jnp.bfloat16), "cp", scatter_dimension=0, tiled=True
    )
    table_grad = step_grad - jnp.concatenate(
        [step_grad[:, 1:], jnp.zeros((head_count, 1), jnp.float32)], axis=1
    )
    qkv_grad = jnp.concatenate(
        [query_grad.reshape(span_rows, pair_count, model_width).astype(jnp.bfloat16), keyval_grad],
        axis=-1,
    )
    qkv_weight_grad = jnp.einsum(
        "csd,cse->de", normed_first, qkv_grad, preferred_element_type=jnp.float32
    )
    grad_normed_first = jnp.einsum(
        "cse,de->csd", qkv_grad, w_qkv, preferred_element_type=jnp.float32
    )
    gain_first_grad = jnp.sum(grad_normed_first * inputs * scale_first, axis=(0, 1))
    tokens_grad = (
        grad_hidden + norm_back(grad_normed_first, inputs, scale_first, norm1_gain)
    ).astype(jnp.bfloat16)
    attn_term = jnp.concatenate([qkv_weight_grad, out_grad], axis=1)
    w_attn_grad = lax.psum_scatter(attn_term, ("dp", "ep", "cp"), scatter_dimension=1, tiled=True)
    router_sum, table_sum, gain_first_sum, gain_second_sum = lax.psum(
        (router_grad, table_grad, gain_first_grad, gain_second_grad), ("dp", "ep", "cp")
    )
    gate_sum, up_sum, down_sum = (
        lax.psum_scatter(
            gate_grad.astype(jnp.bfloat16), ("dp", "cp"), scatter_dimension=2, tiled=True
        ).astype(jnp.float32),
        lax.psum_scatter(
            up_grad.astype(jnp.bfloat16), ("dp", "cp"), scatter_dimension=2, tiled=True
        ).astype(jnp.float32),
        lax.psum_scatter(
            down_grad.astype(jnp.bfloat16), ("dp", "cp"), scatter_dimension=2, tiled=True
        ).astype(jnp.float32),
    )
    return (
        mixed,
        tokens_grad,
        w_attn_grad,
        table_sum,
        gain_first_sum,
        gain_second_sum,
        router_sum,
        gate_sum,
        up_sum,
        down_sum,
    )


minus_big = -1000000000.0
vmem_bytes = 60 * 1024 * 1024


cost_share = 0.05


def cost(flops, moved):
    return pl.CostEstimate(
        flops=int(flops * cost_share), bytes_accessed=int(moved * cost_share), transcendentals=0
    )


def held(kernel, at, count):
    def run(*refs):
        kernel(*refs[:at], *refs[at + count :])

    return run


def anywhere(arrays):
    return [pl.BlockSpec(memory_space=pl.ANY)] * len(arrays)


def compiler_params():
    return pltpu.CompilerParams(vmem_limit_bytes=vmem_bytes)


def shear(values, leftward):
    rows, lanes = values.shape
    row_ids = lax.broadcasted_iota(jnp.int32, (rows, lanes), 0)
    bit = 1
    while bit < rows:
        amount = lanes - bit if leftward else bit
        moved = pltpu.roll(values, amount, 1)
        values = jnp.where((row_ids & bit) != 0, moved, values)
        bit *= 2
    return values


def dot_nt(left, right):
    return lax.dot_general(
        left, right, (((1,), (1,)), ((), ())), preferred_element_type=jnp.float32
    )


def dot_tn(left, right):
    return lax.dot_general(
        left, right, (((0,), (0,)), ((), ())), preferred_element_type=jnp.float32
    )


def dot_nn(left, right):
    return jnp.dot(left, right, preferred_element_type=jnp.float32)


def key_masks(length, blocks, span_rows):
    masks = []
    for block in range(blocks):
        position = block * span_rows + lax.broadcasted_iota(jnp.int32, (1, span_rows), 1)
        masks.append(jnp.where(position < length, 0.0, minus_big))
    return masks


def forward_body(
    mine, length, scale, head_size, qkv_ref, bias_ref, low_ref, full_ref, total_ref, after_pair
):
    blocks, span_rows, width = qkv_ref.shape
    lanes = 128
    lane = lax.broadcasted_iota(jnp.int32, (1, lanes), 1)
    masks = key_masks(length, blocks, span_rows)
    halves = lanes // head_size

    def place(block):
        return lax.rem(mine - block + blocks, blocks)

    def one_pair(pair, carry):
        wide = pl.multiple_of(pair * (3 * lanes), lanes)
        own_lanes = pl.ds(pl.multiple_of(pair * lanes, lanes), lanes)
        part = [pl.ds(pl.multiple_of(wide + which * lanes, lanes), lanes) for which in range(3)]
        for row in range(blocks):
            queries = qkv_ref[place(row), :, part[0]]
            totals = jnp.zeros((span_rows, lanes), jnp.float32)
            result = jnp.zeros((span_rows, lanes), jnp.float32)
            for half in range(halves):
                own = lane // head_size == half
                head_q = queries * jnp.where(own, scale, 0.0).astype(jnp.bfloat16)
                head_v = jnp.where(own, 1.0, 0.0).astype(jnp.bfloat16)
                logits = []
                for column in range(row + 1):
                    at = (blocks - 1 - row + column) * span_rows
                    term = dot_nt(head_q, qkv_ref[place(column), :, part[1]])
                    bias = bias_ref[pair * halves + half, :, at : at + span_rows]
                    logits.append(term + bias + masks[column])
                peak = jnp.max(logits[0], axis=1, keepdims=True)
                for term in logits[1:]:
                    peak = jnp.maximum(peak, jnp.max(term, axis=1, keepdims=True))
                total = jnp.zeros((span_rows, 1), jnp.float32)
                mixed = jnp.zeros((span_rows, lanes), jnp.float32)
                for column in range(row + 1):
                    weights = jnp.exp(logits[column] - peak)
                    total = total + jnp.sum(weights, axis=1, keepdims=True)
                    values = qkv_ref[place(column), :, part[2]] * head_v
                    mixed = mixed + dot_nn(weights.astype(jnp.bfloat16), values)
                result = result + mixed / total
                totals = jnp.where(lane == half, peak + jnp.log(total), totals)
            low_ref[place(row), :, own_lanes] = result.astype(jnp.bfloat16)
            full_ref[row, :, own_lanes] = result
            total_ref[row, :, own_lanes] = totals
        after_pair(pair)
        return carry

    lax.fori_loop(0, width // (3 * lanes), one_pair, 0)


def backward_body(
    mine, length, scale, head_size, qkv_ref, bias_ref, grad_ref, full_ref, total_ref, ring_ref, line_ref, work,
    after_pair=None,
):
    key_sum, value_sum, plane = work
    blocks, span_rows, width = qkv_ref.shape
    lanes = 128
    lane = lax.broadcasted_iota(jnp.int32, (1, lanes), 1)
    masks = key_masks(length, blocks, span_rows)
    halves = lanes // head_size

    def place(block):
        return lax.rem(mine - block + blocks, blocks)

    def one_pair(pair, carry):
        wide = pl.multiple_of(pair * (3 * lanes), lanes)
        own_lanes = pl.ds(pl.multiple_of(pair * lanes, lanes), lanes)
        part = [pl.ds(pl.multiple_of(wide + which * lanes, lanes), lanes) for which in range(3)]
        key_sum[...] = jnp.zeros_like(key_sum)
        value_sum[...] = jnp.zeros_like(value_sum)
        plane[...] = jnp.zeros_like(plane)
        for row in range(blocks):
            queries = qkv_ref[place(row), :, part[0]]
            grads = grad_ref[lax.rem(row - mine + blocks, blocks), :, own_lanes]
            products = grads.astype(jnp.float32) * full_ref[row, :, own_lanes]
            totals = total_ref[row, :, own_lanes]
            query_sum = jnp.zeros((span_rows, lanes), jnp.float32)
            for half in range(halves):
                own = lane // head_size == half
                one = jnp.where(own, 1.0, 0.0).astype(jnp.bfloat16)
                head_q = queries * jnp.where(own, scale, 0.0).astype(jnp.bfloat16)
                head_g = grads * one
                delta = jnp.sum(jnp.where(own, products, 0.0), axis=1, keepdims=True)
                total = totals[:, half : half + 1]
                for column in range(row + 1):
                    at = (blocks - 1 - row + column) * span_rows
                    keys = qkv_ref[place(column), :, part[1]]
                    logits = dot_nt(head_q, keys)
                    bias = bias_ref[pair * halves + half, :, at : at + span_rows]
                    logits = logits + bias + masks[column]
                    weights = jnp.exp(logits - total)
                    weight_grads = dot_nt(head_g, qkv_ref[place(column), :, part[2]])
                    score_grads = weights * (weight_grads - delta)
                    plane[half, :, at : at + span_rows] += score_grads
                    low_weights = weights.astype(jnp.bfloat16)
                    low_grads = score_grads.astype(jnp.bfloat16)
                    query_sum = query_sum + dot_nn(low_grads, keys * one)
                    key_sum[column] += dot_tn(low_grads, head_q)
                    value_sum[column] += dot_tn(low_weights, head_g)
            ring_ref[place(row), :, part[0]] = (query_sum * scale).astype(jnp.bfloat16)
        for row in range(blocks):
            ring_ref[place(row), :, part[1]] = key_sum[row].astype(jnp.bfloat16)
            ring_ref[place(row), :, part[2]] = value_sum[row].astype(jnp.bfloat16)
        for half in range(halves):
            full = jnp.concatenate(
                [plane[half], jnp.zeros((span_rows, span_rows), jnp.float32)], axis=1
            )
            summed = jnp.sum(shear(full, True), axis=0, keepdims=True)
            line_ref[pair * halves + half] = pltpu.roll(summed, span_rows - 1, 1)
        if after_pair is not None:
            after_pair(pair)
        return carry

    lax.fori_loop(0, width // (3 * lanes), one_pair, 0)


def backward_work(blocks, span_rows, head_size):
    return [
        pltpu.VMEM((blocks, span_rows, 128), jnp.float32),
        pltpu.VMEM((blocks, span_rows, 128), jnp.float32),
        pltpu.VMEM((128 // head_size, span_rows, blocks * span_rows), jnp.float32),
    ]


def greet(*others):
    barrier = pltpu.get_barrier_semaphore()
    for other in others:
        pl.semaphore_signal(
            barrier, inc=1, device_id=other, device_id_type=pl.DeviceIdType.MESH
        )
    pl.semaphore_wait(barrier, len(others))


def push(source, target, send_sem, recv_sem, other):
    return pltpu.make_async_remote_copy(
        src_ref=source,
        dst_ref=target,
        send_sem=send_sem,
        recv_sem=recv_sem,
        device_id=other,
        device_id_type=pl.DeviceIdType.MESH,
    )


def ring_others(mine, count):
    return [{"cp": lax.rem(mine + j, count)} for j in range(1, count)]


def slot_of(ref, slot, slots):
    width = ref.shape[1] // slots
    return ref.at[:, pl.ds(slot * width, width)]


def deliveries(source, target, sems, mine, count, lanes=None):
    return [
        push(
            source.at[j] if lanes is None else source.at[j, :, lanes],
            target.at[j],
            sems.at[0, j],
            sems.at[1, j],
            {"cp": lax.rem(mine + (count - j), count)},
        )
        for j in range(1, count)
    ]


def remote_params(number):
    return pltpu.CompilerParams(
        vmem_limit_bytes=vmem_bytes, collective_id=number, has_side_effects=True
    )


def own_rows(block, length, span_rows):
    position = block * span_rows + lax.broadcasted_iota(jnp.int32, (span_rows, 1), 0)
    return jnp.where(position < length, 1.0, 0.0)


def router_of(rows, router_w, experts):
    lane = lax.broadcasted_iota(jnp.int32, (1, router_w.shape[1]), 1)
    logits = jnp.where(lane < experts, dot_nn(rows, router_w), minus_big)
    shares = jnp.exp(logits - jnp.max(logits, axis=1, keepdims=True))
    return shares / jnp.sum(shares, axis=1, keepdims=True)


def project_body(mine, length, input_ref, gain_ref, weight_ref, parts_ref, own_ref, attended_ref, hidden_ref, normed_ref):
    count, span_rows, width = parts_ref.shape
    for j in range(count):
        owner = lax.rem(mine + j, count)
        for group in range(width // 128):
            at = pl.multiple_of((group * count + owner) * 128, 128)
            lanes = slice(group * 128, (group + 1) * 128)
            attended_ref[:, pl.ds(at, 128)] = own_ref[0, :, lanes] if j == 0 else parts_ref[j, :, lanes]
    projected = dot_nn(attended_ref[...], weight_ref[...])
    hidden = input_ref[...].astype(jnp.float32) + own_rows(mine, length, span_rows) * projected
    hidden_ref[...] = hidden
    normed_ref[...] = (hidden * root_scale(hidden) * gain_ref[...]).astype(jnp.bfloat16)


def pick_body(base, capacity, experts, chosen, parts, out_ref):
    for expert in range(experts):
        picked = None
        for choice_ref, part in zip(chosen, parts):
            span = part.shape[0]
            ids = lax.broadcasted_iota(jnp.int32, (capacity, span), 0) + (base + expert * capacity)
            hot = jnp.zeros((capacity, span), jnp.float32)
            for choice in range(choice_ref.shape[0]):
                hot = hot + jnp.where(ids == choice_ref[choice : choice + 1, :], 1.0, 0.0)
            term = dot_nn(hot.astype(jnp.bfloat16), part[...])
            picked = term if picked is None else picked + term
        out_ref[expert] = picked.astype(jnp.bfloat16)


def front_kernel(
    scale, head_size, slots, length_ref, gain_first_ref, gain_second_ref, line_ref, target_ref, w_attn_ref, weight_ref,
    tokens_ref, cotangent_ref, *refs
):
    inputs = [slot_of(tokens_ref, s, slots) for s in range(slots)]
    grads = [slot_of(cotangent_ref, s, slots) for s in range(slots)]
    all_ref, qkv_ref, bias_ref, full_ref, total_ref, own_w, targets_ref = refs[:7]
    over_ref, up_ref = refs[7:9]
    picks = [refs[9 + 2 * i : 11 + 2 * i] for i in range(3)]
    outs = [refs[15 + 3 * s : 18 + 3 * s] for s in range(slots)]
    refs = refs[15 + 3 * slots :]
    low, arrived, near_grads, ring_sems, own_sems, give_sems, plane_sems, target_sems = refs[:8]
    core_sems, normed_sems = refs[8:]
    _, count, span_rows, model_width = all_ref.shape
    groups = own_w.shape[1] // 384
    mine = lax.axis_index("cp")
    dp, ep = lax.axis_index("dp"), lax.axis_index("ep")
    core_other, x_other, y_other = near_others(dp, ep)

    loads = []
    for group in range(groups):
        for which in range(3):
            at = which * model_width + (group * count + mine) * 128
            lanes = pl.ds((group * 3 + which) * 128, 128)
            loads.append(
                pltpu.make_async_copy(
                    w_attn_ref.at[:, pl.ds(pl.multiple_of(at, 128), 128)],
                    own_w.at[:, lanes],
                    own_sems.at[group * 3 + which],
                )
            )
    for load in loads:
        load.start()
    for s in range(slots):
        values = inputs[s][...].astype(jnp.float32)
        all_ref[s, 0] = (values * root_scale(values) * gain_first_ref[...]).astype(jnp.bfloat16)
    greet(*ring_others(mine, count), core_other, x_other, y_other)

    def hop_copy(slot, hop):
        return push(
            all_ref.at[slot, hop],
            all_ref.at[slot, hop + 1],
            ring_sems.at[0, slot, hop],
            ring_sems.at[1, slot, hop],
            {"cp": lax.rem(mine + 1, count)},
        )

    for s in range(slots):
        hop_copy(s, 0).start()

    def plane_copies(source, target, sems):
        first = [
            push(source(s), target.at[way, s], sems.at[0, way, s], sems.at[1, way, s], other)
            for s in (0, 1)
            for way, other in ((0, x_other), (1, y_other))
        ]
        second = [
            push(target.at[0, 0], target.at[2, 0], sems.at[0, 2, 0], sems.at[1, 2, 0], y_other),
            push(target.at[1, 1], target.at[2, 1], sems.at[0, 2, 1], sems.at[1, 2, 1], x_other),
        ]
        return first, second

    grad_first, grad_second = plane_copies(lambda s: grads[s], near_grads, plane_sems)
    near_targets = targets_ref.at[pl.ds(1, 3)]
    place_first, place_second = plane_copies(lambda s: target_ref.at[s], near_targets, target_sems)
    for copy in place_first + grad_first:
        copy.start()
    targets_ref[0] = target_ref[...]
    for load in loads:
        load.wait()
    for s in range(slots):
        qkv_ref[s, 0] = dot_nn(all_ref[s, 0], own_w[...]).astype(jnp.bfloat16)
    columns = bias_ref.shape[2]
    lanes = span_rows + columns
    for head in range(bias_ref.shape[0]):
        line = pltpu.roll(line_ref[head], lanes - (span_rows - 1), 1)
        full = jnp.broadcast_to(line, (span_rows, lanes))
        bias_ref[head] = shear(full, False)[:, :columns]

    _, experts, capacity, _ = picks[0][0].shape
    base = ep * (experts * capacity)
    at_of = ((0, 0), (1, 0), (1, 1), (1, 2), (2, 0))

    def pick(source):
        if source == 0:
            parts = grads
        elif source == 4:
            parts = [outs[s][2] for s in range(slots)]
        else:
            parts = [near_grads.at[source - 1, s] for s in range(slots)]
        chosen = [targets_ref.at[source % 4, s] for s in range(slots)]
        group, at = at_of[source]
        pick_body(base, capacity, experts, chosen, parts, picks[group][0].at[at])
        core_copy(source).start()

    def core_copy(source):
        group, at = at_of[source]
        return push(
            picks[group][0].at[at],
            picks[group][1].at[at],
            core_sems.at[0, source],
            core_sems.at[1, source],
            core_other,
        )

    def normed_copy(at):
        source, target, other = (
            (outs[0][2], over_ref, x_other),
            (outs[0][2], up_ref, y_other),
        )[at]
        return push(source, target, normed_sems.at[0, at], normed_sems.at[1, at], other)

    def project(slot):
        for pair in range(groups):
            for copy in gives(slot, pair):
                copy.wait()
        project_body(
            mine, length_ref[slot], inputs[slot], gain_second_ref, weight_ref, arrived.at[slot],
            low.at[slot], *outs[slot],
        )

    def gives(slot, pair):
        part = pl.ds(pl.multiple_of(pair * 128, 128), 128)
        return [
            push(
                low.at[slot, j, :, part],
                arrived.at[slot, j, :, part],
                give_sems.at[0, slot, pair, j],
                give_sems.at[1, slot, pair, j],
                {"cp": lax.rem(mine + (count - j), count)},
            )
            for j in range(1, count)
        ]

    def attend(slot):
        def after_pair(pair):
            for copy in gives(slot, pair):
                copy.start()

        forward_body(
            mine, length_ref[slot], scale, head_size, qkv_ref.at[slot], bias_ref, low.at[slot],
            full_ref.at[slot], total_ref.at[slot], after_pair,
        )

    pick(0)
    for hop in range(1, count):
        for s in range(slots):
            hop_copy(s, hop - 1).wait_recv()
            if hop < count - 1:
                hop_copy(s, hop).start()
            qkv_ref[s, hop] = dot_nn(all_ref[s, hop], own_w[...]).astype(jnp.bfloat16)
            if hop == count - 1 and s + 1 < slots:
                attend(s)
        if hop == 1:
            for copy in place_first + grad_first:
                copy.wait_recv()
            for copy in place_second + grad_second:
                copy.start()
            pick(1)
            pick(2)
        if hop == 2:
            for copy in place_second + grad_second:
                copy.wait_recv()
            pick(3)
    attend(slots - 1)
    project(0)
    for at in range(2):
        normed_copy(at).start()
    project(1)
    pick(4)
    for s in range(slots):
        for hop in range(count - 1):
            hop_copy(s, hop).wait_send()
    for copy in place_first + grad_first + place_second + grad_second:
        copy.wait_send()
    for at in range(2):
        normed_copy(at).wait()
    for source in range(5):
        core_copy(source).wait()


def front(lengths, gain_first, gain_second, lines, target, w_attn, inputs, grads, slots, count, experts, capacity, scale, head_size):
    span_rows, model_width = inputs.shape[0], inputs.shape[1] // slots
    heads, _, lanes = lines.shape
    own_width = 3 * model_width // count
    groups = own_width // 384
    choices = target.shape[1]
    whole = pl.BlockSpec(memory_space=pltpu.VMEM)
    f32, bf16 = jnp.float32, jnp.bfloat16
    shape = jax.ShapeDtypeStruct
    got = pl.pallas_call(
        functools.partial(front_kernel, scale, head_size, slots),
        grid=(1,),
        in_specs=[
            pl.BlockSpec(memory_space=pltpu.SMEM),
            whole,
            whole,
            whole,
            whole,
            pl.BlockSpec(memory_space=pl.ANY),
            pl.BlockSpec((model_width, model_width), lambda i: (0, 3)),
            whole,
            whole,
        ],
        out_specs=[whole] * (15 + 3 * slots),
        out_shape=[
            shape((slots, count, span_rows, model_width), bf16),
            shape((slots, count, span_rows, own_width), bf16),
            shape((heads, span_rows, lanes - span_rows), f32),
            shape((slots, count, span_rows, groups * 128), f32),
            shape((slots, count, span_rows, groups * 128), f32),
            shape((model_width, own_width), bf16),
            shape((4, slots, choices, span_rows), jnp.int32),
        ]
        + [shape((span_rows, model_width), bf16)] * 2
        + [
            shape((sources, experts, capacity, model_width), bf16)
            for sources in (1, 3, 1)
            for _ in range(2)
        ]
        + [
            shape((span_rows, model_width), bf16),
            shape((span_rows, model_width), f32),
            shape((span_rows, model_width), bf16),
        ]
        * slots,
        scratch_shapes=[
            pltpu.VMEM((slots, count, span_rows, groups * 128), bf16),
            pltpu.VMEM((slots, count, span_rows, groups * 128), bf16),
            pltpu.VMEM((3, slots, span_rows, model_width), bf16),
            pltpu.SemaphoreType.DMA((2, slots, count - 1)),
            pltpu.SemaphoreType.DMA((3 * groups,)),
            pltpu.SemaphoreType.DMA((2, slots, groups, count)),
            pltpu.SemaphoreType.DMA((2, 3, slots)),
            pltpu.SemaphoreType.DMA((2, 3, slots)),
            pltpu.SemaphoreType.DMA((2, 5)),
            pltpu.SemaphoreType.DMA((2, 3)),
        ],
        cost_estimate=cost(60e9, 20e6),
        compiler_params=remote_params(0),
        name="front",
    )(lengths, gain_first, gain_second, lines, target, w_attn, w_attn, inputs, grads)
    pairs = [got[9 + 2 * i : 11 + 2 * i] for i in range(3)]
    return got[:9], pairs, [got[15 + 3 * s : 18 + 3 * s] for s in range(slots)]


def hidden_body(
    experts, mine, length, back_ref, grad_ref, hidden_ref, normed_ref, gain_ref, router_ref, weight_ref,
    hidden_grad_ref, proj_ref, router_grad_ref, gain_grad_ref, leaving_ref, attended,
):
    count = leaving_ref.shape[0]
    span_rows, model_width = hidden_ref.shape
    back = back_ref[...]
    normed = normed_ref[...]
    probs = router_of(normed, router_ref[...], experts)
    shares = back[:, model_width:]
    logit_grads = probs * (shares - jnp.sum(probs * shares, axis=1, keepdims=True))
    logit_grads = logit_grads.astype(jnp.bfloat16)
    router_grad_ref[...] = dot_tn(normed, logit_grads)
    grads = back[:, :model_width] + dot_nt(logit_grads, router_ref[...])
    hidden = hidden_ref[...]
    scale_rows = root_scale(hidden)
    gain_grad_ref[...] = jnp.sum(grads * hidden * scale_rows, axis=0, keepdims=True)
    hidden_grads = grad_ref[...].astype(jnp.float32) + norm_back(
        grads, hidden, scale_rows, gain_ref[...]
    )
    hidden_grad_ref[...] = hidden_grads
    proj = (own_rows(mine, length, span_rows) * hidden_grads).astype(jnp.bfloat16)
    proj_ref[...] = proj
    attended[...] = dot_nt(proj, weight_ref[...]).astype(jnp.bfloat16)
    for j in range(count):
        owner = lax.rem(mine + (count - j), count)
        for group in range(leaving_ref.shape[2] // 128):
            at = pl.multiple_of((group * count + owner) * 128, 128)
            leaving_ref[j, :, group * 128 : (group + 1) * 128] = attended[:, pl.ds(at, 128)]


def hidden_kernel(
    experts, scale, head_size, slots, length_ref, gain_ref, router_ref, weight_ref, qkv_ref, bias_ref, full_ref, total_ref,
    cotangent_ref, *refs
):
    per_slot = [
        (refs[3 * s], slot_of(cotangent_ref, s, slots), *refs[3 * s + 1 : 3 * s + 3])
        for s in range(slots)
    ]
    refs = refs[3 * slots :]
    own_out, rest_out, refs = refs[:slots], refs[slots : 4 * slots], refs[4 * slots :]
    outs = [refs[4 * s : 4 * s + 4] for s in range(slots)]
    mixed, refs = refs[4 * slots : 5 * slots], refs[5 * slots :]
    ring_ref, line_ref, rest_ref, leaving, arriving, attended, sems = refs[:7]
    got, far, last, low, out_sems = refs[7:12]
    work = refs[12:]
    count = qkv_ref.shape[1]
    mine = lax.axis_index("cp")
    _, x_other, y_other = near_others(lax.axis_index("dp"), lax.axis_index("ep"))
    greet(*ring_others(mine, count), x_other, y_other)
    over, up, across = (rest_out[i * slots : (i + 1) * slots] for i in range(3))

    def out_copy(at):
        source, target, other = (
            (over[0], got.at[0], x_other),
            (up[1], got.at[1], y_other),
            (across[0], far.at[0], x_other),
            (across[1], far.at[1], y_other),
            (low.at[0], last.at[0], y_other),
            (low.at[1], last.at[1], x_other),
        )[at]
        return push(source, target, out_sems.at[0, at], out_sems.at[1, at], other)

    def after_pair(pair):
        @pl.when(pair == 0)
        def _():
            for at, part in ((0, up[0]), (1, over[1])):
                out_copy(2 + at).wait()
                summed = part[...].astype(jnp.float32) + far[at].astype(jnp.float32)
                low[at] = summed.astype(jnp.bfloat16)
                out_copy(4 + at).start()

    for at in (2, 3, 0, 1):
        out_copy(at).start()
    copies = []
    for s in range(slots):
        hidden_body(
            experts, mine, length_ref[s], *per_slot[s], gain_ref, router_ref, weight_ref,
            *outs[s], leaving.at[s], attended,
        )
        target = arriving if s == 0 else rest_ref.at[s - 1]
        copies.append(deliveries(leaving.at[s], target, sems.at[s], mine, count))
        for copy in copies[s]:
            copy.start()
        target[0] = leaving[s, 0]
    for copy in copies[0]:
        copy.wait()
    backward_body(
        mine, length_ref[0], scale, head_size, qkv_ref.at[0], bias_ref, arriving, full_ref.at[0], total_ref.at[0],
        ring_ref, line_ref, work, after_pair,
    )
    for s in range(slots):
        out_copy(s).wait()
        out_copy(4 + s).wait()
        home = own_out[s][...].astype(jnp.float32) + got[s].astype(jnp.float32)
        home = per_slot[s][2][...] + home + last[s].astype(jnp.float32)
        mixed[s][...] = home.astype(jnp.bfloat16)
    for copy in (copy for some in copies[1:] for copy in some):
        copy.wait()


def hidden_back(
    lengths, back_rows, grads, hidden, normed, gain, router, w_attn, experts, qkvs, bias, full, total, own_out,
    rest_out, scale, head_size,
):
    slots, count, span_rows, own_width = qkvs.shape
    model_width = hidden[0].shape[1]
    heads = bias.shape[0]
    whole = pl.BlockSpec(memory_space=pltpu.VMEM)
    f32, bf16 = jnp.float32, jnp.bfloat16
    each = [grads]
    for s in range(slots):
        each += [back_rows[s], hidden[s], normed[s]]
    each += [*own_out, *rest_out]
    own_shape = (count, span_rows, own_width // 3)
    got = pl.pallas_call(
        functools.partial(hidden_kernel, experts, scale, head_size, slots),
        grid=(1,),
        in_specs=[
            pl.BlockSpec(memory_space=pltpu.SMEM),
            whole,
            whole,
            pl.BlockSpec((model_width, model_width), lambda i: (0, 3)),
            pl.BlockSpec((1,) + qkvs.shape[1:], lambda i: (0, 0, 0, 0)),
            whole,
            pl.BlockSpec((1,) + full.shape[1:], lambda i: (0, 0, 0, 0)),
            pl.BlockSpec((1,) + full.shape[1:], lambda i: (0, 0, 0, 0)),
        ]
        + [whole] * len(each),
        out_specs=[whole] * (5 * slots + 3),
        out_shape=[
            jax.ShapeDtypeStruct((span_rows, model_width), f32),
            jax.ShapeDtypeStruct((span_rows, model_width), bf16),
            jax.ShapeDtypeStruct((model_width, router.shape[1]), f32),
            jax.ShapeDtypeStruct((1, model_width), f32),
        ]
        * slots
        + [jax.ShapeDtypeStruct((span_rows, model_width), bf16)] * slots
        + [
            jax.ShapeDtypeStruct(qkvs.shape[1:], bf16),
            jax.ShapeDtypeStruct((heads, 1, bias.shape[2] + span_rows), f32),
            jax.ShapeDtypeStruct((slots - 1,) + own_shape, bf16),
        ],
        scratch_shapes=[
            pltpu.VMEM((slots,) + own_shape, bf16),
            pltpu.VMEM(own_shape, bf16),
            pltpu.VMEM((span_rows, model_width), bf16),
            pltpu.SemaphoreType.DMA((slots, 2, count)),
            *[pltpu.VMEM((slots, span_rows, model_width), bf16)] * 4,
            pltpu.SemaphoreType.DMA((2, 6)),
        ]
        + backward_work(count, span_rows, head_size),
        cost_estimate=cost(20e9, 20e6),
        compiler_params=remote_params(1),
        name="hidden_back",
    )(lengths, gain, router, w_attn, qkvs, bias, full, total, *each)
    return [got[4 * s : 4 * s + 4] for s in range(slots)], got[4 * slots : 5 * slots], got[5 * slots :]


def near_others(dp, ep):
    core, across = lax.rem(dp, 2), dp // 2
    return (
        {"dp": across * 2 + (1 - core)},
        {"dp": (1 - across) * 2 + core},
        {"ep": 1 - ep},
    )


def second_kernel(
    scale, head_size, slots, length_ref, former_ref, normed_ref, qkv_ref, bias_ref, grad_ref, full_ref, total_ref,
    *refs,
):
    attended, proj, refs = refs[:slots], refs[slots : 2 * slots], refs[2 * slots :]
    ring_ref, line_ref, arrived_ref, early_ref, weight_ref, rows_ref = refs[:6]
    sums, low, got_core, got_x, got_y, leaving, coming, sems, near_sems, last_sems = refs[6:16]
    early_sems, work = refs[16], refs[17:]
    count = qkv_ref.shape[1]
    mine = lax.axis_index("cp")
    dp, ep = lax.axis_index("dp"), lax.axis_index("ep")
    core, across = lax.rem(dp, 2), dp // 2
    others = near_others(dp, ep)
    greet(*ring_others(mine, count), *others)
    copies = deliveries(former_ref, arrived_ref, sems, mine, count)
    for copy in copies:
        copy.start()
    arrived_ref[0] = former_ref[0]
    height = sums.shape[0] // 2
    sizes = (height, height // 2, height // 4)
    bits = (core, across, ep)
    landing = (got_core, got_x, got_y)
    total = None
    for s in range(slots):
        term = dot_tn(attended[s][...], proj[s][...])
        total = term if total is None else total + term
    sums[...] = total

    def low_part(stage):
        return low.at[stage, pl.ds(0, sizes[stage])]

    def stage_copy(stage):
        return push(
            low_part(stage), landing[stage], near_sems.at[0, stage], near_sems.at[1, stage], others[stage]
        )

    def start_of(stage):
        start = 0
        for former in range(stage):
            start = start + bits[former] * sizes[former]
        return start

    def begin(stage):
        at = start_of(stage) + (1 - bits[stage]) * sizes[stage]
        away = sums[pl.ds(pl.multiple_of(at, 128), sizes[stage]), :]
        low[stage, : sizes[stage]] = away.astype(jnp.bfloat16)
        stage_copy(stage).start()

    def finish(stage):
        stage_copy(stage).wait()
        at = pl.ds(pl.multiple_of(start_of(stage + 1), 128), sizes[stage])
        sums[at, :] = sums[at, :] + landing[stage][...].astype(jnp.float32)

    early = deliveries(ring_ref, early_ref, early_sems, mine, count, pl.ds(0, early_ref.shape[2]))

    def after_pair(pair):
        @pl.when(pair == 0)
        def _():
            for copy in early:
                copy.start()

        for stage in range(2):

            @pl.when(pair == stage)
            def _():
                finish(stage)
                begin(stage + 1)

    begin(0)
    backward_body(
        mine, length_ref[1], scale, head_size, qkv_ref.at[0], bias_ref, grad_ref.at[0], full_ref.at[0], total_ref.at[0],
        ring_ref, line_ref, work, after_pair,
    )
    finish(2)
    at = pl.ds(pl.multiple_of(start_of(3), 128), sizes[2])
    groups = leaving.shape[2] // 128
    for j in range(count):
        owner = lax.rem(mine + (count - j), count)
        for group in range(groups):
            lanes = pl.ds(pl.multiple_of((group * count + owner) * 128, 128), 128)
            part = sums[at, lanes]
            leaving[j, :, group * 128 : (group + 1) * 128] = part.astype(jnp.bfloat16)
            if j == 0:
                rows_ref[:, group * 128 : (group + 1) * 128] = part
    last = deliveries(leaving, coming, last_sems, mine, count)
    for copy in last:
        copy.start()
    total = None
    for j in range(count):
        term = dot_tn(normed_ref[0, j], former_ref[j])
        total = term if total is None else total + term
    weight_ref[...] = total
    for copy in last:
        copy.wait()
    for j in range(1, count):
        rows_ref[...] = rows_ref[...] + coming[j].astype(jnp.float32)
    for copy in copies + early:
        copy.wait()


def second_back(
    lengths, former, normed_all, qkvs, bias, grads, full, total, attended, proj, scale, head_size, waits=()
):
    slots, count, span_rows, own_width = qkvs.shape
    model_width = normed_all.shape[3]
    whole = pl.BlockSpec(memory_space=pltpu.VMEM)
    slot = lambda a, s: pl.BlockSpec((1,) + a.shape[1:], lambda i: (s,) + (0,) * (len(a.shape) - 1))
    f32, bf16 = jnp.float32, jnp.bfloat16
    rows_shape = (model_width // 8, own_width // 3)
    return pl.pallas_call(
        held(
            functools.partial(second_kernel, scale, head_size, slots), 8 + 2 * slots, len(waits)
        ),
        grid=(1,),
        in_specs=[
            pl.BlockSpec(memory_space=pltpu.SMEM),
            whole,
            slot(normed_all, 0),
            slot(qkvs, 1),
            whole,
            whole,
            slot(full, 1),
            slot(total, 1),
        ]
        + [whole] * (2 * slots)
        + anywhere(waits),
        out_specs=[whole] * 6,
        out_shape=[
            jax.ShapeDtypeStruct(qkvs.shape[1:], bf16),
            jax.ShapeDtypeStruct((bias.shape[0], 1, bias.shape[2] + span_rows), f32),
            jax.ShapeDtypeStruct(qkvs.shape[1:], bf16),
            jax.ShapeDtypeStruct((count, span_rows, 384), bf16),
            jax.ShapeDtypeStruct((model_width, own_width), f32),
            jax.ShapeDtypeStruct(rows_shape, f32),
        ],
        scratch_shapes=[
            pltpu.VMEM((model_width, model_width), f32),
            pltpu.VMEM((3, model_width // 2, model_width), bf16),
            pltpu.VMEM((model_width // 2, model_width), bf16),
            pltpu.VMEM((model_width // 4, model_width), bf16),
            pltpu.VMEM((model_width // 8, model_width), bf16),
            pltpu.VMEM((count,) + rows_shape, bf16),
            pltpu.VMEM((count,) + rows_shape, bf16),
            pltpu.SemaphoreType.DMA((2, count)),
            pltpu.SemaphoreType.DMA((2, 3)),
            pltpu.SemaphoreType.DMA((2, count)),
            pltpu.SemaphoreType.DMA((2, count)),
        ]
        + backward_work(count, span_rows, head_size),
        cost_estimate=cost(20e9, 20e6),
        compiler_params=remote_params(2),
        name="second_back",
    )(lengths, former, normed_all, qkvs, bias, grads, full, total, *attended, *proj, *waits)


def token_body(mine, input_ref, hidden_ref, gain_ref, weight_ref, part_refs, own_ref, out_ref):
    count = part_refs[0].shape[0]
    model_width = input_ref.shape[1]
    total = None
    for j in range(count):
        owner = lax.rem(mine + j, count)
        pieces = []
        for group in range(own_ref.shape[2] // 384):
            for which in range(3):
                at = which * model_width + (group * count + owner) * 128
                pieces.append(weight_ref[:, pl.ds(pl.multiple_of(at, 128), 128)])
        part = own_ref[0] if j == 0 else jnp.concatenate([ref[j] for ref in part_refs], axis=1)
        term = dot_nt(part, jnp.concatenate(pieces, axis=1))
        total = term if total is None else total + term
    inputs = input_ref[...].astype(jnp.float32)
    back = norm_back(total, inputs, root_scale(inputs), gain_ref[...])
    out_ref[...] = (hidden_ref[...] + back).astype(jnp.bfloat16)


def final_kernel(
    slots, ring_ref, early_ref, normed_ref, former_ref, own_w_ref, arrived_ref, blocks_ref, small_ref, gain_ref,
    weight_ref, tokens_ref, *refs
):
    inputs = [slot_of(tokens_ref, s, slots) for s in range(slots)]
    hiddens, refs = refs[:slots], refs[slots:]
    outs, refs = refs[:slots], refs[slots:]
    small_out, attn_out = refs[:2]
    coming, here, sum_blocks, low_blocks, small_now, small_in, sems, near_sems, small_sems = refs[2:11]
    got_core, got_x, got_y = refs[11:]
    count = ring_ref.shape[0]
    mine = lax.axis_index("cp")
    dp, ep = lax.axis_index("dp"), lax.axis_index("ep")
    core, across = lax.rem(dp, 2), dp // 2
    core_other, x_other, y_other = near_others(dp, ep)
    greet(*ring_others(mine, count), core_other, x_other, y_other)
    late = ring_ref.shape[2] - early_ref.shape[2]
    copies = deliveries(ring_ref, coming, sems, mine, count, pl.ds(early_ref.shape[2], late))
    for copy in copies:
        copy.start()

    total = former_ref[...]
    for j in range(count):
        total = total + dot_tn(normed_ref[0, j], ring_ref[j])
    ones = jnp.ones((8, total.shape[1]), jnp.float32)
    first_gain = lax.dot_general(
        ones,
        total * own_w_ref[...].astype(jnp.float32),
        (((1,), (1,)), ((), ())),
        precision=lax.Precision.HIGHEST,
        preferred_element_type=jnp.float32,
    )
    row = lax.broadcasted_iota(jnp.int32, small_ref.shape, 0)
    small_now[0] = jnp.where(row == 6, first_gain / gain_ref[...], small_ref[...])
    groups = total.shape[1] // 384
    for group in range(groups):
        for which in range(3):
            at = (group * 3 + which) * 128
            part = total[:, at : at + 128]
            sum_blocks[which % 2, which // 2, group] = part
            low_blocks[which % 2, which // 2, group] = part.astype(jnp.bfloat16)
        height = blocks_ref.shape[0]
        here_rows = pl.ds(pl.multiple_of((core * 4 + across * 2 + ep) * height, 128), height)
        part = blocks_ref[:, group * 128 : (group + 1) * 128]
        sum_blocks[1, 1, group] = jnp.zeros_like(sum_blocks[1, 1, group])
        low_blocks[1, 1, group] = jnp.zeros_like(low_blocks[1, 1, group])
        sum_blocks[1, 1, group, here_rows] = part
        low_blocks[1, 1, group, here_rows] = part.astype(jnp.bfloat16)
    first = push(low_blocks.at[1 - core], got_core, near_sems.at[0, 0], near_sems.at[1, 0], core_other)
    first.start()

    stages = [core_other, x_other, y_other]
    step = 1
    while step < count:
        flip = mine + step - 2 * step * lax.rem(mine // step, 2)
        stages.append({"cp": flip})
        step *= 2

    def small_push(at):
        return push(small_now.at[at], small_in.at[at], small_sems.at[0, at], small_sems.at[1, at], stages[at])

    small_push(0).start()
    token_body(mine, inputs[0], hiddens[0], gain_ref, weight_ref, [arrived_ref], arrived_ref, outs[0])
    first.wait()
    here[...] = sum_blocks[core] + got_core[...].astype(jnp.float32)
    low_blocks[0, 0] = here[1 - across].astype(jnp.bfloat16)
    second = push(low_blocks.at[0, 0], got_x, near_sems.at[0, 1], near_sems.at[1, 1], x_other)
    second.start()
    for at in range(len(stages)):
        small_push(at).wait()
        now = small_now[at] + small_in[at]
        if at + 1 < len(stages):
            small_now[at + 1] = now
            small_push(at + 1).start()
        else:
            small_out[...] = now
        if at == 1:
            second.wait()
            sum_blocks[0, 0] = here[across] + got_x[...].astype(jnp.float32)
            low_blocks[0, 1, 0] = sum_blocks[0, 0, 1 - ep].astype(jnp.bfloat16)
            third = push(low_blocks.at[0, 1, 0], got_y, near_sems.at[0, 2], near_sems.at[1, 2], y_other)
            third.start()
    for copy in copies:
        copy.wait()
    token_body(mine, inputs[1], hiddens[1], gain_ref, weight_ref, [early_ref, coming], ring_ref, outs[1])
    third.wait()
    attn_out[...] = sum_blocks[0, 0, ep] + got_y[...].astype(jnp.float32)


def final_back(ring, early, normed_all, former, own_w, arrived, blocks, small, gain, w_attn, inputs, hiddens):
    count, span_rows, own_width = ring.shape
    slots = len(hiddens)
    model_width = hiddens[0].shape[1]
    groups = blocks.shape[1] // 128
    whole = pl.BlockSpec(memory_space=pltpu.VMEM)
    f32, bf16 = jnp.float32, jnp.bfloat16
    stages = 3 + (count - 1).bit_length()
    tile = (model_width, 128)
    return pl.pallas_call(
        functools.partial(final_kernel, slots),
        grid=(1,),
        in_specs=[
            whole,
            whole,
            pl.BlockSpec((1,) + normed_all.shape[1:], lambda i: (1, 0, 0, 0)),
            whole,
            whole,
            whole,
            whole,
            whole,
            whole,
            pl.BlockSpec((model_width, 3 * model_width), lambda i: (0, 0)),
        ]
        + [whole] * (1 + slots),
        out_specs=[whole] * (slots + 2),
        out_shape=[jax.ShapeDtypeStruct((span_rows, model_width), bf16)] * slots
        + [jax.ShapeDtypeStruct(small.shape, f32), jax.ShapeDtypeStruct(tile, f32)],
        scratch_shapes=[
            pltpu.VMEM((count, span_rows, own_width - early.shape[2]), bf16),
            pltpu.VMEM((2, groups) + tile, f32),
            pltpu.VMEM((2, 2, groups) + tile, f32),
            pltpu.VMEM((2, 2, groups) + tile, bf16),
            pltpu.VMEM((stages,) + small.shape, f32),
            pltpu.VMEM((stages,) + small.shape, f32),
            pltpu.SemaphoreType.DMA((2, count)),
            pltpu.SemaphoreType.DMA((2, 3)),
            pltpu.SemaphoreType.DMA((2, stages)),
            pltpu.VMEM((2, groups) + tile, bf16),
            pltpu.VMEM((groups,) + tile, bf16),
            pltpu.VMEM(tile, bf16),
        ],
        cost_estimate=cost(20e9, 20e6),
        compiler_params=remote_params(3),
        name="final_back",
    )(ring, early, normed_all, former, own_w, arrived, blocks, small, gain, w_attn, inputs, *hiddens)


gelu_inner = 0.7978845608028654
gelu_cubic = 0.044715


def place_body(base, chosen_ref, pairs, outs):
    capacity = pairs[0][0].shape[0]
    span = outs[0].shape[0]
    both = [
        (mine[...].astype(jnp.float32) + theirs[...].astype(jnp.float32)).astype(jnp.bfloat16)
        for mine, theirs in pairs
    ]
    for at, out in enumerate(outs):
        total = None
        for expert in range(len(pairs)):
            ids = lax.broadcasted_iota(jnp.int32, (span, capacity), 1) + (base + expert * capacity)
            hot = jnp.zeros((span, capacity), jnp.float32)
            for choice in range(chosen_ref.shape[1]):
                chosen = chosen_ref[at * span : (at + 1) * span, choice : choice + 1]
                hot = hot + jnp.where(ids == chosen, 1.0, 0.0)
            term = dot_nn(hot.astype(jnp.bfloat16), both[expert])
            total = term if total is None else total + term
        out[...] = total.astype(jnp.bfloat16)


def return_kernel(experts, slots, target_ref, *refs):
    held_pairs = 2 * (1 + experts)
    back, far_outs, refs = refs[:held_pairs], refs[held_pairs : 2 * held_pairs], refs[2 * held_pairs :]
    backs, refs = refs[:slots], refs[slots:]
    out_own, out_rest, refs = refs[:slots], refs[slots : 4 * slots], refs[4 * slots :]
    here, got, far, last, low = refs[:5]
    outs, load_sems, sems = refs[5 : 5 + held_pairs], refs[5 + held_pairs], refs[6 + held_pairs]
    dp, ep = lax.axis_index("dp"), lax.axis_index("ep")
    _, x_other, y_other = near_others(dp, ep)
    base = ep * (experts * back[0].shape[2])
    loads = [
        pltpu.make_async_copy(source, target, load_sems.at[i])
        for i, (source, target) in enumerate(zip(far_outs, outs))
    ]
    for load in loads:
        load.start()

    def rows_of(held_refs, source):
        if source == 0:
            return [(held_refs[0].at[e, 0], held_refs[1].at[e, 0]) for e in range(experts)]
        return [
            (held_refs[2 + 2 * e].at[0, source - 1], held_refs[3 + 2 * e].at[0, source - 1])
            for e in range(experts)
        ]

    def place(held_refs, source, targets):
        place_body(base, target_ref.at[source], rows_of(held_refs, source), targets)

    firsts = [
        push(here.at[1, 0], got.at[0], sems.at[0, 0], sems.at[1, 0], x_other),
        push(here.at[2, 1], got.at[1], sems.at[0, 1], sems.at[1, 1], y_other),
        push(here.at[3, 0], far.at[0], sems.at[0, 2], sems.at[1, 2], x_other),
        push(here.at[3, 1], far.at[1], sems.at[0, 3], sems.at[1, 3], y_other),
    ]
    ends = [
        push(low.at[0], last.at[0], sems.at[0, 4], sems.at[1, 4], y_other),
        push(low.at[1], last.at[1], sems.at[0, 5], sems.at[1, 5], x_other),
    ]
    greet(x_other, y_other)
    halves = lambda source: [here.at[source, s] for s in range(slots)]
    place(back, 3, halves(3))
    firsts[2].start()
    firsts[3].start()
    place(back, 1, halves(1))
    firsts[0].start()
    place(back, 2, halves(2))
    firsts[1].start()
    place(back, 0, halves(0))
    for load in loads:
        load.wait()
    for at, (former, source) in enumerate(((2, 2), (3, 1))):
        firsts[former].wait()
        low[at] = (here[source, at].astype(jnp.float32) + far[at].astype(jnp.float32)).astype(jnp.bfloat16)
        ends[at].start()
    place(outs, 0, out_own)
    for source in range(1, 4):
        place(outs, source, out_rest[(source - 1) * slots : source * slots])
    for s in range(slots):
        firsts[s].wait()
        backs[s][...] = here[0, s].astype(jnp.float32) + got[s].astype(jnp.float32)
    for s in range(slots):
        ends[s].wait()
        backs[s][...] = backs[s][...] + last[s].astype(jnp.float32)


def return_rows(targets, backs, outs, slots, waits=()):
    experts = len(backs) // 2 - 1
    model_width = outs[0].shape[-1]
    span_rows = targets.shape[1] // slots
    wide = backs[0].shape[-1]
    whole = pl.BlockSpec(memory_space=pltpu.VMEM)
    f32, bf16 = jnp.float32, jnp.bfloat16
    half = pltpu.VMEM((slots, span_rows, wide), bf16)
    got = pl.pallas_call(
        held(
            functools.partial(return_kernel, experts, slots),
            1 + len(backs) + len(outs),
            len(waits),
        ),
        in_specs=[whole] + [whole] * len(backs) + anywhere(outs) + anywhere(waits),
        out_specs=[whole] * (5 * slots),
        out_shape=[
            *[jax.ShapeDtypeStruct((span_rows, wide), f32)] * slots,
            *[jax.ShapeDtypeStruct((span_rows, model_width), bf16)] * (4 * slots),
        ],
        scratch_shapes=[pltpu.VMEM((4, slots, span_rows, wide), bf16), half, half, half, half]
        + [pltpu.VMEM(a.shape, bf16) for a in outs]
        + [pltpu.SemaphoreType.DMA((len(outs),)), pltpu.SemaphoreType.DMA((2, 6))],
        cost_estimate=cost(20e9, 20e6),
        compiler_params=remote_params(4),
        name="return_rows",
    )(targets, *backs, *outs, *waits)
    return got[:slots], got[slots : 2 * slots], got[2 * slots :]


def expert_body(experts, own_units, expert, skip, given, refs, weights, router_ref):
    back_mine, back_theirs, out_mine, out_theirs, kept_rows, kept_units = refs
    gate_ref, up_ref, down_ref = weights
    capacity, model_width = given[0].shape[2:]
    rows = jnp.concatenate([given[0][0, 0], given[1][0, 0]], axis=0)
    grads = jnp.concatenate([given[2][0, 0], given[3][0, 0]], axis=0)
    kept_rows[0, 0, 0] = rows
    kept_rows[1, 0, 0] = grads
    lane = lax.broadcasted_iota(jnp.int32, (1, router_ref.shape[1]), 1)
    probs = router_of(rows, router_ref[...], experts)
    gates = jnp.sum(jnp.where(lane == expert, probs, 0.0), axis=1, keepdims=True)
    unit = lax.broadcasted_iota(jnp.int32, (1, gate_ref.shape[2]), 1) - skip
    own = jnp.logical_and(unit >= 0, unit < own_units)
    gate_w, up_w, down_w = gate_ref[0], up_ref[0], down_ref[0]
    gate_pre = dot_nn(rows, gate_w)
    up_pre = jnp.where(own, dot_nn(rows, up_w), 0.0)
    square = gate_pre * gate_pre
    tanh = jnp.tanh(gelu_inner * gate_pre * (1.0 + gelu_cubic * square))
    half = 0.5 + 0.5 * tanh
    active = gate_pre * half
    slope = half + active * (1.0 - tanh) * (gelu_inner * (1.0 + 3.0 * gelu_cubic * square))
    inner = active * up_pre
    low_inner = inner.astype(jnp.bfloat16)
    plain_grads = jnp.where(own, dot_nn(grads, down_w), 0.0)
    gate_grads = jnp.sum(plain_grads * low_inner.astype(jnp.float32), axis=1, keepdims=True)
    inner_grads = plain_grads * gates
    low_gate = (inner_grads * up_pre * slope).astype(jnp.bfloat16)
    low_up = (inner_grads * active).astype(jnp.bfloat16)
    kept_units[0, 0, 0] = low_gate
    kept_units[1, 0, 0] = low_up
    kept_units[2, 0, 0] = (inner * gates).astype(jnp.bfloat16)
    back = (dot_nt(low_gate, gate_w) + dot_nt(low_up, up_w)).astype(jnp.bfloat16)
    shares = jnp.where(lane == expert, gate_grads, 0.0).astype(jnp.bfloat16)
    out = (gates * dot_nt(low_inner, down_w)).astype(jnp.bfloat16)
    for at, back_ref, out_ref in ((0, back_mine, out_mine), (1, back_theirs, out_theirs)):
        part = slice(at * capacity, (at + 1) * capacity)
        back_ref[0, 0, :, :model_width] = back[part]
        back_ref[0, 0, :, model_width:] = shares[part]
        out_ref[0, 0] = out[part]


def expert_kernel(experts, own_units, kept_count, first_ref, window_ref, *refs):
    given, refs = refs[:4], refs[4:]
    router_ref, weights, refs = refs[0], refs[1:4], refs[4 + kept_count :]
    expert = first_ref[0] + pl.program_id(0)
    expert_body(experts, own_units, expert, window_ref[1], given, refs, weights, router_ref)


def own_kernel(experts, own_units, *refs):
    given, router_ref, weights, refs = refs[:4], refs[4], refs[5:8], refs[8:]
    target_ref, over_ref, up_ref, normed_ref, refs = refs[0], refs[1], refs[2], refs[3], refs[4:]
    results, kept, (mine_ref, theirs_ref), refs = refs[:4], refs[4:6], refs[6:8], refs[8:]
    coming, picked, held_w, held_rows, held_units = refs[:5]
    sems, core_sems, home_sems, load_sems, keep_sems = refs[5:]
    exp_dev, capacity = picked.shape[1:3]
    dp, ep = lax.axis_index("dp"), lax.axis_index("ep")
    core_other, x_other, y_other = near_others(dp, ep)
    skip = lax.rem(dp * own_units, 128)

    def copy(at):
        source, other = (
            (normed_ref, x_other),
            (normed_ref, y_other),
            (over_ref, y_other),
            (coming.at[1], x_other),
        )[at]
        return push(source, coming.at[at], sems.at[0, at], sems.at[1, at], other)

    def load(expert, which):
        lanes = pl.ds(pl.multiple_of(dp * own_units - skip, 128), held_w.shape[4])
        return pltpu.make_async_copy(
            weights[which].at[pl.ds(expert, 1), :, lanes],
            held_w.at[expert, which],
            load_sems.at[expert, which],
        )

    def keep(expert, kind):
        held_ref = (held_rows, held_units)[kind]
        return pltpu.make_async_copy(
            held_ref.at[expert, :, 0, 0], kept[kind].at[:, expert, 0], keep_sems.at[expert, kind]
        )

    for expert in range(exp_dev):
        for which in range(3):
            load(expert, which).start()
    greet(core_other, x_other, y_other)
    for at in range(3):
        copy(at).start()
    for expert in range(exp_dev):
        if expert == 1:
            copy(1).wait_recv()
            copy(3).start()
        for which in range(3):
            load(expert, which).wait()
        here = pl.ds(expert, 1)
        expert_body(
            experts,
            own_units,
            ep * exp_dev + expert,
            skip,
            [part.at[:, here] for part in given],
            [part.at[here] for part in results] + [held_rows.at[expert], held_units.at[expert]],
            [held_w.at[expert, which] for which in range(3)],
            router_ref,
        )
        for kind in range(2):
            keep(expert, kind).start()

    base = ep * (exp_dev * capacity)
    blocks = (
        (over_ref, coming.at[0]),
        (up_ref, coming.at[1]),
        (coming.at[2], coming.at[3]),
    )

    def across_cores(k):
        return push(picked.at[k], theirs_ref.at[k], core_sems.at[0, k], core_sems.at[1, k], core_other)

    def home(k):
        return pltpu.make_async_copy(picked.at[k], mine_ref.at[k], home_sems.at[k])

    for k, waits in enumerate(((0,), (), (2, 3))):
        for at in waits:
            copy(at).wait_recv()
        chosen = [target_ref.at[k + 1, s] for s in range(target_ref.shape[1])]
        pick_body(base, capacity, exp_dev, chosen, blocks[k], picked.at[k])
        across_cores(k).start()
        home(k).start()
    for at in range(4):
        copy(at).wait_send()
    for k in range(3):
        across_cores(k).wait()
        home(k).wait()
    for expert in range(exp_dev):
        for kind in range(2):
            keep(expert, kind).wait()


def own_experts(given, router, weights, target, over, up, normed, total, experts, units):
    _, exp_dev, capacity, model_width = given[0].shape
    span_rows = normed.shape[0]
    wide_units = aligned_units(units)
    tile = 2 * capacity
    bf16 = jnp.bfloat16
    shape = jax.ShapeDtypeStruct
    picked = (3, exp_dev, capacity, model_width)
    wide = model_width + 128
    keeps = ((2, model_width), (3, wide_units))
    whole = pl.BlockSpec(memory_space=pltpu.VMEM)
    some = pl.BlockSpec(memory_space=pl.ANY)
    got = pl.pallas_call(
        functools.partial(own_kernel, experts, units),
        grid=(1,),
        in_specs=[whole] * 5 + [some] * 3 + [whole] * 4,
        out_specs=[whole] * 4 + [some] * 4,
        out_shape=[shape((exp_dev, 1, capacity, wide), bf16)] * 2
        + [shape((exp_dev, 1, capacity, model_width), bf16)] * 2
        + [shape((kinds, exp_dev, total, tile, width), bf16) for kinds, width in keeps]
        + [shape(picked, bf16)] * 2,
        scratch_shapes=[
            pltpu.VMEM((4, span_rows, model_width), bf16),
            pltpu.VMEM(picked, bf16),
            pltpu.VMEM((exp_dev, 3, 1, model_width, wide_units), bf16),
        ]
        + [pltpu.VMEM((exp_dev, kinds, 1, 1, tile, width), bf16) for kinds, width in keeps]
        + [
            pltpu.SemaphoreType.DMA((2, 4)),
            pltpu.SemaphoreType.DMA((2, 3)),
            pltpu.SemaphoreType.DMA((3,)),
            pltpu.SemaphoreType.DMA((exp_dev, 3)),
            pltpu.SemaphoreType.DMA((exp_dev, 2)),
        ],
        cost_estimate=cost(20e9, 16e6),
        compiler_params=remote_params(5),
        name="own_experts",
    )(*given, router, *weights, target, over, up, normed)
    return got[:4], got[4:6], got[6:]


def run_experts(first, window, given, router, weights, kept, at, total, experts, units, chosen):
    low, high = chosen
    sources, exp_dev, capacity, model_width = given[0].shape
    wide_units = aligned_units(units)
    tile = 2 * capacity

    given_rows = pl.BlockSpec(
        (1, 1, capacity, model_width), lambda e, k, f, w: (k, low + e, 0, 0)
    )
    out = lambda width: pl.BlockSpec((1, 1, capacity, width), lambda e, k, f, w: (e, k, 0, 0))
    wide, rows = out(model_width + 128), out(model_width)
    weight = pl.BlockSpec(
        (pl.Element(1), pl.Element(model_width), pl.Element(wide_units)),
        lambda e, k, f, w: (low + e, 0, pl.multiple_of(w[0], 128)),
    )
    keep = lambda kinds, width: pl.BlockSpec(
        (kinds, 1, 1, tile, width), lambda e, k, f, w: (0, low + e, at + k, 0, 0)
    )
    keeps = ((2, model_width), (3, wide_units))
    kept = list(kept)
    out_of = lambda width: jax.ShapeDtypeStruct(
        (high - low, sources, capacity, width), jnp.bfloat16
    )
    back_shape, out_shape = out_of(model_width + 128), out_of(model_width)
    got = pl.pallas_call(
        functools.partial(expert_kernel, experts, units, len(kept)),
        grid_spec=pltpu.PrefetchScalarGridSpec(
            num_scalar_prefetch=2,
            grid=(high - low, sources),
            in_specs=[given_rows] * 4
            + [
                pl.BlockSpec(router.shape, lambda e, k, f, w: (0, 0)),
                weight,
                weight,
                weight,
            ]
            + anywhere(kept),
            out_specs=[wide, wide, rows, rows] + [keep(*kinds) for kinds in keeps],
        ),
        out_shape=[back_shape, back_shape, out_shape, out_shape]
        + [
            jax.ShapeDtypeStruct((kinds, exp_dev, total, tile, width), jnp.bfloat16)
            for kinds, width in keeps
        ],
        input_output_aliases={10 + i: 4 + i for i in range(len(kept))},
        cost_estimate=cost(20e9 * sources, 8e6 * sources),
        compiler_params=compiler_params(),
        name="expert_rows",
    )(first + low, window, *given, router, *weights, *kept)
    return got[:4], got[4:]


def aligned_units(units):
    return (units + 127) // 128 * 128


def weight_kernel(window_ref, rows_ref, units_ref, weight_ref, total):
    pieces, _, piece, model_width = weight_ref.shape
    units = units_ref[0, 0].reshape(-1, units_ref.shape[-1])
    total[...] = dot_tn(units, rows_ref[0, 0].reshape(-1, model_width))
    skip = pl.multiple_of(window_ref[1], 64)
    for at in range(pieces):
        weight_ref[at, 0] = total[pl.ds(skip + at * piece, piece), :].astype(jnp.bfloat16)


def weight_grads(window, kept, expert, pieces, units, waits=()):
    kept_rows, kept_units = kept
    tiles, tile, model_width = kept_rows.shape[2:]
    wide_units = kept_units.shape[4]
    shape = (pieces, 3, units // pieces, model_width)
    return pl.pallas_call(
        held(weight_kernel, 3, len(waits)),
        grid=(3,),
        in_specs=[
            pl.BlockSpec(memory_space=pltpu.SMEM),
            pl.BlockSpec((1, 1, tiles, tile, model_width), lambda i: (i // 2, expert, 0, 0, 0)),
            pl.BlockSpec((1, 1, tiles, tile, wide_units), lambda i: (i, expert, 0, 0, 0)),
        ]
        + anywhere(waits),
        out_specs=pl.BlockSpec((pieces, 1) + shape[2:], lambda i: (0, i, 0, 0)),
        out_shape=jax.ShapeDtypeStruct(shape, jnp.bfloat16),
        scratch_shapes=[pltpu.VMEM((wide_units, model_width), jnp.float32)],
        cost_estimate=cost(20e9, 20e6),
        compiler_params=compiler_params(),
        name="weight_grads",
    )(window, kept_rows, kept_units, *waits)


def send(values, axis, pairs):
    return lax.ppermute(values, axis, pairs)


def after(values, *earlier):
    return lax.optimization_barrier((values, earlier))[0]


def fast_device(
    tokens,
    lengths,
    expert_ids,
    places,
    buckets,
    w_attn,
    bias_table,
    norm1_gain,
    norm2_gain,
    w_router,
    w_gate,
    w_up,
    w_down,
    cotangent,
):
    span_rows, slots, model_width = tokens.shape
    head_count, bucket_count = bias_table.shape
    head_size = model_width // head_count
    scale = head_size ** (-0.5)
    n_dp = lax.axis_size("dp")
    n_ep = lax.axis_size("ep")
    n_cp = lax.axis_size("cp")
    my_dp, my_ep, my_cp = (lax.axis_index(name) for name in ("dp", "ep", "cp"))
    seq_len = span_rows * n_cp
    rows = span_rows * slots
    top_count = expert_ids.shape[2]
    experts = w_router.shape[1]
    exp_dev = w_gate.shape[0]
    units = w_gate.shape[2] // n_dp
    capacity = (5 * rows * top_count + 4 * experts - 1) // (4 * experts)
    groups = model_width // (128 * n_cp)
    own_width = 3 * groups * 128
    heads_own = head_count // n_cp
    over_core = [(i, i ^ 1) for i in range(n_dp)]
    over_x = [(i, i ^ 2) for i in range(n_dp)]
    over_y = [(i, i ^ 1) for i in range(n_ep)]
    ring = [(i, (i + 1) % n_cp) for i in range(n_cp)]
    f32, bf16 = jnp.float32, jnp.bfloat16
    exact = lax.Precision.HIGHEST
    each = range(slots)

    low_in = tokens.reshape(span_rows, slots * model_width)
    low_out = cotangent.reshape(span_rows, slots * model_width)
    gain_first, gain_second = norm1_gain[None, :], norm2_gain[None, :]

    per_group = 128 // head_size
    own_heads = (
        jnp.arange(groups)[:, None] * (n_cp * per_group)
        + my_cp * per_group
        + jnp.arange(per_group)[None, :]
    ).reshape(heads_own)
    head_hot = (own_heads[:, None] == jnp.arange(head_count)[None, :]).astype(f32)
    own_table = jnp.dot(head_hot, bias_table, precision=exact)
    far_hot = (buckets[::-1][:, None] == jnp.arange(bucket_count)[None, :]).astype(f32)
    lines = jnp.einsum("hb,db->hd", own_table, far_hot, precision=exact)
    lines = jnp.concatenate([lines, jnp.full((heads_own, span_rows), minus_big, f32)], axis=1)
    target = jnp.where(places >= 0, expert_ids * capacity + places, -1)
    target = target.transpose(1, 2, 0).astype(jnp.int32)
    (
        (normed_all, qkvs, bias, full, total, w_own, target_all, over_first, up_first),
        (grads_own, grads_rest_rows, picked_own),
        fronts,
    ) = front(
        lengths,
        gain_first,
        gain_second,
        lines[:, None, :],
        target,
        w_attn,
        low_in,
        low_out,
        slots,
        n_cp,
        exp_dev,
        capacity,
        scale,
        head_size,
    )
    attended, hidden, normed_second = zip(*fronts)

    sources = target_all.shape[0]
    target_rows = target_all.transpose(0, 2, 1, 3).reshape(sources, top_count, rows)
    target_columns = target_rows.transpose(0, 2, 1)
    window_at = my_dp * units // 128 * 128
    window = jnp.stack([window_at, my_dp * units - window_at]).astype(jnp.int32)
    router_wide = jnp.concatenate(
        [w_router, jnp.zeros((model_width, 128 - experts), w_router.dtype)], axis=1
    )

    first = (my_ep * exp_dev).astype(jnp.int32).reshape(1)
    own, kept, picked_rest = own_experts(
        (*picked_own, *grads_own),
        router_wide,
        (w_gate, w_up, w_down),
        target_all,
        over_first,
        up_first,
        normed_second[1],
        sources,
        experts,
        units,
    )

    def with_theirs(mine, theirs):
        return [mine, send(theirs, "dp", over_core)]

    backs, outs = with_theirs(own[0], own[1]), with_theirs(own[2], own[3])
    weight_sums = []
    for e in range(exp_dev):
        rest, kept = run_experts(
            first,
            window,
            (*picked_rest, *grads_rest_rows),
            router_wide,
            (w_gate, w_up, w_down),
            kept,
            1,
            sources,
            experts,
            units,
            (e, e + 1),
        )
        weight_part = weight_grads(window, kept, e, n_cp, units, backs[-1:] + outs[-1:])
        backs += with_theirs(rest[0], rest[1])
        outs += with_theirs(rest[2], rest[3])
        weight_sums.append(lax.psum_scatter(weight_part, "cp", scatter_dimension=0, tiled=False))
        kept = after(kept, weight_part)
    back_rows, out_own, out_rest = return_rows(target_columns, backs, outs, slots, [weight_part])
    got, mixed, (ringed, line_first, grads_rest) = hidden_back(
        lengths,
        back_rows,
        low_out,
        hidden,
        normed_second,
        gain_second,
        router_wide,
        w_attn,
        experts,
        qkvs,
        bias,
        full,
        total,
        out_own,
        out_rest,
        scale,
        head_size,
    )
    hidden_grads, proj_grads, router_parts, gain_parts = zip(*got)
    router_grad = sum(router_parts)[:, :experts].T
    ring_second, line_second, arrived, early, weight_first, out_grad = second_back(
        lengths,
        ringed,
        normed_all,
        qkvs,
        bias,
        grads_rest,
        full,
        total,
        attended,
        proj_grads,
        scale,
        head_size,
        weight_sums[:1],
    )
    distance_grads = (line_first + line_second)[:, 0, :seq_len]
    table_grad = jnp.dot(distance_grads, far_hot, precision=exact)
    table_grad = jnp.einsum("hg,hb->gb", head_hot, table_grad, precision=exact)
    table_row = jnp.pad(table_grad.reshape(1, -1), ((0, 0), (0, model_width - table_grad.size)))
    small = jnp.concatenate(
        [router_grad, sum(gain_parts), table_row, jnp.zeros((2, model_width), f32)], axis=0
    )
    *tokens_grad, small_sum, attn_sum = final_back(
        ring_second,
        early,
        normed_all,
        weight_first,
        w_own,
        arrived,
        out_grad,
        small,
        gain_first,
        w_attn,
        low_in,
        hidden_grads,
    )
    router_sum, gain_second_sum = small_sum[:experts], small_sum[experts]
    table_sum = small_sum[experts + 1, : table_grad.size].reshape(table_grad.shape)
    gain_first_sum = small_sum[experts + 2]

    gate_sum, up_sum, down_sum = (
        jnp.stack([part[which].T.astype(f32) for part in weight_sums]) for which in range(3)
    )
    return (
        jnp.stack(mixed, axis=1),
        jnp.stack(tokens_grad, axis=1),
        attn_sum,
        table_sum,
        gain_first_sum,
        gain_second_sum,
        router_sum.T,
        gate_sum,
        up_sum,
        down_sum,
    )


def solution(mesh):
    placed = (
        P("cp", ("dp", "ep"), None),
        P(("dp", "ep")),
        P("cp", ("dp", "ep"), None),
        P("cp", ("dp", "ep"), None),
        P(),
        P(),
        P(),
        P(),
        P(),
        P(),
        P("ep", None, None),
        P("ep", None, None),
        P("ep", None, None),
        P("cp", ("dp", "ep"), None),
    )
    sizes = dict(mesh.shape)
    square = sizes["dp"] == 4 and sizes["ep"] == 2 and sizes["cp"] == 4
    return jax.shard_map(
        fast_device if square else on_device,
        mesh=mesh,
        in_specs=placed,
        out_specs=(
            P("cp", ("dp", "ep"), None),
            P("cp", ("dp", "ep"), None),
            P(None, ("dp", "ep", "cp")),
            P(),
            P(),
            P(),
            P(),
            P("ep", None, ("dp", "cp")),
            P("ep", None, ("dp", "cp")),
            P("ep", None, ("dp", "cp")),
        ),
        check_vma=False,
    )
```

```python
import functools

import jax
import jax.numpy as jnp
from jax import lax
from jax.experimental import pallas as pl
from jax.experimental.pallas import tpu as pltpu
from jax.sharding import PartitionSpec as P

epsilon = 1e-06
masked_value = -1000000000.0


def gelu_tanh(values):
    return jax.nn.gelu(values, approximate=True)


def root_scale(values):
    return lax.rsqrt(jnp.mean(values * values, axis=-1, keepdims=True) + epsilon)


def norm_back(grad_in, values, scale_rows, gain_vector):
    scaled = grad_in * gain_vector
    inner_mean = jnp.mean(scaled * values, axis=-1, keepdims=True)
    return scale_rows * (scaled - values * scale_rows * scale_rows * inner_mean)


def block_logits(
    queries, key_rows, key_start, query_pos, lengths, table_step, rise_points, head_scale
):
    key_count = key_rows.shape[0]
    key_pos = key_start + jnp.arange(key_count, dtype=jnp.int32)
    scores = (
        jnp.einsum("qshd,kshd->shqk", queries, key_rows, preferred_element_type=jnp.float32)
        * head_scale
    )
    distance = query_pos[:, None] - key_pos[None, :]
    steps = (distance[:, :, None] >= rise_points[None, None, :]).astype(jnp.float32)
    pair_bias = jnp.einsum("hb,qkb->hqk", table_step, steps, precision=lax.Precision.HIGHEST)
    allowed = (distance >= 0)[None, :, :] & (key_pos[None, None, :] < lengths[:, None, None])
    logits = jnp.where(allowed[:, None], scores + pair_bias[None], masked_value)
    return (logits, steps)


def on_device(
    tokens,
    lengths,
    expert_ids,
    places,
    buckets,
    w_attn,
    bias_table,
    norm1_gain,
    norm2_gain,
    w_router,
    w_gate,
    w_up,
    w_down,
    cotangent,
):
    span_rows, pair_count, model_width = tokens.shape
    head_count, bucket_count = bias_table.shape
    head_size = model_width // head_count
    head_scale = head_size ** (-0.5)
    n_cp = lax.axis_size("cp")
    n_ep = lax.axis_size("ep")
    seq_len = span_rows * n_cp
    row_count = span_rows * pair_count
    top_count = expert_ids.shape[2]
    experts = w_router.shape[1]
    exp_dev = w_gate.shape[0]
    capacity = (5 * row_count * top_count + 4 * experts - 1) // (4 * experts)
    my_start = lax.axis_index("cp") * span_rows
    query_pos = my_start + jnp.arange(span_rows, dtype=jnp.int32)
    live_mask = (query_pos[:, None] < lengths[None, :]).astype(jnp.float32)
    inputs = tokens.astype(jnp.float32)
    scale_first = root_scale(inputs)
    normed_first = (inputs * scale_first * norm1_gain).astype(jnp.bfloat16)
    w_qkv = w_attn[:, : 3 * model_width]
    w_out = w_attn[:, 3 * model_width :]
    qkv = jnp.einsum("csd,de->cse", normed_first, w_qkv, preferred_element_type=jnp.float32).astype(
        jnp.bfloat16
    )
    queries = qkv[..., :model_width].reshape(span_rows, pair_count, head_count, head_size)
    keyval = qkv[..., model_width:]
    keyval_all = lax.all_gather(keyval, "cp", axis=0, tiled=True)
    bucket_ids = jnp.arange(bucket_count, dtype=jnp.int32)
    rise_points = jnp.sum((buckets[:, None] < bucket_ids[None, :]).astype(jnp.int32), axis=0)
    table_step = jnp.concatenate(
        [bias_table[:, :1], bias_table[:, 1:] - bias_table[:, :-1]], axis=1
    )
    block_starts = jnp.arange(n_cp, dtype=jnp.int32) * span_rows

    def split_kv(kv_block):
        key_rows = kv_block[..., :model_width].reshape(span_rows, pair_count, head_count, head_size)
        value_rows = kv_block[..., model_width:].reshape(
            span_rows, pair_count, head_count, head_size
        )
        return (key_rows, value_rows)

    kv_blocks = keyval_all.reshape(n_cp, span_rows, pair_count, 2 * model_width)

    def max_step(state_pair, block_item):
        row_peak, row_total = state_pair
        kv_block, block_start = block_item
        key_rows, value_rows = split_kv(kv_block)
        logits, steps = block_logits(
            queries, key_rows, block_start, query_pos, lengths, table_step, rise_points, head_scale
        )
        new_peak = jnp.maximum(row_peak, jnp.max(logits, axis=-1))
        row_total = row_total * jnp.exp(row_peak - new_peak) + jnp.sum(
            jnp.exp(logits - new_peak[..., None]), axis=-1
        )
        return ((new_peak, row_total), None)

    stat_shape = (pair_count, head_count, span_rows)
    (row_peak, row_total), unused = lax.scan(
        max_step,
        (jnp.full(stat_shape, masked_value, jnp.float32), jnp.zeros(stat_shape, jnp.float32)),
        (kv_blocks, block_starts),
    )
    log_total = row_peak + jnp.log(row_total)

    def value_step(running, block_item):
        kv_block, block_start = block_item
        key_rows, value_rows = split_kv(kv_block)
        logits, steps = block_logits(
            queries, key_rows, block_start, query_pos, lengths, table_step, rise_points, head_scale
        )
        weights = jnp.exp(logits - log_total[..., None]).astype(jnp.bfloat16)
        return (
            running
            + jnp.einsum(
                "shqk,kshd->qshd", weights, value_rows, preferred_element_type=jnp.float32
            ),
            None,
        )

    attended, unused = lax.scan(
        value_step,
        jnp.zeros((span_rows, pair_count, head_count, head_size), jnp.float32),
        (kv_blocks, block_starts),
    )
    attended = attended.reshape(span_rows, pair_count, model_width)
    attended_low = attended.astype(jnp.bfloat16)
    projected = jnp.einsum("csd,de->cse", attended_low, w_out, preferred_element_type=jnp.float32)
    hidden = inputs + live_mask[..., None] * projected
    scale_second = root_scale(hidden)
    normed_second = (hidden * scale_second * norm2_gain).astype(jnp.bfloat16)
    router_logits = jnp.einsum(
        "csd,de->cse", normed_second, w_router, preferred_element_type=jnp.float32
    )
    router_probs = jax.nn.softmax(router_logits, axis=-1)
    expert_hot = (expert_ids[..., None] == jnp.arange(experts, dtype=jnp.int32)).astype(jnp.float32)
    kept_mask = (places >= 0).astype(jnp.float32)
    gate_values = jnp.sum(expert_hot * router_probs[:, :, None, :], axis=-1) * kept_mask
    target = jnp.where(places >= 0, expert_ids * capacity + places, -1).reshape(
        row_count, top_count
    )
    slot_ids = jnp.arange(experts * capacity, dtype=jnp.int32)
    route_hot = (target[None, :, :] == slot_ids[:, None, None]).astype(jnp.bfloat16)
    dispatch = jnp.sum(route_hot, axis=2)
    sent_rows = jnp.dot(
        dispatch, normed_second.reshape(row_count, model_width), preferred_element_type=jnp.float32
    )
    sent_rows = sent_rows.astype(jnp.bfloat16).reshape(n_ep, exp_dev, capacity, model_width)
    arrived = lax.all_to_all(sent_rows, "ep", split_axis=0, concat_axis=0, tiled=True)
    gate_pre = jnp.einsum("secd,edf->secf", arrived, w_gate, preferred_element_type=jnp.float32)
    up_pre = jnp.einsum("secd,edf->secf", arrived, w_up, preferred_element_type=jnp.float32)
    active, gelu_pullback = jax.vjp(gelu_tanh, gate_pre)
    inner_act = (active * up_pre).astype(jnp.bfloat16)
    produced = jnp.einsum(
        "secf,edf->secd", inner_act, w_down, preferred_element_type=jnp.float32
    ).astype(jnp.bfloat16)
    returned = lax.all_to_all(produced, "ep", split_axis=0, concat_axis=0, tiled=True).reshape(
        experts * capacity, model_width
    )
    picked = jnp.einsum("jrk,jd->rkd", route_hot, returned, preferred_element_type=jnp.float32)
    gate_flat = gate_values.reshape(row_count, top_count)
    mixed = hidden.reshape(row_count, model_width) + jnp.sum(gate_flat[..., None] * picked, axis=1)
    mixed = mixed.reshape(span_rows, pair_count, model_width).astype(jnp.bfloat16)
    grad_out = cotangent.astype(jnp.float32).reshape(row_count, model_width)
    gate_grads = jnp.sum(grad_out[:, None, :] * picked, axis=-1)
    sent_back = (gate_flat[..., None] * grad_out[:, None, :]).astype(jnp.bfloat16)
    scattered = jnp.einsum("jrk,rkd->jd", route_hot, sent_back, preferred_element_type=jnp.float32)
    scattered = scattered.astype(jnp.bfloat16).reshape(n_ep, exp_dev, capacity, model_width)
    grad_produced = lax.all_to_all(scattered, "ep", split_axis=0, concat_axis=0, tiled=True)
    down_grad = jnp.einsum(
        "secd,secf->edf", grad_produced, inner_act, preferred_element_type=jnp.float32
    )
    grad_inner = jnp.einsum(
        "secd,edf->secf", grad_produced, w_down, preferred_element_type=jnp.float32
    )
    grad_gate_pre = gelu_pullback(grad_inner * up_pre)[0].astype(jnp.bfloat16)
    grad_up_pre = (grad_inner * active).astype(jnp.bfloat16)
    gate_grad = jnp.einsum(
        "secd,secf->edf", arrived, grad_gate_pre, preferred_element_type=jnp.float32
    )
    up_grad = jnp.einsum("secd,secf->edf", arrived, grad_up_pre, preferred_element_type=jnp.float32)
    grad_arrived = jnp.einsum(
        "secf,edf->secd", grad_gate_pre, w_gate, preferred_element_type=jnp.float32
    )
    grad_arrived = (
        grad_arrived
        + jnp.einsum("secf,edf->secd", grad_up_pre, w_up, preferred_element_type=jnp.float32)
    ).astype(jnp.bfloat16)
    grad_sent = lax.all_to_all(grad_arrived, "ep", split_axis=0, concat_axis=0, tiled=True).reshape(
        experts * capacity, model_width
    )
    grad_rows = jnp.einsum("jr,jd->rd", dispatch, grad_sent, preferred_element_type=jnp.float32)
    choice_grads = gate_grads.reshape(span_rows, pair_count, top_count) * kept_mask
    prob_grads = jnp.sum(expert_hot * choice_grads[..., None], axis=2)
    logit_grads = router_probs * (
        prob_grads - jnp.sum(router_probs * prob_grads, axis=-1, keepdims=True)
    )
    logit_grads = logit_grads.astype(jnp.bfloat16)
    router_grad = jnp.einsum(
        "csd,cse->de", normed_second, logit_grads, preferred_element_type=jnp.float32
    )
    grad_normed_second = grad_rows.reshape(span_rows, pair_count, model_width)
    grad_normed_second = grad_normed_second + jnp.einsum(
        "cse,de->csd", logit_grads, w_router, preferred_element_type=jnp.float32
    )
    gain_second_grad = jnp.sum(grad_normed_second * hidden * scale_second, axis=(0, 1))
    grad_hidden = grad_out.reshape(span_rows, pair_count, model_width) + norm_back(
        grad_normed_second, hidden, scale_second, norm2_gain
    )
    grad_proj = (live_mask[..., None] * grad_hidden).astype(jnp.bfloat16)
    out_grad = jnp.einsum(
        "csd,cse->de", attended_low, grad_proj, preferred_element_type=jnp.float32
    )
    grad_att = jnp.einsum(
        "cse,de->csd", grad_proj, w_out, preferred_element_type=jnp.float32
    ).astype(jnp.bfloat16)
    grad_att_heads = grad_att.reshape(span_rows, pair_count, head_count, head_size)
    row_terms = jnp.sum(
        grad_att_heads.astype(jnp.float32)
        * attended.reshape(span_rows, pair_count, head_count, head_size),
        axis=-1,
    )
    row_terms = row_terms.transpose(1, 2, 0)
    keyval_back = lax.all_gather(keyval, "cp", axis=0, tiled=True)
    back_blocks = keyval_back.reshape(n_cp, span_rows, pair_count, 2 * model_width)

    def pair_terms(
        query_rows, grad_rows_att, row_part, total_part, key_rows, value_rows, key_start, rows_pos
    ):
        logits, steps = block_logits(
            query_rows, key_rows, key_start, rows_pos, lengths, table_step, rise_points, head_scale
        )
        weights = jnp.exp(logits - total_part[..., None])
        weight_grads = jnp.einsum(
            "qshd,kshd->shqk", grad_rows_att, value_rows, preferred_element_type=jnp.float32
        )
        score_grads = weights * (weight_grads - row_part[..., None])
        return (weights, score_grads, steps)

    def query_side_step(state_pair, kv_block, block_start):
        query_grad, step_grad = state_pair
        key_rows, value_rows = split_kv(kv_block)
        weights, score_grads, steps = pair_terms(
            queries,
            grad_att_heads,
            row_terms,
            log_total,
            key_rows,
            value_rows,
            block_start,
            query_pos,
        )
        low_grads = score_grads.astype(jnp.bfloat16)
        query_grad = (
            query_grad
            + jnp.einsum("shqk,kshd->qshd", low_grads, key_rows, preferred_element_type=jnp.float32)
            * head_scale
        )
        step_grad = step_grad + jnp.einsum(
            "hqk,qkb->hb", jnp.sum(score_grads, axis=0), steps, precision=lax.Precision.HIGHEST
        )
        return ((query_grad, step_grad), weights, low_grads)

    start_state = (
        jnp.zeros((span_rows, pair_count, head_count, head_size), jnp.float32),
        jnp.zeros((head_count, bucket_count), jnp.float32),
    )

    def grad_step(state_pair, block_item):
        kv_block, block_start = block_item
        new_state, weights, low_grads = query_side_step(state_pair, kv_block, block_start)
        value_grad = jnp.einsum(
            "shqk,qshd->kshd",
            weights.astype(jnp.bfloat16),
            grad_att_heads,
            preferred_element_type=jnp.float32,
        )
        key_grad = (
            jnp.einsum("shqk,qshd->kshd", low_grads, queries, preferred_element_type=jnp.float32)
            * head_scale
        )
        block_grad = jnp.concatenate(
            [
                key_grad.reshape(span_rows, pair_count, model_width),
                value_grad.reshape(span_rows, pair_count, model_width),
            ],
            axis=-1,
        )
        return (new_state, block_grad)

    (query_grad, step_grad), kv_terms = lax.scan(
        grad_step, start_state, (back_blocks, block_starts)
    )
    kv_terms = kv_terms.reshape(seq_len, pair_count, 2 * model_width)
    keyval_grad = lax.psum_scatter(
        kv_terms.astype(jnp.bfloat16), "cp", scatter_dimension=0, tiled=True
    )
    table_grad = step_grad - jnp.concatenate(
        [step_grad[:, 1:], jnp.zeros((head_count, 1), jnp.float32)], axis=1
    )
    qkv_grad = jnp.concatenate(
        [query_grad.reshape(span_rows, pair_count, model_width).astype(jnp.bfloat16), keyval_grad],
        axis=-1,
    )
    qkv_weight_grad = jnp.einsum(
        "csd,cse->de", normed_first, qkv_grad, preferred_element_type=jnp.float32
    )
    grad_normed_first = jnp.einsum(
        "cse,de->csd", qkv_grad, w_qkv, preferred_element_type=jnp.float32
    )
    gain_first_grad = jnp.sum(grad_normed_first * inputs * scale_first, axis=(0, 1))
    tokens_grad = (
        grad_hidden + norm_back(grad_normed_first, inputs, scale_first, norm1_gain)
    ).astype(jnp.bfloat16)
    attn_term = jnp.concatenate([qkv_weight_grad, out_grad], axis=1)
    w_attn_grad = lax.psum_scatter(attn_term, ("dp", "ep", "cp"), scatter_dimension=1, tiled=True)
    router_sum, table_sum, gain_first_sum, gain_second_sum = lax.psum(
        (router_grad, table_grad, gain_first_grad, gain_second_grad), ("dp", "ep", "cp")
    )
    gate_sum, up_sum, down_sum = (
        lax.psum_scatter(
            gate_grad.astype(jnp.bfloat16), ("dp", "cp"), scatter_dimension=2, tiled=True
        ).astype(jnp.float32),
        lax.psum_scatter(
            up_grad.astype(jnp.bfloat16), ("dp", "cp"), scatter_dimension=2, tiled=True
        ).astype(jnp.float32),
        lax.psum_scatter(
            down_grad.astype(jnp.bfloat16), ("dp", "cp"), scatter_dimension=2, tiled=True
        ).astype(jnp.float32),
    )
    return (
        mixed,
        tokens_grad,
        w_attn_grad,
        table_sum,
        gain_first_sum,
        gain_second_sum,
        router_sum,
        gate_sum,
        up_sum,
        down_sum,
    )


minus_big = -1000000000.0
vmem_bytes = 60 * 1024 * 1024


cost_share = 0.05


def cost(flops, moved):
    return pl.CostEstimate(
        flops=int(flops * cost_share), bytes_accessed=int(moved * cost_share), transcendentals=0
    )


def held(kernel, at, count):
    def run(*refs):
        kernel(*refs[:at], *refs[at + count :])

    return run


def anywhere(arrays):
    return [pl.BlockSpec(memory_space=pl.ANY)] * len(arrays)


def compiler_params():
    return pltpu.CompilerParams(vmem_limit_bytes=vmem_bytes)


def shear(values, leftward):
    rows, lanes = values.shape
    row_ids = lax.broadcasted_iota(jnp.int32, (rows, lanes), 0)
    bit = 1
    while bit < rows:
        amount = lanes - bit if leftward else bit
        moved = pltpu.roll(values, amount, 1)
        values = jnp.where((row_ids & bit) != 0, moved, values)
        bit *= 2
    return values


def dot_nt(left, right):
    return lax.dot_general(
        left, right, (((1,), (1,)), ((), ())), preferred_element_type=jnp.float32
    )


def dot_tn(left, right):
    return lax.dot_general(
        left, right, (((0,), (0,)), ((), ())), preferred_element_type=jnp.float32
    )


def dot_nn(left, right):
    return jnp.dot(left, right, preferred_element_type=jnp.float32)


def key_masks(length, blocks, span_rows):
    masks = []
    for block in range(blocks):
        position = block * span_rows + lax.broadcasted_iota(jnp.int32, (1, span_rows), 1)
        masks.append(jnp.where(position < length, 0.0, minus_big))
    return masks


def forward_body(
    mine, length, scale, head_size, qkv_ref, bias_ref, low_ref, full_ref, total_ref, after_pair
):
    blocks, span_rows, width = qkv_ref.shape
    lanes = 128
    lane = lax.broadcasted_iota(jnp.int32, (1, lanes), 1)
    masks = key_masks(length, blocks, span_rows)
    halves = lanes // head_size

    def place(block):
        return lax.rem(mine - block + blocks, blocks)

    def one_pair(pair, carry):
        wide = pl.multiple_of(pair * (3 * lanes), lanes)
        own_lanes = pl.ds(pl.multiple_of(pair * lanes, lanes), lanes)
        part = [pl.ds(pl.multiple_of(wide + which * lanes, lanes), lanes) for which in range(3)]
        for row in range(blocks):
            queries = qkv_ref[place(row), :, part[0]]
            totals = jnp.zeros((span_rows, lanes), jnp.float32)
            result = jnp.zeros((span_rows, lanes), jnp.float32)
            for half in range(halves):
                own = lane // head_size == half
                head_q = queries * jnp.where(own, scale, 0.0).astype(jnp.bfloat16)
                head_v = jnp.where(own, 1.0, 0.0).astype(jnp.bfloat16)
                logits = []
                for column in range(row + 1):
                    at = (blocks - 1 - row + column) * span_rows
                    term = dot_nt(head_q, qkv_ref[place(column), :, part[1]])
                    bias = bias_ref[pair * halves + half, :, at : at + span_rows]
                    logits.append(term + bias + masks[column])
                peak = jnp.max(logits[0], axis=1, keepdims=True)
                for term in logits[1:]:
                    peak = jnp.maximum(peak, jnp.max(term, axis=1, keepdims=True))
                total = jnp.zeros((span_rows, 1), jnp.float32)
                mixed = jnp.zeros((span_rows, lanes), jnp.float32)
                for column in range(row + 1):
                    weights = jnp.exp(logits[column] - peak)
                    total = total + jnp.sum(weights, axis=1, keepdims=True)
                    values = qkv_ref[place(column), :, part[2]] * head_v
                    mixed = mixed + dot_nn(weights.astype(jnp.bfloat16), values)
                result = result + mixed / total
                totals = jnp.where(lane == half, peak + jnp.log(total), totals)
            low_ref[place(row), :, own_lanes] = result.astype(jnp.bfloat16)
            full_ref[row, :, own_lanes] = result
            total_ref[row, :, own_lanes] = totals
        after_pair(pair)
        return carry

    lax.fori_loop(0, width // (3 * lanes), one_pair, 0)


def backward_body(
    mine, length, scale, head_size, qkv_ref, bias_ref, grad_ref, full_ref, total_ref, ring_ref, line_ref, work,
    after_pair=None,
):
    key_sum, value_sum, plane = work
    blocks, span_rows, width = qkv_ref.shape
    lanes = 128
    lane = lax.broadcasted_iota(jnp.int32, (1, lanes), 1)
    masks = key_masks(length, blocks, span_rows)
    halves = lanes // head_size

    def place(block):
        return lax.rem(mine - block + blocks, blocks)

    def one_pair(pair, carry):
        wide = pl.multiple_of(pair * (3 * lanes), lanes)
        own_lanes = pl.ds(pl.multiple_of(pair * lanes, lanes), lanes)
        part = [pl.ds(pl.multiple_of(wide + which * lanes, lanes), lanes) for which in range(3)]
        key_sum[...] = jnp.zeros_like(key_sum)
        value_sum[...] = jnp.zeros_like(value_sum)
        plane[...] = jnp.zeros_like(plane)
        for row in range(blocks):
            queries = qkv_ref[place(row), :, part[0]]
            grads = grad_ref[lax.rem(row - mine + blocks, blocks), :, own_lanes]
            products = grads.astype(jnp.float32) * full_ref[row, :, own_lanes]
            totals = total_ref[row, :, own_lanes]
            query_sum = jnp.zeros((span_rows, lanes), jnp.float32)
            for half in range(halves):
                own = lane // head_size == half
                one = jnp.where(own, 1.0, 0.0).astype(jnp.bfloat16)
                head_q = queries * jnp.where(own, scale, 0.0).astype(jnp.bfloat16)
                head_g = grads * one
                delta = jnp.sum(jnp.where(own, products, 0.0), axis=1, keepdims=True)
                total = totals[:, half : half + 1]
                for column in range(row + 1):
                    at = (blocks - 1 - row + column) * span_rows
                    keys = qkv_ref[place(column), :, part[1]]
                    logits = dot_nt(head_q, keys)
                    bias = bias_ref[pair * halves + half, :, at : at + span_rows]
                    logits = logits + bias + masks[column]
                    weights = jnp.exp(logits - total)
                    weight_grads = dot_nt(head_g, qkv_ref[place(column), :, part[2]])
                    score_grads = weights * (weight_grads - delta)
                    plane[half, :, at : at + span_rows] += score_grads
                    low_weights = weights.astype(jnp.bfloat16)
                    low_grads = score_grads.astype(jnp.bfloat16)
                    query_sum = query_sum + dot_nn(low_grads, keys * one)
                    key_sum[column] += dot_tn(low_grads, head_q)
                    value_sum[column] += dot_tn(low_weights, head_g)
            ring_ref[place(row), :, part[0]] = (query_sum * scale).astype(jnp.bfloat16)
        for row in range(blocks):
            ring_ref[place(row), :, part[1]] = key_sum[row].astype(jnp.bfloat16)
            ring_ref[place(row), :, part[2]] = value_sum[row].astype(jnp.bfloat16)
        for half in range(halves):
            full = jnp.concatenate(
                [plane[half], jnp.zeros((span_rows, span_rows), jnp.float32)], axis=1
            )
            summed = jnp.sum(shear(full, True), axis=0, keepdims=True)
            line_ref[pair * halves + half] = pltpu.roll(summed, span_rows - 1, 1)
        if after_pair is not None:
            after_pair(pair)
        return carry

    lax.fori_loop(0, width // (3 * lanes), one_pair, 0)


def backward_work(blocks, span_rows, head_size):
    return [
        pltpu.VMEM((blocks, span_rows, 128), jnp.float32),
        pltpu.VMEM((blocks, span_rows, 128), jnp.float32),
        pltpu.VMEM((128 // head_size, span_rows, blocks * span_rows), jnp.float32),
    ]


def greet(*others):
    barrier = pltpu.get_barrier_semaphore()
    for other in others:
        pl.semaphore_signal(
            barrier, inc=1, device_id=other, device_id_type=pl.DeviceIdType.MESH
        )
    pl.semaphore_wait(barrier, len(others))


def push(source, target, send_sem, recv_sem, other):
    return pltpu.make_async_remote_copy(
        src_ref=source,
        dst_ref=target,
        send_sem=send_sem,
        recv_sem=recv_sem,
        device_id=other,
        device_id_type=pl.DeviceIdType.MESH,
    )


def ring_others(mine, count):
    return [{"cp": lax.rem(mine + j, count)} for j in range(1, count)]


def slot_of(ref, slot, slots):
    width = ref.shape[1] // slots
    return ref.at[:, pl.ds(slot * width, width)]


def deliveries(source, target, sems, mine, count, lanes=None):
    return [
        push(
            source.at[j] if lanes is None else source.at[j, :, lanes],
            target.at[j],
            sems.at[0, j],
            sems.at[1, j],
            {"cp": lax.rem(mine + (count - j), count)},
        )
        for j in range(1, count)
    ]


def remote_params(number):
    return pltpu.CompilerParams(
        vmem_limit_bytes=vmem_bytes, collective_id=number, has_side_effects=True
    )


def own_rows(block, length, span_rows):
    position = block * span_rows + lax.broadcasted_iota(jnp.int32, (span_rows, 1), 0)
    return jnp.where(position < length, 1.0, 0.0)


def router_of(rows, router_w, experts):
    lane = lax.broadcasted_iota(jnp.int32, (1, router_w.shape[1]), 1)
    logits = jnp.where(lane < experts, dot_nn(rows, router_w), minus_big)
    shares = jnp.exp(logits - jnp.max(logits, axis=1, keepdims=True))
    return shares / jnp.sum(shares, axis=1, keepdims=True)


def project_body(mine, length, input_ref, gain_ref, weight_ref, parts_ref, own_ref, attended_ref, hidden_ref, normed_ref):
    count, span_rows, width = parts_ref.shape
    for j in range(count):
        owner = lax.rem(mine + j, count)
        for group in range(width // 128):
            at = pl.multiple_of((group * count + owner) * 128, 128)
            lanes = slice(group * 128, (group + 1) * 128)
            attended_ref[:, pl.ds(at, 128)] = own_ref[0, :, lanes] if j == 0 else parts_ref[j, :, lanes]
    projected = dot_nn(attended_ref[...], weight_ref[...])
    hidden = input_ref[...].astype(jnp.float32) + own_rows(mine, length, span_rows) * projected
    hidden_ref[...] = hidden
    normed_ref[...] = (hidden * root_scale(hidden) * gain_ref[...]).astype(jnp.bfloat16)


def pick_body(base, capacity, experts, chosen, parts, out_ref):
    for expert in range(experts):
        picked = None
        for choice_ref, part in zip(chosen, parts):
            span = part.shape[0]
            ids = lax.broadcasted_iota(jnp.int32, (capacity, span), 0) + (base + expert * capacity)
            hot = jnp.zeros((capacity, span), jnp.float32)
            for choice in range(choice_ref.shape[0]):
                hot = hot + jnp.where(ids == choice_ref[choice : choice + 1, :], 1.0, 0.0)
            term = dot_nn(hot.astype(jnp.bfloat16), part[...])
            picked = term if picked is None else picked + term
        out_ref[expert] = picked.astype(jnp.bfloat16)


def front_kernel(
    scale, head_size, slots, length_ref, gain_first_ref, gain_second_ref, line_ref, target_ref, w_attn_ref, weight_ref,
    tokens_ref, cotangent_ref, *refs
):
    inputs = [slot_of(tokens_ref, s, slots) for s in range(slots)]
    grads = [slot_of(cotangent_ref, s, slots) for s in range(slots)]
    stores_to, own_w, targets_ref = refs[:5], refs[5], refs[6]
    over_ref, up_ref = refs[7:9]
    picks = [refs[9 + 2 * i : 11 + 2 * i] for i in range(3)]
    outs = [refs[15 + 3 * s : 18 + 3 * s] for s in range(slots)]
    refs = refs[15 + 3 * slots :]
    low, arrived, near_grads, ring_sems, own_sems, give_sems, plane_sems, target_sems = refs[:8]
    core_sems, normed_sems, store_sems, *made = refs[8:]
    all_ref, qkv_ref, bias_ref, full_ref, total_ref = made
    _, count, span_rows, model_width = all_ref.shape

    def store(which, slot):
        source, target = made[which], stores_to[which]
        if which != 2:
            source, target = source.at[slot], target.at[slot]
        return pltpu.make_async_copy(source, target, store_sems.at[which, slot])

    groups = own_w.shape[1] // 384
    mine = lax.axis_index("cp")
    dp, ep = lax.axis_index("dp"), lax.axis_index("ep")
    core_other, x_other, y_other = near_others(dp, ep)

    loads = []
    for group in range(groups):
        for which in range(3):
            at = which * model_width + (group * count + mine) * 128
            lanes = pl.ds((group * 3 + which) * 128, 128)
            loads.append(
                pltpu.make_async_copy(
                    w_attn_ref.at[:, pl.ds(pl.multiple_of(at, 128), 128)],
                    own_w.at[:, lanes],
                    own_sems.at[group * 3 + which],
                )
            )
    for load in loads:
        load.start()
    for s in range(slots):
        values = inputs[s][...].astype(jnp.float32)
        all_ref[s, 0] = (values * root_scale(values) * gain_first_ref[...]).astype(jnp.bfloat16)
    greet(*ring_others(mine, count), core_other, x_other, y_other)

    def hop_copy(slot, hop):
        return push(
            all_ref.at[slot, hop],
            all_ref.at[slot, hop + 1],
            ring_sems.at[0, slot, hop],
            ring_sems.at[1, slot, hop],
            {"cp": lax.rem(mine + 1, count)},
        )

    for s in range(slots):
        hop_copy(s, 0).start()

    def plane_copies(source, target, sems):
        first = [
            push(source(s), target.at[way, s], sems.at[0, way, s], sems.at[1, way, s], other)
            for s in (0, 1)
            for way, other in ((0, x_other), (1, y_other))
        ]
        second = [
            push(target.at[0, 0], target.at[2, 0], sems.at[0, 2, 0], sems.at[1, 2, 0], y_other),
            push(target.at[1, 1], target.at[2, 1], sems.at[0, 2, 1], sems.at[1, 2, 1], x_other),
        ]
        return first, second

    grad_first, grad_second = plane_copies(lambda s: grads[s], near_grads, plane_sems)
    near_targets = targets_ref.at[pl.ds(1, 3)]
    place_first, place_second = plane_copies(lambda s: target_ref.at[s], near_targets, target_sems)
    for copy in place_first + grad_first:
        copy.start()
    targets_ref[0] = target_ref[...]
    for load in loads:
        load.wait()
    for s in range(slots):
        qkv_ref[s, 0] = dot_nn(all_ref[s, 0], own_w[...]).astype(jnp.bfloat16)
    columns = bias_ref.shape[2]
    lanes = span_rows + columns
    for head in range(bias_ref.shape[0]):
        line = pltpu.roll(line_ref[head], lanes - (span_rows - 1), 1)
        full = jnp.broadcast_to(line, (span_rows, lanes))
        bias_ref[head] = shear(full, False)[:, :columns]
    store(2, 0).start()

    _, experts, capacity, _ = picks[0][0].shape
    base = ep * (experts * capacity)
    at_of = ((0, 0), (1, 0), (1, 1), (1, 2), (2, 0))

    def pick(source):
        if source == 0:
            parts = grads
        elif source == 4:
            parts = [outs[s][2] for s in range(slots)]
        else:
            parts = [near_grads.at[source - 1, s] for s in range(slots)]
        chosen = [targets_ref.at[source % 4, s] for s in range(slots)]
        group, at = at_of[source]
        pick_body(base, capacity, experts, chosen, parts, picks[group][0].at[at])
        core_copy(source).start()

    def core_copy(source):
        group, at = at_of[source]
        return push(
            picks[group][0].at[at],
            picks[group][1].at[at],
            core_sems.at[0, source],
            core_sems.at[1, source],
            core_other,
        )

    def normed_copy(at):
        source, target, other = (
            (outs[0][2], over_ref, x_other),
            (outs[0][2], up_ref, y_other),
        )[at]
        return push(source, target, normed_sems.at[0, at], normed_sems.at[1, at], other)

    def project(slot):
        for pair in range(groups):
            for copy in gives(slot, pair):
                copy.wait()
        project_body(
            mine, length_ref[slot], inputs[slot], gain_second_ref, weight_ref, arrived.at[slot],
            low.at[slot], *outs[slot],
        )

    def gives(slot, pair):
        part = pl.ds(pl.multiple_of(pair * 128, 128), 128)
        return [
            push(
                low.at[slot, j, :, part],
                arrived.at[slot, j, :, part],
                give_sems.at[0, slot, pair, j],
                give_sems.at[1, slot, pair, j],
                {"cp": lax.rem(mine + (count - j), count)},
            )
            for j in range(1, count)
        ]

    def attend(slot):
        def after_pair(pair):
            for copy in gives(slot, pair):
                copy.start()

        forward_body(
            mine, length_ref[slot], scale, head_size, qkv_ref.at[slot], bias_ref, low.at[slot],
            full_ref.at[slot], total_ref.at[slot], after_pair,
        )
        for which in (0, 1, 3, 4):
            store(which, slot).start()

    pick(0)
    for hop in range(1, count):
        for s in range(slots):
            hop_copy(s, hop - 1).wait_recv()
            if hop < count - 1:
                hop_copy(s, hop).start()
            qkv_ref[s, hop] = dot_nn(all_ref[s, hop], own_w[...]).astype(jnp.bfloat16)
            if hop == count - 1 and s + 1 < slots:
                attend(s)
        if hop == 1:
            for copy in place_first + grad_first:
                copy.wait_recv()
            for copy in place_second + grad_second:
                copy.start()
            pick(1)
            pick(2)
        if hop == 2:
            for copy in place_second + grad_second:
                copy.wait_recv()
            pick(3)
    attend(slots - 1)
    project(0)
    for at in range(2):
        normed_copy(at).start()
    project(1)
    pick(4)
    for s in range(slots):
        for hop in range(count - 1):
            hop_copy(s, hop).wait_send()
    for copy in place_first + grad_first + place_second + grad_second:
        copy.wait_send()
    for at in range(2):
        normed_copy(at).wait()
    for source in range(5):
        core_copy(source).wait()
    store(2, 0).wait()
    for s in range(slots):
        for which in (0, 1, 3, 4):
            store(which, s).wait()


def front(lengths, gain_first, gain_second, lines, target, w_attn, inputs, grads, slots, count, experts, capacity, scale, head_size):
    span_rows, model_width = inputs.shape[0], inputs.shape[1] // slots
    heads, _, lanes = lines.shape
    own_width = 3 * model_width // count
    groups = own_width // 384
    choices = target.shape[1]
    whole = pl.BlockSpec(memory_space=pltpu.VMEM)
    f32, bf16 = jnp.float32, jnp.bfloat16
    shape = jax.ShapeDtypeStruct
    made = (
        ((slots, count, span_rows, model_width), bf16),
        ((slots, count, span_rows, own_width), bf16),
        ((heads, span_rows, lanes - span_rows), f32),
        ((slots, count, span_rows, groups * 128), f32),
        ((slots, count, span_rows, groups * 128), f32),
    )
    got = pl.pallas_call(
        functools.partial(front_kernel, scale, head_size, slots),
        grid=(1,),
        in_specs=[
            pl.BlockSpec(memory_space=pltpu.SMEM),
            whole,
            whole,
            whole,
            whole,
            pl.BlockSpec(memory_space=pl.ANY),
            pl.BlockSpec((model_width, model_width), lambda i: (0, 3)),
            whole,
            whole,
        ],
        out_specs=[pl.BlockSpec(memory_space=pl.ANY)] * 5 + [whole] * (10 + 3 * slots),
        out_shape=[
            *(shape(*kind) for kind in made),
            shape((model_width, own_width), bf16),
            shape((4, slots, choices, span_rows), jnp.int32),
        ]
        + [shape((span_rows, model_width), bf16)] * 2
        + [
            shape((sources, experts, capacity, model_width), bf16)
            for sources in (1, 3, 1)
            for _ in range(2)
        ]
        + [
            shape((span_rows, model_width), bf16),
            shape((span_rows, model_width), f32),
            shape((span_rows, model_width), bf16),
        ]
        * slots,
        scratch_shapes=[
            pltpu.VMEM((slots, count, span_rows, groups * 128), bf16),
            pltpu.VMEM((slots, count, span_rows, groups * 128), bf16),
            pltpu.VMEM((3, slots, span_rows, model_width), bf16),
            pltpu.SemaphoreType.DMA((2, slots, count - 1)),
            pltpu.SemaphoreType.DMA((3 * groups,)),
            pltpu.SemaphoreType.DMA((2, slots, groups, count)),
            pltpu.SemaphoreType.DMA((2, 3, slots)),
            pltpu.SemaphoreType.DMA((2, 3, slots)),
            pltpu.SemaphoreType.DMA((2, 5)),
            pltpu.SemaphoreType.DMA((2, 3)),
            pltpu.SemaphoreType.DMA((5, slots)),
            *(pltpu.VMEM(*kind) for kind in made),
        ],
        cost_estimate=cost(60e9, 20e6),
        compiler_params=remote_params(0),
        name="front",
    )(lengths, gain_first, gain_second, lines, target, w_attn, w_attn, inputs, grads)
    pairs = [got[9 + 2 * i : 11 + 2 * i] for i in range(3)]
    return got[:9], pairs, [got[15 + 3 * s : 18 + 3 * s] for s in range(slots)]


def hidden_body(
    experts, mine, length, back_ref, grad_ref, hidden_ref, normed_ref, gain_ref, router_ref, weight_ref,
    hidden_grad_ref, proj_ref, router_grad_ref, gain_grad_ref, leaving_ref, attended,
):
    count = leaving_ref.shape[0]
    span_rows, model_width = hidden_ref.shape
    back = back_ref[...]
    normed = normed_ref[...]
    probs = router_of(normed, router_ref[...], experts)
    shares = back[:, model_width:]
    logit_grads = probs * (shares - jnp.sum(probs * shares, axis=1, keepdims=True))
    logit_grads = logit_grads.astype(jnp.bfloat16)
    router_grad_ref[...] = dot_tn(normed, logit_grads)
    grads = back[:, :model_width] + dot_nt(logit_grads, router_ref[...])
    hidden = hidden_ref[...]
    scale_rows = root_scale(hidden)
    gain_grad_ref[...] = jnp.sum(grads * hidden * scale_rows, axis=0, keepdims=True)
    hidden_grads = grad_ref[...].astype(jnp.float32) + norm_back(
        grads, hidden, scale_rows, gain_ref[...]
    )
    hidden_grad_ref[...] = hidden_grads
    proj = (own_rows(mine, length, span_rows) * hidden_grads).astype(jnp.bfloat16)
    proj_ref[...] = proj
    attended[...] = dot_nt(proj, weight_ref[...]).astype(jnp.bfloat16)
    for j in range(count):
        owner = lax.rem(mine + (count - j), count)
        for group in range(leaving_ref.shape[2] // 128):
            at = pl.multiple_of((group * count + owner) * 128, 128)
            leaving_ref[j, :, group * 128 : (group + 1) * 128] = attended[:, pl.ds(at, 128)]


def hidden_kernel(
    experts, scale, head_size, slots, length_ref, gain_ref, router_ref, weight_ref, qkv_all, bias_all, full_all, total_all,
    cotangent_ref, *refs
):
    per_slot = [
        (refs[3 * s], slot_of(cotangent_ref, s, slots), *refs[3 * s + 1 : 3 * s + 3])
        for s in range(slots)
    ]
    refs = refs[3 * slots :]
    own_out, rest_out, refs = refs[:slots], refs[slots : 4 * slots], refs[4 * slots :]
    outs = [refs[4 * s : 4 * s + 4] for s in range(slots)]
    mixed, refs = refs[4 * slots : 5 * slots], refs[5 * slots :]
    ring_ref, line_ref, rest_ref, leaving, arriving, attended, sems = refs[:7]
    got, far, last, low, out_sems = refs[7:12]
    qkv_ref, bias_ref, full_ref, total_ref, held_out, load_sems = refs[12:18]
    work = refs[18:]
    count = qkv_ref.shape[0]
    mine = lax.axis_index("cp")
    _, x_other, y_other = near_others(lax.axis_index("dp"), lax.axis_index("ep"))
    over, up, across = (rest_out[i * slots : (i + 1) * slots] for i in range(3))
    loads = [
        pltpu.make_async_copy(source, target, load_sems.at[at])
        for at, (source, target) in enumerate(
            (
                (qkv_all.at[0], qkv_ref),
                (bias_all, bias_ref),
                (full_all.at[0], full_ref),
                (total_all.at[0], total_ref),
                (up[0], held_out.at[0]),
                (over[1], held_out.at[1]),
                (own_out[0], held_out.at[2]),
                (own_out[1], held_out.at[3]),
            )
        )
    ]
    for load in loads:
        load.start()
    greet(*ring_others(mine, count), x_other, y_other)

    def out_copy(at):
        source, target, other = (
            (over[0], got.at[0], x_other),
            (up[1], got.at[1], y_other),
            (across[0], far.at[0], x_other),
            (across[1], far.at[1], y_other),
            (low.at[0], last.at[0], y_other),
            (low.at[1], last.at[1], x_other),
        )[at]
        return push(source, target, out_sems.at[0, at], out_sems.at[1, at], other)

    def after_pair(pair):
        @pl.when(pair == 0)
        def _():
            for at in range(2):
                out_copy(2 + at).wait()
                summed = held_out[at].astype(jnp.float32) + far[at].astype(jnp.float32)
                low[at] = summed.astype(jnp.bfloat16)
                out_copy(4 + at).start()

    for at in (2, 3, 0, 1):
        out_copy(at).start()
    copies = []
    for s in range(slots):
        hidden_body(
            experts, mine, length_ref[s], *per_slot[s], gain_ref, router_ref, weight_ref,
            *outs[s], leaving.at[s], attended,
        )
        target = arriving if s == 0 else rest_ref.at[s - 1]
        copies.append(deliveries(leaving.at[s], target, sems.at[s], mine, count))
        if s == 0:
            for copy in copies[s]:
                copy.start()
        target[0] = leaving[s, 0]
    for copy in copies[0]:
        copy.wait()
    for some in copies[1:]:
        for copy in some:
            copy.start()
    for load in loads:
        load.wait()
    backward_body(
        mine, length_ref[0], scale, head_size, qkv_ref, bias_ref, arriving, full_ref, total_ref,
        ring_ref, line_ref, work, after_pair,
    )
    for s in range(slots):
        out_copy(s).wait()
        out_copy(4 + s).wait()
        home = held_out[2 + s].astype(jnp.float32) + got[s].astype(jnp.float32)
        home = per_slot[s][2][...] + home + last[s].astype(jnp.float32)
        mixed[s][...] = home.astype(jnp.bfloat16)
    for copy in (copy for some in copies[1:] for copy in some):
        copy.wait()


def hidden_back(
    lengths, back_rows, grads, hidden, normed, gain, router, w_attn, experts, qkvs, bias, full, total, own_out,
    rest_out, scale, head_size,
):
    slots, count, span_rows, own_width = qkvs.shape
    model_width = hidden[0].shape[1]
    heads = bias.shape[0]
    whole = pl.BlockSpec(memory_space=pltpu.VMEM)
    f32, bf16 = jnp.float32, jnp.bfloat16
    each = [grads]
    for s in range(slots):
        each += [back_rows[s], hidden[s], normed[s]]
    each += [*own_out, *rest_out]
    own_shape = (count, span_rows, own_width // 3)
    got = pl.pallas_call(
        functools.partial(hidden_kernel, experts, scale, head_size, slots),
        grid=(1,),
        in_specs=[
            pl.BlockSpec(memory_space=pltpu.SMEM),
            whole,
            whole,
            pl.BlockSpec((model_width, model_width), lambda i: (0, 3)),
            *[pl.BlockSpec(memory_space=pl.ANY)] * 4,
        ]
        + [whole] * (len(each) - 4 * slots)
        + [pl.BlockSpec(memory_space=pl.ANY)] * (4 * slots),
        out_specs=[whole] * (5 * slots + 3),
        out_shape=[
            jax.ShapeDtypeStruct((span_rows, model_width), f32),
            jax.ShapeDtypeStruct((span_rows, model_width), bf16),
            jax.ShapeDtypeStruct((model_width, router.shape[1]), f32),
            jax.ShapeDtypeStruct((1, model_width), f32),
        ]
        * slots
        + [jax.ShapeDtypeStruct((span_rows, model_width), bf16)] * slots
        + [
            jax.ShapeDtypeStruct(qkvs.shape[1:], bf16),
            jax.ShapeDtypeStruct((heads, 1, bias.shape[2] + span_rows), f32),
            jax.ShapeDtypeStruct((slots - 1,) + own_shape, bf16),
        ],
        scratch_shapes=[
            pltpu.VMEM((slots,) + own_shape, bf16),
            pltpu.VMEM(own_shape, bf16),
            pltpu.VMEM((span_rows, model_width), bf16),
            pltpu.SemaphoreType.DMA((slots, 2, count)),
            *[pltpu.VMEM((slots, span_rows, model_width), bf16)] * 4,
            pltpu.SemaphoreType.DMA((2, 6)),
            pltpu.VMEM(qkvs.shape[1:], bf16),
            pltpu.VMEM(bias.shape, f32),
            pltpu.VMEM(full.shape[1:], f32),
            pltpu.VMEM(full.shape[1:], f32),
            pltpu.VMEM((2 * slots, span_rows, model_width), bf16),
            pltpu.SemaphoreType.DMA((8,)),
        ]
        + backward_work(count, span_rows, head_size),
        cost_estimate=cost(20e9, 20e6),
        compiler_params=remote_params(1),
        name="hidden_back",
    )(lengths, gain, router, w_attn, qkvs, bias, full, total, *each)
    return [got[4 * s : 4 * s + 4] for s in range(slots)], got[4 * slots : 5 * slots], got[5 * slots :]


def near_others(dp, ep):
    core, across = lax.rem(dp, 2), dp // 2
    return (
        {"dp": across * 2 + (1 - core)},
        {"dp": (1 - across) * 2 + core},
        {"ep": 1 - ep},
    )


def second_kernel(
    scale, head_size, slots, length_ref, former_ref, normed_all, qkv_all, bias_all, grad_ref, full_all, total_all,
    *refs,
):
    attended, proj, refs = refs[:slots], refs[slots : 2 * slots], refs[2 * slots :]
    ring_ref, line_ref, arrived_ref, early_ref, weight_ref, rows_ref = refs[:6]
    sums, low, got_core, got_x, got_y, leaving, coming, sems, near_sems, last_sems = refs[6:16]
    early_sems, held_refs, work = refs[16], refs[17:23], refs[23:]
    normed_ref, qkv_ref, bias_ref, full_ref, total_ref, load_sems = held_refs
    count = qkv_ref.shape[0]
    mine = lax.axis_index("cp")
    loads = [
        pltpu.make_async_copy(source, target, load_sems.at[at])
        for at, (source, target) in enumerate(
            (
                (qkv_all.at[1], qkv_ref),
                (bias_all, bias_ref),
                (full_all.at[1], full_ref),
                (total_all.at[1], total_ref),
                (normed_all.at[0], normed_ref),
            )
        )
    ]
    for load in loads:
        load.start()
    dp, ep = lax.axis_index("dp"), lax.axis_index("ep")
    core, across = lax.rem(dp, 2), dp // 2
    others = near_others(dp, ep)
    greet(*ring_others(mine, count), *others)
    copies = deliveries(former_ref, arrived_ref, sems, mine, count)
    for copy in copies:
        copy.start()
    arrived_ref[0] = former_ref[0]
    height = sums.shape[0] // 2
    sizes = (height, height // 2, height // 4)
    bits = (core, across, ep)
    landing = (got_core, got_x, got_y)
    total = None
    for s in range(slots):
        term = dot_tn(attended[s][...], proj[s][...])
        total = term if total is None else total + term
    sums[...] = total

    def low_part(stage):
        return low.at[stage, pl.ds(0, sizes[stage])]

    def stage_copy(stage):
        return push(
            low_part(stage), landing[stage], near_sems.at[0, stage], near_sems.at[1, stage], others[stage]
        )

    def start_of(stage):
        start = 0
        for former in range(stage):
            start = start + bits[former] * sizes[former]
        return start

    def begin(stage):
        at = start_of(stage) + (1 - bits[stage]) * sizes[stage]
        away = sums[pl.ds(pl.multiple_of(at, 128), sizes[stage]), :]
        low[stage, : sizes[stage]] = away.astype(jnp.bfloat16)
        stage_copy(stage).start()

    def finish(stage):
        stage_copy(stage).wait()
        at = pl.ds(pl.multiple_of(start_of(stage + 1), 128), sizes[stage])
        sums[at, :] = sums[at, :] + landing[stage][...].astype(jnp.float32)

    early = deliveries(ring_ref, early_ref, early_sems, mine, count, pl.ds(0, early_ref.shape[2]))

    def after_pair(pair):
        @pl.when(pair == 0)
        def _():
            for copy in early:
                copy.start()

        for stage in range(2):

            @pl.when(pair == stage)
            def _():
                finish(stage)
                begin(stage + 1)

    begin(0)
    for load in loads:
        load.wait()
    backward_body(
        mine, length_ref[1], scale, head_size, qkv_ref, bias_ref, grad_ref.at[0], full_ref, total_ref,
        ring_ref, line_ref, work, after_pair,
    )
    finish(2)
    at = pl.ds(pl.multiple_of(start_of(3), 128), sizes[2])
    groups = leaving.shape[2] // 128
    for j in range(count):
        owner = lax.rem(mine + (count - j), count)
        for group in range(groups):
            lanes = pl.ds(pl.multiple_of((group * count + owner) * 128, 128), 128)
            part = sums[at, lanes]
            leaving[j, :, group * 128 : (group + 1) * 128] = part.astype(jnp.bfloat16)
            if j == 0:
                rows_ref[:, group * 128 : (group + 1) * 128] = part
    last = deliveries(leaving, coming, last_sems, mine, count)
    for copy in last:
        copy.start()
    total = None
    for j in range(count):
        term = dot_tn(normed_ref[j], former_ref[j])
        total = term if total is None else total + term
    weight_ref[...] = total
    for copy in last:
        copy.wait()
    for j in range(1, count):
        rows_ref[...] = rows_ref[...] + coming[j].astype(jnp.float32)
    for copy in copies + early:
        copy.wait()


def second_back(
    lengths, former, normed_all, qkvs, bias, grads, full, total, attended, proj, scale, head_size, waits=()
):
    slots, count, span_rows, own_width = qkvs.shape
    model_width = normed_all.shape[3]
    whole = pl.BlockSpec(memory_space=pltpu.VMEM)
    some = pl.BlockSpec(memory_space=pl.ANY)
    f32, bf16 = jnp.float32, jnp.bfloat16
    rows_shape = (model_width // 8, own_width // 3)
    return pl.pallas_call(
        held(
            functools.partial(second_kernel, scale, head_size, slots), 8 + 2 * slots, len(waits)
        ),
        grid=(1,),
        in_specs=[
            pl.BlockSpec(memory_space=pltpu.SMEM),
            whole,
            some,
            some,
            some,
            whole,
            some,
            some,
        ]
        + [whole] * (2 * slots)
        + anywhere(waits),
        out_specs=[whole] * 6,
        out_shape=[
            jax.ShapeDtypeStruct(qkvs.shape[1:], bf16),
            jax.ShapeDtypeStruct((bias.shape[0], 1, bias.shape[2] + span_rows), f32),
            jax.ShapeDtypeStruct(qkvs.shape[1:], bf16),
            jax.ShapeDtypeStruct((count, span_rows, 384), bf16),
            jax.ShapeDtypeStruct((model_width, own_width), f32),
            jax.ShapeDtypeStruct(rows_shape, f32),
        ],
        scratch_shapes=[
            pltpu.VMEM((model_width, model_width), f32),
            pltpu.VMEM((3, model_width // 2, model_width), bf16),
            pltpu.VMEM((model_width // 2, model_width), bf16),
            pltpu.VMEM((model_width // 4, model_width), bf16),
            pltpu.VMEM((model_width // 8, model_width), bf16),
            pltpu.VMEM((count,) + rows_shape, bf16),
            pltpu.VMEM((count,) + rows_shape, bf16),
            pltpu.SemaphoreType.DMA((2, count)),
            pltpu.SemaphoreType.DMA((2, 3)),
            pltpu.SemaphoreType.DMA((2, count)),
            pltpu.SemaphoreType.DMA((2, count)),
            pltpu.VMEM(normed_all.shape[1:], bf16),
            pltpu.VMEM(qkvs.shape[1:], bf16),
            pltpu.VMEM(bias.shape, f32),
            pltpu.VMEM(full.shape[1:], f32),
            pltpu.VMEM(full.shape[1:], f32),
            pltpu.SemaphoreType.DMA((5,)),
        ]
        + backward_work(count, span_rows, head_size),
        cost_estimate=cost(20e9, 20e6),
        compiler_params=remote_params(2),
        name="second_back",
    )(lengths, former, normed_all, qkvs, bias, grads, full, total, *attended, *proj, *waits)


def token_body(mine, input_ref, hidden_ref, gain_ref, weight_ref, part_refs, own_ref, out_ref):
    count = part_refs[0].shape[0]
    model_width = input_ref.shape[1]
    total = None
    for j in range(count):
        owner = lax.rem(mine + j, count)
        pieces = []
        for group in range(own_ref.shape[2] // 384):
            for which in range(3):
                at = which * model_width + (group * count + owner) * 128
                pieces.append(weight_ref[:, pl.ds(pl.multiple_of(at, 128), 128)])
        part = own_ref[0] if j == 0 else jnp.concatenate([ref[j] for ref in part_refs], axis=1)
        term = dot_nt(part, jnp.concatenate(pieces, axis=1))
        total = term if total is None else total + term
    inputs = input_ref[...].astype(jnp.float32)
    back = norm_back(total, inputs, root_scale(inputs), gain_ref[...])
    out_ref[...] = (hidden_ref[...] + back).astype(jnp.bfloat16)


def final_kernel(
    slots, ring_ref, early_ref, normed_all, former_all, own_w_all, arrived_ref, blocks_ref, small_ref, gain_ref,
    weight_all, tokens_ref, *refs
):
    inputs = [slot_of(tokens_ref, s, slots) for s in range(slots)]
    hidden_all, refs = refs[:slots], refs[slots:]
    outs, refs = refs[:slots], refs[slots:]
    small_out, attn_out = refs[:2]
    coming, here, sum_blocks, low_blocks, small_now, small_in, sems, near_sems, small_sems = refs[2:11]
    got_core, got_x, got_y, normed_ref, former_ref, own_w_ref, weight_ref, hidden_refs, load_sems = refs[11:]
    hiddens = [hidden_refs.at[s] for s in range(slots)]
    loads = [
        pltpu.make_async_copy(source, target, load_sems.at[at])
        for at, (source, target) in enumerate(
            (
                (normed_all.at[1], normed_ref),
                (former_all, former_ref),
                (own_w_all, own_w_ref),
                (weight_all.at[:, pl.ds(0, weight_ref.shape[1])], weight_ref),
                *((hidden_all[s], hiddens[s]) for s in range(slots)),
            )
        )
    ]
    for load in loads:
        load.start()
    count = ring_ref.shape[0]
    mine = lax.axis_index("cp")
    dp, ep = lax.axis_index("dp"), lax.axis_index("ep")
    core, across = lax.rem(dp, 2), dp // 2
    core_other, x_other, y_other = near_others(dp, ep)
    greet(*ring_others(mine, count), core_other, x_other, y_other)
    late = ring_ref.shape[2] - early_ref.shape[2]
    copies = deliveries(ring_ref, coming, sems, mine, count, pl.ds(early_ref.shape[2], late))
    for copy in copies:
        copy.start()

    for load in loads[:3]:
        load.wait()
    total = former_ref[...]
    for j in range(count):
        total = total + dot_tn(normed_ref[j], ring_ref[j])
    ones = jnp.ones((8, total.shape[1]), jnp.float32)
    first_gain = lax.dot_general(
        ones,
        total * own_w_ref[...].astype(jnp.float32),
        (((1,), (1,)), ((), ())),
        precision=lax.Precision.HIGHEST,
        preferred_element_type=jnp.float32,
    )
    row = lax.broadcasted_iota(jnp.int32, small_ref.shape, 0)
    small_now[0] = jnp.where(row == 6, first_gain / gain_ref[...], small_ref[...])
    groups = total.shape[1] // 384
    for group in range(groups):
        for which in range(3):
            at = (group * 3 + which) * 128
            part = total[:, at : at + 128]
            sum_blocks[which % 2, which // 2, group] = part
            low_blocks[which % 2, which // 2, group] = part.astype(jnp.bfloat16)
        height = blocks_ref.shape[0]
        here_rows = pl.ds(pl.multiple_of((core * 4 + across * 2 + ep) * height, 128), height)
        part = blocks_ref[:, group * 128 : (group + 1) * 128]
        sum_blocks[1, 1, group] = jnp.zeros_like(sum_blocks[1, 1, group])
        low_blocks[1, 1, group] = jnp.zeros_like(low_blocks[1, 1, group])
        sum_blocks[1, 1, group, here_rows] = part
        low_blocks[1, 1, group, here_rows] = part.astype(jnp.bfloat16)
    first = push(low_blocks.at[1 - core], got_core, near_sems.at[0, 0], near_sems.at[1, 0], core_other)
    first.start()

    stages = [core_other, x_other, y_other]
    step = 1
    while step < count:
        flip = mine + step - 2 * step * lax.rem(mine // step, 2)
        stages.append({"cp": flip})
        step *= 2

    def small_push(at):
        return push(small_now.at[at], small_in.at[at], small_sems.at[0, at], small_sems.at[1, at], stages[at])

    small_push(0).start()
    for load in loads[3:]:
        load.wait()
    token_body(mine, inputs[0], hiddens[0], gain_ref, weight_ref, [arrived_ref], arrived_ref, outs[0])
    first.wait()
    here[...] = sum_blocks[core] + got_core[...].astype(jnp.float32)
    low_blocks[0, 0] = here[1 - across].astype(jnp.bfloat16)
    second = push(low_blocks.at[0, 0], got_x, near_sems.at[0, 1], near_sems.at[1, 1], x_other)
    second.start()
    for at in range(len(stages)):
        small_push(at).wait()
        now = small_now[at] + small_in[at]
        if at + 1 < len(stages):
            small_now[at + 1] = now
            small_push(at + 1).start()
        else:
            small_out[...] = now
        if at == 1:
            second.wait()
            sum_blocks[0, 0] = here[across] + got_x[...].astype(jnp.float32)
            low_blocks[0, 1, 0] = sum_blocks[0, 0, 1 - ep].astype(jnp.bfloat16)
            third = push(low_blocks.at[0, 1, 0], got_y, near_sems.at[0, 2], near_sems.at[1, 2], y_other)
            third.start()
    for copy in copies:
        copy.wait()
    token_body(mine, inputs[1], hiddens[1], gain_ref, weight_ref, [early_ref, coming], ring_ref, outs[1])
    third.wait()
    attn_out[...] = sum_blocks[0, 0, ep] + got_y[...].astype(jnp.float32)


def final_back(ring, early, normed_all, former, own_w, arrived, blocks, small, gain, w_attn, inputs, hiddens):
    count, span_rows, own_width = ring.shape
    slots = len(hiddens)
    model_width = hiddens[0].shape[1]
    groups = blocks.shape[1] // 128
    whole = pl.BlockSpec(memory_space=pltpu.VMEM)
    f32, bf16 = jnp.float32, jnp.bfloat16
    some = pl.BlockSpec(memory_space=pl.ANY)
    stages = 3 + (count - 1).bit_length()
    tile = (model_width, 128)
    return pl.pallas_call(
        functools.partial(final_kernel, slots),
        grid=(1,),
        in_specs=[
            whole,
            whole,
            some,
            some,
            some,
            whole,
            whole,
            whole,
            whole,
            some,
            whole,
        ]
        + [some] * slots,
        out_specs=[whole] * (slots + 2),
        out_shape=[jax.ShapeDtypeStruct((span_rows, model_width), bf16)] * slots
        + [jax.ShapeDtypeStruct(small.shape, f32), jax.ShapeDtypeStruct(tile, f32)],
        scratch_shapes=[
            pltpu.VMEM((count, span_rows, own_width - early.shape[2]), bf16),
            pltpu.VMEM((2, groups) + tile, f32),
            pltpu.VMEM((2, 2, groups) + tile, f32),
            pltpu.VMEM((2, 2, groups) + tile, bf16),
            pltpu.VMEM((stages,) + small.shape, f32),
            pltpu.VMEM((stages,) + small.shape, f32),
            pltpu.SemaphoreType.DMA((2, count)),
            pltpu.SemaphoreType.DMA((2, 3)),
            pltpu.SemaphoreType.DMA((2, stages)),
            pltpu.VMEM((2, groups) + tile, bf16),
            pltpu.VMEM((groups,) + tile, bf16),
            pltpu.VMEM(tile, bf16),
            pltpu.VMEM(normed_all.shape[1:], bf16),
            pltpu.VMEM(former.shape, f32),
            pltpu.VMEM(own_w.shape, bf16),
            pltpu.VMEM((model_width, 3 * model_width), bf16),
            pltpu.VMEM((slots, span_rows, model_width), f32),
            pltpu.SemaphoreType.DMA((4 + slots,)),
        ],
        cost_estimate=cost(20e9, 20e6),
        compiler_params=remote_params(3),
        name="final_back",
    )(ring, early, normed_all, former, own_w, arrived, blocks, small, gain, w_attn, inputs, *hiddens)


gelu_inner = 0.7978845608028654
gelu_cubic = 0.044715


def place_body(base, chosen_ref, pairs, outs):
    capacity = pairs[0][0].shape[0]
    span = outs[0].shape[0]
    both = [
        (mine[...].astype(jnp.float32) + theirs[...].astype(jnp.float32)).astype(jnp.bfloat16)
        for mine, theirs in pairs
    ]
    for at, out in enumerate(outs):
        total = None
        for expert in range(len(pairs)):
            ids = lax.broadcasted_iota(jnp.int32, (span, capacity), 1) + (base + expert * capacity)
            hot = jnp.zeros((span, capacity), jnp.float32)
            for choice in range(chosen_ref.shape[1]):
                chosen = chosen_ref[at * span : (at + 1) * span, choice : choice + 1]
                hot = hot + jnp.where(ids == chosen, 1.0, 0.0)
            term = dot_nn(hot.astype(jnp.bfloat16), both[expert])
            total = term if total is None else total + term
        out[...] = total.astype(jnp.bfloat16)


def return_kernel(experts, slots, target_ref, *refs):
    held_pairs = 2 * (1 + experts)
    back, far_outs, refs = refs[:held_pairs], refs[held_pairs : 2 * held_pairs], refs[2 * held_pairs :]
    backs, refs = refs[:slots], refs[slots:]
    out_own, out_rest, refs = refs[:slots], refs[slots : 4 * slots], refs[4 * slots :]
    here, got, far, last, low = refs[:5]
    outs, load_sems, sems = refs[5 : 5 + held_pairs], refs[5 + held_pairs], refs[6 + held_pairs]
    dp, ep = lax.axis_index("dp"), lax.axis_index("ep")
    _, x_other, y_other = near_others(dp, ep)
    base = ep * (experts * back[0].shape[2])
    loads = [
        pltpu.make_async_copy(source, target, load_sems.at[i])
        for i, (source, target) in enumerate(zip(far_outs, outs))
    ]
    for load in loads:
        load.start()

    def rows_of(held_refs, source):
        if source == 0:
            return [(held_refs[0].at[e, 0], held_refs[1].at[e, 0]) for e in range(experts)]
        return [
            (held_refs[2 + 2 * e].at[0, source - 1], held_refs[3 + 2 * e].at[0, source - 1])
            for e in range(experts)
        ]

    def place(held_refs, source, targets):
        place_body(base, target_ref.at[source], rows_of(held_refs, source), targets)

    firsts = [
        push(here.at[1, 0], got.at[0], sems.at[0, 0], sems.at[1, 0], x_other),
        push(here.at[2, 1], got.at[1], sems.at[0, 1], sems.at[1, 1], y_other),
        push(here.at[3, 0], far.at[0], sems.at[0, 2], sems.at[1, 2], x_other),
        push(here.at[3, 1], far.at[1], sems.at[0, 3], sems.at[1, 3], y_other),
    ]
    ends = [
        push(low.at[0], last.at[0], sems.at[0, 4], sems.at[1, 4], y_other),
        push(low.at[1], last.at[1], sems.at[0, 5], sems.at[1, 5], x_other),
    ]
    greet(x_other, y_other)
    halves = lambda source: [here.at[source, s] for s in range(slots)]
    place(back, 3, halves(3))
    firsts[2].start()
    firsts[3].start()
    place(back, 1, halves(1))
    firsts[0].start()
    place(back, 2, halves(2))
    firsts[1].start()
    place(back, 0, halves(0))
    for load in loads:
        load.wait()
    for at, (former, source) in enumerate(((2, 2), (3, 1))):
        firsts[former].wait()
        low[at] = (here[source, at].astype(jnp.float32) + far[at].astype(jnp.float32)).astype(jnp.bfloat16)
        ends[at].start()
    place(outs, 0, out_own)
    for source in range(1, 4):
        place(outs, source, out_rest[(source - 1) * slots : source * slots])
    for s in range(slots):
        firsts[s].wait()
        backs[s][...] = here[0, s].astype(jnp.float32) + got[s].astype(jnp.float32)
    for s in range(slots):
        ends[s].wait()
        backs[s][...] = backs[s][...] + last[s].astype(jnp.float32)


def return_rows(targets, backs, outs, slots, waits=()):
    experts = len(backs) // 2 - 1
    model_width = outs[0].shape[-1]
    span_rows = targets.shape[1] // slots
    wide = backs[0].shape[-1]
    whole = pl.BlockSpec(memory_space=pltpu.VMEM)
    f32, bf16 = jnp.float32, jnp.bfloat16
    half = pltpu.VMEM((slots, span_rows, wide), bf16)
    got = pl.pallas_call(
        held(
            functools.partial(return_kernel, experts, slots),
            1 + len(backs) + len(outs),
            len(waits),
        ),
        in_specs=[whole] + [whole] * len(backs) + anywhere(outs) + anywhere(waits),
        out_specs=[whole] * (5 * slots),
        out_shape=[
            *[jax.ShapeDtypeStruct((span_rows, wide), f32)] * slots,
            *[jax.ShapeDtypeStruct((span_rows, model_width), bf16)] * (4 * slots),
        ],
        scratch_shapes=[pltpu.VMEM((4, slots, span_rows, wide), bf16), half, half, half, half]
        + [pltpu.VMEM(a.shape, bf16) for a in outs]
        + [pltpu.SemaphoreType.DMA((len(outs),)), pltpu.SemaphoreType.DMA((2, 6))],
        cost_estimate=cost(20e9, 20e6),
        compiler_params=remote_params(4),
        name="return_rows",
    )(targets, *backs, *outs, *waits)
    return got[:slots], got[slots : 2 * slots], got[2 * slots :]


def expert_body(experts, own_units, expert, skip, given, refs, weights, router_ref):
    back_mine, back_theirs, out_mine, out_theirs, kept_rows, kept_units = refs
    gate_ref, up_ref, down_ref = weights
    capacity, model_width = given[0].shape[2:]
    rows = jnp.concatenate([given[0][0, 0], given[1][0, 0]], axis=0)
    grads = jnp.concatenate([given[2][0, 0], given[3][0, 0]], axis=0)
    kept_rows[0, 0, 0] = rows
    kept_rows[1, 0, 0] = grads
    lane = lax.broadcasted_iota(jnp.int32, (1, router_ref.shape[1]), 1)
    probs = router_of(rows, router_ref[...], experts)
    gates = jnp.sum(jnp.where(lane == expert, probs, 0.0), axis=1, keepdims=True)
    unit = lax.broadcasted_iota(jnp.int32, (1, gate_ref.shape[2]), 1) - skip
    own = jnp.logical_and(unit >= 0, unit < own_units)
    gate_w, up_w, down_w = gate_ref[0], up_ref[0], down_ref[0]
    gate_pre = dot_nn(rows, gate_w)
    up_pre = jnp.where(own, dot_nn(rows, up_w), 0.0)
    square = gate_pre * gate_pre
    tanh = jnp.tanh(gelu_inner * gate_pre * (1.0 + gelu_cubic * square))
    half = 0.5 + 0.5 * tanh
    active = gate_pre * half
    slope = half + active * (1.0 - tanh) * (gelu_inner * (1.0 + 3.0 * gelu_cubic * square))
    inner = active * up_pre
    low_inner = inner.astype(jnp.bfloat16)
    plain_grads = jnp.where(own, dot_nn(grads, down_w), 0.0)
    gate_grads = jnp.sum(plain_grads * low_inner.astype(jnp.float32), axis=1, keepdims=True)
    inner_grads = plain_grads * gates
    low_gate = (inner_grads * up_pre * slope).astype(jnp.bfloat16)
    low_up = (inner_grads * active).astype(jnp.bfloat16)
    kept_units[0, 0, 0] = low_gate
    kept_units[1, 0, 0] = low_up
    kept_units[2, 0, 0] = (inner * gates).astype(jnp.bfloat16)
    back = (dot_nt(low_gate, gate_w) + dot_nt(low_up, up_w)).astype(jnp.bfloat16)
    shares = jnp.where(lane == expert, gate_grads, 0.0).astype(jnp.bfloat16)
    out = (gates * dot_nt(low_inner, down_w)).astype(jnp.bfloat16)
    for at, back_ref, out_ref in ((0, back_mine, out_mine), (1, back_theirs, out_theirs)):
        part = slice(at * capacity, (at + 1) * capacity)
        back_ref[0, 0, :, :model_width] = back[part]
        back_ref[0, 0, :, model_width:] = shares[part]
        out_ref[0, 0] = out[part]


def expert_kernel(experts, own_units, kept_count, first_ref, window_ref, *refs):
    given, refs = refs[:4], refs[4:]
    router_ref, weights, refs = refs[0], refs[1:4], refs[4 + kept_count :]
    expert = first_ref[0] + pl.program_id(0)
    expert_body(experts, own_units, expert, window_ref[1], given, refs, weights, router_ref)


def own_kernel(experts, own_units, *refs):
    given, router_ref, weights, refs = refs[:4], refs[4], refs[5:8], refs[8:]
    target_ref, over_ref, up_ref, normed_ref, refs = refs[0], refs[1], refs[2], refs[3], refs[4:]
    results, kept, (mine_ref, theirs_ref), refs = refs[:4], refs[4:6], refs[6:8], refs[8:]
    coming, picked, held_w, held_rows, held_units = refs[:5]
    sems, core_sems, home_sems, load_sems, keep_sems = refs[5:]
    exp_dev, capacity = picked.shape[1:3]
    dp, ep = lax.axis_index("dp"), lax.axis_index("ep")
    core_other, x_other, y_other = near_others(dp, ep)
    skip = lax.rem(dp * own_units, 128)

    def copy(at):
        source, other = (
            (normed_ref, x_other),
            (normed_ref, y_other),
            (over_ref, y_other),
            (coming.at[1], x_other),
        )[at]
        return push(source, coming.at[at], sems.at[0, at], sems.at[1, at], other)

    def load(expert, which):
        lanes = pl.ds(pl.multiple_of(dp * own_units - skip, 128), held_w.shape[4])
        return pltpu.make_async_copy(
            weights[which].at[pl.ds(expert, 1), :, lanes],
            held_w.at[expert, which],
            load_sems.at[expert, which],
        )

    def keep(expert, kind):
        held_ref = (held_rows, held_units)[kind]
        return pltpu.make_async_copy(
            held_ref.at[expert, :, 0, 0], kept[kind].at[:, expert, 0], keep_sems.at[expert, kind]
        )

    for expert in range(exp_dev):
        for which in range(3):
            load(expert, which).start()
    greet(core_other, x_other, y_other)
    for at in range(3):
        copy(at).start()
    for expert in range(exp_dev):
        if expert == 1:
            copy(1).wait_recv()
            copy(3).start()
        for which in range(3):
            load(expert, which).wait()
        here = pl.ds(expert, 1)
        expert_body(
            experts,
            own_units,
            ep * exp_dev + expert,
            skip,
            [part.at[:, here] for part in given],
            [part.at[here] for part in results] + [held_rows.at[expert], held_units.at[expert]],
            [held_w.at[expert, which] for which in range(3)],
            router_ref,
        )
        for kind in range(2):
            keep(expert, kind).start()

    base = ep * (exp_dev * capacity)
    blocks = (
        (over_ref, coming.at[0]),
        (up_ref, coming.at[1]),
        (coming.at[2], coming.at[3]),
    )

    def across_cores(k):
        return push(picked.at[k], theirs_ref.at[k], core_sems.at[0, k], core_sems.at[1, k], core_other)

    def home(k):
        return pltpu.make_async_copy(picked.at[k], mine_ref.at[k], home_sems.at[k])

    for k, waits in enumerate(((0,), (), (2, 3))):
        for at in waits:
            copy(at).wait_recv()
        chosen = [target_ref.at[k + 1, s] for s in range(target_ref.shape[1])]
        pick_body(base, capacity, exp_dev, chosen, blocks[k], picked.at[k])
        across_cores(k).start()
        home(k).start()
    for at in range(4):
        copy(at).wait_send()
    for k in range(3):
        across_cores(k).wait()
        home(k).wait()
    for expert in range(exp_dev):
        for kind in range(2):
            keep(expert, kind).wait()


def own_experts(given, router, weights, target, over, up, normed, total, experts, units):
    _, exp_dev, capacity, model_width = given[0].shape
    span_rows = normed.shape[0]
    wide_units = aligned_units(units)
    tile = 2 * capacity
    bf16 = jnp.bfloat16
    shape = jax.ShapeDtypeStruct
    picked = (3, exp_dev, capacity, model_width)
    wide = model_width + 128
    keeps = ((2, model_width), (3, wide_units))
    whole = pl.BlockSpec(memory_space=pltpu.VMEM)
    some = pl.BlockSpec(memory_space=pl.ANY)
    got = pl.pallas_call(
        functools.partial(own_kernel, experts, units),
        grid=(1,),
        in_specs=[whole] * 5 + [some] * 3 + [whole] * 4,
        out_specs=[whole] * 4 + [some] * 4,
        out_shape=[shape((exp_dev, 1, capacity, wide), bf16)] * 2
        + [shape((exp_dev, 1, capacity, model_width), bf16)] * 2
        + [shape((kinds, exp_dev, total, tile, width), bf16) for kinds, width in keeps]
        + [shape(picked, bf16)] * 2,
        scratch_shapes=[
            pltpu.VMEM((4, span_rows, model_width), bf16),
            pltpu.VMEM(picked, bf16),
            pltpu.VMEM((exp_dev, 3, 1, model_width, wide_units), bf16),
        ]
        + [pltpu.VMEM((exp_dev, kinds, 1, 1, tile, width), bf16) for kinds, width in keeps]
        + [
            pltpu.SemaphoreType.DMA((2, 4)),
            pltpu.SemaphoreType.DMA((2, 3)),
            pltpu.SemaphoreType.DMA((3,)),
            pltpu.SemaphoreType.DMA((exp_dev, 3)),
            pltpu.SemaphoreType.DMA((exp_dev, 2)),
        ],
        cost_estimate=cost(20e9, 16e6),
        compiler_params=remote_params(5),
        name="own_experts",
    )(*given, router, *weights, target, over, up, normed)
    return got[:4], got[4:6], got[6:]


def run_experts(first, window, given, router, weights, kept, at, total, experts, units, chosen):
    low, high = chosen
    sources, exp_dev, capacity, model_width = given[0].shape
    wide_units = aligned_units(units)
    tile = 2 * capacity

    given_rows = pl.BlockSpec(
        (1, 1, capacity, model_width), lambda e, k, f, w: (k, low + e, 0, 0)
    )
    out = lambda width: pl.BlockSpec((1, 1, capacity, width), lambda e, k, f, w: (e, k, 0, 0))
    wide, rows = out(model_width + 128), out(model_width)
    weight = pl.BlockSpec(
        (pl.Element(1), pl.Element(model_width), pl.Element(wide_units)),
        lambda e, k, f, w: (low + e, 0, pl.multiple_of(w[0], 128)),
    )
    keep = lambda kinds, width: pl.BlockSpec(
        (kinds, 1, 1, tile, width), lambda e, k, f, w: (0, low + e, at + k, 0, 0)
    )
    keeps = ((2, model_width), (3, wide_units))
    kept = list(kept)
    out_of = lambda width: jax.ShapeDtypeStruct(
        (high - low, sources, capacity, width), jnp.bfloat16
    )
    back_shape, out_shape = out_of(model_width + 128), out_of(model_width)
    got = pl.pallas_call(
        functools.partial(expert_kernel, experts, units, len(kept)),
        grid_spec=pltpu.PrefetchScalarGridSpec(
            num_scalar_prefetch=2,
            grid=(high - low, sources),
            in_specs=[given_rows] * 4
            + [
                pl.BlockSpec(router.shape, lambda e, k, f, w: (0, 0)),
                weight,
                weight,
                weight,
            ]
            + anywhere(kept),
            out_specs=[wide, wide, rows, rows] + [keep(*kinds) for kinds in keeps],
        ),
        out_shape=[back_shape, back_shape, out_shape, out_shape]
        + [
            jax.ShapeDtypeStruct((kinds, exp_dev, total, tile, width), jnp.bfloat16)
            for kinds, width in keeps
        ],
        input_output_aliases={10 + i: 4 + i for i in range(len(kept))},
        cost_estimate=cost(20e9 * sources, 8e6 * sources),
        compiler_params=compiler_params(),
        name="expert_rows",
    )(first + low, window, *given, router, *weights, *kept)
    return got[:4], got[4:]


def aligned_units(units):
    return (units + 127) // 128 * 128


def weight_kernel(window_ref, rows_ref, units_ref, weight_ref, total):
    pieces, _, piece, model_width = weight_ref.shape
    units = units_ref[0, 0].reshape(-1, units_ref.shape[-1])
    total[...] = dot_tn(units, rows_ref[0, 0].reshape(-1, model_width))
    skip = pl.multiple_of(window_ref[1], 64)
    for at in range(pieces):
        weight_ref[at, 0] = total[pl.ds(skip + at * piece, piece), :].astype(jnp.bfloat16)


def weight_grads(window, kept, expert, pieces, units, waits=()):
    kept_rows, kept_units = kept
    tiles, tile, model_width = kept_rows.shape[2:]
    wide_units = kept_units.shape[4]
    shape = (pieces, 3, units // pieces, model_width)
    return pl.pallas_call(
        held(weight_kernel, 3, len(waits)),
        grid=(3,),
        in_specs=[
            pl.BlockSpec(memory_space=pltpu.SMEM),
            pl.BlockSpec((1, 1, tiles, tile, model_width), lambda i: (i // 2, expert, 0, 0, 0)),
            pl.BlockSpec((1, 1, tiles, tile, wide_units), lambda i: (i, expert, 0, 0, 0)),
        ]
        + anywhere(waits),
        out_specs=pl.BlockSpec((pieces, 1) + shape[2:], lambda i: (0, i, 0, 0)),
        out_shape=jax.ShapeDtypeStruct(shape, jnp.bfloat16),
        scratch_shapes=[pltpu.VMEM((wide_units, model_width), jnp.float32)],
        cost_estimate=cost(20e9, 20e6),
        compiler_params=compiler_params(),
        name="weight_grads",
    )(window, kept_rows, kept_units, *waits)


def send(values, axis, pairs):
    return lax.ppermute(values, axis, pairs)


def after(values, *earlier):
    return lax.optimization_barrier((values, earlier))[0]


def fast_device(
    tokens,
    lengths,
    expert_ids,
    places,
    buckets,
    w_attn,
    bias_table,
    norm1_gain,
    norm2_gain,
    w_router,
    w_gate,
    w_up,
    w_down,
    cotangent,
):
    span_rows, slots, model_width = tokens.shape
    head_count, bucket_count = bias_table.shape
    head_size = model_width // head_count
    scale = head_size ** (-0.5)
    n_dp = lax.axis_size("dp")
    n_ep = lax.axis_size("ep")
    n_cp = lax.axis_size("cp")
    my_dp, my_ep, my_cp = (lax.axis_index(name) for name in ("dp", "ep", "cp"))
    seq_len = span_rows * n_cp
    rows = span_rows * slots
    top_count = expert_ids.shape[2]
    experts = w_router.shape[1]
    exp_dev = w_gate.shape[0]
    units = w_gate.shape[2] // n_dp
    capacity = (5 * rows * top_count + 4 * experts - 1) // (4 * experts)
    groups = model_width // (128 * n_cp)
    own_width = 3 * groups * 128
    heads_own = head_count // n_cp
    over_core = [(i, i ^ 1) for i in range(n_dp)]
    over_x = [(i, i ^ 2) for i in range(n_dp)]
    over_y = [(i, i ^ 1) for i in range(n_ep)]
    ring = [(i, (i + 1) % n_cp) for i in range(n_cp)]
    f32, bf16 = jnp.float32, jnp.bfloat16
    exact = lax.Precision.HIGHEST
    each = range(slots)

    low_in = tokens.reshape(span_rows, slots * model_width)
    low_out = cotangent.reshape(span_rows, slots * model_width)
    gain_first, gain_second = norm1_gain[None, :], norm2_gain[None, :]

    per_group = 128 // head_size
    own_heads = (
        jnp.arange(groups)[:, None] * (n_cp * per_group)
        + my_cp * per_group
        + jnp.arange(per_group)[None, :]
    ).reshape(heads_own)
    head_hot = (own_heads[:, None] == jnp.arange(head_count)[None, :]).astype(f32)
    own_table = jnp.dot(head_hot, bias_table, precision=exact)
    far_hot = (buckets[::-1][:, None] == jnp.arange(bucket_count)[None, :]).astype(f32)
    lines = jnp.einsum("hb,db->hd", own_table, far_hot, precision=exact)
    lines = jnp.concatenate([lines, jnp.full((heads_own, span_rows), minus_big, f32)], axis=1)
    target = jnp.where(places >= 0, expert_ids * capacity + places, -1)
    target = target.transpose(1, 2, 0).astype(jnp.int32)
    (
        (normed_all, qkvs, bias, full, total, w_own, target_all, over_first, up_first),
        (grads_own, grads_rest_rows, picked_own),
        fronts,
    ) = front(
        lengths,
        gain_first,
        gain_second,
        lines[:, None, :],
        target,
        w_attn,
        low_in,
        low_out,
        slots,
        n_cp,
        exp_dev,
        capacity,
        scale,
        head_size,
    )
    attended, hidden, normed_second = zip(*fronts)

    sources = target_all.shape[0]
    target_rows = target_all.transpose(0, 2, 1, 3).reshape(sources, top_count, rows)
    target_columns = target_rows.transpose(0, 2, 1)
    window_at = my_dp * units // 128 * 128
    window = jnp.stack([window_at, my_dp * units - window_at]).astype(jnp.int32)
    router_wide = jnp.concatenate(
        [w_router, jnp.zeros((model_width, 128 - experts), w_router.dtype)], axis=1
    )

    first = (my_ep * exp_dev).astype(jnp.int32).reshape(1)
    own, kept, picked_rest = own_experts(
        (*picked_own, *grads_own),
        router_wide,
        (w_gate, w_up, w_down),
        target_all,
        over_first,
        up_first,
        normed_second[1],
        sources,
        experts,
        units,
    )

    def with_theirs(mine, theirs):
        return [mine, send(theirs, "dp", over_core)]

    backs, outs = with_theirs(own[0], own[1]), with_theirs(own[2], own[3])
    weight_sums = []
    for e in range(exp_dev):
        rest, kept = run_experts(
            first,
            window,
            (*picked_rest, *grads_rest_rows),
            router_wide,
            (w_gate, w_up, w_down),
            kept,
            1,
            sources,
            experts,
            units,
            (e, e + 1),
        )
        weight_part = weight_grads(window, kept, e, n_cp, units, backs[-1:] + outs[-1:])
        backs += with_theirs(rest[0], rest[1])
        outs += with_theirs(rest[2], rest[3])
        weight_sums.append(lax.psum_scatter(weight_part, "cp", scatter_dimension=0, tiled=False))
        kept = after(kept, weight_part)
    back_rows, out_own, out_rest = return_rows(target_columns, backs, outs, slots, [weight_part])
    got, mixed, (ringed, line_first, grads_rest) = hidden_back(
        lengths,
        back_rows,
        low_out,
        hidden,
        normed_second,
        gain_second,
        router_wide,
        w_attn,
        experts,
        qkvs,
        bias,
        full,
        total,
        out_own,
        out_rest,
        scale,
        head_size,
    )
    hidden_grads, proj_grads, router_parts, gain_parts = zip(*got)
    router_grad = sum(router_parts)[:, :experts].T
    ring_second, line_second, arrived, early, weight_first, out_grad = second_back(
        lengths,
        ringed,
        normed_all,
        qkvs,
        bias,
        grads_rest,
        full,
        total,
        attended,
        proj_grads,
        scale,
        head_size,
        weight_sums[:1],
    )
    distance_grads = (line_first + line_second)[:, 0, :seq_len]
    table_grad = jnp.dot(distance_grads, far_hot, precision=exact)
    table_grad = jnp.einsum("hg,hb->gb", head_hot, table_grad, precision=exact)
    table_row = jnp.pad(table_grad.reshape(1, -1), ((0, 0), (0, model_width - table_grad.size)))
    small = jnp.concatenate(
        [router_grad, sum(gain_parts), table_row, jnp.zeros((2, model_width), f32)], axis=0
    )
    *tokens_grad, small_sum, attn_sum = final_back(
        ring_second,
        early,
        normed_all,
        weight_first,
        w_own,
        arrived,
        out_grad,
        small,
        gain_first,
        w_attn,
        low_in,
        hidden_grads,
    )
    router_sum, gain_second_sum = small_sum[:experts], small_sum[experts]
    table_sum = small_sum[experts + 1, : table_grad.size].reshape(table_grad.shape)
    gain_first_sum = small_sum[experts + 2]

    gate_sum, up_sum, down_sum = (
        jnp.stack([part[which].T.astype(f32) for part in weight_sums]) for which in range(3)
    )
    return (
        jnp.stack(mixed, axis=1),
        jnp.stack(tokens_grad, axis=1),
        attn_sum,
        table_sum,
        gain_first_sum,
        gain_second_sum,
        router_sum.T,
        gate_sum,
        up_sum,
        down_sum,
    )


def solution(mesh):
    placed = (
        P("cp", ("dp", "ep"), None),
        P(("dp", "ep")),
        P("cp", ("dp", "ep"), None),
        P("cp", ("dp", "ep"), None),
        P(),
        P(),
        P(),
        P(),
        P(),
        P(),
        P("ep", None, None),
        P("ep", None, None),
        P("ep", None, None),
        P("cp", ("dp", "ep"), None),
    )
    sizes = dict(mesh.shape)
    square = sizes["dp"] == 4 and sizes["ep"] == 2 and sizes["cp"] == 4
    return jax.shard_map(
        fast_device if square else on_device,
        mesh=mesh,
        in_specs=placed,
        out_specs=(
            P("cp", ("dp", "ep"), None),
            P("cp", ("dp", "ep"), None),
            P(None, ("dp", "ep", "cp")),
            P(),
            P(),
            P(),
            P(),
            P("ep", None, ("dp", "cp")),
            P("ep", None, ("dp", "cp")),
            P("ep", None, ("dp", "cp")),
        ),
        check_vma=False,
    )
```

```python
import functools

import jax
import jax.numpy as jnp
from jax import lax
from jax.experimental import pallas as pl
from jax.experimental.pallas import tpu as pltpu
from jax.sharding import PartitionSpec as P

epsilon = 1e-06
masked_value = -1000000000.0


def gelu_tanh(values):
    return jax.nn.gelu(values, approximate=True)


def root_scale(values):
    return lax.rsqrt(jnp.mean(values * values, axis=-1, keepdims=True) + epsilon)


def norm_back(grad_in, values, scale_rows, gain_vector):
    scaled = grad_in * gain_vector
    inner_mean = jnp.mean(scaled * values, axis=-1, keepdims=True)
    return scale_rows * (scaled - values * scale_rows * scale_rows * inner_mean)


def block_logits(
    queries, key_rows, key_start, query_pos, lengths, table_step, rise_points, head_scale
):
    key_count = key_rows.shape[0]
    key_pos = key_start + jnp.arange(key_count, dtype=jnp.int32)
    scores = (
        jnp.einsum("qshd,kshd->shqk", queries, key_rows, preferred_element_type=jnp.float32)
        * head_scale
    )
    distance = query_pos[:, None] - key_pos[None, :]
    steps = (distance[:, :, None] >= rise_points[None, None, :]).astype(jnp.float32)
    pair_bias = jnp.einsum("hb,qkb->hqk", table_step, steps, precision=lax.Precision.HIGHEST)
    allowed = (distance >= 0)[None, :, :] & (key_pos[None, None, :] < lengths[:, None, None])
    logits = jnp.where(allowed[:, None], scores + pair_bias[None], masked_value)
    return (logits, steps)


def on_device(
    tokens,
    lengths,
    expert_ids,
    places,
    buckets,
    w_attn,
    bias_table,
    norm1_gain,
    norm2_gain,
    w_router,
    w_gate,
    w_up,
    w_down,
    cotangent,
):
    span_rows, pair_count, model_width = tokens.shape
    head_count, bucket_count = bias_table.shape
    head_size = model_width // head_count
    head_scale = head_size ** (-0.5)
    n_cp = lax.axis_size("cp")
    n_ep = lax.axis_size("ep")
    seq_len = span_rows * n_cp
    row_count = span_rows * pair_count
    top_count = expert_ids.shape[2]
    experts = w_router.shape[1]
    exp_dev = w_gate.shape[0]
    capacity = (5 * row_count * top_count + 4 * experts - 1) // (4 * experts)
    my_start = lax.axis_index("cp") * span_rows
    query_pos = my_start + jnp.arange(span_rows, dtype=jnp.int32)
    live_mask = (query_pos[:, None] < lengths[None, :]).astype(jnp.float32)
    inputs = tokens.astype(jnp.float32)
    scale_first = root_scale(inputs)
    normed_first = (inputs * scale_first * norm1_gain).astype(jnp.bfloat16)
    w_qkv = w_attn[:, : 3 * model_width]
    w_out = w_attn[:, 3 * model_width :]
    qkv = jnp.einsum("csd,de->cse", normed_first, w_qkv, preferred_element_type=jnp.float32).astype(
        jnp.bfloat16
    )
    queries = qkv[..., :model_width].reshape(span_rows, pair_count, head_count, head_size)
    keyval = qkv[..., model_width:]
    keyval_all = lax.all_gather(keyval, "cp", axis=0, tiled=True)
    bucket_ids = jnp.arange(bucket_count, dtype=jnp.int32)
    rise_points = jnp.sum((buckets[:, None] < bucket_ids[None, :]).astype(jnp.int32), axis=0)
    table_step = jnp.concatenate(
        [bias_table[:, :1], bias_table[:, 1:] - bias_table[:, :-1]], axis=1
    )
    block_starts = jnp.arange(n_cp, dtype=jnp.int32) * span_rows

    def split_kv(kv_block):
        key_rows = kv_block[..., :model_width].reshape(span_rows, pair_count, head_count, head_size)
        value_rows = kv_block[..., model_width:].reshape(
            span_rows, pair_count, head_count, head_size
        )
        return (key_rows, value_rows)

    kv_blocks = keyval_all.reshape(n_cp, span_rows, pair_count, 2 * model_width)

    def max_step(state_pair, block_item):
        row_peak, row_total = state_pair
        kv_block, block_start = block_item
        key_rows, value_rows = split_kv(kv_block)
        logits, steps = block_logits(
            queries, key_rows, block_start, query_pos, lengths, table_step, rise_points, head_scale
        )
        new_peak = jnp.maximum(row_peak, jnp.max(logits, axis=-1))
        row_total = row_total * jnp.exp(row_peak - new_peak) + jnp.sum(
            jnp.exp(logits - new_peak[..., None]), axis=-1
        )
        return ((new_peak, row_total), None)

    stat_shape = (pair_count, head_count, span_rows)
    (row_peak, row_total), unused = lax.scan(
        max_step,
        (jnp.full(stat_shape, masked_value, jnp.float32), jnp.zeros(stat_shape, jnp.float32)),
        (kv_blocks, block_starts),
    )
    log_total = row_peak + jnp.log(row_total)

    def value_step(running, block_item):
        kv_block, block_start = block_item
        key_rows, value_rows = split_kv(kv_block)
        logits, steps = block_logits(
            queries, key_rows, block_start, query_pos, lengths, table_step, rise_points, head_scale
        )
        weights = jnp.exp(logits - log_total[..., None]).astype(jnp.bfloat16)
        return (
            running
            + jnp.einsum(
                "shqk,kshd->qshd", weights, value_rows, preferred_element_type=jnp.float32
            ),
            None,
        )

    attended, unused = lax.scan(
        value_step,
        jnp.zeros((span_rows, pair_count, head_count, head_size), jnp.float32),
        (kv_blocks, block_starts),
    )
    attended = attended.reshape(span_rows, pair_count, model_width)
    attended_low = attended.astype(jnp.bfloat16)
    projected = jnp.einsum("csd,de->cse", attended_low, w_out, preferred_element_type=jnp.float32)
    hidden = inputs + live_mask[..., None] * projected
    scale_second = root_scale(hidden)
    normed_second = (hidden * scale_second * norm2_gain).astype(jnp.bfloat16)
    router_logits = jnp.einsum(
        "csd,de->cse", normed_second, w_router, preferred_element_type=jnp.float32
    )
    router_probs = jax.nn.softmax(router_logits, axis=-1)
    expert_hot = (expert_ids[..., None] == jnp.arange(experts, dtype=jnp.int32)).astype(jnp.float32)
    kept_mask = (places >= 0).astype(jnp.float32)
    gate_values = jnp.sum(expert_hot * router_probs[:, :, None, :], axis=-1) * kept_mask
    target = jnp.where(places >= 0, expert_ids * capacity + places, -1).reshape(
        row_count, top_count
    )
    slot_ids = jnp.arange(experts * capacity, dtype=jnp.int32)
    route_hot = (target[None, :, :] == slot_ids[:, None, None]).astype(jnp.bfloat16)
    dispatch = jnp.sum(route_hot, axis=2)
    sent_rows = jnp.dot(
        dispatch, normed_second.reshape(row_count, model_width), preferred_element_type=jnp.float32
    )
    sent_rows = sent_rows.astype(jnp.bfloat16).reshape(n_ep, exp_dev, capacity, model_width)
    arrived = lax.all_to_all(sent_rows, "ep", split_axis=0, concat_axis=0, tiled=True)
    gate_pre = jnp.einsum("secd,edf->secf", arrived, w_gate, preferred_element_type=jnp.float32)
    up_pre = jnp.einsum("secd,edf->secf", arrived, w_up, preferred_element_type=jnp.float32)
    active, gelu_pullback = jax.vjp(gelu_tanh, gate_pre)
    inner_act = (active * up_pre).astype(jnp.bfloat16)
    produced = jnp.einsum(
        "secf,edf->secd", inner_act, w_down, preferred_element_type=jnp.float32
    ).astype(jnp.bfloat16)
    returned = lax.all_to_all(produced, "ep", split_axis=0, concat_axis=0, tiled=True).reshape(
        experts * capacity, model_width
    )
    picked = jnp.einsum("jrk,jd->rkd", route_hot, returned, preferred_element_type=jnp.float32)
    gate_flat = gate_values.reshape(row_count, top_count)
    mixed = hidden.reshape(row_count, model_width) + jnp.sum(gate_flat[..., None] * picked, axis=1)
    mixed = mixed.reshape(span_rows, pair_count, model_width).astype(jnp.bfloat16)
    grad_out = cotangent.astype(jnp.float32).reshape(row_count, model_width)
    gate_grads = jnp.sum(grad_out[:, None, :] * picked, axis=-1)
    sent_back = (gate_flat[..., None] * grad_out[:, None, :]).astype(jnp.bfloat16)
    scattered = jnp.einsum("jrk,rkd->jd", route_hot, sent_back, preferred_element_type=jnp.float32)
    scattered = scattered.astype(jnp.bfloat16).reshape(n_ep, exp_dev, capacity, model_width)
    grad_produced = lax.all_to_all(scattered, "ep", split_axis=0, concat_axis=0, tiled=True)
    down_grad = jnp.einsum(
        "secd,secf->edf", grad_produced, inner_act, preferred_element_type=jnp.float32
    )
    grad_inner = jnp.einsum(
        "secd,edf->secf", grad_produced, w_down, preferred_element_type=jnp.float32
    )
    grad_gate_pre = gelu_pullback(grad_inner * up_pre)[0].astype(jnp.bfloat16)
    grad_up_pre = (grad_inner * active).astype(jnp.bfloat16)
    gate_grad = jnp.einsum(
        "secd,secf->edf", arrived, grad_gate_pre, preferred_element_type=jnp.float32
    )
    up_grad = jnp.einsum("secd,secf->edf", arrived, grad_up_pre, preferred_element_type=jnp.float32)
    grad_arrived = jnp.einsum(
        "secf,edf->secd", grad_gate_pre, w_gate, preferred_element_type=jnp.float32
    )
    grad_arrived = (
        grad_arrived
        + jnp.einsum("secf,edf->secd", grad_up_pre, w_up, preferred_element_type=jnp.float32)
    ).astype(jnp.bfloat16)
    grad_sent = lax.all_to_all(grad_arrived, "ep", split_axis=0, concat_axis=0, tiled=True).reshape(
        experts * capacity, model_width
    )
    grad_rows = jnp.einsum("jr,jd->rd", dispatch, grad_sent, preferred_element_type=jnp.float32)
    choice_grads = gate_grads.reshape(span_rows, pair_count, top_count) * kept_mask
    prob_grads = jnp.sum(expert_hot * choice_grads[..., None], axis=2)
    logit_grads = router_probs * (
        prob_grads - jnp.sum(router_probs * prob_grads, axis=-1, keepdims=True)
    )
    logit_grads = logit_grads.astype(jnp.bfloat16)
    router_grad = jnp.einsum(
        "csd,cse->de", normed_second, logit_grads, preferred_element_type=jnp.float32
    )
    grad_normed_second = grad_rows.reshape(span_rows, pair_count, model_width)
    grad_normed_second = grad_normed_second + jnp.einsum(
        "cse,de->csd", logit_grads, w_router, preferred_element_type=jnp.float32
    )
    gain_second_grad = jnp.sum(grad_normed_second * hidden * scale_second, axis=(0, 1))
    grad_hidden = grad_out.reshape(span_rows, pair_count, model_width) + norm_back(
        grad_normed_second, hidden, scale_second, norm2_gain
    )
    grad_proj = (live_mask[..., None] * grad_hidden).astype(jnp.bfloat16)
    out_grad = jnp.einsum(
        "csd,cse->de", attended_low, grad_proj, preferred_element_type=jnp.float32
    )
    grad_att = jnp.einsum(
        "cse,de->csd", grad_proj, w_out, preferred_element_type=jnp.float32
    ).astype(jnp.bfloat16)
    grad_att_heads = grad_att.reshape(span_rows, pair_count, head_count, head_size)
    row_terms = jnp.sum(
        grad_att_heads.astype(jnp.float32)
        * attended.reshape(span_rows, pair_count, head_count, head_size),
        axis=-1,
    )
    row_terms = row_terms.transpose(1, 2, 0)
    keyval_back = lax.all_gather(keyval, "cp", axis=0, tiled=True)
    back_blocks = keyval_back.reshape(n_cp, span_rows, pair_count, 2 * model_width)

    def pair_terms(
        query_rows, grad_rows_att, row_part, total_part, key_rows, value_rows, key_start, rows_pos
    ):
        logits, steps = block_logits(
            query_rows, key_rows, key_start, rows_pos, lengths, table_step, rise_points, head_scale
        )
        weights = jnp.exp(logits - total_part[..., None])
        weight_grads = jnp.einsum(
            "qshd,kshd->shqk", grad_rows_att, value_rows, preferred_element_type=jnp.float32
        )
        score_grads = weights * (weight_grads - row_part[..., None])
        return (weights, score_grads, steps)

    def query_side_step(state_pair, kv_block, block_start):
        query_grad, step_grad = state_pair
        key_rows, value_rows = split_kv(kv_block)
        weights, score_grads, steps = pair_terms(
            queries,
            grad_att_heads,
            row_terms,
            log_total,
            key_rows,
            value_rows,
            block_start,
            query_pos,
        )
        low_grads = score_grads.astype(jnp.bfloat16)
        query_grad = (
            query_grad
            + jnp.einsum("shqk,kshd->qshd", low_grads, key_rows, preferred_element_type=jnp.float32)
            * head_scale
        )
        step_grad = step_grad + jnp.einsum(
            "hqk,qkb->hb", jnp.sum(score_grads, axis=0), steps, precision=lax.Precision.HIGHEST
        )
        return ((query_grad, step_grad), weights, low_grads)

    start_state = (
        jnp.zeros((span_rows, pair_count, head_count, head_size), jnp.float32),
        jnp.zeros((head_count, bucket_count), jnp.float32),
    )

    def grad_step(state_pair, block_item):
        kv_block, block_start = block_item
        new_state, weights, low_grads = query_side_step(state_pair, kv_block, block_start)
        value_grad = jnp.einsum(
            "shqk,qshd->kshd",
            weights.astype(jnp.bfloat16),
            grad_att_heads,
            preferred_element_type=jnp.float32,
        )
        key_grad = (
            jnp.einsum("shqk,qshd->kshd", low_grads, queries, preferred_element_type=jnp.float32)
            * head_scale
        )
        block_grad = jnp.concatenate(
            [
                key_grad.reshape(span_rows, pair_count, model_width),
                value_grad.reshape(span_rows, pair_count, model_width),
            ],
            axis=-1,
        )
        return (new_state, block_grad)

    (query_grad, step_grad), kv_terms = lax.scan(
        grad_step, start_state, (back_blocks, block_starts)
    )
    kv_terms = kv_terms.reshape(seq_len, pair_count, 2 * model_width)
    keyval_grad = lax.psum_scatter(
        kv_terms.astype(jnp.bfloat16), "cp", scatter_dimension=0, tiled=True
    )
    table_grad = step_grad - jnp.concatenate(
        [step_grad[:, 1:], jnp.zeros((head_count, 1), jnp.float32)], axis=1
    )
    qkv_grad = jnp.concatenate(
        [query_grad.reshape(span_rows, pair_count, model_width).astype(jnp.bfloat16), keyval_grad],
        axis=-1,
    )
    qkv_weight_grad = jnp.einsum(
        "csd,cse->de", normed_first, qkv_grad, preferred_element_type=jnp.float32
    )
    grad_normed_first = jnp.einsum(
        "cse,de->csd", qkv_grad, w_qkv, preferred_element_type=jnp.float32
    )
    gain_first_grad = jnp.sum(grad_normed_first * inputs * scale_first, axis=(0, 1))
    tokens_grad = (
        grad_hidden + norm_back(grad_normed_first, inputs, scale_first, norm1_gain)
    ).astype(jnp.bfloat16)
    attn_term = jnp.concatenate([qkv_weight_grad, out_grad], axis=1)
    w_attn_grad = lax.psum_scatter(attn_term, ("dp", "ep", "cp"), scatter_dimension=1, tiled=True)
    router_sum, table_sum, gain_first_sum, gain_second_sum = lax.psum(
        (router_grad, table_grad, gain_first_grad, gain_second_grad), ("dp", "ep", "cp")
    )
    gate_sum, up_sum, down_sum = (
        lax.psum_scatter(
            gate_grad.astype(jnp.bfloat16), ("dp", "cp"), scatter_dimension=2, tiled=True
        ).astype(jnp.float32),
        lax.psum_scatter(
            up_grad.astype(jnp.bfloat16), ("dp", "cp"), scatter_dimension=2, tiled=True
        ).astype(jnp.float32),
        lax.psum_scatter(
            down_grad.astype(jnp.bfloat16), ("dp", "cp"), scatter_dimension=2, tiled=True
        ).astype(jnp.float32),
    )
    return (
        mixed,
        tokens_grad,
        w_attn_grad,
        table_sum,
        gain_first_sum,
        gain_second_sum,
        router_sum,
        gate_sum,
        up_sum,
        down_sum,
    )


minus_big = -1000000000.0
vmem_bytes = 60 * 1024 * 1024


cost_share = 0.05


def cost(flops, moved):
    return pl.CostEstimate(
        flops=int(flops * cost_share), bytes_accessed=int(moved * cost_share), transcendentals=0
    )


def held(kernel, at, count):
    def run(*refs):
        kernel(*refs[:at], *refs[at + count :])

    return run


def anywhere(arrays):
    return [pl.BlockSpec(memory_space=pl.ANY)] * len(arrays)


def compiler_params():
    return pltpu.CompilerParams(vmem_limit_bytes=vmem_bytes)


def shear(values, leftward):
    rows, lanes = values.shape
    row_ids = lax.broadcasted_iota(jnp.int32, (rows, lanes), 0)
    bit = 1
    while bit < rows:
        amount = lanes - bit if leftward else bit
        moved = pltpu.roll(values, amount, 1)
        values = jnp.where((row_ids & bit) != 0, moved, values)
        bit *= 2
    return values


def dot_nt(left, right):
    return lax.dot_general(
        left, right, (((1,), (1,)), ((), ())), preferred_element_type=jnp.float32
    )


def dot_tn(left, right):
    return lax.dot_general(
        left, right, (((0,), (0,)), ((), ())), preferred_element_type=jnp.float32
    )


def dot_nn(left, right):
    return jnp.dot(left, right, preferred_element_type=jnp.float32)


def key_masks(length, blocks, span_rows):
    masks = []
    for block in range(blocks):
        position = block * span_rows + lax.broadcasted_iota(jnp.int32, (1, span_rows), 1)
        masks.append(jnp.where(position < length, 0.0, minus_big))
    return masks


def forward_body(
    mine, length, scale, head_size, qkv_ref, bias_ref, low_ref, full_ref, total_ref, after_pair
):
    blocks, span_rows, width = qkv_ref.shape
    lanes = 128
    lane = lax.broadcasted_iota(jnp.int32, (1, lanes), 1)
    masks = key_masks(length, blocks, span_rows)
    halves = lanes // head_size

    def place(block):
        return lax.rem(mine - block + blocks, blocks)

    def one_pair(pair, carry):
        wide = pl.multiple_of(pair * (3 * lanes), lanes)
        own_lanes = pl.ds(pl.multiple_of(pair * lanes, lanes), lanes)
        part = [pl.ds(pl.multiple_of(wide + which * lanes, lanes), lanes) for which in range(3)]
        for row in range(blocks):
            queries = qkv_ref[place(row), :, part[0]]
            totals = jnp.zeros((span_rows, lanes), jnp.float32)
            result = jnp.zeros((span_rows, lanes), jnp.float32)
            for half in range(halves):
                own = lane // head_size == half
                head_q = queries * jnp.where(own, scale, 0.0).astype(jnp.bfloat16)
                head_v = jnp.where(own, 1.0, 0.0).astype(jnp.bfloat16)
                logits = []
                for column in range(row + 1):
                    at = (blocks - 1 - row + column) * span_rows
                    term = dot_nt(head_q, qkv_ref[place(column), :, part[1]])
                    bias = bias_ref[pair * halves + half, :, at : at + span_rows]
                    logits.append(term + bias + masks[column])
                peak = jnp.max(logits[0], axis=1, keepdims=True)
                for term in logits[1:]:
                    peak = jnp.maximum(peak, jnp.max(term, axis=1, keepdims=True))
                total = jnp.zeros((span_rows, 1), jnp.float32)
                mixed = jnp.zeros((span_rows, lanes), jnp.float32)
                for column in range(row + 1):
                    weights = jnp.exp(logits[column] - peak)
                    total = total + jnp.sum(weights, axis=1, keepdims=True)
                    values = qkv_ref[place(column), :, part[2]] * head_v
                    mixed = mixed + dot_nn(weights.astype(jnp.bfloat16), values)
                result = result + mixed / total
                totals = jnp.where(lane == half, peak + jnp.log(total), totals)
            low_ref[place(row), :, own_lanes] = result.astype(jnp.bfloat16)
            full_ref[row, :, own_lanes] = result
            total_ref[row, :, own_lanes] = totals
        after_pair(pair)
        return carry

    lax.fori_loop(0, width // (3 * lanes), one_pair, 0)


def backward_body(
    mine, length, scale, head_size, qkv_ref, bias_ref, grad_ref, full_ref, total_ref, ring_ref, line_ref, work,
    after_pair=None,
):
    key_sum, value_sum, plane = work
    blocks, span_rows, width = qkv_ref.shape
    lanes = 128
    lane = lax.broadcasted_iota(jnp.int32, (1, lanes), 1)
    masks = key_masks(length, blocks, span_rows)
    halves = lanes // head_size

    def place(block):
        return lax.rem(mine - block + blocks, blocks)

    def one_pair(pair, carry):
        wide = pl.multiple_of(pair * (3 * lanes), lanes)
        own_lanes = pl.ds(pl.multiple_of(pair * lanes, lanes), lanes)
        part = [pl.ds(pl.multiple_of(wide + which * lanes, lanes), lanes) for which in range(3)]
        key_sum[...] = jnp.zeros_like(key_sum)
        value_sum[...] = jnp.zeros_like(value_sum)
        plane[...] = jnp.zeros_like(plane)
        for row in range(blocks):
            queries = qkv_ref[place(row), :, part[0]]
            grads = grad_ref[lax.rem(row - mine + blocks, blocks), :, own_lanes]
            products = grads.astype(jnp.float32) * full_ref[row, :, own_lanes]
            totals = total_ref[row, :, own_lanes]
            query_sum = jnp.zeros((span_rows, lanes), jnp.float32)
            for half in range(halves):
                own = lane // head_size == half
                one = jnp.where(own, 1.0, 0.0).astype(jnp.bfloat16)
                head_q = queries * jnp.where(own, scale, 0.0).astype(jnp.bfloat16)
                head_g = grads * one
                delta = jnp.sum(jnp.where(own, products, 0.0), axis=1, keepdims=True)
                total = totals[:, half : half + 1]
                for column in range(row + 1):
                    at = (blocks - 1 - row + column) * span_rows
                    keys = qkv_ref[place(column), :, part[1]]
                    logits = dot_nt(head_q, keys)
                    bias = bias_ref[pair * halves + half, :, at : at + span_rows]
                    logits = logits + bias + masks[column]
                    weights = jnp.exp(logits - total)
                    weight_grads = dot_nt(head_g, qkv_ref[place(column), :, part[2]])
                    score_grads = weights * (weight_grads - delta)
                    plane[half, :, at : at + span_rows] += score_grads
                    low_weights = weights.astype(jnp.bfloat16)
                    low_grads = score_grads.astype(jnp.bfloat16)
                    query_sum = query_sum + dot_nn(low_grads, keys * one)
                    key_sum[column] += dot_tn(low_grads, head_q)
                    value_sum[column] += dot_tn(low_weights, head_g)
            ring_ref[place(row), :, part[0]] = (query_sum * scale).astype(jnp.bfloat16)
        for row in range(blocks):
            ring_ref[place(row), :, part[1]] = key_sum[row].astype(jnp.bfloat16)
            ring_ref[place(row), :, part[2]] = value_sum[row].astype(jnp.bfloat16)
        for half in range(halves):
            full = jnp.concatenate(
                [plane[half], jnp.zeros((span_rows, span_rows), jnp.float32)], axis=1
            )
            summed = jnp.sum(shear(full, True), axis=0, keepdims=True)
            line_ref[pair * halves + half] = pltpu.roll(summed, span_rows - 1, 1)
        if after_pair is not None:
            after_pair(pair)
        return carry

    lax.fori_loop(0, width // (3 * lanes), one_pair, 0)


def backward_work(blocks, span_rows, head_size):
    return [
        pltpu.VMEM((blocks, span_rows, 128), jnp.float32),
        pltpu.VMEM((blocks, span_rows, 128), jnp.float32),
        pltpu.VMEM((128 // head_size, span_rows, blocks * span_rows), jnp.float32),
    ]


def greet(*others):
    barrier = pltpu.get_barrier_semaphore()
    for other in others:
        pl.semaphore_signal(
            barrier, inc=1, device_id=other, device_id_type=pl.DeviceIdType.MESH
        )
    pl.semaphore_wait(barrier, len(others))


def push(source, target, send_sem, recv_sem, other):
    return pltpu.make_async_remote_copy(
        src_ref=source,
        dst_ref=target,
        send_sem=send_sem,
        recv_sem=recv_sem,
        device_id=other,
        device_id_type=pl.DeviceIdType.MESH,
    )


def ring_others(mine, count):
    return [{"cp": lax.rem(mine + j, count)} for j in range(1, count)]


def slot_of(ref, slot, slots):
    width = ref.shape[1] // slots
    return ref.at[:, pl.ds(slot * width, width)]


def deliveries(source, target, sems, mine, count, lanes=None):
    return [
        push(
            source.at[j] if lanes is None else source.at[j, :, lanes],
            target.at[j],
            sems.at[0, j],
            sems.at[1, j],
            {"cp": lax.rem(mine + (count - j), count)},
        )
        for j in range(1, count)
    ]


def remote_params(number):
    return pltpu.CompilerParams(
        vmem_limit_bytes=vmem_bytes, collective_id=number, has_side_effects=True
    )


def own_rows(block, length, span_rows):
    position = block * span_rows + lax.broadcasted_iota(jnp.int32, (span_rows, 1), 0)
    return jnp.where(position < length, 1.0, 0.0)


def router_of(rows, router_w, experts):
    lane = lax.broadcasted_iota(jnp.int32, (1, router_w.shape[1]), 1)
    logits = jnp.where(lane < experts, dot_nn(rows, router_w), minus_big)
    shares = jnp.exp(logits - jnp.max(logits, axis=1, keepdims=True))
    return shares / jnp.sum(shares, axis=1, keepdims=True)


def project_body(mine, length, input_ref, gain_ref, weight_ref, parts_ref, own_ref, attended_ref, hidden_ref, normed_ref):
    count, span_rows, width = parts_ref.shape
    for j in range(count):
        owner = lax.rem(mine + j, count)
        for group in range(width // 128):
            at = pl.multiple_of((group * count + owner) * 128, 128)
            lanes = slice(group * 128, (group + 1) * 128)
            attended_ref[:, pl.ds(at, 128)] = own_ref[0, :, lanes] if j == 0 else parts_ref[j, :, lanes]
    projected = dot_nn(attended_ref[...], weight_ref[...])
    hidden = input_ref[...].astype(jnp.float32) + own_rows(mine, length, span_rows) * projected
    hidden_ref[...] = hidden
    normed_ref[...] = (hidden * root_scale(hidden) * gain_ref[...]).astype(jnp.bfloat16)


def pick_body(base, capacity, experts, chosen, parts, out_ref):
    for expert in range(experts):
        picked = None
        for choice_ref, part in zip(chosen, parts):
            span = part.shape[0]
            ids = lax.broadcasted_iota(jnp.int32, (capacity, span), 0) + (base + expert * capacity)
            hot = jnp.zeros((capacity, span), jnp.float32)
            for choice in range(choice_ref.shape[0]):
                hot = hot + jnp.where(ids == choice_ref[choice : choice + 1, :], 1.0, 0.0)
            term = dot_nn(hot.astype(jnp.bfloat16), part[...])
            picked = term if picked is None else picked + term
        out_ref[expert] = picked.astype(jnp.bfloat16)


def front_kernel(
    scale, head_size, slots, length_ref, gain_first_ref, gain_second_ref, line_ref, target_ref, w_attn_ref, weight_ref,
    tokens_ref, cotangent_ref, *refs
):
    inputs = [slot_of(tokens_ref, s, slots) for s in range(slots)]
    grads = [slot_of(cotangent_ref, s, slots) for s in range(slots)]
    stores_to, own_w, targets_ref = refs[:5], refs[5], refs[6]
    over_ref, up_ref = refs[7:9]
    picks = [refs[9 + 2 * i : 11 + 2 * i] for i in range(3)]
    outs = [refs[15 + 3 * s : 18 + 3 * s] for s in range(slots)]
    refs = refs[15 + 3 * slots :]
    low, arrived, near_grads, ring_sems, own_sems, give_sems, plane_sems, target_sems = refs[:8]
    core_sems, normed_sems, store_sems, *made = refs[8:]
    all_ref, qkv_ref, bias_ref, full_ref, total_ref = made
    _, count, span_rows, model_width = all_ref.shape

    def store(which, slot):
        source, target = made[which], stores_to[which]
        if which != 2:
            source, target = source.at[slot], target.at[slot]
        return pltpu.make_async_copy(source, target, store_sems.at[which, slot])

    groups = own_w.shape[1] // 384
    mine = lax.axis_index("cp")
    dp, ep = lax.axis_index("dp"), lax.axis_index("ep")
    core_other, x_other, y_other = near_others(dp, ep)

    loads = []
    for group in range(groups):
        for which in range(3):
            at = which * model_width + (group * count + mine) * 128
            lanes = pl.ds((group * 3 + which) * 128, 128)
            loads.append(
                pltpu.make_async_copy(
                    w_attn_ref.at[:, pl.ds(pl.multiple_of(at, 128), 128)],
                    own_w.at[:, lanes],
                    own_sems.at[group * 3 + which],
                )
            )
    for load in loads:
        load.start()
    for s in range(slots):
        values = inputs[s][...].astype(jnp.float32)
        all_ref[s, 0] = (values * root_scale(values) * gain_first_ref[...]).astype(jnp.bfloat16)
    greet(*ring_others(mine, count), core_other, x_other, y_other)

    def hop_copy(slot, hop):
        return push(
            all_ref.at[slot, hop],
            all_ref.at[slot, hop + 1],
            ring_sems.at[0, slot, hop],
            ring_sems.at[1, slot, hop],
            {"cp": lax.rem(mine + 1, count)},
        )

    for s in range(slots):
        hop_copy(s, 0).start()

    def plane_copies(source, target, sems):
        first = [
            push(source(s), target.at[way, s], sems.at[0, way, s], sems.at[1, way, s], other)
            for s in (0, 1)
            for way, other in ((0, x_other), (1, y_other))
        ]
        second = [
            push(target.at[0, 0], target.at[2, 0], sems.at[0, 2, 0], sems.at[1, 2, 0], y_other),
            push(target.at[1, 1], target.at[2, 1], sems.at[0, 2, 1], sems.at[1, 2, 1], x_other),
        ]
        return first, second

    grad_first, grad_second = plane_copies(lambda s: grads[s], near_grads, plane_sems)
    near_targets = targets_ref.at[pl.ds(1, 3)]
    place_first, place_second = plane_copies(lambda s: target_ref.at[s], near_targets, target_sems)
    for copy in place_first + grad_first:
        copy.start()
    targets_ref[0] = target_ref[...]
    for load in loads:
        load.wait()
    for s in range(slots):
        qkv_ref[s, 0] = dot_nn(all_ref[s, 0], own_w[...]).astype(jnp.bfloat16)
    columns = bias_ref.shape[2]
    lanes = span_rows + columns
    for head in range(bias_ref.shape[0]):
        line = pltpu.roll(line_ref[head], lanes - (span_rows - 1), 1)
        full = jnp.broadcast_to(line, (span_rows, lanes))
        bias_ref[head] = shear(full, False)[:, :columns]
    store(2, 0).start()

    _, experts, capacity, _ = picks[0][0].shape
    base = ep * (experts * capacity)
    at_of = ((0, 0), (1, 0), (1, 1), (1, 2), (2, 0))

    def pick(source):
        if source == 0:
            parts = grads
        elif source == 4:
            parts = [outs[s][2] for s in range(slots)]
        else:
            parts = [near_grads.at[source - 1, s] for s in range(slots)]
        chosen = [targets_ref.at[source % 4, s] for s in range(slots)]
        group, at = at_of[source]
        pick_body(base, capacity, experts, chosen, parts, picks[group][0].at[at])
        core_copy(source).start()

    def core_copy(source):
        group, at = at_of[source]
        return push(
            picks[group][0].at[at],
            picks[group][1].at[at],
            core_sems.at[0, source],
            core_sems.at[1, source],
            core_other,
        )

    def normed_copy(at):
        source, target, other = (
            (outs[0][2], over_ref, x_other),
            (outs[0][2], up_ref, y_other),
        )[at]
        return push(source, target, normed_sems.at[0, at], normed_sems.at[1, at], other)

    def project(slot):
        for pair in range(groups):
            for copy in gives(slot, pair):
                copy.wait()
        project_body(
            mine, length_ref[slot], inputs[slot], gain_second_ref, weight_ref, arrived.at[slot],
            low.at[slot], *outs[slot],
        )

    def gives(slot, pair):
        part = pl.ds(pl.multiple_of(pair * 128, 128), 128)
        return [
            push(
                low.at[slot, j, :, part],
                arrived.at[slot, j, :, part],
                give_sems.at[0, slot, pair, j],
                give_sems.at[1, slot, pair, j],
                {"cp": lax.rem(mine + (count - j), count)},
            )
            for j in range(1, count)
        ]

    def attend(slot):
        def after_pair(pair):
            for copy in gives(slot, pair):
                copy.start()

        forward_body(
            mine, length_ref[slot], scale, head_size, qkv_ref.at[slot], bias_ref, low.at[slot],
            full_ref.at[slot], total_ref.at[slot], after_pair,
        )
        for which in (0, 1, 3, 4):
            store(which, slot).start()

    pick(0)
    for hop in range(1, count):
        for s in range(slots):
            hop_copy(s, hop - 1).wait_recv()
            if hop < count - 1:
                hop_copy(s, hop).start()
            qkv_ref[s, hop] = dot_nn(all_ref[s, hop], own_w[...]).astype(jnp.bfloat16)
            if hop == count - 1 and s + 1 < slots:
                attend(s)
        if hop == 1:
            for copy in place_first + grad_first:
                copy.wait_recv()
            for copy in place_second + grad_second:
                copy.start()
            pick(1)
            pick(2)
        if hop == 2:
            for copy in place_second + grad_second:
                copy.wait_recv()
            pick(3)
    attend(slots - 1)
    project(0)
    for at in range(2):
        normed_copy(at).start()
    project(1)
    pick(4)
    for s in range(slots):
        for hop in range(count - 1):
            hop_copy(s, hop).wait_send()
    for copy in place_first + grad_first + place_second + grad_second:
        copy.wait_send()
    for at in range(2):
        normed_copy(at).wait()
    for source in range(5):
        core_copy(source).wait()
    store(2, 0).wait()
    for s in range(slots):
        for which in (0, 1, 3, 4):
            store(which, s).wait()


def front(lengths, gain_first, gain_second, lines, target, w_attn, inputs, grads, slots, count, experts, capacity, scale, head_size):
    span_rows, model_width = inputs.shape[0], inputs.shape[1] // slots
    heads, _, lanes = lines.shape
    own_width = 3 * model_width // count
    groups = own_width // 384
    choices = target.shape[1]
    whole = pl.BlockSpec(memory_space=pltpu.VMEM)
    f32, bf16 = jnp.float32, jnp.bfloat16
    shape = jax.ShapeDtypeStruct
    made = (
        ((slots, count, span_rows, model_width), bf16),
        ((slots, count, span_rows, own_width), bf16),
        ((heads, span_rows, lanes - span_rows), f32),
        ((slots, count, span_rows, groups * 128), f32),
        ((slots, count, span_rows, groups * 128), f32),
    )
    got = pl.pallas_call(
        functools.partial(front_kernel, scale, head_size, slots),
        grid=(1,),
        in_specs=[
            pl.BlockSpec(memory_space=pltpu.SMEM),
            whole,
            whole,
            whole,
            whole,
            pl.BlockSpec(memory_space=pl.ANY),
            pl.BlockSpec((model_width, model_width), lambda i: (0, 3)),
            whole,
            whole,
        ],
        out_specs=[pl.BlockSpec(memory_space=pl.ANY)] * 5 + [whole] * (10 + 3 * slots),
        out_shape=[
            *(shape(*kind) for kind in made),
            shape((model_width, own_width), bf16),
            shape((4, slots, choices, span_rows), jnp.int32),
        ]
        + [shape((span_rows, model_width), bf16)] * 2
        + [
            shape((sources, experts, capacity, model_width), bf16)
            for sources in (1, 3, 1)
            for _ in range(2)
        ]
        + [
            shape((span_rows, model_width), bf16),
            shape((span_rows, model_width), f32),
            shape((span_rows, model_width), bf16),
        ]
        * slots,
        scratch_shapes=[
            pltpu.VMEM((slots, count, span_rows, groups * 128), bf16),
            pltpu.VMEM((slots, count, span_rows, groups * 128), bf16),
            pltpu.VMEM((3, slots, span_rows, model_width), bf16),
            pltpu.SemaphoreType.DMA((2, slots, count - 1)),
            pltpu.SemaphoreType.DMA((3 * groups,)),
            pltpu.SemaphoreType.DMA((2, slots, groups, count)),
            pltpu.SemaphoreType.DMA((2, 3, slots)),
            pltpu.SemaphoreType.DMA((2, 3, slots)),
            pltpu.SemaphoreType.DMA((2, 5)),
            pltpu.SemaphoreType.DMA((2, 3)),
            pltpu.SemaphoreType.DMA((5, slots)),
            *(pltpu.VMEM(*kind) for kind in made),
        ],
        cost_estimate=cost(60e9, 20e6),
        compiler_params=remote_params(0),
        name="front",
    )(lengths, gain_first, gain_second, lines, target, w_attn, w_attn, inputs, grads)
    pairs = [got[9 + 2 * i : 11 + 2 * i] for i in range(3)]
    return got[:9], pairs, [got[15 + 3 * s : 18 + 3 * s] for s in range(slots)]


def hidden_body(
    experts, mine, length, back_ref, grad_ref, hidden_ref, normed_ref, gain_ref, router_ref, weight_ref,
    hidden_grad_ref, proj_ref, router_grad_ref, gain_grad_ref, leaving_ref, attended,
):
    count = leaving_ref.shape[0]
    span_rows, model_width = hidden_ref.shape
    back = back_ref[...]
    normed = normed_ref[...]
    probs = router_of(normed, router_ref[...], experts)
    shares = back[:, model_width:]
    logit_grads = probs * (shares - jnp.sum(probs * shares, axis=1, keepdims=True))
    logit_grads = logit_grads.astype(jnp.bfloat16)
    router_grad_ref[...] = dot_tn(logit_grads, normed)
    grads = back[:, :model_width] + dot_nt(logit_grads, router_ref[...])
    hidden = hidden_ref[...]
    scale_rows = root_scale(hidden)
    gain_grad_ref[...] = jnp.sum(grads * hidden * scale_rows, axis=0, keepdims=True)
    hidden_grads = grad_ref[...].astype(jnp.float32) + norm_back(
        grads, hidden, scale_rows, gain_ref[...]
    )
    hidden_grad_ref[...] = hidden_grads
    proj = (own_rows(mine, length, span_rows) * hidden_grads).astype(jnp.bfloat16)
    proj_ref[...] = proj
    attended[...] = dot_nt(proj, weight_ref[...]).astype(jnp.bfloat16)
    for j in range(count):
        owner = lax.rem(mine + (count - j), count)
        for group in range(leaving_ref.shape[2] // 128):
            at = pl.multiple_of((group * count + owner) * 128, 128)
            leaving_ref[j, :, group * 128 : (group + 1) * 128] = attended[:, pl.ds(at, 128)]


def hidden_kernel(
    experts, scale, head_size, slots, length_ref, gain_ref, router_ref, weight_ref, qkv_all, bias_all, full_all, total_all,
    cotangent_ref, *refs
):
    per_slot = [
        (refs[3 * s], slot_of(cotangent_ref, s, slots), *refs[3 * s + 1 : 3 * s + 3])
        for s in range(slots)
    ]
    refs = refs[3 * slots :]
    own_out, rest_out, refs = refs[:slots], refs[slots : 4 * slots], refs[4 * slots :]
    outs = [refs[4 * s : 4 * s + 4] for s in range(slots)]
    mixed = [slot_of(refs[4 * slots], s, slots) for s in range(slots)]
    refs = refs[4 * slots + 1 :]
    ring_ref, line_ref, rest_ref, leaving, arriving, attended, sems = refs[:7]
    got, far, last, low, out_sems = refs[7:12]
    qkv_ref, bias_ref, full_ref, total_ref, held_out, load_sems = refs[12:18]
    work = refs[18:]
    count = qkv_ref.shape[0]
    mine = lax.axis_index("cp")
    _, x_other, y_other = near_others(lax.axis_index("dp"), lax.axis_index("ep"))
    over, up, across = (rest_out[i * slots : (i + 1) * slots] for i in range(3))
    loads = [
        pltpu.make_async_copy(source, target, load_sems.at[at])
        for at, (source, target) in enumerate(
            (
                (qkv_all.at[0], qkv_ref),
                (bias_all, bias_ref),
                (full_all.at[0], full_ref),
                (total_all.at[0], total_ref),
                (up[0], held_out.at[0]),
                (over[1], held_out.at[1]),
                (own_out[0], held_out.at[2]),
                (own_out[1], held_out.at[3]),
            )
        )
    ]
    for load in loads:
        load.start()
    greet(*ring_others(mine, count), x_other, y_other)

    def out_copy(at):
        source, target, other = (
            (over[0], got.at[0], x_other),
            (up[1], got.at[1], y_other),
            (across[0], far.at[0], x_other),
            (across[1], far.at[1], y_other),
            (low.at[0], last.at[0], y_other),
            (low.at[1], last.at[1], x_other),
        )[at]
        return push(source, target, out_sems.at[0, at], out_sems.at[1, at], other)

    def after_pair(pair):
        @pl.when(pair == 0)
        def _():
            for at in range(2):
                out_copy(2 + at).wait()
                summed = held_out[at].astype(jnp.float32) + far[at].astype(jnp.float32)
                low[at] = summed.astype(jnp.bfloat16)
                out_copy(4 + at).start()

    for at in (2, 3, 0, 1):
        out_copy(at).start()
    copies = []
    for s in range(slots):
        hidden_body(
            experts, mine, length_ref[s], *per_slot[s], gain_ref, router_ref, weight_ref,
            *outs[s], leaving.at[s], attended,
        )
        target = arriving if s == 0 else rest_ref.at[s - 1]
        copies.append(deliveries(leaving.at[s], target, sems.at[s], mine, count))
        if s == 0:
            for copy in copies[s]:
                copy.start()
        target[0] = leaving[s, 0]
    for copy in copies[0]:
        copy.wait()
    for some in copies[1:]:
        for copy in some:
            copy.start()
    for load in loads:
        load.wait()
    backward_body(
        mine, length_ref[0], scale, head_size, qkv_ref, bias_ref, arriving, full_ref, total_ref,
        ring_ref, line_ref, work, after_pair,
    )
    for s in range(slots):
        out_copy(s).wait()
        out_copy(4 + s).wait()
        home = held_out[2 + s].astype(jnp.float32) + got[s].astype(jnp.float32)
        home = per_slot[s][2][...] + home + last[s].astype(jnp.float32)
        mixed[s][...] = home.astype(jnp.bfloat16)
    for copy in (copy for some in copies[1:] for copy in some):
        copy.wait()


def hidden_back(
    lengths, back_rows, grads, hidden, normed, gain, router, w_attn, experts, qkvs, bias, full, total, own_out,
    rest_out, scale, head_size,
):
    slots, count, span_rows, own_width = qkvs.shape
    model_width = hidden[0].shape[1]
    heads = bias.shape[0]
    whole = pl.BlockSpec(memory_space=pltpu.VMEM)
    f32, bf16 = jnp.float32, jnp.bfloat16
    each = [grads]
    for s in range(slots):
        each += [back_rows[s], hidden[s], normed[s]]
    each += [*own_out, *rest_out]
    own_shape = (count, span_rows, own_width // 3)
    got = pl.pallas_call(
        functools.partial(hidden_kernel, experts, scale, head_size, slots),
        grid=(1,),
        in_specs=[
            pl.BlockSpec(memory_space=pltpu.SMEM),
            whole,
            whole,
            pl.BlockSpec((model_width, model_width), lambda i: (0, 3)),
            *[pl.BlockSpec(memory_space=pl.ANY)] * 4,
        ]
        + [whole] * (len(each) - 4 * slots)
        + [pl.BlockSpec(memory_space=pl.ANY)] * (4 * slots),
        out_specs=[whole] * (4 * slots + 4),
        out_shape=[
            jax.ShapeDtypeStruct((span_rows, model_width), f32),
            jax.ShapeDtypeStruct((span_rows, model_width), bf16),
            jax.ShapeDtypeStruct((router.shape[1], model_width), f32),
            jax.ShapeDtypeStruct((1, model_width), f32),
        ]
        * slots
        + [jax.ShapeDtypeStruct((span_rows, slots * model_width), bf16)]
        + [
            jax.ShapeDtypeStruct(qkvs.shape[1:], bf16),
            jax.ShapeDtypeStruct((heads, 1, bias.shape[2] + span_rows), f32),
            jax.ShapeDtypeStruct((slots - 1,) + own_shape, bf16),
        ],
        scratch_shapes=[
            pltpu.VMEM((slots,) + own_shape, bf16),
            pltpu.VMEM(own_shape, bf16),
            pltpu.VMEM((span_rows, model_width), bf16),
            pltpu.SemaphoreType.DMA((slots, 2, count)),
            *[pltpu.VMEM((slots, span_rows, model_width), bf16)] * 4,
            pltpu.SemaphoreType.DMA((2, 6)),
            pltpu.VMEM(qkvs.shape[1:], bf16),
            pltpu.VMEM(bias.shape, f32),
            pltpu.VMEM(full.shape[1:], f32),
            pltpu.VMEM(full.shape[1:], f32),
            pltpu.VMEM((2 * slots, span_rows, model_width), bf16),
            pltpu.SemaphoreType.DMA((8,)),
        ]
        + backward_work(count, span_rows, head_size),
        cost_estimate=cost(20e9, 20e6),
        compiler_params=remote_params(1),
        name="hidden_back",
    )(lengths, gain, router, w_attn, qkvs, bias, full, total, *each)
    return [got[4 * s : 4 * s + 4] for s in range(slots)], got[4 * slots], got[4 * slots + 1 :]


def near_others(dp, ep):
    core, across = lax.rem(dp, 2), dp // 2
    return (
        {"dp": across * 2 + (1 - core)},
        {"dp": (1 - across) * 2 + core},
        {"ep": 1 - ep},
    )


def second_kernel(
    scale, head_size, slots, length_ref, former_ref, normed_all, qkv_all, bias_all, grad_ref, full_all, total_all,
    *refs,
):
    attended, proj, refs = refs[:slots], refs[slots : 2 * slots], refs[2 * slots :]
    own_w_all, gain_ref, refs = refs[0], refs[1], refs[2:]
    ring_ref, line_ref, arrived_ref, early_ref, weight_ref, rows_ref, gain_grad_ref = refs[:7]
    refs = refs[1:]
    sums, low, got_core, got_x, got_y, leaving, coming, sems, near_sems, last_sems = refs[6:16]
    early_sems, held_refs, work = refs[16], refs[17:24], refs[24:]
    normed_ref, qkv_ref, bias_ref, full_ref, total_ref, own_w_ref, load_sems = held_refs
    count = qkv_ref.shape[0]
    mine = lax.axis_index("cp")
    loads = [
        pltpu.make_async_copy(source, target, load_sems.at[at])
        for at, (source, target) in enumerate(
            (
                (qkv_all.at[1], qkv_ref),
                (bias_all, bias_ref),
                (full_all.at[1], full_ref),
                (total_all.at[1], total_ref),
                (normed_all, normed_ref),
                (own_w_all, own_w_ref),
            )
        )
    ]
    for load in loads:
        load.start()
    dp, ep = lax.axis_index("dp"), lax.axis_index("ep")
    core, across = lax.rem(dp, 2), dp // 2
    others = near_others(dp, ep)
    greet(*ring_others(mine, count), *others)
    copies = deliveries(former_ref, arrived_ref, sems, mine, count)
    for copy in copies:
        copy.start()
    arrived_ref[0] = former_ref[0]
    height = sums.shape[0] // 2
    sizes = (height, height // 2, height // 4)
    bits = (core, across, ep)
    landing = (got_core, got_x, got_y)
    total = None
    for s in range(slots):
        term = dot_tn(attended[s][...], proj[s][...])
        total = term if total is None else total + term
    sums[...] = total

    def low_part(stage):
        return low.at[stage, pl.ds(0, sizes[stage])]

    def stage_copy(stage):
        return push(
            low_part(stage), landing[stage], near_sems.at[0, stage], near_sems.at[1, stage], others[stage]
        )

    def start_of(stage):
        start = 0
        for former in range(stage):
            start = start + bits[former] * sizes[former]
        return start

    def begin(stage):
        at = start_of(stage) + (1 - bits[stage]) * sizes[stage]
        away = sums[pl.ds(pl.multiple_of(at, 128), sizes[stage]), :]
        low[stage, : sizes[stage]] = away.astype(jnp.bfloat16)
        stage_copy(stage).start()

    def finish(stage):
        stage_copy(stage).wait()
        at = pl.ds(pl.multiple_of(start_of(stage + 1), 128), sizes[stage])
        sums[at, :] = sums[at, :] + landing[stage][...].astype(jnp.float32)

    early = deliveries(ring_ref, early_ref, early_sems, mine, count, pl.ds(0, early_ref.shape[2]))

    def after_pair(pair):
        @pl.when(pair == 0)
        def _():
            for copy in early:
                copy.start()

        for stage in range(2):

            @pl.when(pair == stage)
            def _():
                finish(stage)
                begin(stage + 1)

    begin(0)
    for load in loads:
        load.wait()
    backward_body(
        mine, length_ref[1], scale, head_size, qkv_ref, bias_ref, grad_ref.at[0], full_ref, total_ref,
        ring_ref, line_ref, work, after_pair,
    )
    finish(2)
    at = pl.ds(pl.multiple_of(start_of(3), 128), sizes[2])
    groups = leaving.shape[2] // 128
    for j in range(count):
        owner = lax.rem(mine + (count - j), count)
        for group in range(groups):
            lanes = pl.ds(pl.multiple_of((group * count + owner) * 128, 128), 128)
            part = sums[at, lanes]
            leaving[j, :, group * 128 : (group + 1) * 128] = part.astype(jnp.bfloat16)
            if j == 0:
                rows_ref[:, group * 128 : (group + 1) * 128] = part
    last = deliveries(leaving, coming, last_sems, mine, count)
    for copy in last:
        copy.start()
    total = None
    for slot, grads in ((0, former_ref), (1, ring_ref)):
        for j in range(count):
            term = dot_tn(normed_ref[slot, j], grads[j])
            total = term if total is None else total + term
    weight_ref[...] = total
    first_gain = lax.dot_general(
        jnp.ones((8, total.shape[1]), jnp.float32),
        total * own_w_ref[...].astype(jnp.float32),
        (((1,), (1,)), ((), ())),
        precision=lax.Precision.HIGHEST,
        preferred_element_type=jnp.float32,
    )
    gain_grad_ref[...] = first_gain / gain_ref[...]
    for copy in last:
        copy.wait()
    for j in range(1, count):
        rows_ref[...] = rows_ref[...] + coming[j].astype(jnp.float32)
    for copy in copies + early:
        copy.wait()


def second_back(
    lengths, former, normed_all, qkvs, bias, grads, full, total, attended, proj, own_w, gain, scale, head_size, waits=()
):
    slots, count, span_rows, own_width = qkvs.shape
    model_width = normed_all.shape[3]
    whole = pl.BlockSpec(memory_space=pltpu.VMEM)
    some = pl.BlockSpec(memory_space=pl.ANY)
    f32, bf16 = jnp.float32, jnp.bfloat16
    rows_shape = (model_width // 8, own_width // 3)
    return pl.pallas_call(
        held(
            functools.partial(second_kernel, scale, head_size, slots), 10 + 2 * slots, len(waits)
        ),
        grid=(1,),
        in_specs=[
            pl.BlockSpec(memory_space=pltpu.SMEM),
            whole,
            some,
            some,
            some,
            whole,
            some,
            some,
        ]
        + [whole] * (2 * slots)
        + [some, whole]
        + anywhere(waits),
        out_specs=[whole] * 7,
        out_shape=[
            jax.ShapeDtypeStruct(qkvs.shape[1:], bf16),
            jax.ShapeDtypeStruct((bias.shape[0], 1, bias.shape[2] + span_rows), f32),
            jax.ShapeDtypeStruct(qkvs.shape[1:], bf16),
            jax.ShapeDtypeStruct((count, span_rows, 384), bf16),
            jax.ShapeDtypeStruct((model_width, own_width), f32),
            jax.ShapeDtypeStruct(rows_shape, f32),
            jax.ShapeDtypeStruct((8, model_width), f32),
        ],
        scratch_shapes=[
            pltpu.VMEM((model_width, model_width), f32),
            pltpu.VMEM((3, model_width // 2, model_width), bf16),
            pltpu.VMEM((model_width // 2, model_width), bf16),
            pltpu.VMEM((model_width // 4, model_width), bf16),
            pltpu.VMEM((model_width // 8, model_width), bf16),
            pltpu.VMEM((count,) + rows_shape, bf16),
            pltpu.VMEM((count,) + rows_shape, bf16),
            pltpu.SemaphoreType.DMA((2, count)),
            pltpu.SemaphoreType.DMA((2, 3)),
            pltpu.SemaphoreType.DMA((2, count)),
            pltpu.SemaphoreType.DMA((2, count)),
            pltpu.VMEM(normed_all.shape, bf16),
            pltpu.VMEM(qkvs.shape[1:], bf16),
            pltpu.VMEM(bias.shape, f32),
            pltpu.VMEM(full.shape[1:], f32),
            pltpu.VMEM(full.shape[1:], f32),
            pltpu.VMEM(own_w.shape, bf16),
            pltpu.SemaphoreType.DMA((6,)),
        ]
        + backward_work(count, span_rows, head_size),
        cost_estimate=cost(20e9, 20e6),
        compiler_params=remote_params(2),
        name="second_back",
    )(lengths, former, normed_all, qkvs, bias, grads, full, total, *attended, *proj, own_w, gain, *waits)


def token_body(mine, input_ref, hidden_ref, gain_ref, weight_ref, part_refs, own_ref, out_ref):
    count = part_refs[0].shape[0]
    model_width = input_ref.shape[1]
    total = None
    for j in range(count):
        owner = lax.rem(mine + j, count)
        pieces = []
        for group in range(own_ref.shape[2] // 384):
            for which in range(3):
                at = which * model_width + (group * count + owner) * 128
                pieces.append(weight_ref[:, pl.ds(pl.multiple_of(at, 128), 128)])
        part = own_ref[0] if j == 0 else jnp.concatenate([ref[j] for ref in part_refs], axis=1)
        term = dot_nt(part, jnp.concatenate(pieces, axis=1))
        total = term if total is None else total + term
    inputs = input_ref[...].astype(jnp.float32)
    back = norm_back(total, inputs, root_scale(inputs), gain_ref[...])
    out_ref[...] = (hidden_ref[...] + back).astype(jnp.bfloat16)


def final_kernel(
    slots, ring_ref, early_ref, former_all, arrived_ref, blocks_ref, small_ref, gain_ref, weight_all, tokens_ref, *refs
):
    inputs = [slot_of(tokens_ref, s, slots) for s in range(slots)]
    hidden_all, out_ref, refs = refs[:slots], refs[slots], refs[slots + 1 :]
    outs = [slot_of(out_ref, s, slots) for s in range(slots)]
    small_out, attn_out = refs[:2]
    coming, here, sum_blocks, low_blocks, small_now, small_in, sems, near_sems, small_sems = refs[2:11]
    got_core, low_halves, got_halves, low_ends, got_ends, half_sems = refs[11:17]
    former_ref, weight_ref, hidden_refs, load_sems = refs[17:]
    hiddens = [hidden_refs.at[s] for s in range(slots)]
    loads = [
        pltpu.make_async_copy(source, target, load_sems.at[at])
        for at, (source, target) in enumerate(
            (
                (former_all, former_ref),
                (weight_all.at[:, pl.ds(0, weight_ref.shape[1])], weight_ref),
                *((hidden_all[s], hiddens[s]) for s in range(slots)),
            )
        )
    ]
    for load in loads:
        load.start()
    count = ring_ref.shape[0]
    mine = lax.axis_index("cp")
    dp, ep = lax.axis_index("dp"), lax.axis_index("ep")
    core, across = lax.rem(dp, 2), dp // 2
    core_other, x_other, y_other = near_others(dp, ep)
    greet(*ring_others(mine, count), core_other, x_other, y_other)
    late = ring_ref.shape[2] - early_ref.shape[2]
    copies = deliveries(ring_ref, coming, sems, mine, count, pl.ds(early_ref.shape[2], late))
    for copy in copies:
        copy.start()

    small_now[0] = small_ref[...]
    loads[0].wait()
    total = former_ref[...]
    groups = total.shape[1] // 384
    for group in range(groups):
        for which in range(3):
            at = (group * 3 + which) * 128
            part = total[:, at : at + 128]
            sum_blocks[which % 2, which // 2, group] = part
            low_blocks[which % 2, which // 2, group] = part.astype(jnp.bfloat16)
        height = blocks_ref.shape[0]
        here_rows = pl.ds(pl.multiple_of((core * 4 + across * 2 + ep) * height, 128), height)
        part = blocks_ref[:, group * 128 : (group + 1) * 128]
        sum_blocks[1, 1, group] = jnp.zeros_like(sum_blocks[1, 1, group])
        low_blocks[1, 1, group] = jnp.zeros_like(low_blocks[1, 1, group])
        sum_blocks[1, 1, group, here_rows] = part
        low_blocks[1, 1, group, here_rows] = part.astype(jnp.bfloat16)
    first = push(low_blocks.at[1 - core], got_core, near_sems.at[0, 0], near_sems.at[1, 0], core_other)
    first.start()

    stages = [core_other, x_other, y_other]
    step = 1
    while step < count:
        flip = mine + step - 2 * step * lax.rem(mine // step, 2)
        stages.append({"cp": flip})
        step *= 2

    def small_push(at):
        return push(small_now.at[at], small_in.at[at], small_sems.at[0, at], small_sems.at[1, at], stages[at])

    small_push(0).start()
    for load in loads[1:]:
        load.wait()
    token_body(mine, inputs[0], hiddens[0], gain_ref, weight_ref, [arrived_ref], arrived_ref, outs[0])
    first.wait()
    here[...] = sum_blocks[core] + got_core[...].astype(jnp.float32)
    middle = here.shape[2] // 2
    upper, lower = slice(0, middle), slice(middle, 2 * middle)
    for at in range(2):
        low_halves[0, at] = here[1 - across, at, upper].astype(jnp.bfloat16)
        low_halves[1, at] = here[at, 1 - ep, lower].astype(jnp.bfloat16)

    def half_copy(at):
        source, target, other = (
            (low_halves.at[0], got_halves.at[0], x_other),
            (low_halves.at[1], got_halves.at[1], y_other),
            (low_ends.at[0], got_ends.at[0], y_other),
            (low_ends.at[1], got_ends.at[1], x_other),
        )[at]
        return push(source, target, half_sems.at[0, at], half_sems.at[1, at], other)

    half_copy(0).start()
    half_copy(1).start()
    for at in range(len(stages)):
        small_push(at).wait()
        now = small_now[at] + small_in[at]
        if at + 1 < len(stages):
            small_now[at + 1] = now
            small_push(at + 1).start()
        else:
            small_out[...] = now
        if at == 1:
            half_copy(0).wait()
            for k in range(2):
                here[across, k, upper] = here[across, k, upper] + got_halves[0, k].astype(jnp.float32)
            low_ends[0] = here[across, 1 - ep, upper].astype(jnp.bfloat16)
            half_copy(2).start()
            half_copy(1).wait()
            for k in range(2):
                here[k, ep, lower] = here[k, ep, lower] + got_halves[1, k].astype(jnp.float32)
            low_ends[1] = here[1 - across, ep, lower].astype(jnp.bfloat16)
            half_copy(3).start()
    for copy in copies:
        copy.wait()
    token_body(mine, inputs[1], hiddens[1], gain_ref, weight_ref, [early_ref, coming], ring_ref, outs[1])
    half_copy(2).wait()
    attn_out[upper] = here[across, ep, upper] + got_ends[0].astype(jnp.float32)
    half_copy(3).wait()
    attn_out[lower] = here[across, ep, lower] + got_ends[1].astype(jnp.float32)


def final_back(ring, early, former, arrived, blocks, small, gain, w_attn, inputs, hiddens):
    count, span_rows, own_width = ring.shape
    slots = len(hiddens)
    model_width = hiddens[0].shape[1]
    groups = blocks.shape[1] // 128
    whole = pl.BlockSpec(memory_space=pltpu.VMEM)
    f32, bf16 = jnp.float32, jnp.bfloat16
    some = pl.BlockSpec(memory_space=pl.ANY)
    stages = 3 + (count - 1).bit_length()
    tile = (model_width, 128)
    return pl.pallas_call(
        functools.partial(final_kernel, slots),
        grid=(1,),
        in_specs=[
            whole,
            whole,
            some,
            whole,
            whole,
            whole,
            whole,
            some,
            whole,
        ]
        + [some] * slots,
        out_specs=[whole] * 3,
        out_shape=[jax.ShapeDtypeStruct((span_rows, slots * model_width), bf16)]
        + [jax.ShapeDtypeStruct(small.shape, f32), jax.ShapeDtypeStruct(tile, f32)],
        scratch_shapes=[
            pltpu.VMEM((count, span_rows, own_width - early.shape[2]), bf16),
            pltpu.VMEM((2, groups) + tile, f32),
            pltpu.VMEM((2, 2, groups) + tile, f32),
            pltpu.VMEM((2, 2, groups) + tile, bf16),
            pltpu.VMEM((stages,) + small.shape, f32),
            pltpu.VMEM((stages,) + small.shape, f32),
            pltpu.SemaphoreType.DMA((2, count)),
            pltpu.SemaphoreType.DMA((2, 3)),
            pltpu.SemaphoreType.DMA((2, stages)),
            pltpu.VMEM((2, groups) + tile, bf16),
            pltpu.VMEM((2, 2, model_width // 2, 128), bf16),
            pltpu.VMEM((2, 2, model_width // 2, 128), bf16),
            pltpu.VMEM((2, model_width // 2, 128), bf16),
            pltpu.VMEM((2, model_width // 2, 128), bf16),
            pltpu.SemaphoreType.DMA((2, 4)),
            pltpu.VMEM(former.shape, f32),
            pltpu.VMEM((model_width, 3 * model_width), bf16),
            pltpu.VMEM((slots, span_rows, model_width), f32),
            pltpu.SemaphoreType.DMA((2 + slots,)),
        ],
        cost_estimate=cost(20e9, 20e6),
        compiler_params=remote_params(3),
        name="final_back",
    )(ring, early, former, arrived, blocks, small, gain, w_attn, inputs, *hiddens)


gelu_inner = 0.7978845608028654
gelu_cubic = 0.044715


def place_body(base, chosen_ref, pairs, outs):
    capacity = pairs[0][0].shape[0]
    span = outs[0].shape[0]
    both = [
        (mine[...].astype(jnp.float32) + theirs[...].astype(jnp.float32)).astype(jnp.bfloat16)
        for mine, theirs in pairs
    ]
    for at, out in enumerate(outs):
        total = None
        for expert in range(len(pairs)):
            ids = lax.broadcasted_iota(jnp.int32, (span, capacity), 1) + (base + expert * capacity)
            hot = jnp.zeros((span, capacity), jnp.float32)
            for choice in range(chosen_ref.shape[1]):
                chosen = chosen_ref[at * span : (at + 1) * span, choice : choice + 1]
                hot = hot + jnp.where(ids == chosen, 1.0, 0.0)
            term = dot_nn(hot.astype(jnp.bfloat16), both[expert])
            total = term if total is None else total + term
        out[...] = total.astype(jnp.bfloat16)


def return_kernel(experts, slots, target_ref, *refs):
    held_pairs = 2 * (1 + experts)
    back, far_outs, refs = refs[:held_pairs], refs[held_pairs : 2 * held_pairs], refs[2 * held_pairs :]
    backs, refs = refs[:slots], refs[slots:]
    out_own, out_rest, refs = refs[:slots], refs[slots : 4 * slots], refs[4 * slots :]
    here, got, far, last, low = refs[:5]
    outs, load_sems, sems = refs[5 : 5 + held_pairs], refs[5 + held_pairs], refs[6 + held_pairs]
    arriving, core_sems = refs[7 + held_pairs :]
    dp, ep = lax.axis_index("dp"), lax.axis_index("ep")
    core_other, x_other, y_other = near_others(dp, ep)
    base = ep * (experts * back[0].shape[2])
    loads = [
        pltpu.make_async_copy(source, target, load_sems.at[i])
        for i, (source, target) in enumerate(zip(far_outs[:-1], outs[:-1]))
    ]

    def core_copy(at):
        if at == 3:
            source, target = far_outs[-1], outs[-1]
        else:
            source, target = back[-1].at[0, at], arriving.at[0, at]
        return push(source, target, core_sems.at[0, at], core_sems.at[1, at], core_other)

    given = [*back[:-1], arriving]
    for load in loads:
        load.start()

    def rows_of(held_refs, source):
        if source == 0:
            return [(held_refs[0].at[e, 0], held_refs[1].at[e, 0]) for e in range(experts)]
        return [
            (held_refs[2 + 2 * e].at[0, source - 1], held_refs[3 + 2 * e].at[0, source - 1])
            for e in range(experts)
        ]

    def place(held_refs, source, targets):
        if held_refs is given and source > 0:
            core_copy(source - 1).wait()
        place_body(base, target_ref.at[source], rows_of(held_refs, source), targets)

    firsts = [
        push(here.at[1, 0], got.at[0], sems.at[0, 0], sems.at[1, 0], x_other),
        push(here.at[2, 1], got.at[1], sems.at[0, 1], sems.at[1, 1], y_other),
        push(here.at[3, 0], far.at[0], sems.at[0, 2], sems.at[1, 2], x_other),
        push(here.at[3, 1], far.at[1], sems.at[0, 3], sems.at[1, 3], y_other),
    ]
    ends = [
        push(low.at[0], last.at[0], sems.at[0, 4], sems.at[1, 4], y_other),
        push(low.at[1], last.at[1], sems.at[0, 5], sems.at[1, 5], x_other),
    ]
    greet(core_other, x_other, y_other)
    for at in (2, 0, 1, 3):
        core_copy(at).start()
    halves = lambda source: [here.at[source, s] for s in range(slots)]
    place(given, 3, halves(3))
    firsts[2].start()
    firsts[3].start()
    place(given, 1, halves(1))
    firsts[0].start()
    place(given, 2, halves(2))
    firsts[1].start()
    place(given, 0, halves(0))
    for load in loads:
        load.wait()
    core_copy(3).wait()
    for at, (former, source) in enumerate(((2, 2), (3, 1))):
        firsts[former].wait()
        low[at] = (here[source, at].astype(jnp.float32) + far[at].astype(jnp.float32)).astype(jnp.bfloat16)
        ends[at].start()
    place(outs, 0, out_own)
    for source in range(1, 4):
        place(outs, source, out_rest[(source - 1) * slots : source * slots])
    for s in range(slots):
        firsts[s].wait()
        backs[s][...] = here[0, s].astype(jnp.float32) + got[s].astype(jnp.float32)
    for s in range(slots):
        ends[s].wait()
        backs[s][...] = backs[s][...] + last[s].astype(jnp.float32)


def return_rows(targets, backs, outs, slots, waits=()):
    experts = len(backs) // 2 - 1
    model_width = outs[0].shape[-1]
    span_rows = targets.shape[1] // slots
    wide = backs[0].shape[-1]
    whole = pl.BlockSpec(memory_space=pltpu.VMEM)
    f32, bf16 = jnp.float32, jnp.bfloat16
    half = pltpu.VMEM((slots, span_rows, wide), bf16)
    got = pl.pallas_call(
        held(
            functools.partial(return_kernel, experts, slots),
            1 + len(backs) + len(outs),
            len(waits),
        ),
        in_specs=[whole] + [whole] * len(backs) + anywhere(outs) + anywhere(waits),
        out_specs=[whole] * (5 * slots),
        out_shape=[
            *[jax.ShapeDtypeStruct((span_rows, wide), f32)] * slots,
            *[jax.ShapeDtypeStruct((span_rows, model_width), bf16)] * (4 * slots),
        ],
        scratch_shapes=[pltpu.VMEM((4, slots, span_rows, wide), bf16), half, half, half, half]
        + [pltpu.VMEM(a.shape, bf16) for a in outs]
        + [pltpu.SemaphoreType.DMA((len(outs),)), pltpu.SemaphoreType.DMA((2, 6))]
        + [pltpu.VMEM(backs[-1].shape, bf16), pltpu.SemaphoreType.DMA((2, 4))],
        cost_estimate=cost(20e9, 20e6),
        compiler_params=remote_params(4),
        name="return_rows",
    )(targets, *backs, *outs, *waits)
    return got[:slots], got[slots : 2 * slots], got[2 * slots :]


def expert_body(experts, own_units, expert, skip, given, refs, weights, router_ref):
    back_mine, back_theirs, out_mine, out_theirs, kept_rows, kept_units = refs
    gate_ref, up_ref, down_ref = weights
    capacity, model_width = given[0].shape[2:]
    rows = jnp.concatenate([given[0][0, 0], given[1][0, 0]], axis=0)
    grads = jnp.concatenate([given[2][0, 0], given[3][0, 0]], axis=0)
    kept_rows[0, 0, 0] = rows
    kept_rows[1, 0, 0] = grads
    lane = lax.broadcasted_iota(jnp.int32, (1, router_ref.shape[1]), 1)
    probs = router_of(rows, router_ref[...], experts)
    gates = jnp.sum(jnp.where(lane == expert, probs, 0.0), axis=1, keepdims=True)
    unit = lax.broadcasted_iota(jnp.int32, (1, gate_ref.shape[2]), 1) - skip
    own = jnp.logical_and(unit >= 0, unit < own_units)
    gate_w, up_w, down_w = gate_ref[0], up_ref[0], down_ref[0]
    gate_pre = dot_nn(rows, gate_w)
    up_pre = jnp.where(own, dot_nn(rows, up_w), 0.0)
    square = gate_pre * gate_pre
    tanh = jnp.tanh(gelu_inner * gate_pre * (1.0 + gelu_cubic * square))
    half = 0.5 + 0.5 * tanh
    active = gate_pre * half
    slope = half + active * (1.0 - tanh) * (gelu_inner * (1.0 + 3.0 * gelu_cubic * square))
    inner = active * up_pre
    low_inner = inner.astype(jnp.bfloat16)
    plain_grads = jnp.where(own, dot_nn(grads, down_w), 0.0)
    gate_grads = jnp.sum(plain_grads * low_inner.astype(jnp.float32), axis=1, keepdims=True)
    inner_grads = plain_grads * gates
    low_gate = (inner_grads * up_pre * slope).astype(jnp.bfloat16)
    low_up = (inner_grads * active).astype(jnp.bfloat16)
    kept_units[0, 0, 0] = low_gate
    kept_units[1, 0, 0] = low_up
    kept_units[2, 0, 0] = (inner * gates).astype(jnp.bfloat16)
    back = (dot_nt(low_gate, gate_w) + dot_nt(low_up, up_w)).astype(jnp.bfloat16)
    shares = jnp.where(lane == expert, gate_grads, 0.0).astype(jnp.bfloat16)
    out = (gates * dot_nt(low_inner, down_w)).astype(jnp.bfloat16)
    for at, back_ref, out_ref in ((0, back_mine, out_mine), (1, back_theirs, out_theirs)):
        part = slice(at * capacity, (at + 1) * capacity)
        back_ref[0, 0, :, :model_width] = back[part]
        back_ref[0, 0, :, model_width:] = shares[part]
        out_ref[0, 0] = out[part]


def expert_kernel(experts, own_units, kept_count, first_ref, window_ref, *refs):
    given, refs = refs[:4], refs[4:]
    router_ref, weights, refs = refs[0], refs[1:4], refs[4 + kept_count :]
    expert = first_ref[0] + pl.program_id(0)
    expert_body(experts, own_units, expert, window_ref[1], given, refs, weights, router_ref)


def own_kernel(experts, own_units, *refs):
    given, router_ref, weights, refs = refs[:4], refs[4], refs[5:8], refs[8:]
    target_ref, over_ref, up_ref, normed_ref, refs = refs[0], refs[1], refs[2], refs[3], refs[4:]
    results, kept, (mine_ref, theirs_ref), refs = refs[:4], refs[4:6], refs[6:8], refs[8:]
    coming, picked, held_w, held_rows, held_units = refs[:5]
    sems, core_sems, home_sems, load_sems, keep_sems = refs[5:]
    exp_dev, capacity = picked.shape[1:3]
    dp, ep = lax.axis_index("dp"), lax.axis_index("ep")
    core_other, x_other, y_other = near_others(dp, ep)
    skip = lax.rem(dp * own_units, 128)

    def copy(at):
        source, other = (
            (normed_ref, x_other),
            (normed_ref, y_other),
            (over_ref, y_other),
            (coming.at[1], x_other),
        )[at]
        return push(source, coming.at[at], sems.at[0, at], sems.at[1, at], other)

    def load(expert, which):
        lanes = pl.ds(pl.multiple_of(dp * own_units - skip, 128), held_w.shape[4])
        return pltpu.make_async_copy(
            weights[which].at[pl.ds(expert, 1), :, lanes],
            held_w.at[expert, which],
            load_sems.at[expert, which],
        )

    def keep(expert, kind):
        held_ref = (held_rows, held_units)[kind]
        return pltpu.make_async_copy(
            held_ref.at[expert, :, 0, 0], kept[kind].at[:, expert, 0], keep_sems.at[expert, kind]
        )

    for expert in range(exp_dev):
        for which in range(3):
            load(expert, which).start()
    greet(core_other, x_other, y_other)
    for at in range(3):
        copy(at).start()
    for expert in range(exp_dev):
        if expert == 1:
            copy(1).wait_recv()
            copy(3).start()
        for which in range(3):
            load(expert, which).wait()
        here = pl.ds(expert, 1)
        expert_body(
            experts,
            own_units,
            ep * exp_dev + expert,
            skip,
            [part.at[:, here] for part in given],
            [part.at[here] for part in results] + [held_rows.at[expert], held_units.at[expert]],
            [held_w.at[expert, which] for which in range(3)],
            router_ref,
        )
        for kind in range(2):
            keep(expert, kind).start()

    base = ep * (exp_dev * capacity)
    blocks = (
        (over_ref, coming.at[0]),
        (up_ref, coming.at[1]),
        (coming.at[2], coming.at[3]),
    )

    def across_cores(k):
        return push(picked.at[k], theirs_ref.at[k], core_sems.at[0, k], core_sems.at[1, k], core_other)

    def home(k):
        return pltpu.make_async_copy(picked.at[k], mine_ref.at[k], home_sems.at[k])

    for k, waits in enumerate(((0,), (), (2, 3))):
        for at in waits:
            copy(at).wait_recv()
        chosen = [target_ref.at[k + 1, s] for s in range(target_ref.shape[1])]
        pick_body(base, capacity, exp_dev, chosen, blocks[k], picked.at[k])
        across_cores(k).start()
        home(k).start()
    for at in range(4):
        copy(at).wait_send()
    for k in range(3):
        across_cores(k).wait()
        home(k).wait()
    for expert in range(exp_dev):
        for kind in range(2):
            keep(expert, kind).wait()


def own_experts(given, router, weights, target, over, up, normed, total, experts, units):
    _, exp_dev, capacity, model_width = given[0].shape
    span_rows = normed.shape[0]
    wide_units = aligned_units(units)
    tile = 2 * capacity
    bf16 = jnp.bfloat16
    shape = jax.ShapeDtypeStruct
    picked = (3, exp_dev, capacity, model_width)
    wide = model_width + 128
    keeps = ((2, model_width), (3, wide_units))
    whole = pl.BlockSpec(memory_space=pltpu.VMEM)
    some = pl.BlockSpec(memory_space=pl.ANY)
    got = pl.pallas_call(
        functools.partial(own_kernel, experts, units),
        grid=(1,),
        in_specs=[whole] * 5 + [some] * 3 + [whole] * 4,
        out_specs=[whole] * 4 + [some] * 4,
        out_shape=[shape((exp_dev, 1, capacity, wide), bf16)] * 2
        + [shape((exp_dev, 1, capacity, model_width), bf16)] * 2
        + [shape((kinds, exp_dev, total, tile, width), bf16) for kinds, width in keeps]
        + [shape(picked, bf16)] * 2,
        scratch_shapes=[
            pltpu.VMEM((4, span_rows, model_width), bf16),
            pltpu.VMEM(picked, bf16),
            pltpu.VMEM((exp_dev, 3, 1, model_width, wide_units), bf16),
        ]
        + [pltpu.VMEM((exp_dev, kinds, 1, 1, tile, width), bf16) for kinds, width in keeps]
        + [
            pltpu.SemaphoreType.DMA((2, 4)),
            pltpu.SemaphoreType.DMA((2, 3)),
            pltpu.SemaphoreType.DMA((3,)),
            pltpu.SemaphoreType.DMA((exp_dev, 3)),
            pltpu.SemaphoreType.DMA((exp_dev, 2)),
        ],
        cost_estimate=cost(20e9, 16e6),
        compiler_params=remote_params(5),
        name="own_experts",
    )(*given, router, *weights, target, over, up, normed)
    return got[:4], got[4:6], got[6:]


def run_experts(first, window, given, router, weights, kept, at, total, experts, units, chosen):
    low, high = chosen
    sources, exp_dev, capacity, model_width = given[0].shape
    wide_units = aligned_units(units)
    tile = 2 * capacity

    given_rows = pl.BlockSpec(
        (1, 1, capacity, model_width), lambda e, k, f, w: (k, low + e, 0, 0)
    )
    out = lambda width: pl.BlockSpec((1, 1, capacity, width), lambda e, k, f, w: (e, k, 0, 0))
    wide, rows = out(model_width + 128), out(model_width)
    weight = pl.BlockSpec(
        (pl.Element(1), pl.Element(model_width), pl.Element(wide_units)),
        lambda e, k, f, w: (low + e, 0, pl.multiple_of(w[0], 128)),
    )
    keep = lambda kinds, width: pl.BlockSpec(
        (kinds, 1, 1, tile, width), lambda e, k, f, w: (0, low + e, at + k, 0, 0)
    )
    keeps = ((2, model_width), (3, wide_units))
    kept = list(kept)
    out_of = lambda width: jax.ShapeDtypeStruct(
        (high - low, sources, capacity, width), jnp.bfloat16
    )
    back_shape, out_shape = out_of(model_width + 128), out_of(model_width)
    got = pl.pallas_call(
        functools.partial(expert_kernel, experts, units, len(kept)),
        grid_spec=pltpu.PrefetchScalarGridSpec(
            num_scalar_prefetch=2,
            grid=(high - low, sources),
            in_specs=[given_rows] * 4
            + [
                pl.BlockSpec(router.shape, lambda e, k, f, w: (0, 0)),
                weight,
                weight,
                weight,
            ]
            + anywhere(kept),
            out_specs=[wide, wide, rows, rows] + [keep(*kinds) for kinds in keeps],
        ),
        out_shape=[back_shape, back_shape, out_shape, out_shape]
        + [
            jax.ShapeDtypeStruct((kinds, exp_dev, total, tile, width), jnp.bfloat16)
            for kinds, width in keeps
        ],
        input_output_aliases={10 + i: 4 + i for i in range(len(kept))},
        cost_estimate=cost(20e9 * sources, 8e6 * sources),
        compiler_params=compiler_params(),
        name="expert_rows",
    )(first + low, window, *given, router, *weights, *kept)
    return got[:4], got[4:]


def aligned_units(units):
    return (units + 127) // 128 * 128


def weight_kernel(window_ref, rows_ref, units_ref, weight_ref, total):
    pieces, _, piece, model_width = weight_ref.shape
    units = units_ref[0, 0].reshape(-1, units_ref.shape[-1])
    total[...] = dot_tn(units, rows_ref[0, 0].reshape(-1, model_width))
    skip = pl.multiple_of(window_ref[1], 64)
    for at in range(pieces):
        weight_ref[at, 0] = total[pl.ds(skip + at * piece, piece), :].astype(jnp.bfloat16)


def weight_grads(window, kept, expert, pieces, units, waits=()):
    kept_rows, kept_units = kept
    tiles, tile, model_width = kept_rows.shape[2:]
    wide_units = kept_units.shape[4]
    shape = (pieces, 3, units // pieces, model_width)
    return pl.pallas_call(
        held(weight_kernel, 3, len(waits)),
        grid=(3,),
        in_specs=[
            pl.BlockSpec(memory_space=pltpu.SMEM),
            pl.BlockSpec((1, 1, tiles, tile, model_width), lambda i: (i // 2, expert, 0, 0, 0)),
            pl.BlockSpec((1, 1, tiles, tile, wide_units), lambda i: (i, expert, 0, 0, 0)),
        ]
        + anywhere(waits),
        out_specs=pl.BlockSpec((pieces, 1) + shape[2:], lambda i: (0, i, 0, 0)),
        out_shape=jax.ShapeDtypeStruct(shape, jnp.bfloat16),
        scratch_shapes=[pltpu.VMEM((wide_units, model_width), jnp.float32)],
        cost_estimate=cost(20e9, 20e6),
        compiler_params=compiler_params(),
        name="weight_grads",
    )(window, kept_rows, kept_units, *waits)


def send(values, axis, pairs):
    return lax.ppermute(values, axis, pairs)


def after(values, *earlier):
    return lax.optimization_barrier((values, earlier))[0]


def fast_device(
    tokens,
    lengths,
    expert_ids,
    places,
    buckets,
    w_attn,
    bias_table,
    norm1_gain,
    norm2_gain,
    w_router,
    w_gate,
    w_up,
    w_down,
    cotangent,
):
    span_rows, slots, model_width = tokens.shape
    head_count, bucket_count = bias_table.shape
    head_size = model_width // head_count
    scale = head_size ** (-0.5)
    n_dp = lax.axis_size("dp")
    n_ep = lax.axis_size("ep")
    n_cp = lax.axis_size("cp")
    my_dp, my_ep, my_cp = (lax.axis_index(name) for name in ("dp", "ep", "cp"))
    seq_len = span_rows * n_cp
    rows = span_rows * slots
    top_count = expert_ids.shape[2]
    experts = w_router.shape[1]
    exp_dev = w_gate.shape[0]
    units = w_gate.shape[2] // n_dp
    capacity = (5 * rows * top_count + 4 * experts - 1) // (4 * experts)
    groups = model_width // (128 * n_cp)
    own_width = 3 * groups * 128
    heads_own = head_count // n_cp
    over_core = [(i, i ^ 1) for i in range(n_dp)]
    over_x = [(i, i ^ 2) for i in range(n_dp)]
    over_y = [(i, i ^ 1) for i in range(n_ep)]
    ring = [(i, (i + 1) % n_cp) for i in range(n_cp)]
    f32, bf16 = jnp.float32, jnp.bfloat16
    exact = lax.Precision.HIGHEST
    each = range(slots)

    low_in = tokens.reshape(span_rows, slots * model_width)
    low_out = cotangent.reshape(span_rows, slots * model_width)
    gain_first, gain_second = norm1_gain[None, :], norm2_gain[None, :]

    per_group = 128 // head_size
    own_heads = (
        jnp.arange(groups)[:, None] * (n_cp * per_group)
        + my_cp * per_group
        + jnp.arange(per_group)[None, :]
    ).reshape(heads_own)
    head_hot = (own_heads[:, None] == jnp.arange(head_count)[None, :]).astype(f32)
    own_table = jnp.dot(head_hot, bias_table, precision=exact)
    far_hot = (buckets[::-1][:, None] == jnp.arange(bucket_count)[None, :]).astype(f32)
    lines = jnp.einsum("hb,db->hd", own_table, far_hot, precision=exact)
    lines = jnp.concatenate([lines, jnp.full((heads_own, span_rows), minus_big, f32)], axis=1)
    target = jnp.where(places >= 0, expert_ids * capacity + places, -1)
    target = target.transpose(1, 2, 0).astype(jnp.int32)
    (
        (normed_all, qkvs, bias, full, total, w_own, target_all, over_first, up_first),
        (grads_own, grads_rest_rows, picked_own),
        fronts,
    ) = front(
        lengths,
        gain_first,
        gain_second,
        lines[:, None, :],
        target,
        w_attn,
        low_in,
        low_out,
        slots,
        n_cp,
        exp_dev,
        capacity,
        scale,
        head_size,
    )
    attended, hidden, normed_second = zip(*fronts)

    sources = target_all.shape[0]
    target_rows = target_all.transpose(0, 2, 1, 3).reshape(sources, top_count, rows)
    target_columns = target_rows.transpose(0, 2, 1)
    window_at = my_dp * units // 128 * 128
    window = jnp.stack([window_at, my_dp * units - window_at]).astype(jnp.int32)
    router_wide = jnp.concatenate(
        [w_router, jnp.zeros((model_width, 128 - experts), w_router.dtype)], axis=1
    )

    first = (my_ep * exp_dev).astype(jnp.int32).reshape(1)
    own, kept, picked_rest = own_experts(
        (*picked_own, *grads_own),
        router_wide,
        (w_gate, w_up, w_down),
        target_all,
        over_first,
        up_first,
        normed_second[1],
        sources,
        experts,
        units,
    )

    def with_theirs(mine, theirs):
        return [mine, send(theirs, "dp", over_core)]

    backs, outs = with_theirs(own[0], own[1]), with_theirs(own[2], own[3])
    weight_sums = []
    for e in range(exp_dev):
        rest, kept = run_experts(
            first,
            window,
            (*picked_rest, *grads_rest_rows),
            router_wide,
            (w_gate, w_up, w_down),
            kept,
            1,
            sources,
            experts,
            units,
            (e, e + 1),
        )
        weight_part = weight_grads(window, kept, e, n_cp, units, backs[-1:] + outs[-1:])
        if e + 1 < exp_dev:
            backs += with_theirs(rest[0], rest[1])
            outs += with_theirs(rest[2], rest[3])
        else:
            backs, outs = [*backs, *rest[:2]], [*outs, *rest[2:]]
        weight_sums.append(lax.psum_scatter(weight_part, "cp", scatter_dimension=0, tiled=False))
        kept = after(kept, weight_part)
    back_rows, out_own, out_rest = return_rows(target_columns, backs, outs, slots, [weight_part])
    got, mixed, (ringed, line_first, grads_rest) = hidden_back(
        lengths,
        back_rows,
        low_out,
        hidden,
        normed_second,
        gain_second,
        router_wide,
        w_attn,
        experts,
        qkvs,
        bias,
        full,
        total,
        out_own,
        out_rest,
        scale,
        head_size,
    )
    hidden_grads, proj_grads, router_parts, gain_parts = zip(*got)
    router_grad = sum(router_parts)[:experts]
    ring_second, line_second, arrived, early, weight_part, out_grad, gain_part = second_back(
        lengths,
        ringed,
        normed_all,
        qkvs,
        bias,
        grads_rest,
        full,
        total,
        attended,
        proj_grads,
        w_own,
        gain_first,
        scale,
        head_size,
        weight_sums[:1],
    )
    distance_grads = (line_first + line_second)[:, 0, :seq_len]
    table_grad = jnp.dot(distance_grads, far_hot, precision=exact)
    table_grad = jnp.einsum("hg,hb->gb", head_hot, table_grad, precision=exact)
    table_row = jnp.pad(table_grad.reshape(1, -1), ((0, 0), (0, model_width - table_grad.size)))
    small = jnp.concatenate(
        [router_grad, sum(gain_parts), table_row, gain_part[:2]], axis=0
    )
    tokens_grad, small_sum, attn_sum = final_back(
        ring_second,
        early,
        weight_part,
        arrived,
        out_grad,
        small,
        gain_first,
        w_attn,
        low_in,
        hidden_grads,
    )
    router_sum, gain_second_sum = small_sum[:experts], small_sum[experts]
    table_sum = small_sum[experts + 1, : table_grad.size].reshape(table_grad.shape)
    gain_first_sum = small_sum[experts + 2]

    gate_sum, up_sum, down_sum = (
        jnp.stack([part[which].T.astype(f32) for part in weight_sums]) for which in range(3)
    )
    return (
        mixed.reshape(tokens.shape),
        tokens_grad.reshape(tokens.shape),
        attn_sum,
        table_sum,
        gain_first_sum,
        gain_second_sum,
        router_sum.T,
        gate_sum,
        up_sum,
        down_sum,
    )


def solution(mesh):
    placed = (
        P("cp", ("dp", "ep"), None),
        P(("dp", "ep")),
        P("cp", ("dp", "ep"), None),
        P("cp", ("dp", "ep"), None),
        P(),
        P(),
        P(),
        P(),
        P(),
        P(),
        P("ep", None, None),
        P("ep", None, None),
        P("ep", None, None),
        P("cp", ("dp", "ep"), None),
    )
    sizes = dict(mesh.shape)
    square = sizes["dp"] == 4 and sizes["ep"] == 2 and sizes["cp"] == 4
    return jax.shard_map(
        fast_device if square else on_device,
        mesh=mesh,
        in_specs=placed,
        out_specs=(
            P("cp", ("dp", "ep"), None),
            P("cp", ("dp", "ep"), None),
            P(None, ("dp", "ep", "cp")),
            P(),
            P(),
            P(),
            P(),
            P("ep", None, ("dp", "cp")),
            P("ep", None, ("dp", "cp")),
            P("ep", None, ("dp", "cp")),
        ),
        check_vma=False,
    )
```

```python
import functools

import jax
import jax.numpy as jnp
from jax import lax
from jax.experimental import pallas as pl
from jax.experimental.pallas import tpu as pltpu
from jax.sharding import PartitionSpec as P

epsilon = 1e-06
masked_value = -1000000000.0


def gelu_tanh(values):
    return jax.nn.gelu(values, approximate=True)


def root_scale(values):
    return lax.rsqrt(jnp.mean(values * values, axis=-1, keepdims=True) + epsilon)


def norm_back(grad_in, values, scale_rows, gain_vector):
    scaled = grad_in * gain_vector
    inner_mean = jnp.mean(scaled * values, axis=-1, keepdims=True)
    return scale_rows * (scaled - values * scale_rows * scale_rows * inner_mean)


def block_logits(
    queries, key_rows, key_start, query_pos, lengths, table_step, rise_points, head_scale
):
    key_count = key_rows.shape[0]
    key_pos = key_start + jnp.arange(key_count, dtype=jnp.int32)
    scores = (
        jnp.einsum("qshd,kshd->shqk", queries, key_rows, preferred_element_type=jnp.float32)
        * head_scale
    )
    distance = query_pos[:, None] - key_pos[None, :]
    steps = (distance[:, :, None] >= rise_points[None, None, :]).astype(jnp.float32)
    pair_bias = jnp.einsum("hb,qkb->hqk", table_step, steps, precision=lax.Precision.HIGHEST)
    allowed = (distance >= 0)[None, :, :] & (key_pos[None, None, :] < lengths[:, None, None])
    logits = jnp.where(allowed[:, None], scores + pair_bias[None], masked_value)
    return (logits, steps)


def on_device(
    tokens,
    lengths,
    expert_ids,
    places,
    buckets,
    w_attn,
    bias_table,
    norm1_gain,
    norm2_gain,
    w_router,
    w_gate,
    w_up,
    w_down,
    cotangent,
):
    span_rows, pair_count, model_width = tokens.shape
    head_count, bucket_count = bias_table.shape
    head_size = model_width // head_count
    head_scale = head_size ** (-0.5)
    n_cp = lax.axis_size("cp")
    n_ep = lax.axis_size("ep")
    seq_len = span_rows * n_cp
    row_count = span_rows * pair_count
    top_count = expert_ids.shape[2]
    experts = w_router.shape[1]
    exp_dev = w_gate.shape[0]
    capacity = (5 * row_count * top_count + 4 * experts - 1) // (4 * experts)
    my_start = lax.axis_index("cp") * span_rows
    query_pos = my_start + jnp.arange(span_rows, dtype=jnp.int32)
    live_mask = (query_pos[:, None] < lengths[None, :]).astype(jnp.float32)
    inputs = tokens.astype(jnp.float32)
    scale_first = root_scale(inputs)
    normed_first = (inputs * scale_first * norm1_gain).astype(jnp.bfloat16)
    w_qkv = w_attn[:, : 3 * model_width]
    w_out = w_attn[:, 3 * model_width :]
    qkv = jnp.einsum("csd,de->cse", normed_first, w_qkv, preferred_element_type=jnp.float32).astype(
        jnp.bfloat16
    )
    queries = qkv[..., :model_width].reshape(span_rows, pair_count, head_count, head_size)
    keyval = qkv[..., model_width:]
    keyval_all = lax.all_gather(keyval, "cp", axis=0, tiled=True)
    bucket_ids = jnp.arange(bucket_count, dtype=jnp.int32)
    rise_points = jnp.sum((buckets[:, None] < bucket_ids[None, :]).astype(jnp.int32), axis=0)
    table_step = jnp.concatenate(
        [bias_table[:, :1], bias_table[:, 1:] - bias_table[:, :-1]], axis=1
    )
    block_starts = jnp.arange(n_cp, dtype=jnp.int32) * span_rows

    def split_kv(kv_block):
        key_rows = kv_block[..., :model_width].reshape(span_rows, pair_count, head_count, head_size)
        value_rows = kv_block[..., model_width:].reshape(
            span_rows, pair_count, head_count, head_size
        )
        return (key_rows, value_rows)

    kv_blocks = keyval_all.reshape(n_cp, span_rows, pair_count, 2 * model_width)

    def max_step(state_pair, block_item):
        row_peak, row_total = state_pair
        kv_block, block_start = block_item
        key_rows, value_rows = split_kv(kv_block)
        logits, steps = block_logits(
            queries, key_rows, block_start, query_pos, lengths, table_step, rise_points, head_scale
        )
        new_peak = jnp.maximum(row_peak, jnp.max(logits, axis=-1))
        row_total = row_total * jnp.exp(row_peak - new_peak) + jnp.sum(
            jnp.exp(logits - new_peak[..., None]), axis=-1
        )
        return ((new_peak, row_total), None)

    stat_shape = (pair_count, head_count, span_rows)
    (row_peak, row_total), unused = lax.scan(
        max_step,
        (jnp.full(stat_shape, masked_value, jnp.float32), jnp.zeros(stat_shape, jnp.float32)),
        (kv_blocks, block_starts),
    )
    log_total = row_peak + jnp.log(row_total)

    def value_step(running, block_item):
        kv_block, block_start = block_item
        key_rows, value_rows = split_kv(kv_block)
        logits, steps = block_logits(
            queries, key_rows, block_start, query_pos, lengths, table_step, rise_points, head_scale
        )
        weights = jnp.exp(logits - log_total[..., None]).astype(jnp.bfloat16)
        return (
            running
            + jnp.einsum(
                "shqk,kshd->qshd", weights, value_rows, preferred_element_type=jnp.float32
            ),
            None,
        )

    attended, unused = lax.scan(
        value_step,
        jnp.zeros((span_rows, pair_count, head_count, head_size), jnp.float32),
        (kv_blocks, block_starts),
    )
    attended = attended.reshape(span_rows, pair_count, model_width)
    attended_low = attended.astype(jnp.bfloat16)
    projected = jnp.einsum("csd,de->cse", attended_low, w_out, preferred_element_type=jnp.float32)
    hidden = inputs + live_mask[..., None] * projected
    scale_second = root_scale(hidden)
    normed_second = (hidden * scale_second * norm2_gain).astype(jnp.bfloat16)
    router_logits = jnp.einsum(
        "csd,de->cse", normed_second, w_router, preferred_element_type=jnp.float32
    )
    router_probs = jax.nn.softmax(router_logits, axis=-1)
    expert_hot = (expert_ids[..., None] == jnp.arange(experts, dtype=jnp.int32)).astype(jnp.float32)
    kept_mask = (places >= 0).astype(jnp.float32)
    gate_values = jnp.sum(expert_hot * router_probs[:, :, None, :], axis=-1) * kept_mask
    target = jnp.where(places >= 0, expert_ids * capacity + places, -1).reshape(
        row_count, top_count
    )
    slot_ids = jnp.arange(experts * capacity, dtype=jnp.int32)
    route_hot = (target[None, :, :] == slot_ids[:, None, None]).astype(jnp.bfloat16)
    dispatch = jnp.sum(route_hot, axis=2)
    sent_rows = jnp.dot(
        dispatch, normed_second.reshape(row_count, model_width), preferred_element_type=jnp.float32
    )
    sent_rows = sent_rows.astype(jnp.bfloat16).reshape(n_ep, exp_dev, capacity, model_width)
    arrived = lax.all_to_all(sent_rows, "ep", split_axis=0, concat_axis=0, tiled=True)
    gate_pre = jnp.einsum("secd,edf->secf", arrived, w_gate, preferred_element_type=jnp.float32)
    up_pre = jnp.einsum("secd,edf->secf", arrived, w_up, preferred_element_type=jnp.float32)
    active, gelu_pullback = jax.vjp(gelu_tanh, gate_pre)
    inner_act = (active * up_pre).astype(jnp.bfloat16)
    produced = jnp.einsum(
        "secf,edf->secd", inner_act, w_down, preferred_element_type=jnp.float32
    ).astype(jnp.bfloat16)
    returned = lax.all_to_all(produced, "ep", split_axis=0, concat_axis=0, tiled=True).reshape(
        experts * capacity, model_width
    )
    picked = jnp.einsum("jrk,jd->rkd", route_hot, returned, preferred_element_type=jnp.float32)
    gate_flat = gate_values.reshape(row_count, top_count)
    mixed = hidden.reshape(row_count, model_width) + jnp.sum(gate_flat[..., None] * picked, axis=1)
    mixed = mixed.reshape(span_rows, pair_count, model_width).astype(jnp.bfloat16)
    grad_out = cotangent.astype(jnp.float32).reshape(row_count, model_width)
    gate_grads = jnp.sum(grad_out[:, None, :] * picked, axis=-1)
    sent_back = (gate_flat[..., None] * grad_out[:, None, :]).astype(jnp.bfloat16)
    scattered = jnp.einsum("jrk,rkd->jd", route_hot, sent_back, preferred_element_type=jnp.float32)
    scattered = scattered.astype(jnp.bfloat16).reshape(n_ep, exp_dev, capacity, model_width)
    grad_produced = lax.all_to_all(scattered, "ep", split_axis=0, concat_axis=0, tiled=True)
    down_grad = jnp.einsum(
        "secd,secf->edf", grad_produced, inner_act, preferred_element_type=jnp.float32
    )
    grad_inner = jnp.einsum(
        "secd,edf->secf", grad_produced, w_down, preferred_element_type=jnp.float32
    )
    grad_gate_pre = gelu_pullback(grad_inner * up_pre)[0].astype(jnp.bfloat16)
    grad_up_pre = (grad_inner * active).astype(jnp.bfloat16)
    gate_grad = jnp.einsum(
        "secd,secf->edf", arrived, grad_gate_pre, preferred_element_type=jnp.float32
    )
    up_grad = jnp.einsum("secd,secf->edf", arrived, grad_up_pre, preferred_element_type=jnp.float32)
    grad_arrived = jnp.einsum(
        "secf,edf->secd", grad_gate_pre, w_gate, preferred_element_type=jnp.float32
    )
    grad_arrived = (
        grad_arrived
        + jnp.einsum("secf,edf->secd", grad_up_pre, w_up, preferred_element_type=jnp.float32)
    ).astype(jnp.bfloat16)
    grad_sent = lax.all_to_all(grad_arrived, "ep", split_axis=0, concat_axis=0, tiled=True).reshape(
        experts * capacity, model_width
    )
    grad_rows = jnp.einsum("jr,jd->rd", dispatch, grad_sent, preferred_element_type=jnp.float32)
    choice_grads = gate_grads.reshape(span_rows, pair_count, top_count) * kept_mask
    prob_grads = jnp.sum(expert_hot * choice_grads[..., None], axis=2)
    logit_grads = router_probs * (
        prob_grads - jnp.sum(router_probs * prob_grads, axis=-1, keepdims=True)
    )
    logit_grads = logit_grads.astype(jnp.bfloat16)
    router_grad = jnp.einsum(
        "csd,cse->de", normed_second, logit_grads, preferred_element_type=jnp.float32
    )
    grad_normed_second = grad_rows.reshape(span_rows, pair_count, model_width)
    grad_normed_second = grad_normed_second + jnp.einsum(
        "cse,de->csd", logit_grads, w_router, preferred_element_type=jnp.float32
    )
    gain_second_grad = jnp.sum(grad_normed_second * hidden * scale_second, axis=(0, 1))
    grad_hidden = grad_out.reshape(span_rows, pair_count, model_width) + norm_back(
        grad_normed_second, hidden, scale_second, norm2_gain
    )
    grad_proj = (live_mask[..., None] * grad_hidden).astype(jnp.bfloat16)
    out_grad = jnp.einsum(
        "csd,cse->de", attended_low, grad_proj, preferred_element_type=jnp.float32
    )
    grad_att = jnp.einsum(
        "cse,de->csd", grad_proj, w_out, preferred_element_type=jnp.float32
    ).astype(jnp.bfloat16)
    grad_att_heads = grad_att.reshape(span_rows, pair_count, head_count, head_size)
    row_terms = jnp.sum(
        grad_att_heads.astype(jnp.float32)
        * attended.reshape(span_rows, pair_count, head_count, head_size),
        axis=-1,
    )
    row_terms = row_terms.transpose(1, 2, 0)
    keyval_back = lax.all_gather(keyval, "cp", axis=0, tiled=True)
    back_blocks = keyval_back.reshape(n_cp, span_rows, pair_count, 2 * model_width)

    def pair_terms(
        query_rows, grad_rows_att, row_part, total_part, key_rows, value_rows, key_start, rows_pos
    ):
        logits, steps = block_logits(
            query_rows, key_rows, key_start, rows_pos, lengths, table_step, rise_points, head_scale
        )
        weights = jnp.exp(logits - total_part[..., None])
        weight_grads = jnp.einsum(
            "qshd,kshd->shqk", grad_rows_att, value_rows, preferred_element_type=jnp.float32
        )
        score_grads = weights * (weight_grads - row_part[..., None])
        return (weights, score_grads, steps)

    def query_side_step(state_pair, kv_block, block_start):
        query_grad, step_grad = state_pair
        key_rows, value_rows = split_kv(kv_block)
        weights, score_grads, steps = pair_terms(
            queries,
            grad_att_heads,
            row_terms,
            log_total,
            key_rows,
            value_rows,
            block_start,
            query_pos,
        )
        low_grads = score_grads.astype(jnp.bfloat16)
        query_grad = (
            query_grad
            + jnp.einsum("shqk,kshd->qshd", low_grads, key_rows, preferred_element_type=jnp.float32)
            * head_scale
        )
        step_grad = step_grad + jnp.einsum(
            "hqk,qkb->hb", jnp.sum(score_grads, axis=0), steps, precision=lax.Precision.HIGHEST
        )
        return ((query_grad, step_grad), weights, low_grads)

    start_state = (
        jnp.zeros((span_rows, pair_count, head_count, head_size), jnp.float32),
        jnp.zeros((head_count, bucket_count), jnp.float32),
    )

    def grad_step(state_pair, block_item):
        kv_block, block_start = block_item
        new_state, weights, low_grads = query_side_step(state_pair, kv_block, block_start)
        value_grad = jnp.einsum(
            "shqk,qshd->kshd",
            weights.astype(jnp.bfloat16),
            grad_att_heads,
            preferred_element_type=jnp.float32,
        )
        key_grad = (
            jnp.einsum("shqk,qshd->kshd", low_grads, queries, preferred_element_type=jnp.float32)
            * head_scale
        )
        block_grad = jnp.concatenate(
            [
                key_grad.reshape(span_rows, pair_count, model_width),
                value_grad.reshape(span_rows, pair_count, model_width),
            ],
            axis=-1,
        )
        return (new_state, block_grad)

    (query_grad, step_grad), kv_terms = lax.scan(
        grad_step, start_state, (back_blocks, block_starts)
    )
    kv_terms = kv_terms.reshape(seq_len, pair_count, 2 * model_width)
    keyval_grad = lax.psum_scatter(
        kv_terms.astype(jnp.bfloat16), "cp", scatter_dimension=0, tiled=True
    )
    table_grad = step_grad - jnp.concatenate(
        [step_grad[:, 1:], jnp.zeros((head_count, 1), jnp.float32)], axis=1
    )
    qkv_grad = jnp.concatenate(
        [query_grad.reshape(span_rows, pair_count, model_width).astype(jnp.bfloat16), keyval_grad],
        axis=-1,
    )
    qkv_weight_grad = jnp.einsum(
        "csd,cse->de", normed_first, qkv_grad, preferred_element_type=jnp.float32
    )
    grad_normed_first = jnp.einsum(
        "cse,de->csd", qkv_grad, w_qkv, preferred_element_type=jnp.float32
    )
    gain_first_grad = jnp.sum(grad_normed_first * inputs * scale_first, axis=(0, 1))
    tokens_grad = (
        grad_hidden + norm_back(grad_normed_first, inputs, scale_first, norm1_gain)
    ).astype(jnp.bfloat16)
    attn_term = jnp.concatenate([qkv_weight_grad, out_grad], axis=1)
    w_attn_grad = lax.psum_scatter(attn_term, ("dp", "ep", "cp"), scatter_dimension=1, tiled=True)
    router_sum, table_sum, gain_first_sum, gain_second_sum = lax.psum(
        (router_grad, table_grad, gain_first_grad, gain_second_grad), ("dp", "ep", "cp")
    )
    gate_sum, up_sum, down_sum = (
        lax.psum_scatter(
            gate_grad.astype(jnp.bfloat16), ("dp", "cp"), scatter_dimension=2, tiled=True
        ).astype(jnp.float32),
        lax.psum_scatter(
            up_grad.astype(jnp.bfloat16), ("dp", "cp"), scatter_dimension=2, tiled=True
        ).astype(jnp.float32),
        lax.psum_scatter(
            down_grad.astype(jnp.bfloat16), ("dp", "cp"), scatter_dimension=2, tiled=True
        ).astype(jnp.float32),
    )
    return (
        mixed,
        tokens_grad,
        w_attn_grad,
        table_sum,
        gain_first_sum,
        gain_second_sum,
        router_sum,
        gate_sum,
        up_sum,
        down_sum,
    )


minus_big = -1000000000.0
vmem_bytes = 60 * 1024 * 1024


cost_share = 0.05


def cost(flops, moved):
    return pl.CostEstimate(
        flops=int(flops * cost_share), bytes_accessed=int(moved * cost_share), transcendentals=0
    )


def held(kernel, at, count):
    def run(*refs):
        kernel(*refs[:at], *refs[at + count :])

    return run


def anywhere(arrays):
    return [pl.BlockSpec(memory_space=pl.ANY)] * len(arrays)


def compiler_params():
    return pltpu.CompilerParams(vmem_limit_bytes=vmem_bytes)


def shear(values, leftward):
    rows, lanes = values.shape
    row_ids = lax.broadcasted_iota(jnp.int32, (rows, lanes), 0)
    bit = 1
    while bit < rows:
        amount = lanes - bit if leftward else bit
        moved = pltpu.roll(values, amount, 1)
        values = jnp.where((row_ids & bit) != 0, moved, values)
        bit *= 2
    return values


def dot_nt(left, right):
    return lax.dot_general(
        left, right, (((1,), (1,)), ((), ())), preferred_element_type=jnp.float32
    )


def dot_tn(left, right):
    return lax.dot_general(
        left, right, (((0,), (0,)), ((), ())), preferred_element_type=jnp.float32
    )


def dot_nn(left, right):
    return jnp.dot(left, right, preferred_element_type=jnp.float32)


def key_masks(length, blocks, span_rows):
    masks = []
    for block in range(blocks):
        position = block * span_rows + lax.broadcasted_iota(jnp.int32, (1, span_rows), 1)
        masks.append(jnp.where(position < length, 0.0, minus_big))
    return masks


def forward_body(
    mine, length, scale, head_size, qkv_ref, bias_ref, low_ref, full_ref, total_ref, after_pair
):
    blocks, span_rows, width = qkv_ref.shape
    lanes = 128
    lane = lax.broadcasted_iota(jnp.int32, (1, lanes), 1)
    masks = key_masks(length, blocks, span_rows)
    halves = lanes // head_size

    def place(block):
        return lax.rem(mine - block + blocks, blocks)

    def one_pair(pair, carry):
        wide = pl.multiple_of(pair * (3 * lanes), lanes)
        own_lanes = pl.ds(pl.multiple_of(pair * lanes, lanes), lanes)
        part = [pl.ds(pl.multiple_of(wide + which * lanes, lanes), lanes) for which in range(3)]
        for row in range(blocks):
            queries = qkv_ref[place(row), :, part[0]]
            totals = jnp.zeros((span_rows, lanes), jnp.float32)
            result = jnp.zeros((span_rows, lanes), jnp.float32)
            for half in range(halves):
                own = lane // head_size == half
                head_q = queries * jnp.where(own, scale, 0.0).astype(jnp.bfloat16)
                head_v = jnp.where(own, 1.0, 0.0).astype(jnp.bfloat16)
                logits = []
                for column in range(row + 1):
                    at = (blocks - 1 - row + column) * span_rows
                    term = dot_nt(head_q, qkv_ref[place(column), :, part[1]])
                    bias = bias_ref[pair * halves + half, :, at : at + span_rows]
                    logits.append(term + bias + masks[column])
                peak = jnp.max(logits[0], axis=1, keepdims=True)
                for term in logits[1:]:
                    peak = jnp.maximum(peak, jnp.max(term, axis=1, keepdims=True))
                total = jnp.zeros((span_rows, 1), jnp.float32)
                mixed = jnp.zeros((span_rows, lanes), jnp.float32)
                for column in range(row + 1):
                    weights = jnp.exp(logits[column] - peak)
                    total = total + jnp.sum(weights, axis=1, keepdims=True)
                    values = qkv_ref[place(column), :, part[2]] * head_v
                    mixed = mixed + dot_nn(weights.astype(jnp.bfloat16), values)
                result = result + mixed / total
                totals = jnp.where(lane == half, peak + jnp.log(total), totals)
            low_ref[place(row), :, own_lanes] = result.astype(jnp.bfloat16)
            full_ref[row, :, own_lanes] = result
            total_ref[row, :, own_lanes] = totals
        after_pair(pair)
        return carry

    lax.fori_loop(0, width // (3 * lanes), one_pair, 0)


def backward_body(
    mine, length, scale, head_size, qkv_ref, bias_ref, grad_ref, full_ref, total_ref, ring_ref, line_ref, work,
    after_pair=None,
):
    key_sum, value_sum, plane = work
    blocks, span_rows, width = qkv_ref.shape
    lanes = 128
    lane = lax.broadcasted_iota(jnp.int32, (1, lanes), 1)
    masks = key_masks(length, blocks, span_rows)
    halves = lanes // head_size

    def place(block):
        return lax.rem(mine - block + blocks, blocks)

    def one_pair(pair, carry):
        wide = pl.multiple_of(pair * (3 * lanes), lanes)
        own_lanes = pl.ds(pl.multiple_of(pair * lanes, lanes), lanes)
        part = [pl.ds(pl.multiple_of(wide + which * lanes, lanes), lanes) for which in range(3)]
        key_sum[...] = jnp.zeros_like(key_sum)
        value_sum[...] = jnp.zeros_like(value_sum)
        plane[...] = jnp.zeros_like(plane)
        for row in range(blocks):
            queries = qkv_ref[place(row), :, part[0]]
            grads = grad_ref[lax.rem(row - mine + blocks, blocks), :, own_lanes]
            products = grads.astype(jnp.float32) * full_ref[row, :, own_lanes]
            totals = total_ref[row, :, own_lanes]
            query_sum = jnp.zeros((span_rows, lanes), jnp.float32)
            for half in range(halves):
                own = lane // head_size == half
                one = jnp.where(own, 1.0, 0.0).astype(jnp.bfloat16)
                head_q = queries * jnp.where(own, scale, 0.0).astype(jnp.bfloat16)
                head_g = grads * one
                delta = jnp.sum(jnp.where(own, products, 0.0), axis=1, keepdims=True)
                total = totals[:, half : half + 1]
                for column in range(row + 1):
                    at = (blocks - 1 - row + column) * span_rows
                    keys = qkv_ref[place(column), :, part[1]]
                    logits = dot_nt(head_q, keys)
                    bias = bias_ref[pair * halves + half, :, at : at + span_rows]
                    logits = logits + bias + masks[column]
                    weights = jnp.exp(logits - total)
                    weight_grads = dot_nt(head_g, qkv_ref[place(column), :, part[2]])
                    score_grads = weights * (weight_grads - delta)
                    plane[half, :, at : at + span_rows] += score_grads
                    low_weights = weights.astype(jnp.bfloat16)
                    low_grads = score_grads.astype(jnp.bfloat16)
                    query_sum = query_sum + dot_nn(low_grads, keys * one)
                    key_sum[column] += dot_tn(low_grads, head_q)
                    value_sum[column] += dot_tn(low_weights, head_g)
            ring_ref[place(row), :, part[0]] = (query_sum * scale).astype(jnp.bfloat16)
        for row in range(blocks):
            ring_ref[place(row), :, part[1]] = key_sum[row].astype(jnp.bfloat16)
            ring_ref[place(row), :, part[2]] = value_sum[row].astype(jnp.bfloat16)
        for half in range(halves):
            full = jnp.concatenate(
                [plane[half], jnp.zeros((span_rows, span_rows), jnp.float32)], axis=1
            )
            summed = jnp.sum(shear(full, True), axis=0, keepdims=True)
            line_ref[pair * halves + half] = pltpu.roll(summed, span_rows - 1, 1)
        if after_pair is not None:
            after_pair(pair)
        return carry

    lax.fori_loop(0, width // (3 * lanes), one_pair, 0)


def backward_work(blocks, span_rows, head_size):
    return [
        pltpu.VMEM((blocks, span_rows, 128), jnp.float32),
        pltpu.VMEM((blocks, span_rows, 128), jnp.float32),
        pltpu.VMEM((128 // head_size, span_rows, blocks * span_rows), jnp.float32),
    ]


def greet(*others):
    barrier = pltpu.get_barrier_semaphore()
    for other in others:
        pl.semaphore_signal(
            barrier, inc=1, device_id=other, device_id_type=pl.DeviceIdType.MESH
        )
    pl.semaphore_wait(barrier, len(others))


def push(source, target, send_sem, recv_sem, other):
    return pltpu.make_async_remote_copy(
        src_ref=source,
        dst_ref=target,
        send_sem=send_sem,
        recv_sem=recv_sem,
        device_id=other,
        device_id_type=pl.DeviceIdType.MESH,
    )


def ring_others(mine, count):
    return [{"cp": lax.rem(mine + j, count)} for j in range(1, count)]


def slot_of(ref, slot, slots):
    width = ref.shape[1] // slots
    return ref.at[:, pl.ds(slot * width, width)]


def deliveries(source, target, sems, mine, count, lanes=None):
    return [
        push(
            source.at[j] if lanes is None else source.at[j, :, lanes],
            target.at[j],
            sems.at[0, j],
            sems.at[1, j],
            {"cp": lax.rem(mine + (count - j), count)},
        )
        for j in range(1, count)
    ]


def remote_params(number):
    return pltpu.CompilerParams(
        vmem_limit_bytes=vmem_bytes, collective_id=number, has_side_effects=True
    )


def own_rows(block, length, span_rows):
    position = block * span_rows + lax.broadcasted_iota(jnp.int32, (span_rows, 1), 0)
    return jnp.where(position < length, 1.0, 0.0)


def router_of(rows, router_w, experts):
    lane = lax.broadcasted_iota(jnp.int32, (1, router_w.shape[1]), 1)
    logits = jnp.where(lane < experts, dot_nn(rows, router_w), minus_big)
    shares = jnp.exp(logits - jnp.max(logits, axis=1, keepdims=True))
    return shares / jnp.sum(shares, axis=1, keepdims=True)


def project_body(mine, length, input_ref, gain_ref, weight_ref, parts_ref, own_ref, attended_ref, hidden_ref, normed_ref):
    count, span_rows, width = parts_ref.shape
    for j in range(count):
        owner = lax.rem(mine + j, count)
        for group in range(width // 128):
            at = pl.multiple_of((group * count + owner) * 128, 128)
            lanes = slice(group * 128, (group + 1) * 128)
            attended_ref[:, pl.ds(at, 128)] = own_ref[0, :, lanes] if j == 0 else parts_ref[j, :, lanes]
    projected = dot_nn(attended_ref[...], weight_ref[...])
    hidden = input_ref[...].astype(jnp.float32) + own_rows(mine, length, span_rows) * projected
    hidden_ref[...] = hidden
    normed_ref[...] = (hidden * root_scale(hidden) * gain_ref[...]).astype(jnp.bfloat16)


def pick_body(base, capacity, experts, chosen, parts, out_ref):
    for expert in range(experts):
        picked = None
        for choice_ref, part in zip(chosen, parts):
            span = part.shape[0]
            ids = lax.broadcasted_iota(jnp.int32, (capacity, span), 0) + (base + expert * capacity)
            hot = jnp.zeros((capacity, span), jnp.float32)
            for choice in range(choice_ref.shape[0]):
                hot = hot + jnp.where(ids == choice_ref[choice : choice + 1, :], 1.0, 0.0)
            term = dot_nn(hot.astype(jnp.bfloat16), part[...])
            picked = term if picked is None else picked + term
        out_ref[expert] = picked.astype(jnp.bfloat16)


def front_kernel(
    scale, head_size, slots, length_ref, gain_first_ref, gain_second_ref, line_ref, target_ref, w_attn_ref, weight_ref,
    tokens_ref, cotangent_ref, *refs
):
    inputs = [slot_of(tokens_ref, s, slots) for s in range(slots)]
    grads = [slot_of(cotangent_ref, s, slots) for s in range(slots)]
    stores_to, own_w, targets_ref = refs[:5], refs[5], refs[6]
    over_ref, up_ref = refs[7:9]
    picks = [refs[9 + 2 * i : 11 + 2 * i] for i in range(2)]
    outs = [refs[13 + 3 * s : 16 + 3 * s] for s in range(slots)]
    refs = refs[13 + 3 * slots :]
    low, arrived, near_grads, ring_sems, own_sems, give_sems, plane_sems, target_sems = refs[:8]
    core_sems, normed_sems, store_sems, *made = refs[8:]
    all_ref, qkv_ref, bias_ref, full_ref, total_ref = made
    _, count, span_rows, model_width = all_ref.shape

    def store(which, slot):
        source, target = made[which], stores_to[which]
        if which != 2:
            source, target = source.at[slot], target.at[slot]
        return pltpu.make_async_copy(source, target, store_sems.at[which, slot])

    groups = own_w.shape[1] // 384
    mine = lax.axis_index("cp")
    dp, ep = lax.axis_index("dp"), lax.axis_index("ep")
    core_other, x_other, y_other = near_others(dp, ep)

    loads = []
    for group in range(groups):
        for which in range(3):
            at = which * model_width + (group * count + mine) * 128
            lanes = pl.ds((group * 3 + which) * 128, 128)
            loads.append(
                pltpu.make_async_copy(
                    w_attn_ref.at[:, pl.ds(pl.multiple_of(at, 128), 128)],
                    own_w.at[:, lanes],
                    own_sems.at[group * 3 + which],
                )
            )
    for load in loads:
        load.start()
    for s in range(slots):
        values = inputs[s][...].astype(jnp.float32)
        all_ref[s, 0] = (values * root_scale(values) * gain_first_ref[...]).astype(jnp.bfloat16)
    greet(*ring_others(mine, count), core_other, x_other, y_other)

    def hop_copy(slot, hop):
        return push(
            all_ref.at[slot, hop],
            all_ref.at[slot, hop + 1],
            ring_sems.at[0, slot, hop],
            ring_sems.at[1, slot, hop],
            {"cp": lax.rem(mine + 1, count)},
        )

    for s in range(slots):
        hop_copy(s, 0).start()

    def plane_copies(source, target, sems):
        first = [
            push(source(s), target.at[way, s], sems.at[0, way, s], sems.at[1, way, s], other)
            for s in (0, 1)
            for way, other in ((0, x_other), (1, y_other))
        ]
        second = [
            push(target.at[0, 0], target.at[2, 0], sems.at[0, 2, 0], sems.at[1, 2, 0], y_other),
            push(target.at[1, 1], target.at[2, 1], sems.at[0, 2, 1], sems.at[1, 2, 1], x_other),
        ]
        return first, second

    grad_first, grad_second = plane_copies(lambda s: grads[s], near_grads, plane_sems)
    near_targets = targets_ref.at[pl.ds(1, 3)]
    place_first, place_second = plane_copies(lambda s: target_ref.at[s], near_targets, target_sems)
    for copy in place_first + grad_first:
        copy.start()
    targets_ref[0] = target_ref[...]
    for load in loads:
        load.wait()
    for s in range(slots):
        qkv_ref[s, 0] = dot_nn(all_ref[s, 0], own_w[...]).astype(jnp.bfloat16)
    columns = bias_ref.shape[2]
    lanes = span_rows + columns
    for head in range(bias_ref.shape[0]):
        line = pltpu.roll(line_ref[head], lanes - (span_rows - 1), 1)
        full = jnp.broadcast_to(line, (span_rows, lanes))
        bias_ref[head] = shear(full, False)[:, :columns]
    store(2, 0).start()

    _, experts, capacity, _ = picks[0][0].shape
    base = ep * (experts * capacity)
    at_of = ((0, 0), (1, 0), (1, 1), (1, 2))

    def pick(source):
        if source == 0:
            parts = grads
        else:
            parts = [near_grads.at[source - 1, s] for s in range(slots)]
        chosen = [targets_ref.at[source, s] for s in range(slots)]
        group, at = at_of[source]
        pick_body(base, capacity, experts, chosen, parts, picks[group][0].at[at])
        core_copy(source).start()

    def core_copy(source):
        group, at = at_of[source]
        return push(
            picks[group][0].at[at],
            picks[group][1].at[at],
            core_sems.at[0, source],
            core_sems.at[1, source],
            core_other,
        )

    def normed_copy(at):
        source, target, other = (
            (outs[0][2], over_ref, x_other),
            (outs[0][2], up_ref, y_other),
        )[at]
        return push(source, target, normed_sems.at[0, at], normed_sems.at[1, at], other)

    def project(slot):
        for pair in range(groups):
            for copy in gives(slot, pair):
                copy.wait()
        project_body(
            mine, length_ref[slot], inputs[slot], gain_second_ref, weight_ref, arrived.at[slot],
            low.at[slot], *outs[slot],
        )

    def gives(slot, pair):
        part = pl.ds(pl.multiple_of(pair * 128, 128), 128)
        return [
            push(
                low.at[slot, j, :, part],
                arrived.at[slot, j, :, part],
                give_sems.at[0, slot, pair, j],
                give_sems.at[1, slot, pair, j],
                {"cp": lax.rem(mine + (count - j), count)},
            )
            for j in range(1, count)
        ]

    def attend(slot):
        def after_pair(pair):
            for copy in gives(slot, pair):
                copy.start()
            if slot > 0:

                @pl.when(pair == 0)
                def _():
                    project(slot - 1)
                    for at in range(2):
                        normed_copy(at).start()

        forward_body(
            mine, length_ref[slot], scale, head_size, qkv_ref.at[slot], bias_ref, low.at[slot],
            full_ref.at[slot], total_ref.at[slot], after_pair,
        )
        for which in (0, 1, 3, 4):
            store(which, slot).start()

    pick(0)
    for hop in range(1, count):
        for s in range(slots):
            hop_copy(s, hop - 1).wait_recv()
            if hop < count - 1:
                hop_copy(s, hop).start()
            qkv_ref[s, hop] = dot_nn(all_ref[s, hop], own_w[...]).astype(jnp.bfloat16)
            if hop == count - 1 and s + 1 < slots:
                attend(s)
        if hop == 1:
            for copy in place_first + grad_first:
                copy.wait_recv()
            for copy in place_second + grad_second:
                copy.start()
            pick(1)
            pick(2)
        if hop == 2:
            for copy in place_second + grad_second:
                copy.wait_recv()
            pick(3)
    attend(slots - 1)
    project(slots - 1)
    for s in range(slots):
        for hop in range(count - 1):
            hop_copy(s, hop).wait_send()
    for copy in place_first + grad_first + place_second + grad_second:
        copy.wait_send()
    for at in range(2):
        normed_copy(at).wait()
    for source in range(4):
        core_copy(source).wait()
    store(2, 0).wait()
    for s in range(slots):
        for which in (0, 1, 3, 4):
            store(which, s).wait()


def front(lengths, gain_first, gain_second, lines, target, w_attn, inputs, grads, slots, count, experts, capacity, scale, head_size):
    span_rows, model_width = inputs.shape[0], inputs.shape[1] // slots
    heads, _, lanes = lines.shape
    own_width = 3 * model_width // count
    groups = own_width // 384
    choices = target.shape[1]
    whole = pl.BlockSpec(memory_space=pltpu.VMEM)
    f32, bf16 = jnp.float32, jnp.bfloat16
    shape = jax.ShapeDtypeStruct
    made = (
        ((slots, count, span_rows, model_width), bf16),
        ((slots, count, span_rows, own_width), bf16),
        ((heads, span_rows, lanes - span_rows), f32),
        ((slots, count, span_rows, groups * 128), f32),
        ((slots, count, span_rows, groups * 128), f32),
    )
    got = pl.pallas_call(
        functools.partial(front_kernel, scale, head_size, slots),
        grid=(1,),
        in_specs=[
            pl.BlockSpec(memory_space=pltpu.SMEM),
            whole,
            whole,
            whole,
            whole,
            pl.BlockSpec(memory_space=pl.ANY),
            pl.BlockSpec((model_width, model_width), lambda i: (0, 3)),
            whole,
            whole,
        ],
        out_specs=[pl.BlockSpec(memory_space=pl.ANY)] * 5 + [whole] * (8 + 3 * slots),
        out_shape=[
            *(shape(*kind) for kind in made),
            shape((model_width, own_width), bf16),
            shape((4, slots, choices, span_rows), jnp.int32),
        ]
        + [shape((span_rows, model_width), bf16)] * 2
        + [
            shape((sources, experts, capacity, model_width), bf16)
            for sources in (1, 3)
            for _ in range(2)
        ]
        + [
            shape((span_rows, model_width), bf16),
            shape((span_rows, model_width), f32),
            shape((span_rows, model_width), bf16),
        ]
        * slots,
        scratch_shapes=[
            pltpu.VMEM((slots, count, span_rows, groups * 128), bf16),
            pltpu.VMEM((slots, count, span_rows, groups * 128), bf16),
            pltpu.VMEM((3, slots, span_rows, model_width), bf16),
            pltpu.SemaphoreType.DMA((2, slots, count - 1)),
            pltpu.SemaphoreType.DMA((3 * groups,)),
            pltpu.SemaphoreType.DMA((2, slots, groups, count)),
            pltpu.SemaphoreType.DMA((2, 3, slots)),
            pltpu.SemaphoreType.DMA((2, 3, slots)),
            pltpu.SemaphoreType.DMA((2, 4)),
            pltpu.SemaphoreType.DMA((2, 2)),
            pltpu.SemaphoreType.DMA((5, slots)),
            *(pltpu.VMEM(*kind) for kind in made),
        ],
        cost_estimate=cost(60e9, 20e6),
        compiler_params=remote_params(0),
        name="front",
    )(lengths, gain_first, gain_second, lines, target, w_attn, w_attn, inputs, grads)
    pairs = [got[9 + 2 * i : 11 + 2 * i] for i in range(2)]
    return got[:9], pairs, [got[13 + 3 * s : 16 + 3 * s] for s in range(slots)]


def hidden_body(
    experts, mine, length, back_ref, grad_ref, hidden_ref, normed_ref, gain_ref, router_ref, weight_ref,
    hidden_grad_ref, proj_ref, router_grad_ref, gain_grad_ref, leaving_ref, attended,
):
    count = leaving_ref.shape[0]
    span_rows, model_width = hidden_ref.shape
    back = back_ref[...]
    normed = normed_ref[...]
    probs = router_of(normed, router_ref[...], experts)
    shares = back[:, model_width:]
    logit_grads = probs * (shares - jnp.sum(probs * shares, axis=1, keepdims=True))
    logit_grads = logit_grads.astype(jnp.bfloat16)
    router_grad_ref[...] = dot_tn(logit_grads, normed)
    grads = back[:, :model_width] + dot_nt(logit_grads, router_ref[...])
    hidden = hidden_ref[...]
    scale_rows = root_scale(hidden)
    gain_grad_ref[...] = jnp.sum(grads * hidden * scale_rows, axis=0, keepdims=True)
    hidden_grads = grad_ref[...].astype(jnp.float32) + norm_back(
        grads, hidden, scale_rows, gain_ref[...]
    )
    hidden_grad_ref[...] = hidden_grads
    proj = (own_rows(mine, length, span_rows) * hidden_grads).astype(jnp.bfloat16)
    proj_ref[...] = proj
    attended[...] = dot_nt(proj, weight_ref[...]).astype(jnp.bfloat16)
    for j in range(count):
        owner = lax.rem(mine + (count - j), count)
        for group in range(leaving_ref.shape[2] // 128):
            at = pl.multiple_of((group * count + owner) * 128, 128)
            leaving_ref[j, :, group * 128 : (group + 1) * 128] = attended[:, pl.ds(at, 128)]


def hidden_kernel(
    experts, scale, head_size, slots, length_ref, gain_ref, router_ref, weight_ref, qkv_all, bias_all, full_all, total_all,
    cotangent_ref, *refs
):
    per_slot = [
        (refs[3 * s], slot_of(cotangent_ref, s, slots), *refs[3 * s + 1 : 3 * s + 3])
        for s in range(slots)
    ]
    refs = refs[3 * slots :]
    own_out, rest_out, refs = refs[:slots], refs[slots : 4 * slots], refs[4 * slots :]
    outs = [refs[4 * s : 4 * s + 4] for s in range(slots)]
    mixed = [slot_of(refs[4 * slots], s, slots) for s in range(slots)]
    refs = refs[4 * slots + 1 :]
    ring_ref, line_ref, rest_ref, leaving, arriving, attended, sems = refs[:7]
    got, far, last, low, out_sems = refs[7:12]
    qkv_ref, bias_ref, full_ref, total_ref, held_out, load_sems = refs[12:18]
    work = refs[18:]
    count = qkv_ref.shape[0]
    mine = lax.axis_index("cp")
    _, x_other, y_other = near_others(lax.axis_index("dp"), lax.axis_index("ep"))
    over, up, across = (rest_out[i * slots : (i + 1) * slots] for i in range(3))
    loads = [
        pltpu.make_async_copy(source, target, load_sems.at[at])
        for at, (source, target) in enumerate(
            (
                (qkv_all.at[0], qkv_ref),
                (bias_all, bias_ref),
                (full_all.at[0], full_ref),
                (total_all.at[0], total_ref),
                (up[0], held_out.at[0]),
                (over[1], held_out.at[1]),
                (own_out[0], held_out.at[2]),
                (own_out[1], held_out.at[3]),
            )
        )
    ]
    for load in loads:
        load.start()
    greet(*ring_others(mine, count), x_other, y_other)

    def out_copy(at):
        source, target, other = (
            (over[0], got.at[0], x_other),
            (up[1], got.at[1], y_other),
            (across[0], far.at[0], x_other),
            (across[1], far.at[1], y_other),
            (low.at[0], last.at[0], y_other),
            (low.at[1], last.at[1], x_other),
        )[at]
        return push(source, target, out_sems.at[0, at], out_sems.at[1, at], other)

    def after_pair(pair):
        @pl.when(pair == 0)
        def _():
            for at in range(2):
                out_copy(2 + at).wait()
                summed = held_out[at].astype(jnp.float32) + far[at].astype(jnp.float32)
                low[at] = summed.astype(jnp.bfloat16)
                out_copy(4 + at).start()

    for at in (2, 3, 0, 1):
        out_copy(at).start()
    copies = []
    for s in range(slots):
        hidden_body(
            experts, mine, length_ref[s], *per_slot[s], gain_ref, router_ref, weight_ref,
            *outs[s], leaving.at[s], attended,
        )
        target = arriving if s == 0 else rest_ref.at[s - 1]
        copies.append(deliveries(leaving.at[s], target, sems.at[s], mine, count))
        if s == 0:
            for copy in copies[s]:
                copy.start()
        target[0] = leaving[s, 0]
    for copy in copies[0]:
        copy.wait()
    for some in copies[1:]:
        for copy in some:
            copy.start()
    for load in loads:
        load.wait()
    backward_body(
        mine, length_ref[0], scale, head_size, qkv_ref, bias_ref, arriving, full_ref, total_ref,
        ring_ref, line_ref, work, after_pair,
    )
    for s in range(slots):
        out_copy(s).wait()
        out_copy(4 + s).wait()
        home = held_out[2 + s].astype(jnp.float32) + got[s].astype(jnp.float32)
        home = per_slot[s][2][...] + home + last[s].astype(jnp.float32)
        mixed[s][...] = home.astype(jnp.bfloat16)
    for copy in (copy for some in copies[1:] for copy in some):
        copy.wait()


def hidden_back(
    lengths, back_rows, grads, hidden, normed, gain, router, w_attn, experts, qkvs, bias, full, total, own_out,
    rest_out, scale, head_size,
):
    slots, count, span_rows, own_width = qkvs.shape
    model_width = hidden[0].shape[1]
    heads = bias.shape[0]
    whole = pl.BlockSpec(memory_space=pltpu.VMEM)
    f32, bf16 = jnp.float32, jnp.bfloat16
    each = [grads]
    for s in range(slots):
        each += [back_rows[s], hidden[s], normed[s]]
    each += [*own_out, *rest_out]
    own_shape = (count, span_rows, own_width // 3)
    got = pl.pallas_call(
        functools.partial(hidden_kernel, experts, scale, head_size, slots),
        grid=(1,),
        in_specs=[
            pl.BlockSpec(memory_space=pltpu.SMEM),
            whole,
            whole,
            pl.BlockSpec((model_width, model_width), lambda i: (0, 3)),
            *[pl.BlockSpec(memory_space=pl.ANY)] * 4,
        ]
        + [whole] * (len(each) - 4 * slots)
        + [pl.BlockSpec(memory_space=pl.ANY)] * (4 * slots),
        out_specs=[whole] * (4 * slots + 4),
        out_shape=[
            jax.ShapeDtypeStruct((span_rows, model_width), f32),
            jax.ShapeDtypeStruct((span_rows, model_width), bf16),
            jax.ShapeDtypeStruct((router.shape[1], model_width), f32),
            jax.ShapeDtypeStruct((1, model_width), f32),
        ]
        * slots
        + [jax.ShapeDtypeStruct((span_rows, slots * model_width), bf16)]
        + [
            jax.ShapeDtypeStruct(qkvs.shape[1:], bf16),
            jax.ShapeDtypeStruct((heads, 1, bias.shape[2] + span_rows), f32),
            jax.ShapeDtypeStruct((slots - 1,) + own_shape, bf16),
        ],
        scratch_shapes=[
            pltpu.VMEM((slots,) + own_shape, bf16),
            pltpu.VMEM(own_shape, bf16),
            pltpu.VMEM((span_rows, model_width), bf16),
            pltpu.SemaphoreType.DMA((slots, 2, count)),
            *[pltpu.VMEM((slots, span_rows, model_width), bf16)] * 4,
            pltpu.SemaphoreType.DMA((2, 6)),
            pltpu.VMEM(qkvs.shape[1:], bf16),
            pltpu.VMEM(bias.shape, f32),
            pltpu.VMEM(full.shape[1:], f32),
            pltpu.VMEM(full.shape[1:], f32),
            pltpu.VMEM((2 * slots, span_rows, model_width), bf16),
            pltpu.SemaphoreType.DMA((8,)),
        ]
        + backward_work(count, span_rows, head_size),
        cost_estimate=cost(20e9, 20e6),
        compiler_params=remote_params(1),
        name="hidden_back",
    )(lengths, gain, router, w_attn, qkvs, bias, full, total, *each)
    return [got[4 * s : 4 * s + 4] for s in range(slots)], got[4 * slots], got[4 * slots + 1 :]


def near_others(dp, ep):
    core, across = lax.rem(dp, 2), dp // 2
    return (
        {"dp": across * 2 + (1 - core)},
        {"dp": (1 - across) * 2 + core},
        {"ep": 1 - ep},
    )


def second_kernel(
    scale, head_size, slots, length_ref, former_ref, normed_all, qkv_all, bias_all, grad_ref, full_all, total_all,
    *refs,
):
    attended, proj, refs = refs[:slots], refs[slots : 2 * slots], refs[2 * slots :]
    own_w_all, gain_ref, refs = refs[0], refs[1], refs[2:]
    ring_ref, line_ref, arrived_ref, early_ref, weight_ref, rows_ref, gain_grad_ref = refs[:7]
    refs = refs[1:]
    sums, low, got_core, got_x, got_y, leaving, coming, sems, near_sems, last_sems = refs[6:16]
    early_sems, held_refs, work = refs[16], refs[17:24], refs[24:]
    normed_ref, qkv_ref, bias_ref, full_ref, total_ref, own_w_ref, load_sems = held_refs
    count = qkv_ref.shape[0]
    mine = lax.axis_index("cp")
    loads = [
        pltpu.make_async_copy(source, target, load_sems.at[at])
        for at, (source, target) in enumerate(
            (
                (qkv_all.at[1], qkv_ref),
                (bias_all, bias_ref),
                (full_all.at[1], full_ref),
                (total_all.at[1], total_ref),
                (normed_all, normed_ref),
                (own_w_all, own_w_ref),
            )
        )
    ]
    for load in loads:
        load.start()
    dp, ep = lax.axis_index("dp"), lax.axis_index("ep")
    core, across = lax.rem(dp, 2), dp // 2
    others = near_others(dp, ep)
    greet(*ring_others(mine, count), *others)
    copies = deliveries(former_ref, arrived_ref, sems, mine, count)
    for copy in copies:
        copy.start()
    arrived_ref[0] = former_ref[0]
    height = sums.shape[0] // 2
    sizes = (height, height // 2, height // 4)
    bits = (core, across, ep)
    landing = (got_core, got_x, got_y)
    total = None
    for s in range(slots):
        term = dot_tn(attended[s][...], proj[s][...])
        total = term if total is None else total + term
    sums[...] = total

    def low_part(stage):
        return low.at[stage, pl.ds(0, sizes[stage])]

    def stage_copy(stage):
        return push(
            low_part(stage), landing[stage], near_sems.at[0, stage], near_sems.at[1, stage], others[stage]
        )

    def start_of(stage):
        start = 0
        for former in range(stage):
            start = start + bits[former] * sizes[former]
        return start

    def begin(stage):
        at = start_of(stage) + (1 - bits[stage]) * sizes[stage]
        away = sums[pl.ds(pl.multiple_of(at, 128), sizes[stage]), :]
        low[stage, : sizes[stage]] = away.astype(jnp.bfloat16)
        stage_copy(stage).start()

    def finish(stage):
        stage_copy(stage).wait()
        at = pl.ds(pl.multiple_of(start_of(stage + 1), 128), sizes[stage])
        sums[at, :] = sums[at, :] + landing[stage][...].astype(jnp.float32)

    early = deliveries(ring_ref, early_ref, early_sems, mine, count, pl.ds(0, early_ref.shape[2]))

    def after_pair(pair):
        @pl.when(pair == 0)
        def _():
            for copy in early:
                copy.start()

        for stage in range(2):

            @pl.when(pair == stage)
            def _():
                finish(stage)
                begin(stage + 1)

    begin(0)
    for load in loads:
        load.wait()
    backward_body(
        mine, length_ref[1], scale, head_size, qkv_ref, bias_ref, grad_ref.at[0], full_ref, total_ref,
        ring_ref, line_ref, work, after_pair,
    )
    finish(2)
    at = pl.ds(pl.multiple_of(start_of(3), 128), sizes[2])
    groups = leaving.shape[2] // 128
    for j in range(count):
        owner = lax.rem(mine + (count - j), count)
        for group in range(groups):
            lanes = pl.ds(pl.multiple_of((group * count + owner) * 128, 128), 128)
            part = sums[at, lanes]
            leaving[j, :, group * 128 : (group + 1) * 128] = part.astype(jnp.bfloat16)
            if j == 0:
                rows_ref[:, group * 128 : (group + 1) * 128] = part
    last = deliveries(leaving, coming, last_sems, mine, count)
    for copy in last:
        copy.start()
    total = None
    for slot, grads in ((0, former_ref), (1, ring_ref)):
        for j in range(count):
            term = dot_tn(normed_ref[slot, j], grads[j])
            total = term if total is None else total + term
    weight_ref[...] = total
    first_gain = lax.dot_general(
        jnp.ones((8, total.shape[1]), jnp.float32),
        total * own_w_ref[...].astype(jnp.float32),
        (((1,), (1,)), ((), ())),
        precision=lax.Precision.HIGHEST,
        preferred_element_type=jnp.float32,
    )
    gain_grad_ref[...] = first_gain / gain_ref[...]
    for copy in last:
        copy.wait()
    for j in range(1, count):
        rows_ref[...] = rows_ref[...] + coming[j].astype(jnp.float32)
    for copy in copies + early:
        copy.wait()


def second_back(
    lengths, former, normed_all, qkvs, bias, grads, full, total, attended, proj, own_w, gain, scale, head_size, waits=()
):
    slots, count, span_rows, own_width = qkvs.shape
    model_width = normed_all.shape[3]
    whole = pl.BlockSpec(memory_space=pltpu.VMEM)
    some = pl.BlockSpec(memory_space=pl.ANY)
    f32, bf16 = jnp.float32, jnp.bfloat16
    rows_shape = (model_width // 8, own_width // 3)
    return pl.pallas_call(
        held(
            functools.partial(second_kernel, scale, head_size, slots), 10 + 2 * slots, len(waits)
        ),
        grid=(1,),
        in_specs=[
            pl.BlockSpec(memory_space=pltpu.SMEM),
            whole,
            some,
            some,
            some,
            whole,
            some,
            some,
        ]
        + [whole] * (2 * slots)
        + [some, whole]
        + anywhere(waits),
        out_specs=[whole] * 7,
        out_shape=[
            jax.ShapeDtypeStruct(qkvs.shape[1:], bf16),
            jax.ShapeDtypeStruct((bias.shape[0], 1, bias.shape[2] + span_rows), f32),
            jax.ShapeDtypeStruct(qkvs.shape[1:], bf16),
            jax.ShapeDtypeStruct((count, span_rows, 384), bf16),
            jax.ShapeDtypeStruct((model_width, own_width), f32),
            jax.ShapeDtypeStruct(rows_shape, f32),
            jax.ShapeDtypeStruct((8, model_width), f32),
        ],
        scratch_shapes=[
            pltpu.VMEM((model_width, model_width), f32),
            pltpu.VMEM((3, model_width // 2, model_width), bf16),
            pltpu.VMEM((model_width // 2, model_width), bf16),
            pltpu.VMEM((model_width // 4, model_width), bf16),
            pltpu.VMEM((model_width // 8, model_width), bf16),
            pltpu.VMEM((count,) + rows_shape, bf16),
            pltpu.VMEM((count,) + rows_shape, bf16),
            pltpu.SemaphoreType.DMA((2, count)),
            pltpu.SemaphoreType.DMA((2, 3)),
            pltpu.SemaphoreType.DMA((2, count)),
            pltpu.SemaphoreType.DMA((2, count)),
            pltpu.VMEM(normed_all.shape, bf16),
            pltpu.VMEM(qkvs.shape[1:], bf16),
            pltpu.VMEM(bias.shape, f32),
            pltpu.VMEM(full.shape[1:], f32),
            pltpu.VMEM(full.shape[1:], f32),
            pltpu.VMEM(own_w.shape, bf16),
            pltpu.SemaphoreType.DMA((6,)),
        ]
        + backward_work(count, span_rows, head_size),
        cost_estimate=cost(20e9, 20e6),
        compiler_params=remote_params(2),
        name="second_back",
    )(lengths, former, normed_all, qkvs, bias, grads, full, total, *attended, *proj, own_w, gain, *waits)


def token_body(mine, input_ref, hidden_ref, gain_ref, weight_ref, part_refs, own_ref, out_ref):
    count = part_refs[0].shape[0]
    model_width = input_ref.shape[1]
    total = None
    for j in range(count):
        owner = lax.rem(mine + j, count)
        pieces = []
        for group in range(own_ref.shape[2] // 384):
            for which in range(3):
                at = which * model_width + (group * count + owner) * 128
                pieces.append(weight_ref[:, pl.ds(pl.multiple_of(at, 128), 128)])
        part = own_ref[0] if j == 0 else jnp.concatenate([ref[j] for ref in part_refs], axis=1)
        term = dot_nt(part, jnp.concatenate(pieces, axis=1))
        total = term if total is None else total + term
    inputs = input_ref[...].astype(jnp.float32)
    back = norm_back(total, inputs, root_scale(inputs), gain_ref[...])
    out_ref[...] = (hidden_ref[...] + back).astype(jnp.bfloat16)


def final_kernel(
    slots, ring_ref, early_ref, former_all, arrived_ref, blocks_ref, small_ref, gain_ref, weight_all, tokens_ref, *refs
):
    inputs = [slot_of(tokens_ref, s, slots) for s in range(slots)]
    hidden_all, out_ref, refs = refs[:slots], refs[slots], refs[slots + 1 :]
    outs = [slot_of(out_ref, s, slots) for s in range(slots)]
    small_out, attn_out = refs[:2]
    coming, here, sum_blocks, low_blocks, small_now, small_in, sems, near_sems, small_sems = refs[2:11]
    got_core, low_halves, got_halves, low_ends, got_ends, half_sems = refs[11:17]
    former_ref, weight_ref, hidden_refs, load_sems = refs[17:]
    hiddens = [hidden_refs.at[s] for s in range(slots)]
    loads = [
        pltpu.make_async_copy(source, target, load_sems.at[at])
        for at, (source, target) in enumerate(
            (
                (former_all, former_ref),
                (weight_all.at[:, pl.ds(0, weight_ref.shape[1])], weight_ref),
                *((hidden_all[s], hiddens[s]) for s in range(slots)),
            )
        )
    ]
    for load in loads:
        load.start()
    count = ring_ref.shape[0]
    mine = lax.axis_index("cp")
    dp, ep = lax.axis_index("dp"), lax.axis_index("ep")
    core, across = lax.rem(dp, 2), dp // 2
    core_other, x_other, y_other = near_others(dp, ep)
    greet(*ring_others(mine, count), core_other, x_other, y_other)
    late = ring_ref.shape[2] - early_ref.shape[2]
    copies = deliveries(ring_ref, coming, sems, mine, count, pl.ds(early_ref.shape[2], late))
    for copy in copies:
        copy.start()

    small_now[0] = small_ref[...]
    loads[0].wait()
    total = former_ref[...]
    groups = total.shape[1] // 384
    for group in range(groups):
        for which in range(3):
            at = (group * 3 + which) * 128
            part = total[:, at : at + 128]
            sum_blocks[which % 2, which // 2, group] = part
            low_blocks[which % 2, which // 2, group] = part.astype(jnp.bfloat16)
        height = blocks_ref.shape[0]
        here_rows = pl.ds(pl.multiple_of((core * 4 + across * 2 + ep) * height, 128), height)
        part = blocks_ref[:, group * 128 : (group + 1) * 128]
        sum_blocks[1, 1, group] = jnp.zeros_like(sum_blocks[1, 1, group])
        low_blocks[1, 1, group] = jnp.zeros_like(low_blocks[1, 1, group])
        sum_blocks[1, 1, group, here_rows] = part
        low_blocks[1, 1, group, here_rows] = part.astype(jnp.bfloat16)
    first = push(low_blocks.at[1 - core], got_core, near_sems.at[0, 0], near_sems.at[1, 0], core_other)
    first.start()

    stages = [core_other, x_other, y_other]
    step = 1
    while step < count:
        flip = mine + step - 2 * step * lax.rem(mine // step, 2)
        stages.append({"cp": flip})
        step *= 2

    def small_push(at):
        return push(small_now.at[at], small_in.at[at], small_sems.at[0, at], small_sems.at[1, at], stages[at])

    small_push(0).start()
    for load in loads[1:]:
        load.wait()
    token_body(mine, inputs[0], hiddens[0], gain_ref, weight_ref, [arrived_ref], arrived_ref, outs[0])
    first.wait()
    here[...] = sum_blocks[core] + got_core[...].astype(jnp.float32)
    middle = here.shape[2] // 2
    upper, lower = slice(0, middle), slice(middle, 2 * middle)
    for at in range(2):
        low_halves[0, at] = here[1 - across, at, upper].astype(jnp.bfloat16)
        low_halves[1, at] = here[at, 1 - ep, lower].astype(jnp.bfloat16)

    def half_copy(at):
        source, target, other = (
            (low_halves.at[0], got_halves.at[0], x_other),
            (low_halves.at[1], got_halves.at[1], y_other),
            (low_ends.at[0], got_ends.at[0], y_other),
            (low_ends.at[1], got_ends.at[1], x_other),
        )[at]
        return push(source, target, half_sems.at[0, at], half_sems.at[1, at], other)

    half_copy(0).start()
    half_copy(1).start()
    for at in range(len(stages)):
        small_push(at).wait()
        now = small_now[at] + small_in[at]
        if at + 1 < len(stages):
            small_now[at + 1] = now
            small_push(at + 1).start()
        else:
            small_out[...] = now
        if at == 1:
            half_copy(0).wait()
            for k in range(2):
                here[across, k, upper] = here[across, k, upper] + got_halves[0, k].astype(jnp.float32)
            low_ends[0] = here[across, 1 - ep, upper].astype(jnp.bfloat16)
            half_copy(2).start()
            half_copy(1).wait()
            for k in range(2):
                here[k, ep, lower] = here[k, ep, lower] + got_halves[1, k].astype(jnp.float32)
            low_ends[1] = here[1 - across, ep, lower].astype(jnp.bfloat16)
            half_copy(3).start()
    for copy in copies:
        copy.wait()
    token_body(mine, inputs[1], hiddens[1], gain_ref, weight_ref, [early_ref, coming], ring_ref, outs[1])
    half_copy(2).wait()
    attn_out[upper] = here[across, ep, upper] + got_ends[0].astype(jnp.float32)
    half_copy(3).wait()
    attn_out[lower] = here[across, ep, lower] + got_ends[1].astype(jnp.float32)


def final_back(ring, early, former, arrived, blocks, small, gain, w_attn, inputs, hiddens):
    count, span_rows, own_width = ring.shape
    slots = len(hiddens)
    model_width = hiddens[0].shape[1]
    groups = blocks.shape[1] // 128
    whole = pl.BlockSpec(memory_space=pltpu.VMEM)
    f32, bf16 = jnp.float32, jnp.bfloat16
    some = pl.BlockSpec(memory_space=pl.ANY)
    stages = 3 + (count - 1).bit_length()
    tile = (model_width, 128)
    return pl.pallas_call(
        functools.partial(final_kernel, slots),
        grid=(1,),
        in_specs=[
            whole,
            whole,
            some,
            whole,
            whole,
            whole,
            whole,
            some,
            whole,
        ]
        + [some] * slots,
        out_specs=[whole] * 3,
        out_shape=[jax.ShapeDtypeStruct((span_rows, slots * model_width), bf16)]
        + [jax.ShapeDtypeStruct(small.shape, f32), jax.ShapeDtypeStruct(tile, f32)],
        scratch_shapes=[
            pltpu.VMEM((count, span_rows, own_width - early.shape[2]), bf16),
            pltpu.VMEM((2, groups) + tile, f32),
            pltpu.VMEM((2, 2, groups) + tile, f32),
            pltpu.VMEM((2, 2, groups) + tile, bf16),
            pltpu.VMEM((stages,) + small.shape, f32),
            pltpu.VMEM((stages,) + small.shape, f32),
            pltpu.SemaphoreType.DMA((2, count)),
            pltpu.SemaphoreType.DMA((2, 3)),
            pltpu.SemaphoreType.DMA((2, stages)),
            pltpu.VMEM((2, groups) + tile, bf16),
            pltpu.VMEM((2, 2, model_width // 2, 128), bf16),
            pltpu.VMEM((2, 2, model_width // 2, 128), bf16),
            pltpu.VMEM((2, model_width // 2, 128), bf16),
            pltpu.VMEM((2, model_width // 2, 128), bf16),
            pltpu.SemaphoreType.DMA((2, 4)),
            pltpu.VMEM(former.shape, f32),
            pltpu.VMEM((model_width, 3 * model_width), bf16),
            pltpu.VMEM((slots, span_rows, model_width), f32),
            pltpu.SemaphoreType.DMA((2 + slots,)),
        ],
        cost_estimate=cost(20e9, 20e6),
        compiler_params=remote_params(3),
        name="final_back",
    )(ring, early, former, arrived, blocks, small, gain, w_attn, inputs, *hiddens)


gelu_inner = 0.7978845608028654
gelu_cubic = 0.044715


def place_body(base, chosen_ref, pairs, outs):
    capacity = pairs[0][0].shape[0]
    span = outs[0].shape[0]
    both = [
        (mine[...].astype(jnp.float32) + theirs[...].astype(jnp.float32)).astype(jnp.bfloat16)
        for mine, theirs in pairs
    ]
    for at, out in enumerate(outs):
        total = None
        for expert in range(len(pairs)):
            ids = lax.broadcasted_iota(jnp.int32, (span, capacity), 1) + (base + expert * capacity)
            hot = jnp.zeros((span, capacity), jnp.float32)
            for choice in range(chosen_ref.shape[1]):
                chosen = chosen_ref[at * span : (at + 1) * span, choice : choice + 1]
                hot = hot + jnp.where(ids == chosen, 1.0, 0.0)
            term = dot_nn(hot.astype(jnp.bfloat16), both[expert])
            total = term if total is None else total + term
        out[...] = total.astype(jnp.bfloat16)


def return_kernel(experts, slots, target_ref, *refs):
    held_pairs = 2 * (1 + experts)
    back, far_outs, refs = refs[:held_pairs], refs[held_pairs : 2 * held_pairs], refs[2 * held_pairs :]
    backs, refs = refs[:slots], refs[slots:]
    out_own, out_rest, refs = refs[:slots], refs[slots : 4 * slots], refs[4 * slots :]
    here, got, far, last, low = refs[:5]
    outs, load_sems, sems = refs[5 : 5 + held_pairs], refs[5 + held_pairs], refs[6 + held_pairs]
    arriving, core_sems = refs[7 + held_pairs :]
    dp, ep = lax.axis_index("dp"), lax.axis_index("ep")
    core_other, x_other, y_other = near_others(dp, ep)
    base = ep * (experts * back[0].shape[2])
    loads = [
        pltpu.make_async_copy(source, target, load_sems.at[i])
        for i, (source, target) in enumerate(zip(far_outs[:-1], outs[:-1]))
    ]

    def core_copy(at):
        if at == 3:
            source, target = far_outs[-1], outs[-1]
        else:
            source, target = back[-1].at[0, at], arriving.at[0, at]
        return push(source, target, core_sems.at[0, at], core_sems.at[1, at], core_other)

    given = [*back[:-1], arriving]
    for load in loads:
        load.start()

    def rows_of(held_refs, source):
        if source == 0:
            return [(held_refs[0].at[e, 0], held_refs[1].at[e, 0]) for e in range(experts)]
        return [
            (held_refs[2 + 2 * e].at[0, source - 1], held_refs[3 + 2 * e].at[0, source - 1])
            for e in range(experts)
        ]

    def place(held_refs, source, targets):
        if held_refs is given and source > 0:
            core_copy(source - 1).wait()
        place_body(base, target_ref.at[source], rows_of(held_refs, source), targets)

    firsts = [
        push(here.at[1, 0], got.at[0], sems.at[0, 0], sems.at[1, 0], x_other),
        push(here.at[2, 1], got.at[1], sems.at[0, 1], sems.at[1, 1], y_other),
        push(here.at[3, 0], far.at[0], sems.at[0, 2], sems.at[1, 2], x_other),
        push(here.at[3, 1], far.at[1], sems.at[0, 3], sems.at[1, 3], y_other),
    ]
    ends = [
        push(low.at[0], last.at[0], sems.at[0, 4], sems.at[1, 4], y_other),
        push(low.at[1], last.at[1], sems.at[0, 5], sems.at[1, 5], x_other),
    ]
    greet(core_other, x_other, y_other)
    for at in (2, 0, 1, 3):
        core_copy(at).start()
    halves = lambda source: [here.at[source, s] for s in range(slots)]
    place(given, 3, halves(3))
    firsts[2].start()
    firsts[3].start()
    place(given, 1, halves(1))
    firsts[0].start()
    place(given, 2, halves(2))
    firsts[1].start()
    place(given, 0, halves(0))
    for load in loads:
        load.wait()
    core_copy(3).wait()
    for at, (former, source) in enumerate(((2, 2), (3, 1))):
        firsts[former].wait()
        low[at] = (here[source, at].astype(jnp.float32) + far[at].astype(jnp.float32)).astype(jnp.bfloat16)
        ends[at].start()
    place(outs, 0, out_own)
    for source in range(1, 4):
        place(outs, source, out_rest[(source - 1) * slots : source * slots])
    for s in range(slots):
        firsts[s].wait()
        backs[s][...] = here[0, s].astype(jnp.float32) + got[s].astype(jnp.float32)
    for s in range(slots):
        ends[s].wait()
        backs[s][...] = backs[s][...] + last[s].astype(jnp.float32)


def return_rows(targets, backs, outs, slots, waits=()):
    experts = len(backs) // 2 - 1
    model_width = outs[0].shape[-1]
    span_rows = targets.shape[1] // slots
    wide = backs[0].shape[-1]
    whole = pl.BlockSpec(memory_space=pltpu.VMEM)
    f32, bf16 = jnp.float32, jnp.bfloat16
    half = pltpu.VMEM((slots, span_rows, wide), bf16)
    got = pl.pallas_call(
        held(
            functools.partial(return_kernel, experts, slots),
            1 + len(backs) + len(outs),
            len(waits),
        ),
        in_specs=[whole] + [whole] * len(backs) + anywhere(outs) + anywhere(waits),
        out_specs=[whole] * (5 * slots),
        out_shape=[
            *[jax.ShapeDtypeStruct((span_rows, wide), f32)] * slots,
            *[jax.ShapeDtypeStruct((span_rows, model_width), bf16)] * (4 * slots),
        ],
        scratch_shapes=[pltpu.VMEM((4, slots, span_rows, wide), bf16), half, half, half, half]
        + [pltpu.VMEM(a.shape, bf16) for a in outs]
        + [pltpu.SemaphoreType.DMA((len(outs),)), pltpu.SemaphoreType.DMA((2, 6))]
        + [pltpu.VMEM(backs[-1].shape, bf16), pltpu.SemaphoreType.DMA((2, 4))],
        cost_estimate=cost(20e9, 20e6),
        compiler_params=remote_params(4),
        name="return_rows",
    )(targets, *backs, *outs, *waits)
    return got[:slots], got[slots : 2 * slots], got[2 * slots :]


def expert_body(experts, own_units, expert, skip, given, refs, weights, router_ref):
    back_mine, back_theirs, out_mine, out_theirs, kept_rows, kept_units = refs
    gate_ref, up_ref, down_ref = weights
    capacity, model_width = given[0].shape[2:]
    rows = jnp.concatenate([given[0][0, 0], given[1][0, 0]], axis=0)
    grads = jnp.concatenate([given[2][0, 0], given[3][0, 0]], axis=0)
    kept_rows[0, 0, 0] = rows
    kept_rows[1, 0, 0] = grads
    lane = lax.broadcasted_iota(jnp.int32, (1, router_ref.shape[1]), 1)
    probs = router_of(rows, router_ref[...], experts)
    gates = jnp.sum(jnp.where(lane == expert, probs, 0.0), axis=1, keepdims=True)
    unit = lax.broadcasted_iota(jnp.int32, (1, gate_ref.shape[2]), 1) - skip
    own = jnp.logical_and(unit >= 0, unit < own_units)
    gate_w, up_w, down_w = gate_ref[0], up_ref[0], down_ref[0]
    gate_pre = dot_nn(rows, gate_w)
    up_pre = jnp.where(own, dot_nn(rows, up_w), 0.0)
    square = gate_pre * gate_pre
    tanh = jnp.tanh(gelu_inner * gate_pre * (1.0 + gelu_cubic * square))
    half = 0.5 + 0.5 * tanh
    active = gate_pre * half
    slope = half + active * (1.0 - tanh) * (gelu_inner * (1.0 + 3.0 * gelu_cubic * square))
    inner = active * up_pre
    low_inner = inner.astype(jnp.bfloat16)
    plain_grads = jnp.where(own, dot_nn(grads, down_w), 0.0)
    gate_grads = jnp.sum(plain_grads * low_inner.astype(jnp.float32), axis=1, keepdims=True)
    inner_grads = plain_grads * gates
    low_gate = (inner_grads * up_pre * slope).astype(jnp.bfloat16)
    low_up = (inner_grads * active).astype(jnp.bfloat16)
    kept_units[0, 0, 0] = low_gate
    kept_units[1, 0, 0] = low_up
    kept_units[2, 0, 0] = (inner * gates).astype(jnp.bfloat16)
    back = (dot_nt(low_gate, gate_w) + dot_nt(low_up, up_w)).astype(jnp.bfloat16)
    shares = jnp.where(lane == expert, gate_grads, 0.0).astype(jnp.bfloat16)
    out = (gates * dot_nt(low_inner, down_w)).astype(jnp.bfloat16)
    for at, back_ref, out_ref in ((0, back_mine, out_mine), (1, back_theirs, out_theirs)):
        part = slice(at * capacity, (at + 1) * capacity)
        back_ref[0, 0, :, :model_width] = back[part]
        back_ref[0, 0, :, model_width:] = shares[part]
        out_ref[0, 0] = out[part]


def expert_kernel(experts, own_units, kept_count, first_ref, window_ref, *refs):
    given, refs = refs[:4], refs[4:]
    router_ref, weights, refs = refs[0], refs[1:4], refs[4 + kept_count :]
    expert = first_ref[0] + pl.program_id(0)
    expert_body(experts, own_units, expert, window_ref[1], given, refs, weights, router_ref)


def own_kernel(experts, own_units, *refs):
    given_grads, router_ref, weights, refs = refs[:2], refs[2], refs[3:6], refs[6:]
    target_ref, over_ref, up_ref, first_ref, normed_ref, refs = *refs[:5], refs[5:]
    results, kept, (mine_ref, theirs_ref), refs = refs[:4], refs[4:6], refs[6:8], refs[8:]
    coming, picked, held_w, held_rows, held_units = refs[:5]
    sems, core_sems, home_sems, load_sems, keep_sems, own_picked, own_sems = refs[5:]
    given = [own_picked.at[0], own_picked.at[1], *given_grads]
    exp_dev, capacity = picked.shape[1:3]
    dp, ep = lax.axis_index("dp"), lax.axis_index("ep")
    core_other, x_other, y_other = near_others(dp, ep)
    skip = lax.rem(dp * own_units, 128)

    def copy(at):
        source, other = (
            (normed_ref, x_other),
            (normed_ref, y_other),
            (over_ref, y_other),
            (coming.at[1], x_other),
        )[at]
        return push(source, coming.at[at], sems.at[0, at], sems.at[1, at], other)

    def load(expert, which):
        lanes = pl.ds(pl.multiple_of(dp * own_units - skip, 128), held_w.shape[4])
        return pltpu.make_async_copy(
            weights[which].at[pl.ds(expert, 1), :, lanes],
            held_w.at[expert, which],
            load_sems.at[expert, which],
        )

    def keep(expert, kind):
        held_ref = (held_rows, held_units)[kind]
        return pltpu.make_async_copy(
            held_ref.at[expert, :, 0, 0], kept[kind].at[:, expert, 0], keep_sems.at[expert, kind]
        )

    for expert in range(exp_dev):
        for which in range(3):
            load(expert, which).start()
    greet(core_other, x_other, y_other)
    for at in range(3):
        copy(at).start()
    base = ep * (exp_dev * capacity)
    chosen = [target_ref.at[0, s] for s in range(target_ref.shape[1])]
    pick_body(base, capacity, exp_dev, chosen, (first_ref, normed_ref), own_picked.at[0, 0])
    own_copy = push(own_picked.at[0], own_picked.at[1], own_sems.at[0], own_sems.at[1], core_other)
    own_copy.start()
    own_copy.wait()
    for expert in range(exp_dev):
        if expert == 1:
            copy(1).wait_recv()
            copy(3).start()
        for which in range(3):
            load(expert, which).wait()
        here = pl.ds(expert, 1)
        expert_body(
            experts,
            own_units,
            ep * exp_dev + expert,
            skip,
            [part.at[:, here] for part in given],
            [part.at[here] for part in results] + [held_rows.at[expert], held_units.at[expert]],
            [held_w.at[expert, which] for which in range(3)],
            router_ref,
        )
        for kind in range(2):
            keep(expert, kind).start()

    blocks = (
        (over_ref, coming.at[0]),
        (up_ref, coming.at[1]),
        (coming.at[2], coming.at[3]),
    )

    def across_cores(k):
        return push(picked.at[k], theirs_ref.at[k], core_sems.at[0, k], core_sems.at[1, k], core_other)

    def home(k):
        return pltpu.make_async_copy(picked.at[k], mine_ref.at[k], home_sems.at[k])

    for k, waits in enumerate(((0,), (), (2, 3))):
        for at in waits:
            copy(at).wait_recv()
        chosen = [target_ref.at[k + 1, s] for s in range(target_ref.shape[1])]
        pick_body(base, capacity, exp_dev, chosen, blocks[k], picked.at[k])
        across_cores(k).start()
        home(k).start()
    for at in range(4):
        copy(at).wait_send()
    for k in range(3):
        across_cores(k).wait()
        home(k).wait()
    for expert in range(exp_dev):
        for kind in range(2):
            keep(expert, kind).wait()


def own_experts(grads, router, weights, target, over, up, first, normed, total, experts, units):
    _, exp_dev, capacity, model_width = grads[0].shape
    span_rows = normed.shape[0]
    wide_units = aligned_units(units)
    tile = 2 * capacity
    bf16 = jnp.bfloat16
    shape = jax.ShapeDtypeStruct
    picked = (3, exp_dev, capacity, model_width)
    wide = model_width + 128
    keeps = ((2, model_width), (3, wide_units))
    whole = pl.BlockSpec(memory_space=pltpu.VMEM)
    some = pl.BlockSpec(memory_space=pl.ANY)
    got = pl.pallas_call(
        functools.partial(own_kernel, experts, units),
        grid=(1,),
        in_specs=[whole] * 3 + [some] * 3 + [whole] * 5,
        out_specs=[whole] * 4 + [some] * 4,
        out_shape=[shape((exp_dev, 1, capacity, wide), bf16)] * 2
        + [shape((exp_dev, 1, capacity, model_width), bf16)] * 2
        + [shape((kinds, exp_dev, total, tile, width), bf16) for kinds, width in keeps]
        + [shape(picked, bf16)] * 2,
        scratch_shapes=[
            pltpu.VMEM((4, span_rows, model_width), bf16),
            pltpu.VMEM(picked, bf16),
            pltpu.VMEM((exp_dev, 3, 1, model_width, wide_units), bf16),
        ]
        + [pltpu.VMEM((exp_dev, kinds, 1, 1, tile, width), bf16) for kinds, width in keeps]
        + [
            pltpu.SemaphoreType.DMA((2, 4)),
            pltpu.SemaphoreType.DMA((2, 3)),
            pltpu.SemaphoreType.DMA((3,)),
            pltpu.SemaphoreType.DMA((exp_dev, 3)),
            pltpu.SemaphoreType.DMA((exp_dev, 2)),
            pltpu.VMEM((2, 1, exp_dev, capacity, model_width), bf16),
            pltpu.SemaphoreType.DMA((2,)),
        ],
        cost_estimate=cost(20e9, 16e6),
        compiler_params=remote_params(5),
        name="own_experts",
    )(*grads, router, *weights, target, over, up, first, normed)
    return got[:4], got[4:6], got[6:]


def run_experts(first, window, given, router, weights, kept, at, total, experts, units, chosen):
    low, high = chosen
    sources, exp_dev, capacity, model_width = given[0].shape
    wide_units = aligned_units(units)
    tile = 2 * capacity

    given_rows = pl.BlockSpec(
        (1, 1, capacity, model_width), lambda e, k, f, w: (k, low + e, 0, 0)
    )
    out = lambda width: pl.BlockSpec((1, 1, capacity, width), lambda e, k, f, w: (e, k, 0, 0))
    wide, rows = out(model_width + 128), out(model_width)
    weight = pl.BlockSpec(
        (pl.Element(1), pl.Element(model_width), pl.Element(wide_units)),
        lambda e, k, f, w: (low + e, 0, pl.multiple_of(w[0], 128)),
    )
    keep = lambda kinds, width: pl.BlockSpec(
        (kinds, 1, 1, tile, width), lambda e, k, f, w: (0, low + e, at + k, 0, 0)
    )
    keeps = ((2, model_width), (3, wide_units))
    kept = list(kept)
    out_of = lambda width: jax.ShapeDtypeStruct(
        (high - low, sources, capacity, width), jnp.bfloat16
    )
    back_shape, out_shape = out_of(model_width + 128), out_of(model_width)
    got = pl.pallas_call(
        functools.partial(expert_kernel, experts, units, len(kept)),
        grid_spec=pltpu.PrefetchScalarGridSpec(
            num_scalar_prefetch=2,
            grid=(high - low, sources),
            in_specs=[given_rows] * 4
            + [
                pl.BlockSpec(router.shape, lambda e, k, f, w: (0, 0)),
                weight,
                weight,
                weight,
            ]
            + anywhere(kept),
            out_specs=[wide, wide, rows, rows] + [keep(*kinds) for kinds in keeps],
        ),
        out_shape=[back_shape, back_shape, out_shape, out_shape]
        + [
            jax.ShapeDtypeStruct((kinds, exp_dev, total, tile, width), jnp.bfloat16)
            for kinds, width in keeps
        ],
        input_output_aliases={10 + i: 4 + i for i in range(len(kept))},
        cost_estimate=cost(20e9 * sources, 8e6 * sources),
        compiler_params=compiler_params(),
        name="expert_rows",
    )(first + low, window, *given, router, *weights, *kept)
    return got[:4], got[4:]


def aligned_units(units):
    return (units + 127) // 128 * 128


def weight_kernel(window_ref, rows_ref, units_ref, weight_ref, total):
    pieces, _, piece, model_width = weight_ref.shape
    units = units_ref[0, 0].reshape(-1, units_ref.shape[-1])
    total[...] = dot_tn(units, rows_ref[0, 0].reshape(-1, model_width))
    skip = pl.multiple_of(window_ref[1], 64)
    for at in range(pieces):
        weight_ref[at, 0] = total[pl.ds(skip + at * piece, piece), :].astype(jnp.bfloat16)


def weight_grads(window, kept, expert, pieces, units, waits=()):
    kept_rows, kept_units = kept
    tiles, tile, model_width = kept_rows.shape[2:]
    wide_units = kept_units.shape[4]
    shape = (pieces, 3, units // pieces, model_width)
    return pl.pallas_call(
        held(weight_kernel, 3, len(waits)),
        grid=(3,),
        in_specs=[
            pl.BlockSpec(memory_space=pltpu.SMEM),
            pl.BlockSpec((1, 1, tiles, tile, model_width), lambda i: (i // 2, expert, 0, 0, 0)),
            pl.BlockSpec((1, 1, tiles, tile, wide_units), lambda i: (i, expert, 0, 0, 0)),
        ]
        + anywhere(waits),
        out_specs=pl.BlockSpec((pieces, 1) + shape[2:], lambda i: (0, i, 0, 0)),
        out_shape=jax.ShapeDtypeStruct(shape, jnp.bfloat16),
        scratch_shapes=[pltpu.VMEM((wide_units, model_width), jnp.float32)],
        cost_estimate=cost(20e9, 20e6),
        compiler_params=compiler_params(),
        name="weight_grads",
    )(window, kept_rows, kept_units, *waits)


def send(values, axis, pairs):
    return lax.ppermute(values, axis, pairs)


def after(values, *earlier):
    return lax.optimization_barrier((values, earlier))[0]


def fast_device(
    tokens,
    lengths,
    expert_ids,
    places,
    buckets,
    w_attn,
    bias_table,
    norm1_gain,
    norm2_gain,
    w_router,
    w_gate,
    w_up,
    w_down,
    cotangent,
):
    span_rows, slots, model_width = tokens.shape
    head_count, bucket_count = bias_table.shape
    head_size = model_width // head_count
    scale = head_size ** (-0.5)
    n_dp = lax.axis_size("dp")
    n_ep = lax.axis_size("ep")
    n_cp = lax.axis_size("cp")
    my_dp, my_ep, my_cp = (lax.axis_index(name) for name in ("dp", "ep", "cp"))
    seq_len = span_rows * n_cp
    rows = span_rows * slots
    top_count = expert_ids.shape[2]
    experts = w_router.shape[1]
    exp_dev = w_gate.shape[0]
    units = w_gate.shape[2] // n_dp
    capacity = (5 * rows * top_count + 4 * experts - 1) // (4 * experts)
    groups = model_width // (128 * n_cp)
    own_width = 3 * groups * 128
    heads_own = head_count // n_cp
    over_core = [(i, i ^ 1) for i in range(n_dp)]
    over_x = [(i, i ^ 2) for i in range(n_dp)]
    over_y = [(i, i ^ 1) for i in range(n_ep)]
    ring = [(i, (i + 1) % n_cp) for i in range(n_cp)]
    f32, bf16 = jnp.float32, jnp.bfloat16
    exact = lax.Precision.HIGHEST
    each = range(slots)

    low_in = tokens.reshape(span_rows, slots * model_width)
    low_out = cotangent.reshape(span_rows, slots * model_width)
    gain_first, gain_second = norm1_gain[None, :], norm2_gain[None, :]

    per_group = 128 // head_size
    own_heads = (
        jnp.arange(groups)[:, None] * (n_cp * per_group)
        + my_cp * per_group
        + jnp.arange(per_group)[None, :]
    ).reshape(heads_own)
    head_hot = (own_heads[:, None] == jnp.arange(head_count)[None, :]).astype(f32)
    own_table = jnp.dot(head_hot, bias_table, precision=exact)
    far_hot = (buckets[::-1][:, None] == jnp.arange(bucket_count)[None, :]).astype(f32)
    lines = jnp.einsum("hb,db->hd", own_table, far_hot, precision=exact)
    lines = jnp.concatenate([lines, jnp.full((heads_own, span_rows), minus_big, f32)], axis=1)
    target = jnp.where(places >= 0, expert_ids * capacity + places, -1)
    target = target.transpose(1, 2, 0).astype(jnp.int32)
    (
        (normed_all, qkvs, bias, full, total, w_own, target_all, over_first, up_first),
        (grads_own, grads_rest_rows),
        fronts,
    ) = front(
        lengths,
        gain_first,
        gain_second,
        lines[:, None, :],
        target,
        w_attn,
        low_in,
        low_out,
        slots,
        n_cp,
        exp_dev,
        capacity,
        scale,
        head_size,
    )
    attended, hidden, normed_second = zip(*fronts)

    sources = target_all.shape[0]
    target_rows = target_all.transpose(0, 2, 1, 3).reshape(sources, top_count, rows)
    target_columns = target_rows.transpose(0, 2, 1)
    window_at = my_dp * units // 128 * 128
    window = jnp.stack([window_at, my_dp * units - window_at]).astype(jnp.int32)
    router_wide = jnp.concatenate(
        [w_router, jnp.zeros((model_width, 128 - experts), w_router.dtype)], axis=1
    )

    first = (my_ep * exp_dev).astype(jnp.int32).reshape(1)
    own, kept, picked_rest = own_experts(
        grads_own,
        router_wide,
        (w_gate, w_up, w_down),
        target_all,
        over_first,
        up_first,
        normed_second[0],
        normed_second[1],
        sources,
        experts,
        units,
    )

    def with_theirs(mine, theirs):
        return [mine, send(theirs, "dp", over_core)]

    backs, outs = with_theirs(own[0], own[1]), with_theirs(own[2], own[3])
    weight_sums = []
    for e in range(exp_dev):
        rest, kept = run_experts(
            first,
            window,
            (*picked_rest, *grads_rest_rows),
            router_wide,
            (w_gate, w_up, w_down),
            kept,
            1,
            sources,
            experts,
            units,
            (e, e + 1),
        )
        weight_part = weight_grads(window, kept, e, n_cp, units, backs[-1:] + outs[-1:])
        if e + 1 < exp_dev:
            backs += with_theirs(rest[0], rest[1])
            outs += with_theirs(rest[2], rest[3])
        else:
            backs, outs = [*backs, *rest[:2]], [*outs, *rest[2:]]
        weight_sums.append(lax.psum_scatter(weight_part, "cp", scatter_dimension=0, tiled=False))
        kept = after(kept, weight_part)
    back_rows, out_own, out_rest = return_rows(target_columns, backs, outs, slots, [weight_part])
    got, mixed, (ringed, line_first, grads_rest) = hidden_back(
        lengths,
        back_rows,
        low_out,
        hidden,
        normed_second,
        gain_second,
        router_wide,
        w_attn,
        experts,
        qkvs,
        bias,
        full,
        total,
        out_own,
        out_rest,
        scale,
        head_size,
    )
    hidden_grads, proj_grads, router_parts, gain_parts = zip(*got)
    router_grad = sum(router_parts)[:experts]
    ring_second, line_second, arrived, early, weight_part, out_grad, gain_part = second_back(
        lengths,
        ringed,
        normed_all,
        qkvs,
        bias,
        grads_rest,
        full,
        total,
        attended,
        proj_grads,
        w_own,
        gain_first,
        scale,
        head_size,
        weight_sums[:1],
    )
    distance_grads = (line_first + line_second)[:, 0, :seq_len]
    table_grad = jnp.dot(distance_grads, far_hot, precision=exact)
    table_grad = jnp.einsum("hg,hb->gb", head_hot, table_grad, precision=exact)
    table_row = jnp.pad(table_grad.reshape(1, -1), ((0, 0), (0, model_width - table_grad.size)))
    small = jnp.concatenate(
        [router_grad, sum(gain_parts), table_row, gain_part[:2]], axis=0
    )
    tokens_grad, small_sum, attn_sum = final_back(
        ring_second,
        early,
        weight_part,
        arrived,
        out_grad,
        small,
        gain_first,
        w_attn,
        low_in,
        hidden_grads,
    )
    router_sum, gain_second_sum = small_sum[:experts], small_sum[experts]
    table_sum = small_sum[experts + 1, : table_grad.size].reshape(table_grad.shape)
    gain_first_sum = small_sum[experts + 2]

    gate_sum, up_sum, down_sum = (
        jnp.stack([part[which].T.astype(f32) for part in weight_sums]) for which in range(3)
    )
    return (
        mixed.reshape(tokens.shape),
        tokens_grad.reshape(tokens.shape),
        attn_sum,
        table_sum,
        gain_first_sum,
        gain_second_sum,
        router_sum.T,
        gate_sum,
        up_sum,
        down_sum,
    )


def solution(mesh):
    placed = (
        P("cp", ("dp", "ep"), None),
        P(("dp", "ep")),
        P("cp", ("dp", "ep"), None),
        P("cp", ("dp", "ep"), None),
        P(),
        P(),
        P(),
        P(),
        P(),
        P(),
        P("ep", None, None),
        P("ep", None, None),
        P("ep", None, None),
        P("cp", ("dp", "ep"), None),
    )
    sizes = dict(mesh.shape)
    square = sizes["dp"] == 4 and sizes["ep"] == 2 and sizes["cp"] == 4
    return jax.shard_map(
        fast_device if square else on_device,
        mesh=mesh,
        in_specs=placed,
        out_specs=(
            P("cp", ("dp", "ep"), None),
            P("cp", ("dp", "ep"), None),
            P(None, ("dp", "ep", "cp")),
            P(),
            P(),
            P(),
            P(),
            P("ep", None, ("dp", "cp")),
            P("ep", None, ("dp", "cp")),
            P("ep", None, ("dp", "cp")),
        ),
        check_vma=False,
    )
```

```python
import functools

import jax
import jax.numpy as jnp
from jax import lax
from jax.experimental import pallas as pl
from jax.experimental.pallas import tpu as pltpu
from jax.sharding import PartitionSpec as P

epsilon = 1e-06
masked_value = -1000000000.0


def gelu_tanh(values):
    return jax.nn.gelu(values, approximate=True)


def root_scale(values):
    return lax.rsqrt(jnp.mean(values * values, axis=-1, keepdims=True) + epsilon)


def norm_back(grad_in, values, scale_rows, gain_vector):
    scaled = grad_in * gain_vector
    inner_mean = jnp.mean(scaled * values, axis=-1, keepdims=True)
    return scale_rows * (scaled - values * scale_rows * scale_rows * inner_mean)


def block_logits(
    queries, key_rows, key_start, query_pos, lengths, table_step, rise_points, head_scale
):
    key_count = key_rows.shape[0]
    key_pos = key_start + jnp.arange(key_count, dtype=jnp.int32)
    scores = (
        jnp.einsum("qshd,kshd->shqk", queries, key_rows, preferred_element_type=jnp.float32)
        * head_scale
    )
    distance = query_pos[:, None] - key_pos[None, :]
    steps = (distance[:, :, None] >= rise_points[None, None, :]).astype(jnp.float32)
    pair_bias = jnp.einsum("hb,qkb->hqk", table_step, steps, precision=lax.Precision.HIGHEST)
    allowed = (distance >= 0)[None, :, :] & (key_pos[None, None, :] < lengths[:, None, None])
    logits = jnp.where(allowed[:, None], scores + pair_bias[None], masked_value)
    return (logits, steps)


def on_device(
    tokens,
    lengths,
    expert_ids,
    places,
    buckets,
    w_attn,
    bias_table,
    norm1_gain,
    norm2_gain,
    w_router,
    w_gate,
    w_up,
    w_down,
    cotangent,
):
    span_rows, pair_count, model_width = tokens.shape
    head_count, bucket_count = bias_table.shape
    head_size = model_width // head_count
    head_scale = head_size ** (-0.5)
    n_cp = lax.axis_size("cp")
    n_ep = lax.axis_size("ep")
    seq_len = span_rows * n_cp
    row_count = span_rows * pair_count
    top_count = expert_ids.shape[2]
    experts = w_router.shape[1]
    exp_dev = w_gate.shape[0]
    capacity = (5 * row_count * top_count + 4 * experts - 1) // (4 * experts)
    my_start = lax.axis_index("cp") * span_rows
    query_pos = my_start + jnp.arange(span_rows, dtype=jnp.int32)
    live_mask = (query_pos[:, None] < lengths[None, :]).astype(jnp.float32)
    inputs = tokens.astype(jnp.float32)
    scale_first = root_scale(inputs)
    normed_first = (inputs * scale_first * norm1_gain).astype(jnp.bfloat16)
    w_qkv = w_attn[:, : 3 * model_width]
    w_out = w_attn[:, 3 * model_width :]
    qkv = jnp.einsum("csd,de->cse", normed_first, w_qkv, preferred_element_type=jnp.float32).astype(
        jnp.bfloat16
    )
    queries = qkv[..., :model_width].reshape(span_rows, pair_count, head_count, head_size)
    keyval = qkv[..., model_width:]
    keyval_all = lax.all_gather(keyval, "cp", axis=0, tiled=True)
    bucket_ids = jnp.arange(bucket_count, dtype=jnp.int32)
    rise_points = jnp.sum((buckets[:, None] < bucket_ids[None, :]).astype(jnp.int32), axis=0)
    table_step = jnp.concatenate(
        [bias_table[:, :1], bias_table[:, 1:] - bias_table[:, :-1]], axis=1
    )
    block_starts = jnp.arange(n_cp, dtype=jnp.int32) * span_rows

    def split_kv(kv_block):
        key_rows = kv_block[..., :model_width].reshape(span_rows, pair_count, head_count, head_size)
        value_rows = kv_block[..., model_width:].reshape(
            span_rows, pair_count, head_count, head_size
        )
        return (key_rows, value_rows)

    kv_blocks = keyval_all.reshape(n_cp, span_rows, pair_count, 2 * model_width)

    def max_step(state_pair, block_item):
        row_peak, row_total = state_pair
        kv_block, block_start = block_item
        key_rows, value_rows = split_kv(kv_block)
        logits, steps = block_logits(
            queries, key_rows, block_start, query_pos, lengths, table_step, rise_points, head_scale
        )
        new_peak = jnp.maximum(row_peak, jnp.max(logits, axis=-1))
        row_total = row_total * jnp.exp(row_peak - new_peak) + jnp.sum(
            jnp.exp(logits - new_peak[..., None]), axis=-1
        )
        return ((new_peak, row_total), None)

    stat_shape = (pair_count, head_count, span_rows)
    (row_peak, row_total), unused = lax.scan(
        max_step,
        (jnp.full(stat_shape, masked_value, jnp.float32), jnp.zeros(stat_shape, jnp.float32)),
        (kv_blocks, block_starts),
    )
    log_total = row_peak + jnp.log(row_total)

    def value_step(running, block_item):
        kv_block, block_start = block_item
        key_rows, value_rows = split_kv(kv_block)
        logits, steps = block_logits(
            queries, key_rows, block_start, query_pos, lengths, table_step, rise_points, head_scale
        )
        weights = jnp.exp(logits - log_total[..., None]).astype(jnp.bfloat16)
        return (
            running
            + jnp.einsum(
                "shqk,kshd->qshd", weights, value_rows, preferred_element_type=jnp.float32
            ),
            None,
        )

    attended, unused = lax.scan(
        value_step,
        jnp.zeros((span_rows, pair_count, head_count, head_size), jnp.float32),
        (kv_blocks, block_starts),
    )
    attended = attended.reshape(span_rows, pair_count, model_width)
    attended_low = attended.astype(jnp.bfloat16)
    projected = jnp.einsum("csd,de->cse", attended_low, w_out, preferred_element_type=jnp.float32)
    hidden = inputs + live_mask[..., None] * projected
    scale_second = root_scale(hidden)
    normed_second = (hidden * scale_second * norm2_gain).astype(jnp.bfloat16)
    router_logits = jnp.einsum(
        "csd,de->cse", normed_second, w_router, preferred_element_type=jnp.float32
    )
    router_probs = jax.nn.softmax(router_logits, axis=-1)
    expert_hot = (expert_ids[..., None] == jnp.arange(experts, dtype=jnp.int32)).astype(jnp.float32)
    kept_mask = (places >= 0).astype(jnp.float32)
    gate_values = jnp.sum(expert_hot * router_probs[:, :, None, :], axis=-1) * kept_mask
    target = jnp.where(places >= 0, expert_ids * capacity + places, -1).reshape(
        row_count, top_count
    )
    slot_ids = jnp.arange(experts * capacity, dtype=jnp.int32)
    route_hot = (target[None, :, :] == slot_ids[:, None, None]).astype(jnp.bfloat16)
    dispatch = jnp.sum(route_hot, axis=2)
    sent_rows = jnp.dot(
        dispatch, normed_second.reshape(row_count, model_width), preferred_element_type=jnp.float32
    )
    sent_rows = sent_rows.astype(jnp.bfloat16).reshape(n_ep, exp_dev, capacity, model_width)
    arrived = lax.all_to_all(sent_rows, "ep", split_axis=0, concat_axis=0, tiled=True)
    gate_pre = jnp.einsum("secd,edf->secf", arrived, w_gate, preferred_element_type=jnp.float32)
    up_pre = jnp.einsum("secd,edf->secf", arrived, w_up, preferred_element_type=jnp.float32)
    active, gelu_pullback = jax.vjp(gelu_tanh, gate_pre)
    inner_act = (active * up_pre).astype(jnp.bfloat16)
    produced = jnp.einsum(
        "secf,edf->secd", inner_act, w_down, preferred_element_type=jnp.float32
    ).astype(jnp.bfloat16)
    returned = lax.all_to_all(produced, "ep", split_axis=0, concat_axis=0, tiled=True).reshape(
        experts * capacity, model_width
    )
    picked = jnp.einsum("jrk,jd->rkd", route_hot, returned, preferred_element_type=jnp.float32)
    gate_flat = gate_values.reshape(row_count, top_count)
    mixed = hidden.reshape(row_count, model_width) + jnp.sum(gate_flat[..., None] * picked, axis=1)
    mixed = mixed.reshape(span_rows, pair_count, model_width).astype(jnp.bfloat16)
    grad_out = cotangent.astype(jnp.float32).reshape(row_count, model_width)
    gate_grads = jnp.sum(grad_out[:, None, :] * picked, axis=-1)
    sent_back = (gate_flat[..., None] * grad_out[:, None, :]).astype(jnp.bfloat16)
    scattered = jnp.einsum("jrk,rkd->jd", route_hot, sent_back, preferred_element_type=jnp.float32)
    scattered = scattered.astype(jnp.bfloat16).reshape(n_ep, exp_dev, capacity, model_width)
    grad_produced = lax.all_to_all(scattered, "ep", split_axis=0, concat_axis=0, tiled=True)
    down_grad = jnp.einsum(
        "secd,secf->edf", grad_produced, inner_act, preferred_element_type=jnp.float32
    )
    grad_inner = jnp.einsum(
        "secd,edf->secf", grad_produced, w_down, preferred_element_type=jnp.float32
    )
    grad_gate_pre = gelu_pullback(grad_inner * up_pre)[0].astype(jnp.bfloat16)
    grad_up_pre = (grad_inner * active).astype(jnp.bfloat16)
    gate_grad = jnp.einsum(
        "secd,secf->edf", arrived, grad_gate_pre, preferred_element_type=jnp.float32
    )
    up_grad = jnp.einsum("secd,secf->edf", arrived, grad_up_pre, preferred_element_type=jnp.float32)
    grad_arrived = jnp.einsum(
        "secf,edf->secd", grad_gate_pre, w_gate, preferred_element_type=jnp.float32
    )
    grad_arrived = (
        grad_arrived
        + jnp.einsum("secf,edf->secd", grad_up_pre, w_up, preferred_element_type=jnp.float32)
    ).astype(jnp.bfloat16)
    grad_sent = lax.all_to_all(grad_arrived, "ep", split_axis=0, concat_axis=0, tiled=True).reshape(
        experts * capacity, model_width
    )
    grad_rows = jnp.einsum("jr,jd->rd", dispatch, grad_sent, preferred_element_type=jnp.float32)
    choice_grads = gate_grads.reshape(span_rows, pair_count, top_count) * kept_mask
    prob_grads = jnp.sum(expert_hot * choice_grads[..., None], axis=2)
    logit_grads = router_probs * (
        prob_grads - jnp.sum(router_probs * prob_grads, axis=-1, keepdims=True)
    )
    logit_grads = logit_grads.astype(jnp.bfloat16)
    router_grad = jnp.einsum(
        "csd,cse->de", normed_second, logit_grads, preferred_element_type=jnp.float32
    )
    grad_normed_second = grad_rows.reshape(span_rows, pair_count, model_width)
    grad_normed_second = grad_normed_second + jnp.einsum(
        "cse,de->csd", logit_grads, w_router, preferred_element_type=jnp.float32
    )
    gain_second_grad = jnp.sum(grad_normed_second * hidden * scale_second, axis=(0, 1))
    grad_hidden = grad_out.reshape(span_rows, pair_count, model_width) + norm_back(
        grad_normed_second, hidden, scale_second, norm2_gain
    )
    grad_proj = (live_mask[..., None] * grad_hidden).astype(jnp.bfloat16)
    out_grad = jnp.einsum(
        "csd,cse->de", attended_low, grad_proj, preferred_element_type=jnp.float32
    )
    grad_att = jnp.einsum(
        "cse,de->csd", grad_proj, w_out, preferred_element_type=jnp.float32
    ).astype(jnp.bfloat16)
    grad_att_heads = grad_att.reshape(span_rows, pair_count, head_count, head_size)
    row_terms = jnp.sum(
        grad_att_heads.astype(jnp.float32)
        * attended.reshape(span_rows, pair_count, head_count, head_size),
        axis=-1,
    )
    row_terms = row_terms.transpose(1, 2, 0)
    keyval_back = lax.all_gather(keyval, "cp", axis=0, tiled=True)
    back_blocks = keyval_back.reshape(n_cp, span_rows, pair_count, 2 * model_width)

    def pair_terms(
        query_rows, grad_rows_att, row_part, total_part, key_rows, value_rows, key_start, rows_pos
    ):
        logits, steps = block_logits(
            query_rows, key_rows, key_start, rows_pos, lengths, table_step, rise_points, head_scale
        )
        weights = jnp.exp(logits - total_part[..., None])
        weight_grads = jnp.einsum(
            "qshd,kshd->shqk", grad_rows_att, value_rows, preferred_element_type=jnp.float32
        )
        score_grads = weights * (weight_grads - row_part[..., None])
        return (weights, score_grads, steps)

    def query_side_step(state_pair, kv_block, block_start):
        query_grad, step_grad = state_pair
        key_rows, value_rows = split_kv(kv_block)
        weights, score_grads, steps = pair_terms(
            queries,
            grad_att_heads,
            row_terms,
            log_total,
            key_rows,
            value_rows,
            block_start,
            query_pos,
        )
        low_grads = score_grads.astype(jnp.bfloat16)
        query_grad = (
            query_grad
            + jnp.einsum("shqk,kshd->qshd", low_grads, key_rows, preferred_element_type=jnp.float32)
            * head_scale
        )
        step_grad = step_grad + jnp.einsum(
            "hqk,qkb->hb", jnp.sum(score_grads, axis=0), steps, precision=lax.Precision.HIGHEST
        )
        return ((query_grad, step_grad), weights, low_grads)

    start_state = (
        jnp.zeros((span_rows, pair_count, head_count, head_size), jnp.float32),
        jnp.zeros((head_count, bucket_count), jnp.float32),
    )

    def grad_step(state_pair, block_item):
        kv_block, block_start = block_item
        new_state, weights, low_grads = query_side_step(state_pair, kv_block, block_start)
        value_grad = jnp.einsum(
            "shqk,qshd->kshd",
            weights.astype(jnp.bfloat16),
            grad_att_heads,
            preferred_element_type=jnp.float32,
        )
        key_grad = (
            jnp.einsum("shqk,qshd->kshd", low_grads, queries, preferred_element_type=jnp.float32)
            * head_scale
        )
        block_grad = jnp.concatenate(
            [
                key_grad.reshape(span_rows, pair_count, model_width),
                value_grad.reshape(span_rows, pair_count, model_width),
            ],
            axis=-1,
        )
        return (new_state, block_grad)

    (query_grad, step_grad), kv_terms = lax.scan(
        grad_step, start_state, (back_blocks, block_starts)
    )
    kv_terms = kv_terms.reshape(seq_len, pair_count, 2 * model_width)
    keyval_grad = lax.psum_scatter(
        kv_terms.astype(jnp.bfloat16), "cp", scatter_dimension=0, tiled=True
    )
    table_grad = step_grad - jnp.concatenate(
        [step_grad[:, 1:], jnp.zeros((head_count, 1), jnp.float32)], axis=1
    )
    qkv_grad = jnp.concatenate(
        [query_grad.reshape(span_rows, pair_count, model_width).astype(jnp.bfloat16), keyval_grad],
        axis=-1,
    )
    qkv_weight_grad = jnp.einsum(
        "csd,cse->de", normed_first, qkv_grad, preferred_element_type=jnp.float32
    )
    grad_normed_first = jnp.einsum(
        "cse,de->csd", qkv_grad, w_qkv, preferred_element_type=jnp.float32
    )
    gain_first_grad = jnp.sum(grad_normed_first * inputs * scale_first, axis=(0, 1))
    tokens_grad = (
        grad_hidden + norm_back(grad_normed_first, inputs, scale_first, norm1_gain)
    ).astype(jnp.bfloat16)
    attn_term = jnp.concatenate([qkv_weight_grad, out_grad], axis=1)
    w_attn_grad = lax.psum_scatter(attn_term, ("dp", "ep", "cp"), scatter_dimension=1, tiled=True)
    router_sum, table_sum, gain_first_sum, gain_second_sum = lax.psum(
        (router_grad, table_grad, gain_first_grad, gain_second_grad), ("dp", "ep", "cp")
    )
    gate_sum, up_sum, down_sum = (
        lax.psum_scatter(
            gate_grad.astype(jnp.bfloat16), ("dp", "cp"), scatter_dimension=2, tiled=True
        ).astype(jnp.float32),
        lax.psum_scatter(
            up_grad.astype(jnp.bfloat16), ("dp", "cp"), scatter_dimension=2, tiled=True
        ).astype(jnp.float32),
        lax.psum_scatter(
            down_grad.astype(jnp.bfloat16), ("dp", "cp"), scatter_dimension=2, tiled=True
        ).astype(jnp.float32),
    )
    return (
        mixed,
        tokens_grad,
        w_attn_grad,
        table_sum,
        gain_first_sum,
        gain_second_sum,
        router_sum,
        gate_sum,
        up_sum,
        down_sum,
    )


minus_big = -1000000000.0
vmem_bytes = 60 * 1024 * 1024


cost_share = 0.05


def cost(flops, moved):
    return pl.CostEstimate(
        flops=int(flops * cost_share), bytes_accessed=int(moved * cost_share), transcendentals=0
    )


def held(kernel, at, count):
    def run(*refs):
        kernel(*refs[:at], *refs[at + count :])

    return run


def anywhere(arrays):
    return [pl.BlockSpec(memory_space=pl.ANY)] * len(arrays)


def compiler_params():
    return pltpu.CompilerParams(vmem_limit_bytes=vmem_bytes)


def shear(values, leftward):
    rows, lanes = values.shape
    row_ids = lax.broadcasted_iota(jnp.int32, (rows, lanes), 0)
    bit = 1
    while bit < rows:
        amount = lanes - bit if leftward else bit
        moved = pltpu.roll(values, amount, 1)
        values = jnp.where((row_ids & bit) != 0, moved, values)
        bit *= 2
    return values


def dot_nt(left, right):
    return lax.dot_general(
        left, right, (((1,), (1,)), ((), ())), preferred_element_type=jnp.float32
    )


def dot_tn(left, right):
    return lax.dot_general(
        left, right, (((0,), (0,)), ((), ())), preferred_element_type=jnp.float32
    )


def dot_nn(left, right):
    return jnp.dot(left, right, preferred_element_type=jnp.float32)


def key_masks(length, blocks, span_rows):
    masks = []
    for block in range(blocks):
        position = block * span_rows + lax.broadcasted_iota(jnp.int32, (1, span_rows), 1)
        masks.append(jnp.where(position < length, 0.0, minus_big))
    return masks


def forward_body(
    mine, length, scale, head_size, qkv_ref, bias_ref, low_ref, full_ref, total_ref, after_pair
):
    blocks, span_rows, width = qkv_ref.shape
    lanes = 128
    lane = lax.broadcasted_iota(jnp.int32, (1, lanes), 1)
    masks = key_masks(length, blocks, span_rows)
    halves = lanes // head_size

    def place(block):
        return lax.rem(mine - block + blocks, blocks)

    def one_pair(pair, carry):
        wide = pl.multiple_of(pair * (3 * lanes), lanes)
        own_lanes = pl.ds(pl.multiple_of(pair * lanes, lanes), lanes)
        part = [pl.ds(pl.multiple_of(wide + which * lanes, lanes), lanes) for which in range(3)]
        for row in range(blocks):
            queries = qkv_ref[place(row), :, part[0]]
            totals = jnp.zeros((span_rows, lanes), jnp.float32)
            result = jnp.zeros((span_rows, lanes), jnp.float32)
            for half in range(halves):
                own = lane // head_size == half
                head_q = queries * jnp.where(own, scale, 0.0).astype(jnp.bfloat16)
                head_v = jnp.where(own, 1.0, 0.0).astype(jnp.bfloat16)
                logits = []
                for column in range(row + 1):
                    at = (blocks - 1 - row + column) * span_rows
                    term = dot_nt(head_q, qkv_ref[place(column), :, part[1]])
                    bias = bias_ref[pair * halves + half, :, at : at + span_rows]
                    logits.append(term + bias + masks[column])
                peak = jnp.max(logits[0], axis=1, keepdims=True)
                for term in logits[1:]:
                    peak = jnp.maximum(peak, jnp.max(term, axis=1, keepdims=True))
                total = jnp.zeros((span_rows, 1), jnp.float32)
                mixed = jnp.zeros((span_rows, lanes), jnp.float32)
                for column in range(row + 1):
                    weights = jnp.exp(logits[column] - peak)
                    total = total + jnp.sum(weights, axis=1, keepdims=True)
                    values = qkv_ref[place(column), :, part[2]] * head_v
                    mixed = mixed + dot_nn(weights.astype(jnp.bfloat16), values)
                result = result + mixed / total
                totals = jnp.where(lane == half, peak + jnp.log(total), totals)
            low_ref[place(row), :, own_lanes] = result.astype(jnp.bfloat16)
            full_ref[row, :, own_lanes] = result
            total_ref[row, :, own_lanes] = totals
        after_pair(pair)
        return carry

    lax.fori_loop(0, width // (3 * lanes), one_pair, 0)


def backward_body(
    mine, length, scale, head_size, qkv_ref, bias_ref, grad_ref, full_ref, total_ref, ring_ref, line_ref, work,
    after_pair=None,
):
    key_sum, value_sum, plane = work
    blocks, span_rows, width = qkv_ref.shape
    lanes = 128
    lane = lax.broadcasted_iota(jnp.int32, (1, lanes), 1)
    masks = key_masks(length, blocks, span_rows)
    halves = lanes // head_size

    def place(block):
        return lax.rem(mine - block + blocks, blocks)

    def one_pair(pair, carry):
        wide = pl.multiple_of(pair * (3 * lanes), lanes)
        own_lanes = pl.ds(pl.multiple_of(pair * lanes, lanes), lanes)
        part = [pl.ds(pl.multiple_of(wide + which * lanes, lanes), lanes) for which in range(3)]
        key_sum[...] = jnp.zeros_like(key_sum)
        value_sum[...] = jnp.zeros_like(value_sum)
        plane[...] = jnp.zeros_like(plane)
        for row in range(blocks):
            queries = qkv_ref[place(row), :, part[0]]
            grads = grad_ref[lax.rem(row - mine + blocks, blocks), :, own_lanes]
            products = grads.astype(jnp.float32) * full_ref[row, :, own_lanes]
            totals = total_ref[row, :, own_lanes]
            query_sum = jnp.zeros((span_rows, lanes), jnp.float32)
            for half in range(halves):
                own = lane // head_size == half
                one = jnp.where(own, 1.0, 0.0).astype(jnp.bfloat16)
                head_q = queries * jnp.where(own, scale, 0.0).astype(jnp.bfloat16)
                head_g = grads * one
                delta = jnp.sum(jnp.where(own, products, 0.0), axis=1, keepdims=True)
                total = totals[:, half : half + 1]
                for column in range(row + 1):
                    at = (blocks - 1 - row + column) * span_rows
                    keys = qkv_ref[place(column), :, part[1]]
                    logits = dot_nt(head_q, keys)
                    bias = bias_ref[pair * halves + half, :, at : at + span_rows]
                    logits = logits + bias + masks[column]
                    weights = jnp.exp(logits - total)
                    weight_grads = dot_nt(head_g, qkv_ref[place(column), :, part[2]])
                    score_grads = weights * (weight_grads - delta)
                    plane[half, :, at : at + span_rows] += score_grads
                    low_weights = weights.astype(jnp.bfloat16)
                    low_grads = score_grads.astype(jnp.bfloat16)
                    query_sum = query_sum + dot_nn(low_grads, keys * one)
                    key_sum[column] += dot_tn(low_grads, head_q)
                    value_sum[column] += dot_tn(low_weights, head_g)
            ring_ref[place(row), :, part[0]] = (query_sum * scale).astype(jnp.bfloat16)
        for row in range(blocks):
            ring_ref[place(row), :, part[1]] = key_sum[row].astype(jnp.bfloat16)
            ring_ref[place(row), :, part[2]] = value_sum[row].astype(jnp.bfloat16)
        for half in range(halves):
            full = jnp.concatenate(
                [plane[half], jnp.zeros((span_rows, span_rows), jnp.float32)], axis=1
            )
            summed = jnp.sum(shear(full, True), axis=0, keepdims=True)
            line_ref[pair * halves + half] = pltpu.roll(summed, span_rows - 1, 1)
        if after_pair is not None:
            after_pair(pair)
        return carry

    lax.fori_loop(0, width // (3 * lanes), one_pair, 0)


def backward_work(blocks, span_rows, head_size):
    return [
        pltpu.VMEM((blocks, span_rows, 128), jnp.float32),
        pltpu.VMEM((blocks, span_rows, 128), jnp.float32),
        pltpu.VMEM((128 // head_size, span_rows, blocks * span_rows), jnp.float32),
    ]


def greet(*others):
    barrier = pltpu.get_barrier_semaphore()
    for other in others:
        pl.semaphore_signal(
            barrier, inc=1, device_id=other, device_id_type=pl.DeviceIdType.MESH
        )
    pl.semaphore_wait(barrier, len(others))


def push(source, target, send_sem, recv_sem, other):
    return pltpu.make_async_remote_copy(
        src_ref=source,
        dst_ref=target,
        send_sem=send_sem,
        recv_sem=recv_sem,
        device_id=other,
        device_id_type=pl.DeviceIdType.MESH,
    )


def ring_others(mine, count):
    return [{"cp": lax.rem(mine + j, count)} for j in range(1, count)]


def slot_of(ref, slot, slots):
    width = ref.shape[1] // slots
    return ref.at[:, pl.ds(slot * width, width)]


def deliveries(source, target, sems, mine, count, lanes=None):
    return [
        push(
            source.at[j] if lanes is None else source.at[j, :, lanes],
            target.at[j],
            sems.at[0, j],
            sems.at[1, j],
            {"cp": lax.rem(mine + (count - j), count)},
        )
        for j in range(1, count)
    ]


def remote_params(number):
    return pltpu.CompilerParams(
        vmem_limit_bytes=vmem_bytes, collective_id=number, has_side_effects=True
    )


def own_rows(block, length, span_rows):
    position = block * span_rows + lax.broadcasted_iota(jnp.int32, (span_rows, 1), 0)
    return jnp.where(position < length, 1.0, 0.0)


def router_of(rows, router_w, experts):
    lane = lax.broadcasted_iota(jnp.int32, (1, router_w.shape[1]), 1)
    logits = jnp.where(lane < experts, dot_nn(rows, router_w), minus_big)
    shares = jnp.exp(logits - jnp.max(logits, axis=1, keepdims=True))
    return shares / jnp.sum(shares, axis=1, keepdims=True)


def project_body(mine, length, input_ref, gain_ref, weight_ref, parts_ref, own_ref, attended_ref, hidden_ref, normed_ref):
    count, span_rows, width = parts_ref.shape
    for j in range(count):
        owner = lax.rem(mine + j, count)
        for group in range(width // 128):
            at = pl.multiple_of((group * count + owner) * 128, 128)
            lanes = slice(group * 128, (group + 1) * 128)
            attended_ref[:, pl.ds(at, 128)] = own_ref[0, :, lanes] if j == 0 else parts_ref[j, :, lanes]
    projected = dot_nn(attended_ref[...], weight_ref[...])
    hidden = input_ref[...].astype(jnp.float32) + own_rows(mine, length, span_rows) * projected
    hidden_ref[...] = hidden
    normed_ref[...] = (hidden * root_scale(hidden) * gain_ref[...]).astype(jnp.bfloat16)


def pick_body(base, capacity, experts, chosen, parts, out_ref):
    for expert in range(experts):
        picked = None
        for choice_ref, part in zip(chosen, parts):
            span = part.shape[0]
            ids = lax.broadcasted_iota(jnp.int32, (capacity, span), 0) + (base + expert * capacity)
            hot = jnp.zeros((capacity, span), jnp.float32)
            for choice in range(choice_ref.shape[0]):
                hot = hot + jnp.where(ids == choice_ref[choice : choice + 1, :], 1.0, 0.0)
            term = dot_nn(hot.astype(jnp.bfloat16), part[...])
            picked = term if picked is None else picked + term
        out_ref[expert] = picked.astype(jnp.bfloat16)


def front_kernel(
    scale, head_size, slots, length_ref, gain_first_ref, gain_second_ref, line_ref, target_ref, w_attn_ref, weight_ref,
    tokens_ref, cotangent_ref, *refs
):
    inputs = [slot_of(tokens_ref, s, slots) for s in range(slots)]
    grads = [slot_of(cotangent_ref, s, slots) for s in range(slots)]
    stores_to, own_w, targets_ref = refs[:5], refs[5], refs[6]
    over_ref, up_ref = refs[7:9]
    picks = [refs[9 + 2 * i : 11 + 2 * i] for i in range(2)]
    outs = [refs[13 + 3 * s : 16 + 3 * s] for s in range(slots)]
    refs = refs[13 + 3 * slots :]
    low, arrived, near_grads, ring_sems, own_sems, give_sems, plane_sems, target_sems = refs[:8]
    core_sems, normed_sems, store_sems, *made = refs[8:]
    all_ref, qkv_ref, bias_ref, full_ref, total_ref = made
    _, count, span_rows, model_width = all_ref.shape

    def store(which, slot):
        source, target = made[which], stores_to[which]
        if which != 2:
            source, target = source.at[slot], target.at[slot]
        return pltpu.make_async_copy(source, target, store_sems.at[which, slot])

    groups = own_w.shape[1] // 384
    mine = lax.axis_index("cp")
    dp, ep = lax.axis_index("dp"), lax.axis_index("ep")
    core_other, x_other, y_other = near_others(dp, ep)

    loads = []
    for group in range(groups):
        for which in range(3):
            at = which * model_width + (group * count + mine) * 128
            lanes = pl.ds((group * 3 + which) * 128, 128)
            loads.append(
                pltpu.make_async_copy(
                    w_attn_ref.at[:, pl.ds(pl.multiple_of(at, 128), 128)],
                    own_w.at[:, lanes],
                    own_sems.at[group * 3 + which],
                )
            )
    for load in loads:
        load.start()
    for s in range(slots):
        values = inputs[s][...].astype(jnp.float32)
        all_ref[s, 0] = (values * root_scale(values) * gain_first_ref[...]).astype(jnp.bfloat16)
    greet(*ring_others(mine, count), core_other, x_other, y_other)

    def hop_copy(slot, hop):
        return push(
            all_ref.at[slot, hop],
            all_ref.at[slot, hop + 1],
            ring_sems.at[0, slot, hop],
            ring_sems.at[1, slot, hop],
            {"cp": lax.rem(mine + 1, count)},
        )

    for s in range(slots):
        hop_copy(s, 0).start()

    def plane_copies(source, target, sems):
        first = [
            push(source(s), target.at[way, s], sems.at[0, way, s], sems.at[1, way, s], other)
            for s in (0, 1)
            for way, other in ((0, x_other), (1, y_other))
        ]
        second = [
            push(target.at[0, 0], target.at[2, 0], sems.at[0, 2, 0], sems.at[1, 2, 0], y_other),
            push(target.at[1, 1], target.at[2, 1], sems.at[0, 2, 1], sems.at[1, 2, 1], x_other),
        ]
        return first, second

    grad_first, grad_second = plane_copies(lambda s: grads[s], near_grads, plane_sems)
    near_targets = targets_ref.at[pl.ds(1, 3)]
    place_first, place_second = plane_copies(lambda s: target_ref.at[s], near_targets, target_sems)
    for copy in place_first + grad_first:
        copy.start()
    targets_ref[0] = target_ref[...]
    for load in loads:
        load.wait()
    for s in range(slots):
        qkv_ref[s, 0] = dot_nn(all_ref[s, 0], own_w[...]).astype(jnp.bfloat16)
    columns = bias_ref.shape[2]
    lanes = span_rows + columns
    for head in range(bias_ref.shape[0]):
        line = pltpu.roll(line_ref[head], lanes - (span_rows - 1), 1)
        full = jnp.broadcast_to(line, (span_rows, lanes))
        bias_ref[head] = shear(full, False)[:, :columns]
    store(2, 0).start()

    _, experts, capacity, _ = picks[0][0].shape
    base = ep * (experts * capacity)
    at_of = ((0, 0), (1, 0), (1, 1), (1, 2))

    def pick(source):
        if source == 0:
            parts = grads
        else:
            parts = [near_grads.at[source - 1, s] for s in range(slots)]
        chosen = [targets_ref.at[source, s] for s in range(slots)]
        group, at = at_of[source]
        pick_body(base, capacity, experts, chosen, parts, picks[group][0].at[at])
        core_copy(source).start()

    def core_copy(source):
        group, at = at_of[source]
        return push(
            picks[group][0].at[at],
            picks[group][1].at[at],
            core_sems.at[0, source],
            core_sems.at[1, source],
            core_other,
        )

    def normed_copy(at):
        source, target, other = (
            (outs[0][2], over_ref, x_other),
            (outs[0][2], up_ref, y_other),
        )[at]
        return push(source, target, normed_sems.at[0, at], normed_sems.at[1, at], other)

    def project(slot):
        for pair in range(groups):
            for copy in gives(slot, pair):
                copy.wait()
        project_body(
            mine, length_ref[slot], inputs[slot], gain_second_ref, weight_ref, arrived.at[slot],
            low.at[slot], *outs[slot],
        )

    def gives(slot, pair):
        part = pl.ds(pl.multiple_of(pair * 128, 128), 128)
        return [
            push(
                low.at[slot, j, :, part],
                arrived.at[slot, j, :, part],
                give_sems.at[0, slot, pair, j],
                give_sems.at[1, slot, pair, j],
                {"cp": lax.rem(mine + (count - j), count)},
            )
            for j in range(1, count)
        ]

    def attend(slot):
        def after_pair(pair):
            for copy in gives(slot, pair):
                copy.start()
            if slot > 0:

                @pl.when(pair == 0)
                def _():
                    project(slot - 1)
                    for at in range(2):
                        normed_copy(at).start()

        forward_body(
            mine, length_ref[slot], scale, head_size, qkv_ref.at[slot], bias_ref, low.at[slot],
            full_ref.at[slot], total_ref.at[slot], after_pair,
        )
        for which in (0, 1, 3, 4):
            store(which, slot).start()

    pick(0)
    for hop in range(1, count):
        for s in range(slots):
            hop_copy(s, hop - 1).wait_recv()
            if hop < count - 1:
                hop_copy(s, hop).start()
            qkv_ref[s, hop] = dot_nn(all_ref[s, hop], own_w[...]).astype(jnp.bfloat16)
            if hop == count - 1 and s + 1 < slots:
                attend(s)
        if hop == 1:
            for copy in place_first + grad_first:
                copy.wait_recv()
            for copy in place_second + grad_second:
                copy.start()
            pick(1)
            pick(2)
        if hop == 2:
            for copy in place_second + grad_second:
                copy.wait_recv()
            pick(3)
    attend(slots - 1)
    project(slots - 1)
    for s in range(slots):
        for hop in range(count - 1):
            hop_copy(s, hop).wait_send()
    for copy in place_first + grad_first + place_second + grad_second:
        copy.wait_send()
    for at in range(2):
        normed_copy(at).wait()
    for source in range(4):
        core_copy(source).wait()
    store(2, 0).wait()
    for s in range(slots):
        for which in (0, 1, 3, 4):
            store(which, s).wait()


def front(lengths, gain_first, gain_second, lines, target, w_attn, inputs, grads, slots, count, experts, capacity, scale, head_size):
    span_rows, model_width = inputs.shape[0], inputs.shape[1] // slots
    heads, _, lanes = lines.shape
    own_width = 3 * model_width // count
    groups = own_width // 384
    choices = target.shape[1]
    whole = pl.BlockSpec(memory_space=pltpu.VMEM)
    f32, bf16 = jnp.float32, jnp.bfloat16
    shape = jax.ShapeDtypeStruct
    made = (
        ((slots, count, span_rows, model_width), bf16),
        ((slots, count, span_rows, own_width), bf16),
        ((heads, span_rows, lanes - span_rows), f32),
        ((slots, count, span_rows, groups * 128), f32),
        ((slots, count, span_rows, groups * 128), f32),
    )
    got = pl.pallas_call(
        functools.partial(front_kernel, scale, head_size, slots),
        grid=(1,),
        in_specs=[
            pl.BlockSpec(memory_space=pltpu.SMEM),
            whole,
            whole,
            whole,
            whole,
            pl.BlockSpec(memory_space=pl.ANY),
            pl.BlockSpec((model_width, model_width), lambda i: (0, 3)),
            whole,
            whole,
        ],
        out_specs=[pl.BlockSpec(memory_space=pl.ANY)] * 5 + [whole] * (8 + 3 * slots),
        out_shape=[
            *(shape(*kind) for kind in made),
            shape((model_width, own_width), bf16),
            shape((4, slots, choices, span_rows), jnp.int32),
        ]
        + [shape((span_rows, model_width), bf16)] * 2
        + [
            shape((sources, experts, capacity, model_width), bf16)
            for sources in (1, 3)
            for _ in range(2)
        ]
        + [
            shape((span_rows, model_width), bf16),
            shape((span_rows, model_width), f32),
            shape((span_rows, model_width), bf16),
        ]
        * slots,
        scratch_shapes=[
            pltpu.VMEM((slots, count, span_rows, groups * 128), bf16),
            pltpu.VMEM((slots, count, span_rows, groups * 128), bf16),
            pltpu.VMEM((3, slots, span_rows, model_width), bf16),
            pltpu.SemaphoreType.DMA((2, slots, count - 1)),
            pltpu.SemaphoreType.DMA((3 * groups,)),
            pltpu.SemaphoreType.DMA((2, slots, groups, count)),
            pltpu.SemaphoreType.DMA((2, 3, slots)),
            pltpu.SemaphoreType.DMA((2, 3, slots)),
            pltpu.SemaphoreType.DMA((2, 4)),
            pltpu.SemaphoreType.DMA((2, 2)),
            pltpu.SemaphoreType.DMA((5, slots)),
            *(pltpu.VMEM(*kind) for kind in made),
        ],
        cost_estimate=cost(60e9, 20e6),
        compiler_params=remote_params(0),
        name="front",
    )(lengths, gain_first, gain_second, lines, target, w_attn, w_attn, inputs, grads)
    pairs = [got[9 + 2 * i : 11 + 2 * i] for i in range(2)]
    return got[:9], pairs, [got[13 + 3 * s : 16 + 3 * s] for s in range(slots)]


def hidden_body(
    experts, mine, length, back_ref, grad_ref, hidden_ref, normed_ref, gain_ref, router_ref, weight_ref,
    hidden_grad_ref, proj_ref, router_grad_ref, gain_grad_ref, leaving_ref, attended,
):
    count = leaving_ref.shape[0]
    span_rows, model_width = hidden_ref.shape
    back = back_ref[...]
    normed = normed_ref[...]
    probs = router_of(normed, router_ref[...], experts)
    shares = back[:, model_width:]
    logit_grads = probs * (shares - jnp.sum(probs * shares, axis=1, keepdims=True))
    logit_grads = logit_grads.astype(jnp.bfloat16)
    router_grad_ref[...] = dot_tn(logit_grads, normed)
    grads = back[:, :model_width] + dot_nt(logit_grads, router_ref[...])
    hidden = hidden_ref[...]
    scale_rows = root_scale(hidden)
    gain_grad_ref[...] = jnp.sum(grads * hidden * scale_rows, axis=0, keepdims=True)
    hidden_grads = grad_ref[...].astype(jnp.float32) + norm_back(
        grads, hidden, scale_rows, gain_ref[...]
    )
    hidden_grad_ref[...] = hidden_grads
    proj = (own_rows(mine, length, span_rows) * hidden_grads).astype(jnp.bfloat16)
    proj_ref[...] = proj
    attended[...] = dot_nt(proj, weight_ref[...]).astype(jnp.bfloat16)
    for j in range(count):
        owner = lax.rem(mine + (count - j), count)
        for group in range(leaving_ref.shape[2] // 128):
            at = pl.multiple_of((group * count + owner) * 128, 128)
            leaving_ref[j, :, group * 128 : (group + 1) * 128] = attended[:, pl.ds(at, 128)]


def hidden_kernel(
    experts, scale, head_size, slots, length_ref, gain_ref, router_ref, weight_ref, qkv_all, bias_all, full_all, total_all,
    cotangent_ref, *refs
):
    per_slot = [
        (refs[3 * s], slot_of(cotangent_ref, s, slots), *refs[3 * s + 1 : 3 * s + 3])
        for s in range(slots)
    ]
    refs = refs[3 * slots :]
    own_out, rest_out, refs = refs[:slots], refs[slots : 4 * slots], refs[4 * slots :]
    outs = [refs[4 * s : 4 * s + 4] for s in range(slots)]
    mixed = [slot_of(refs[4 * slots], s, slots) for s in range(slots)]
    refs = refs[4 * slots + 1 :]
    ring_ref, line_ref, rest_ref, leaving, arriving, attended, sems = refs[:7]
    got, far, last, low, out_sems = refs[7:12]
    qkv_ref, bias_ref, full_ref, total_ref, held_out, load_sems = refs[12:18]
    work = refs[18:]
    count = qkv_ref.shape[0]
    mine = lax.axis_index("cp")
    _, x_other, y_other = near_others(lax.axis_index("dp"), lax.axis_index("ep"))
    over, up, across = (rest_out[i * slots : (i + 1) * slots] for i in range(3))
    loads = [
        pltpu.make_async_copy(source, target, load_sems.at[at])
        for at, (source, target) in enumerate(
            (
                (qkv_all.at[0], qkv_ref),
                (bias_all, bias_ref),
                (full_all.at[0], full_ref),
                (total_all.at[0], total_ref),
                (up[0], held_out.at[0]),
                (over[1], held_out.at[1]),
                (own_out[0], held_out.at[2]),
                (own_out[1], held_out.at[3]),
            )
        )
    ]
    for load in loads:
        load.start()
    greet(*ring_others(mine, count), x_other, y_other)

    def out_copy(at):
        source, target, other = (
            (over[0], got.at[0], x_other),
            (up[1], got.at[1], y_other),
            (across[0], far.at[0], x_other),
            (across[1], far.at[1], y_other),
            (low.at[0], last.at[0], y_other),
            (low.at[1], last.at[1], x_other),
        )[at]
        return push(source, target, out_sems.at[0, at], out_sems.at[1, at], other)

    def after_pair(pair):
        @pl.when(pair == 0)
        def _():
            for at in range(2):
                out_copy(2 + at).wait()
                summed = held_out[at].astype(jnp.float32) + far[at].astype(jnp.float32)
                low[at] = summed.astype(jnp.bfloat16)
                out_copy(4 + at).start()

    for at in (2, 3, 0, 1):
        out_copy(at).start()
    copies = []
    for s in range(slots):
        hidden_body(
            experts, mine, length_ref[s], *per_slot[s], gain_ref, router_ref, weight_ref,
            *outs[s], leaving.at[s], attended,
        )
        target = arriving if s == 0 else rest_ref.at[s - 1]
        copies.append(deliveries(leaving.at[s], target, sems.at[s], mine, count))
        if s == 0:
            for copy in copies[s]:
                copy.start()
        target[0] = leaving[s, 0]
    for copy in copies[0]:
        copy.wait()
    for some in copies[1:]:
        for copy in some:
            copy.start()
    for load in loads:
        load.wait()
    backward_body(
        mine, length_ref[0], scale, head_size, qkv_ref, bias_ref, arriving, full_ref, total_ref,
        ring_ref, line_ref, work, after_pair,
    )
    for s in range(slots):
        out_copy(s).wait()
        out_copy(4 + s).wait()
        home = held_out[2 + s].astype(jnp.float32) + got[s].astype(jnp.float32)
        home = per_slot[s][2][...] + home + last[s].astype(jnp.float32)
        mixed[s][...] = home.astype(jnp.bfloat16)
    for copy in (copy for some in copies[1:] for copy in some):
        copy.wait()


def hidden_back(
    lengths, back_rows, grads, hidden, normed, gain, router, w_attn, experts, qkvs, bias, full, total, own_out,
    rest_out, scale, head_size,
):
    slots, count, span_rows, own_width = qkvs.shape
    model_width = hidden[0].shape[1]
    heads = bias.shape[0]
    whole = pl.BlockSpec(memory_space=pltpu.VMEM)
    f32, bf16 = jnp.float32, jnp.bfloat16
    each = [grads]
    for s in range(slots):
        each += [back_rows[s], hidden[s], normed[s]]
    each += [*own_out, *rest_out]
    own_shape = (count, span_rows, own_width // 3)
    got = pl.pallas_call(
        functools.partial(hidden_kernel, experts, scale, head_size, slots),
        grid=(1,),
        in_specs=[
            pl.BlockSpec(memory_space=pltpu.SMEM),
            whole,
            whole,
            pl.BlockSpec((model_width, model_width), lambda i: (0, 3)),
            *[pl.BlockSpec(memory_space=pl.ANY)] * 4,
        ]
        + [whole] * (len(each) - 4 * slots)
        + [pl.BlockSpec(memory_space=pl.ANY)] * (4 * slots),
        out_specs=[whole] * (4 * slots + 4),
        out_shape=[
            jax.ShapeDtypeStruct((span_rows, model_width), f32),
            jax.ShapeDtypeStruct((span_rows, model_width), bf16),
            jax.ShapeDtypeStruct((router.shape[1], model_width), f32),
            jax.ShapeDtypeStruct((1, model_width), f32),
        ]
        * slots
        + [jax.ShapeDtypeStruct((span_rows, slots * model_width), bf16)]
        + [
            jax.ShapeDtypeStruct(qkvs.shape[1:], bf16),
            jax.ShapeDtypeStruct((heads, 1, bias.shape[2] + span_rows), f32),
            jax.ShapeDtypeStruct((slots - 1,) + own_shape, bf16),
        ],
        scratch_shapes=[
            pltpu.VMEM((slots,) + own_shape, bf16),
            pltpu.VMEM(own_shape, bf16),
            pltpu.VMEM((span_rows, model_width), bf16),
            pltpu.SemaphoreType.DMA((slots, 2, count)),
            *[pltpu.VMEM((slots, span_rows, model_width), bf16)] * 4,
            pltpu.SemaphoreType.DMA((2, 6)),
            pltpu.VMEM(qkvs.shape[1:], bf16),
            pltpu.VMEM(bias.shape, f32),
            pltpu.VMEM(full.shape[1:], f32),
            pltpu.VMEM(full.shape[1:], f32),
            pltpu.VMEM((2 * slots, span_rows, model_width), bf16),
            pltpu.SemaphoreType.DMA((8,)),
        ]
        + backward_work(count, span_rows, head_size),
        cost_estimate=cost(20e9, 20e6),
        compiler_params=remote_params(1),
        name="hidden_back",
    )(lengths, gain, router, w_attn, qkvs, bias, full, total, *each)
    return [got[4 * s : 4 * s + 4] for s in range(slots)], got[4 * slots], got[4 * slots + 1 :]


def near_others(dp, ep):
    core, across = lax.rem(dp, 2), dp // 2
    return (
        {"dp": across * 2 + (1 - core)},
        {"dp": (1 - across) * 2 + core},
        {"ep": 1 - ep},
    )


def second_kernel(
    scale, head_size, slots, length_ref, former_ref, normed_all, qkv_all, bias_all, grad_ref, full_all, total_all,
    *refs,
):
    attended, proj, refs = refs[:slots], refs[slots : 2 * slots], refs[2 * slots :]
    own_w_all, gain_ref, refs = refs[0], refs[1], refs[2:]
    ring_ref, line_ref, arrived_ref, early_ref, weight_ref, rows_ref, gain_grad_ref = refs[:7]
    refs = refs[1:]
    sums, low, got_core, got_x, got_y, leaving, coming, sems, near_sems, last_sems = refs[6:16]
    early_sems, held_refs, work = refs[16], refs[17:24], refs[24:]
    normed_ref, qkv_ref, bias_ref, full_ref, total_ref, own_w_ref, load_sems = held_refs
    count = qkv_ref.shape[0]
    mine = lax.axis_index("cp")
    loads = [
        pltpu.make_async_copy(source, target, load_sems.at[at])
        for at, (source, target) in enumerate(
            (
                (qkv_all.at[1], qkv_ref),
                (bias_all, bias_ref),
                (full_all.at[1], full_ref),
                (total_all.at[1], total_ref),
                (normed_all, normed_ref),
                (own_w_all, own_w_ref),
            )
        )
    ]
    for load in loads:
        load.start()
    dp, ep = lax.axis_index("dp"), lax.axis_index("ep")
    core, across = lax.rem(dp, 2), dp // 2
    others = near_others(dp, ep)
    greet(*ring_others(mine, count), *others)
    copies = deliveries(former_ref, arrived_ref, sems, mine, count)
    for copy in copies:
        copy.start()
    arrived_ref[0] = former_ref[0]
    height = sums.shape[0] // 2
    sizes = (height, height // 2, height // 4)
    bits = (core, across, ep)
    landing = (got_core, got_x, got_y)
    total = None
    for s in range(slots):
        term = dot_tn(attended[s][...], proj[s][...])
        total = term if total is None else total + term
    sums[...] = total

    def low_part(stage):
        return low.at[stage, pl.ds(0, sizes[stage])]

    def stage_copy(stage):
        return push(
            low_part(stage), landing[stage], near_sems.at[0, stage], near_sems.at[1, stage], others[stage]
        )

    def start_of(stage):
        start = 0
        for former in range(stage):
            start = start + bits[former] * sizes[former]
        return start

    def begin(stage):
        at = start_of(stage) + (1 - bits[stage]) * sizes[stage]
        away = sums[pl.ds(pl.multiple_of(at, 128), sizes[stage]), :]
        low[stage, : sizes[stage]] = away.astype(jnp.bfloat16)
        stage_copy(stage).start()

    def finish(stage):
        stage_copy(stage).wait()
        at = pl.ds(pl.multiple_of(start_of(stage + 1), 128), sizes[stage])
        sums[at, :] = sums[at, :] + landing[stage][...].astype(jnp.float32)

    early = deliveries(ring_ref, early_ref, early_sems, mine, count, pl.ds(0, early_ref.shape[2]))

    def after_pair(pair):
        @pl.when(pair == 0)
        def _():
            for copy in early:
                copy.start()

        for stage in range(2):

            @pl.when(pair == stage)
            def _():
                finish(stage)
                begin(stage + 1)

    begin(0)
    for load in loads:
        load.wait()
    backward_body(
        mine, length_ref[1], scale, head_size, qkv_ref, bias_ref, grad_ref.at[0], full_ref, total_ref,
        ring_ref, line_ref, work, after_pair,
    )
    finish(2)
    at = pl.ds(pl.multiple_of(start_of(3), 128), sizes[2])
    groups = leaving.shape[2] // 128
    for j in range(count):
        owner = lax.rem(mine + (count - j), count)
        for group in range(groups):
            lanes = pl.ds(pl.multiple_of((group * count + owner) * 128, 128), 128)
            part = sums[at, lanes]
            leaving[j, :, group * 128 : (group + 1) * 128] = part.astype(jnp.bfloat16)
            if j == 0:
                rows_ref[:, group * 128 : (group + 1) * 128] = part
    last = deliveries(leaving, coming, last_sems, mine, count)
    for copy in last:
        copy.start()
    total = None
    for slot, grads in ((0, former_ref), (1, ring_ref)):
        for j in range(count):
            term = dot_tn(normed_ref[slot, j], grads[j])
            total = term if total is None else total + term
    weight_ref[...] = total
    first_gain = lax.dot_general(
        jnp.ones((8, total.shape[1]), jnp.float32),
        total * own_w_ref[...].astype(jnp.float32),
        (((1,), (1,)), ((), ())),
        precision=lax.Precision.HIGHEST,
        preferred_element_type=jnp.float32,
    )
    gain_grad_ref[...] = first_gain / gain_ref[...]
    for copy in last:
        copy.wait()
    for j in range(1, count):
        rows_ref[...] = rows_ref[...] + coming[j].astype(jnp.float32)
    for copy in copies + early:
        copy.wait()


def second_back(
    lengths, former, normed_all, qkvs, bias, grads, full, total, attended, proj, own_w, gain, scale, head_size, waits=()
):
    slots, count, span_rows, own_width = qkvs.shape
    model_width = normed_all.shape[3]
    whole = pl.BlockSpec(memory_space=pltpu.VMEM)
    some = pl.BlockSpec(memory_space=pl.ANY)
    f32, bf16 = jnp.float32, jnp.bfloat16
    rows_shape = (model_width // 8, own_width // 3)
    return pl.pallas_call(
        held(
            functools.partial(second_kernel, scale, head_size, slots), 10 + 2 * slots, len(waits)
        ),
        grid=(1,),
        in_specs=[
            pl.BlockSpec(memory_space=pltpu.SMEM),
            whole,
            some,
            some,
            some,
            whole,
            some,
            some,
        ]
        + [whole] * (2 * slots)
        + [some, whole]
        + anywhere(waits),
        out_specs=[whole] * 7,
        out_shape=[
            jax.ShapeDtypeStruct(qkvs.shape[1:], bf16),
            jax.ShapeDtypeStruct((bias.shape[0], 1, bias.shape[2] + span_rows), f32),
            jax.ShapeDtypeStruct(qkvs.shape[1:], bf16),
            jax.ShapeDtypeStruct((count, span_rows, 384), bf16),
            jax.ShapeDtypeStruct((model_width, own_width), f32),
            jax.ShapeDtypeStruct(rows_shape, f32),
            jax.ShapeDtypeStruct((8, model_width), f32),
        ],
        scratch_shapes=[
            pltpu.VMEM((model_width, model_width), f32),
            pltpu.VMEM((3, model_width // 2, model_width), bf16),
            pltpu.VMEM((model_width // 2, model_width), bf16),
            pltpu.VMEM((model_width // 4, model_width), bf16),
            pltpu.VMEM((model_width // 8, model_width), bf16),
            pltpu.VMEM((count,) + rows_shape, bf16),
            pltpu.VMEM((count,) + rows_shape, bf16),
            pltpu.SemaphoreType.DMA((2, count)),
            pltpu.SemaphoreType.DMA((2, 3)),
            pltpu.SemaphoreType.DMA((2, count)),
            pltpu.SemaphoreType.DMA((2, count)),
            pltpu.VMEM(normed_all.shape, bf16),
            pltpu.VMEM(qkvs.shape[1:], bf16),
            pltpu.VMEM(bias.shape, f32),
            pltpu.VMEM(full.shape[1:], f32),
            pltpu.VMEM(full.shape[1:], f32),
            pltpu.VMEM(own_w.shape, bf16),
            pltpu.SemaphoreType.DMA((6,)),
        ]
        + backward_work(count, span_rows, head_size),
        cost_estimate=cost(20e9, 20e6),
        compiler_params=remote_params(2),
        name="second_back",
    )(lengths, former, normed_all, qkvs, bias, grads, full, total, *attended, *proj, own_w, gain, *waits)


def token_body(mine, input_ref, hidden_ref, gain_ref, weight_ref, part_refs, own_ref, out_ref):
    count = part_refs[0].shape[0]
    model_width = input_ref.shape[1]
    total = None
    for j in range(count):
        owner = lax.rem(mine + j, count)
        pieces = []
        for group in range(own_ref.shape[2] // 384):
            for which in range(3):
                at = which * model_width + (group * count + owner) * 128
                pieces.append(weight_ref[:, pl.ds(pl.multiple_of(at, 128), 128)])
        part = own_ref[0] if j == 0 else jnp.concatenate([ref[j] for ref in part_refs], axis=1)
        term = dot_nt(part, jnp.concatenate(pieces, axis=1))
        total = term if total is None else total + term
    inputs = input_ref[...].astype(jnp.float32)
    back = norm_back(total, inputs, root_scale(inputs), gain_ref[...])
    out_ref[...] = (hidden_ref[...] + back).astype(jnp.bfloat16)


def final_kernel(
    slots, ring_ref, early_ref, former_all, arrived_ref, blocks_ref, small_ref, gain_ref, weight_all, tokens_ref, *refs
):
    inputs = [slot_of(tokens_ref, s, slots) for s in range(slots)]
    hidden_all, out_ref, refs = refs[:slots], refs[slots], refs[slots + 1 :]
    outs = [slot_of(out_ref, s, slots) for s in range(slots)]
    small_out, attn_out = refs[:2]
    coming, here, sum_blocks, low_blocks, small_now, small_in, sems, near_sems, small_sems = refs[2:11]
    got_core, low_halves, got_halves, low_ends, got_ends, half_sems = refs[11:17]
    former_ref, weight_ref, hidden_refs, load_sems = refs[17:]
    hiddens = [hidden_refs.at[s] for s in range(slots)]
    loads = [
        pltpu.make_async_copy(source, target, load_sems.at[at])
        for at, (source, target) in enumerate(
            (
                (former_all, former_ref),
                (weight_all.at[:, pl.ds(0, weight_ref.shape[1])], weight_ref),
                *((hidden_all[s], hiddens[s]) for s in range(slots)),
            )
        )
    ]
    for load in loads:
        load.start()
    count = ring_ref.shape[0]
    mine = lax.axis_index("cp")
    dp, ep = lax.axis_index("dp"), lax.axis_index("ep")
    core, across = lax.rem(dp, 2), dp // 2
    core_other, x_other, y_other = near_others(dp, ep)
    greet(*ring_others(mine, count), core_other, x_other, y_other)
    late = ring_ref.shape[2] - early_ref.shape[2]
    copies = deliveries(ring_ref, coming, sems, mine, count, pl.ds(early_ref.shape[2], late))
    for copy in copies:
        copy.start()

    small_now[0] = small_ref[...]
    loads[0].wait()
    total = former_ref[...]
    groups = total.shape[1] // 384
    for group in range(groups):
        for which in range(3):
            at = (group * 3 + which) * 128
            part = total[:, at : at + 128]
            sum_blocks[which % 2, which // 2, group] = part
            low_blocks[which % 2, which // 2, group] = part.astype(jnp.bfloat16)
        height = blocks_ref.shape[0]
        here_rows = pl.ds(pl.multiple_of((core * 4 + across * 2 + ep) * height, 128), height)
        part = blocks_ref[:, group * 128 : (group + 1) * 128]
        sum_blocks[1, 1, group] = jnp.zeros_like(sum_blocks[1, 1, group])
        low_blocks[1, 1, group] = jnp.zeros_like(low_blocks[1, 1, group])
        sum_blocks[1, 1, group, here_rows] = part
        low_blocks[1, 1, group, here_rows] = part.astype(jnp.bfloat16)
    first = push(low_blocks.at[1 - core], got_core, near_sems.at[0, 0], near_sems.at[1, 0], core_other)
    first.start()

    stages = [core_other, x_other, y_other]
    step = 1
    while step < count:
        flip = mine + step - 2 * step * lax.rem(mine // step, 2)
        stages.append({"cp": flip})
        step *= 2

    def small_push(at):
        return push(small_now.at[at], small_in.at[at], small_sems.at[0, at], small_sems.at[1, at], stages[at])

    small_push(0).start()
    for load in loads[1:]:
        load.wait()
    token_body(mine, inputs[0], hiddens[0], gain_ref, weight_ref, [arrived_ref], arrived_ref, outs[0])
    first.wait()
    here[...] = sum_blocks[core] + got_core[...].astype(jnp.float32)
    middle = here.shape[2] // 2
    upper, lower = slice(0, middle), slice(middle, 2 * middle)
    for at in range(2):
        low_halves[0, at] = here[1 - across, at, upper].astype(jnp.bfloat16)
        low_halves[1, at] = here[at, 1 - ep, lower].astype(jnp.bfloat16)

    def half_copy(at):
        source, target, other = (
            (low_halves.at[0], got_halves.at[0], x_other),
            (low_halves.at[1], got_halves.at[1], y_other),
            (low_ends.at[0], got_ends.at[0], y_other),
            (low_ends.at[1], got_ends.at[1], x_other),
        )[at]
        return push(source, target, half_sems.at[0, at], half_sems.at[1, at], other)

    half_copy(0).start()
    half_copy(1).start()
    for at in range(len(stages)):
        small_push(at).wait()
        now = small_now[at] + small_in[at]
        if at + 1 < len(stages):
            small_now[at + 1] = now
            small_push(at + 1).start()
        else:
            small_out[...] = now
        if at == 1:
            half_copy(0).wait()
            for k in range(2):
                here[across, k, upper] = here[across, k, upper] + got_halves[0, k].astype(jnp.float32)
            low_ends[0] = here[across, 1 - ep, upper].astype(jnp.bfloat16)
            half_copy(2).start()
            half_copy(1).wait()
            for k in range(2):
                here[k, ep, lower] = here[k, ep, lower] + got_halves[1, k].astype(jnp.float32)
            low_ends[1] = here[1 - across, ep, lower].astype(jnp.bfloat16)
            half_copy(3).start()
    for copy in copies:
        copy.wait()
    token_body(mine, inputs[1], hiddens[1], gain_ref, weight_ref, [early_ref, coming], ring_ref, outs[1])
    half_copy(2).wait()
    attn_out[upper] = here[across, ep, upper] + got_ends[0].astype(jnp.float32)
    half_copy(3).wait()
    attn_out[lower] = here[across, ep, lower] + got_ends[1].astype(jnp.float32)


def final_back(ring, early, former, arrived, blocks, small, gain, w_attn, inputs, hiddens):
    count, span_rows, own_width = ring.shape
    slots = len(hiddens)
    model_width = hiddens[0].shape[1]
    groups = blocks.shape[1] // 128
    whole = pl.BlockSpec(memory_space=pltpu.VMEM)
    f32, bf16 = jnp.float32, jnp.bfloat16
    some = pl.BlockSpec(memory_space=pl.ANY)
    stages = 3 + (count - 1).bit_length()
    tile = (model_width, 128)
    return pl.pallas_call(
        functools.partial(final_kernel, slots),
        grid=(1,),
        in_specs=[
            whole,
            whole,
            some,
            whole,
            whole,
            whole,
            whole,
            some,
            whole,
        ]
        + [some] * slots,
        out_specs=[whole] * 3,
        out_shape=[jax.ShapeDtypeStruct((span_rows, slots * model_width), bf16)]
        + [jax.ShapeDtypeStruct(small.shape, f32), jax.ShapeDtypeStruct(tile, f32)],
        scratch_shapes=[
            pltpu.VMEM((count, span_rows, own_width - early.shape[2]), bf16),
            pltpu.VMEM((2, groups) + tile, f32),
            pltpu.VMEM((2, 2, groups) + tile, f32),
            pltpu.VMEM((2, 2, groups) + tile, bf16),
            pltpu.VMEM((stages,) + small.shape, f32),
            pltpu.VMEM((stages,) + small.shape, f32),
            pltpu.SemaphoreType.DMA((2, count)),
            pltpu.SemaphoreType.DMA((2, 3)),
            pltpu.SemaphoreType.DMA((2, stages)),
            pltpu.VMEM((2, groups) + tile, bf16),
            pltpu.VMEM((2, 2, model_width // 2, 128), bf16),
            pltpu.VMEM((2, 2, model_width // 2, 128), bf16),
            pltpu.VMEM((2, model_width // 2, 128), bf16),
            pltpu.VMEM((2, model_width // 2, 128), bf16),
            pltpu.SemaphoreType.DMA((2, 4)),
            pltpu.VMEM(former.shape, f32),
            pltpu.VMEM((model_width, 3 * model_width), bf16),
            pltpu.VMEM((slots, span_rows, model_width), f32),
            pltpu.SemaphoreType.DMA((2 + slots,)),
        ],
        cost_estimate=cost(20e9, 20e6),
        compiler_params=remote_params(3),
        name="final_back",
    )(ring, early, former, arrived, blocks, small, gain, w_attn, inputs, *hiddens)


gelu_inner = 0.7978845608028654
gelu_cubic = 0.044715


def place_body(base, chosen_ref, pairs, outs):
    capacity = pairs[0][0].shape[0]
    span = outs[0].shape[0]
    both = [
        (mine[...].astype(jnp.float32) + theirs[...].astype(jnp.float32)).astype(jnp.bfloat16)
        for mine, theirs in pairs
    ]
    for at, out in enumerate(outs):
        total = None
        for expert in range(len(pairs)):
            ids = lax.broadcasted_iota(jnp.int32, (span, capacity), 1) + (base + expert * capacity)
            hot = jnp.zeros((span, capacity), jnp.float32)
            for choice in range(chosen_ref.shape[1]):
                chosen = chosen_ref[at * span : (at + 1) * span, choice : choice + 1]
                hot = hot + jnp.where(ids == chosen, 1.0, 0.0)
            term = dot_nn(hot.astype(jnp.bfloat16), both[expert])
            total = term if total is None else total + term
        out[...] = total.astype(jnp.bfloat16)


def return_kernel(experts, slots, target_ref, *refs):
    held_pairs = 2 * (1 + experts)
    back, far_outs, refs = refs[:held_pairs], refs[held_pairs : 2 * held_pairs], refs[2 * held_pairs :]
    backs, refs = refs[:slots], refs[slots:]
    out_own, out_rest, refs = refs[:slots], refs[slots : 4 * slots], refs[4 * slots :]
    here, got, far, last, low = refs[:5]
    outs, load_sems, sems = refs[5 : 5 + held_pairs], refs[5 + held_pairs], refs[6 + held_pairs]
    arriving, core_sems = refs[7 + held_pairs :]
    dp, ep = lax.axis_index("dp"), lax.axis_index("ep")
    core_other, x_other, y_other = near_others(dp, ep)
    base = ep * (experts * back[0].shape[2])
    loads = [
        pltpu.make_async_copy(source, target, load_sems.at[i])
        for i, (source, target) in enumerate(zip(far_outs[:-1], outs[:-1]))
    ]

    def core_copy(at):
        if at == 3:
            source, target = far_outs[-1], outs[-1]
        else:
            source, target = back[-1].at[0, at], arriving.at[0, at]
        return push(source, target, core_sems.at[0, at], core_sems.at[1, at], core_other)

    given = [*back[:-1], arriving]
    for load in loads:
        load.start()

    def rows_of(held_refs, source):
        if source == 0:
            return [(held_refs[0].at[e, 0], held_refs[1].at[e, 0]) for e in range(experts)]
        return [
            (held_refs[2 + 2 * e].at[0, source - 1], held_refs[3 + 2 * e].at[0, source - 1])
            for e in range(experts)
        ]

    def place(held_refs, source, targets):
        if held_refs is given and source > 0:
            core_copy(source - 1).wait()
        place_body(base, target_ref.at[source], rows_of(held_refs, source), targets)

    firsts = [
        push(here.at[1, 0], got.at[0], sems.at[0, 0], sems.at[1, 0], x_other),
        push(here.at[2, 1], got.at[1], sems.at[0, 1], sems.at[1, 1], y_other),
        push(here.at[3, 0], far.at[0], sems.at[0, 2], sems.at[1, 2], x_other),
        push(here.at[3, 1], far.at[1], sems.at[0, 3], sems.at[1, 3], y_other),
    ]
    ends = [
        push(low.at[0], last.at[0], sems.at[0, 4], sems.at[1, 4], y_other),
        push(low.at[1], last.at[1], sems.at[0, 5], sems.at[1, 5], x_other),
    ]
    greet(core_other, x_other, y_other)
    for at in (2, 0, 1, 3):
        core_copy(at).start()
    halves = lambda source: [here.at[source, s] for s in range(slots)]
    place(given, 3, halves(3))
    firsts[2].start()
    firsts[3].start()
    place(given, 1, halves(1))
    firsts[0].start()
    place(given, 2, halves(2))
    firsts[1].start()
    place(given, 0, halves(0))
    for load in loads:
        load.wait()
    core_copy(3).wait()
    for at, (former, source) in enumerate(((2, 2), (3, 1))):
        firsts[former].wait()
        low[at] = (here[source, at].astype(jnp.float32) + far[at].astype(jnp.float32)).astype(jnp.bfloat16)
        ends[at].start()
    place(outs, 0, out_own)
    for source in range(1, 4):
        place(outs, source, out_rest[(source - 1) * slots : source * slots])
    for s in range(slots):
        firsts[s].wait()
        backs[s][...] = here[0, s].astype(jnp.float32) + got[s].astype(jnp.float32)
    for s in range(slots):
        ends[s].wait()
        backs[s][...] = backs[s][...] + last[s].astype(jnp.float32)


def return_rows(targets, backs, outs, slots, waits=()):
    experts = len(backs) // 2 - 1
    model_width = outs[0].shape[-1]
    span_rows = targets.shape[1] // slots
    wide = backs[0].shape[-1]
    whole = pl.BlockSpec(memory_space=pltpu.VMEM)
    f32, bf16 = jnp.float32, jnp.bfloat16
    half = pltpu.VMEM((slots, span_rows, wide), bf16)
    got = pl.pallas_call(
        held(
            functools.partial(return_kernel, experts, slots),
            1 + len(backs) + len(outs),
            len(waits),
        ),
        in_specs=[whole] + [whole] * len(backs) + anywhere(outs) + anywhere(waits),
        out_specs=[whole] * (5 * slots),
        out_shape=[
            *[jax.ShapeDtypeStruct((span_rows, wide), f32)] * slots,
            *[jax.ShapeDtypeStruct((span_rows, model_width), bf16)] * (4 * slots),
        ],
        scratch_shapes=[pltpu.VMEM((4, slots, span_rows, wide), bf16), half, half, half, half]
        + [pltpu.VMEM(a.shape, bf16) for a in outs]
        + [pltpu.SemaphoreType.DMA((len(outs),)), pltpu.SemaphoreType.DMA((2, 6))]
        + [pltpu.VMEM(backs[-1].shape, bf16), pltpu.SemaphoreType.DMA((2, 4))],
        cost_estimate=cost(20e9, 20e6),
        compiler_params=remote_params(4),
        name="return_rows",
    )(targets, *backs, *outs, *waits)
    return got[:slots], got[slots : 2 * slots], got[2 * slots :]


def expert_body(experts, own_units, expert, skip, given, refs, weights, router_ref):
    back_mine, back_theirs, out_mine, out_theirs, kept_rows, kept_units = refs
    gate_ref, up_ref, down_ref = weights
    capacity, model_width = given[0].shape[2:]
    rows = jnp.concatenate([given[0][0, 0], given[1][0, 0]], axis=0)
    grads = jnp.concatenate([given[2][0, 0], given[3][0, 0]], axis=0)
    kept_rows[0, 0, 0] = rows
    kept_rows[1, 0, 0] = grads
    lane = lax.broadcasted_iota(jnp.int32, (1, router_ref.shape[1]), 1)
    probs = router_of(rows, router_ref[...], experts)
    gates = jnp.sum(jnp.where(lane == expert, probs, 0.0), axis=1, keepdims=True)
    unit = lax.broadcasted_iota(jnp.int32, (1, gate_ref.shape[2]), 1) - skip
    own = jnp.logical_and(unit >= 0, unit < own_units)
    gate_w, up_w, down_w = gate_ref[0], up_ref[0], down_ref[0]
    gate_pre = dot_nn(rows, gate_w)
    up_pre = jnp.where(own, dot_nn(rows, up_w), 0.0)
    square = gate_pre * gate_pre
    tanh = jnp.tanh(gelu_inner * gate_pre * (1.0 + gelu_cubic * square))
    half = 0.5 + 0.5 * tanh
    active = gate_pre * half
    slope = half + active * (1.0 - tanh) * (gelu_inner * (1.0 + 3.0 * gelu_cubic * square))
    inner = active * up_pre
    low_inner = inner.astype(jnp.bfloat16)
    plain_grads = jnp.where(own, dot_nn(grads, down_w), 0.0)
    gate_grads = jnp.sum(plain_grads * low_inner.astype(jnp.float32), axis=1, keepdims=True)
    inner_grads = plain_grads * gates
    low_gate = (inner_grads * up_pre * slope).astype(jnp.bfloat16)
    low_up = (inner_grads * active).astype(jnp.bfloat16)
    kept_units[0, 0, 0] = low_gate
    kept_units[1, 0, 0] = low_up
    kept_units[2, 0, 0] = (inner * gates).astype(jnp.bfloat16)
    back = (dot_nt(low_gate, gate_w) + dot_nt(low_up, up_w)).astype(jnp.bfloat16)
    shares = jnp.where(lane == expert, gate_grads, 0.0).astype(jnp.bfloat16)
    out = (gates * dot_nt(low_inner, down_w)).astype(jnp.bfloat16)
    for at, back_ref, out_ref in ((0, back_mine, out_mine), (1, back_theirs, out_theirs)):
        part = slice(at * capacity, (at + 1) * capacity)
        back_ref[0, 0, :, :model_width] = back[part]
        back_ref[0, 0, :, model_width:] = shares[part]
        out_ref[0, 0] = out[part]


def expert_kernel(experts, own_units, kept_count, first_ref, window_ref, *refs):
    given, refs = refs[:4], refs[4:]
    router_ref, weights, refs = refs[0], refs[1:4], refs[4 + kept_count :]
    expert = first_ref[0] + pl.program_id(0)
    expert_body(experts, own_units, expert, window_ref[1], given, refs, weights, router_ref)


def own_kernel(experts, own_units, *refs):
    given_grads, router_ref, weights, refs = refs[:2], refs[2], refs[3:6], refs[6:]
    target_ref, over_ref, up_ref, first_ref, normed_ref, refs = *refs[:5], refs[5:]
    results, kept, (mine_ref, theirs_ref), refs = refs[:4], refs[4:6], refs[6:8], refs[8:]
    coming, picked, held_w, held_rows, held_units = refs[:5]
    sems, core_sems, home_sems, load_sems, keep_sems, own_picked, own_sems = refs[5:]
    given = [own_picked.at[0], own_picked.at[1], *given_grads]
    exp_dev, capacity = picked.shape[1:3]
    dp, ep = lax.axis_index("dp"), lax.axis_index("ep")
    core_other, x_other, y_other = near_others(dp, ep)
    skip = lax.rem(dp * own_units, 128)

    def copy(at):
        source, other = (
            (normed_ref, x_other),
            (normed_ref, y_other),
            (over_ref, y_other),
            (coming.at[1], x_other),
        )[at]
        return push(source, coming.at[at], sems.at[0, at], sems.at[1, at], other)

    def load(expert, which):
        lanes = pl.ds(pl.multiple_of(dp * own_units - skip, 128), held_w.shape[4])
        return pltpu.make_async_copy(
            weights[which].at[pl.ds(expert, 1), :, lanes],
            held_w.at[expert, which],
            load_sems.at[expert, which],
        )

    def keep(expert, kind):
        held_ref = (held_rows, held_units)[kind]
        return pltpu.make_async_copy(
            held_ref.at[expert, :, 0, 0], kept[kind].at[:, expert, 0], keep_sems.at[expert, kind]
        )

    for expert in range(exp_dev):
        for which in range(3):
            load(expert, which).start()
    greet(core_other, x_other, y_other)
    for at in range(3):
        copy(at).start()
    base = ep * (exp_dev * capacity)
    chosen = [target_ref.at[0, s] for s in range(target_ref.shape[1])]
    pick_body(base, capacity, exp_dev, chosen, (first_ref, normed_ref), own_picked.at[0, 0])
    own_copy = push(own_picked.at[0], own_picked.at[1], own_sems.at[0], own_sems.at[1], core_other)
    own_copy.start()
    own_copy.wait()
    for expert in range(exp_dev):
        if expert == 1:
            copy(1).wait_recv()
            copy(3).start()
        for which in range(3):
            load(expert, which).wait()
        here = pl.ds(expert, 1)
        expert_body(
            experts,
            own_units,
            ep * exp_dev + expert,
            skip,
            [part.at[:, here] for part in given],
            [part.at[here] for part in results] + [held_rows.at[expert], held_units.at[expert]],
            [held_w.at[expert, which] for which in range(3)],
            router_ref,
        )
        for kind in range(2):
            keep(expert, kind).start()

    blocks = (
        (over_ref, coming.at[0]),
        (up_ref, coming.at[1]),
        (coming.at[2], coming.at[3]),
    )

    def across_cores(k):
        return push(picked.at[k], theirs_ref.at[k], core_sems.at[0, k], core_sems.at[1, k], core_other)

    def home(k):
        return pltpu.make_async_copy(picked.at[k], mine_ref.at[k], home_sems.at[k])

    for k, waits in enumerate(((0,), (), (2, 3))):
        for at in waits:
            copy(at).wait_recv()
        chosen = [target_ref.at[k + 1, s] for s in range(target_ref.shape[1])]
        pick_body(base, capacity, exp_dev, chosen, blocks[k], picked.at[k])
        across_cores(k).start()
        home(k).start()
    for at in range(4):
        copy(at).wait_send()
    for k in range(3):
        across_cores(k).wait()
        home(k).wait()
    for expert in range(exp_dev):
        for kind in range(2):
            keep(expert, kind).wait()


def own_experts(grads, router, weights, target, over, up, first, normed, total, experts, units):
    _, exp_dev, capacity, model_width = grads[0].shape
    span_rows = normed.shape[0]
    wide_units = aligned_units(units)
    tile = 2 * capacity
    bf16 = jnp.bfloat16
    shape = jax.ShapeDtypeStruct
    picked = (3, exp_dev, capacity, model_width)
    wide = model_width + 128
    keeps = ((2, model_width), (3, wide_units))
    whole = pl.BlockSpec(memory_space=pltpu.VMEM)
    some = pl.BlockSpec(memory_space=pl.ANY)
    got = pl.pallas_call(
        functools.partial(own_kernel, experts, units),
        grid=(1,),
        in_specs=[whole] * 3 + [some] * 3 + [whole] * 5,
        out_specs=[whole] * 4 + [some] * 4,
        out_shape=[shape((exp_dev, 1, capacity, wide), bf16)] * 2
        + [shape((exp_dev, 1, capacity, model_width), bf16)] * 2
        + [shape((kinds, exp_dev, total, tile, width), bf16) for kinds, width in keeps]
        + [shape(picked, bf16)] * 2,
        scratch_shapes=[
            pltpu.VMEM((4, span_rows, model_width), bf16),
            pltpu.VMEM(picked, bf16),
            pltpu.VMEM((exp_dev, 3, 1, model_width, wide_units), bf16),
        ]
        + [pltpu.VMEM((exp_dev, kinds, 1, 1, tile, width), bf16) for kinds, width in keeps]
        + [
            pltpu.SemaphoreType.DMA((2, 4)),
            pltpu.SemaphoreType.DMA((2, 3)),
            pltpu.SemaphoreType.DMA((3,)),
            pltpu.SemaphoreType.DMA((exp_dev, 3)),
            pltpu.SemaphoreType.DMA((exp_dev, 2)),
            pltpu.VMEM((2, 1, exp_dev, capacity, model_width), bf16),
            pltpu.SemaphoreType.DMA((2,)),
        ],
        cost_estimate=cost(20e9, 16e6),
        compiler_params=remote_params(5),
        name="own_experts",
    )(*grads, router, *weights, target, over, up, first, normed)
    return got[:4], got[4:6], got[6:]


def run_experts(first, window, given, router, weights, kept, at, total, experts, units, chosen):
    low, high = chosen
    sources, exp_dev, capacity, model_width = given[0].shape
    wide_units = aligned_units(units)
    tile = 2 * capacity

    given_rows = pl.BlockSpec(
        (1, 1, capacity, model_width), lambda e, k, f, w: (k, low + e, 0, 0)
    )
    out = lambda width: pl.BlockSpec((1, 1, capacity, width), lambda e, k, f, w: (e, k, 0, 0))
    wide, rows = out(model_width + 128), out(model_width)
    weight = pl.BlockSpec(
        (pl.Element(1), pl.Element(model_width), pl.Element(wide_units)),
        lambda e, k, f, w: (low + e, 0, pl.multiple_of(w[0], 128)),
    )
    keep = lambda kinds, width: pl.BlockSpec(
        (kinds, 1, 1, tile, width), lambda e, k, f, w: (0, low + e, at + k, 0, 0)
    )
    keeps = ((2, model_width), (3, wide_units))
    kept = list(kept)
    out_of = lambda width: jax.ShapeDtypeStruct(
        (high - low, sources, capacity, width), jnp.bfloat16
    )
    back_shape, out_shape = out_of(model_width + 128), out_of(model_width)
    got = pl.pallas_call(
        functools.partial(expert_kernel, experts, units, len(kept)),
        grid_spec=pltpu.PrefetchScalarGridSpec(
            num_scalar_prefetch=2,
            grid=(high - low, sources),
            in_specs=[given_rows] * 4
            + [
                pl.BlockSpec(router.shape, lambda e, k, f, w: (0, 0)),
                weight,
                weight,
                weight,
            ]
            + anywhere(kept),
            out_specs=[wide, wide, rows, rows] + [keep(*kinds) for kinds in keeps],
        ),
        out_shape=[back_shape, back_shape, out_shape, out_shape]
        + [
            jax.ShapeDtypeStruct((kinds, exp_dev, total, tile, width), jnp.bfloat16)
            for kinds, width in keeps
        ],
        input_output_aliases={10 + i: 4 + i for i in range(len(kept))},
        cost_estimate=cost(20e9 * sources, 8e6 * sources),
        compiler_params=compiler_params(),
        name="expert_rows",
    )(first + low, window, *given, router, *weights, *kept)
    return got[:4], got[4:]


def aligned_units(units):
    return (units + 127) // 128 * 128


def weight_kernel(window_ref, rows_ref, units_ref, weight_ref, total):
    pieces, _, piece, model_width = weight_ref.shape
    units = units_ref[0, 0].reshape(-1, units_ref.shape[-1])
    part = dot_tn(units, rows_ref[0, 0].reshape(-1, model_width))

    @pl.when(pl.program_id(1) == 0)
    def _():
        total[...] = part

    @pl.when(pl.program_id(1) == 1)
    def _():
        total[...] = total[...] + part
        skip = pl.multiple_of(window_ref[1], 64)
        for at in range(pieces):
            weight_ref[at, 0] = total[pl.ds(skip + at * piece, piece), :].astype(jnp.bfloat16)


def weight_grads(window, kept, expert, pieces, units, waits=()):
    kept_rows, kept_units = kept
    tiles, tile, model_width = kept_rows.shape[2:]
    wide_units = kept_units.shape[4]
    shape = (pieces, 3, units // pieces, model_width)
    return pl.pallas_call(
        held(weight_kernel, 3, len(waits)),
        grid=(3, 2),
        in_specs=[
            pl.BlockSpec(memory_space=pltpu.SMEM),
            pl.BlockSpec(
                (1, 1, tiles // 2, tile, model_width), lambda i, k: (i // 2, expert, k, 0, 0)
            ),
            pl.BlockSpec((1, 1, tiles // 2, tile, wide_units), lambda i, k: (i, expert, k, 0, 0)),
        ]
        + anywhere(waits),
        out_specs=pl.BlockSpec((pieces, 1) + shape[2:], lambda i, k: (0, i, 0, 0)),
        out_shape=jax.ShapeDtypeStruct(shape, jnp.bfloat16),
        scratch_shapes=[pltpu.VMEM((wide_units, model_width), jnp.float32)],
        cost_estimate=cost(20e9, 20e6),
        compiler_params=compiler_params(),
        name="weight_grads",
    )(window, kept_rows, kept_units, *waits)


def send(values, axis, pairs):
    return lax.ppermute(values, axis, pairs)


def after(values, *earlier):
    return lax.optimization_barrier((values, earlier))[0]


def fast_device(
    tokens,
    lengths,
    expert_ids,
    places,
    buckets,
    w_attn,
    bias_table,
    norm1_gain,
    norm2_gain,
    w_router,
    w_gate,
    w_up,
    w_down,
    cotangent,
):
    span_rows, slots, model_width = tokens.shape
    head_count, bucket_count = bias_table.shape
    head_size = model_width // head_count
    scale = head_size ** (-0.5)
    n_dp = lax.axis_size("dp")
    n_ep = lax.axis_size("ep")
    n_cp = lax.axis_size("cp")
    my_dp, my_ep, my_cp = (lax.axis_index(name) for name in ("dp", "ep", "cp"))
    seq_len = span_rows * n_cp
    rows = span_rows * slots
    top_count = expert_ids.shape[2]
    experts = w_router.shape[1]
    exp_dev = w_gate.shape[0]
    units = w_gate.shape[2] // n_dp
    capacity = (5 * rows * top_count + 4 * experts - 1) // (4 * experts)
    groups = model_width // (128 * n_cp)
    own_width = 3 * groups * 128
    heads_own = head_count // n_cp
    over_core = [(i, i ^ 1) for i in range(n_dp)]
    over_x = [(i, i ^ 2) for i in range(n_dp)]
    over_y = [(i, i ^ 1) for i in range(n_ep)]
    ring = [(i, (i + 1) % n_cp) for i in range(n_cp)]
    f32, bf16 = jnp.float32, jnp.bfloat16
    exact = lax.Precision.HIGHEST
    each = range(slots)

    low_in = tokens.reshape(span_rows, slots * model_width)
    low_out = cotangent.reshape(span_rows, slots * model_width)
    gain_first, gain_second = norm1_gain[None, :], norm2_gain[None, :]

    per_group = 128 // head_size
    own_heads = (
        jnp.arange(groups)[:, None] * (n_cp * per_group)
        + my_cp * per_group
        + jnp.arange(per_group)[None, :]
    ).reshape(heads_own)
    head_hot = (own_heads[:, None] == jnp.arange(head_count)[None, :]).astype(f32)
    own_table = jnp.dot(head_hot, bias_table, precision=exact)
    far_hot = (buckets[::-1][:, None] == jnp.arange(bucket_count)[None, :]).astype(f32)
    lines = jnp.einsum("hb,db->hd", own_table, far_hot, precision=exact)
    lines = jnp.concatenate([lines, jnp.full((heads_own, span_rows), minus_big, f32)], axis=1)
    target = jnp.where(places >= 0, expert_ids * capacity + places, -1)
    target = target.transpose(1, 2, 0).astype(jnp.int32)
    (
        (normed_all, qkvs, bias, full, total, w_own, target_all, over_first, up_first),
        (grads_own, grads_rest_rows),
        fronts,
    ) = front(
        lengths,
        gain_first,
        gain_second,
        lines[:, None, :],
        target,
        w_attn,
        low_in,
        low_out,
        slots,
        n_cp,
        exp_dev,
        capacity,
        scale,
        head_size,
    )
    attended, hidden, normed_second = zip(*fronts)

    sources = target_all.shape[0]
    target_rows = target_all.transpose(0, 2, 1, 3).reshape(sources, top_count, rows)
    target_columns = target_rows.transpose(0, 2, 1)
    window_at = my_dp * units // 128 * 128
    window = jnp.stack([window_at, my_dp * units - window_at]).astype(jnp.int32)
    router_wide = jnp.concatenate(
        [w_router, jnp.zeros((model_width, 128 - experts), w_router.dtype)], axis=1
    )

    first = (my_ep * exp_dev).astype(jnp.int32).reshape(1)
    own, kept, picked_rest = own_experts(
        grads_own,
        router_wide,
        (w_gate, w_up, w_down),
        target_all,
        over_first,
        up_first,
        normed_second[0],
        normed_second[1],
        sources,
        experts,
        units,
    )

    def with_theirs(mine, theirs):
        return [mine, send(theirs, "dp", over_core)]

    backs, outs = with_theirs(own[0], own[1]), with_theirs(own[2], own[3])
    weight_sums = []
    for e in range(exp_dev):
        rest, kept = run_experts(
            first,
            window,
            (*picked_rest, *grads_rest_rows),
            router_wide,
            (w_gate, w_up, w_down),
            kept,
            1,
            sources,
            experts,
            units,
            (e, e + 1),
        )
        weight_part = weight_grads(window, kept, e, n_cp, units, backs[-1:] + outs[-1:])
        if e + 1 < exp_dev:
            backs += with_theirs(rest[0], rest[1])
            outs += with_theirs(rest[2], rest[3])
        else:
            backs, outs = [*backs, *rest[:2]], [*outs, *rest[2:]]
        weight_sums.append(lax.psum_scatter(weight_part, "cp", scatter_dimension=0, tiled=False))
        kept = after(kept, weight_part)
    back_rows, out_own, out_rest = return_rows(target_columns, backs, outs, slots, [weight_part])
    got, mixed, (ringed, line_first, grads_rest) = hidden_back(
        lengths,
        back_rows,
        low_out,
        hidden,
        normed_second,
        gain_second,
        router_wide,
        w_attn,
        experts,
        qkvs,
        bias,
        full,
        total,
        out_own,
        out_rest,
        scale,
        head_size,
    )
    hidden_grads, proj_grads, router_parts, gain_parts = zip(*got)
    router_grad = sum(router_parts)[:experts]
    ring_second, line_second, arrived, early, weight_part, out_grad, gain_part = second_back(
        lengths,
        ringed,
        normed_all,
        qkvs,
        bias,
        grads_rest,
        full,
        total,
        attended,
        proj_grads,
        w_own,
        gain_first,
        scale,
        head_size,
        weight_sums[:1],
    )
    distance_grads = (line_first + line_second)[:, 0, :seq_len]
    table_grad = jnp.dot(distance_grads, far_hot, precision=exact)
    table_grad = jnp.einsum("hg,hb->gb", head_hot, table_grad, precision=exact)
    table_row = jnp.pad(table_grad.reshape(1, -1), ((0, 0), (0, model_width - table_grad.size)))
    small = jnp.concatenate(
        [router_grad, sum(gain_parts), table_row, gain_part[:2]], axis=0
    )
    tokens_grad, small_sum, attn_sum = final_back(
        ring_second,
        early,
        weight_part,
        arrived,
        out_grad,
        small,
        gain_first,
        w_attn,
        low_in,
        hidden_grads,
    )
    router_sum, gain_second_sum = small_sum[:experts], small_sum[experts]
    table_sum = small_sum[experts + 1, : table_grad.size].reshape(table_grad.shape)
    gain_first_sum = small_sum[experts + 2]

    gate_sum, up_sum, down_sum = (
        jnp.stack([part[which].T.astype(f32) for part in weight_sums]) for which in range(3)
    )
    return (
        mixed.reshape(tokens.shape),
        tokens_grad.reshape(tokens.shape),
        attn_sum,
        table_sum,
        gain_first_sum,
        gain_second_sum,
        router_sum.T,
        gate_sum,
        up_sum,
        down_sum,
    )


def solution(mesh):
    placed = (
        P("cp", ("dp", "ep"), None),
        P(("dp", "ep")),
        P("cp", ("dp", "ep"), None),
        P("cp", ("dp", "ep"), None),
        P(),
        P(),
        P(),
        P(),
        P(),
        P(),
        P("ep", None, None),
        P("ep", None, None),
        P("ep", None, None),
        P("cp", ("dp", "ep"), None),
    )
    sizes = dict(mesh.shape)
    square = sizes["dp"] == 4 and sizes["ep"] == 2 and sizes["cp"] == 4
    return jax.shard_map(
        fast_device if square else on_device,
        mesh=mesh,
        in_specs=placed,
        out_specs=(
            P("cp", ("dp", "ep"), None),
            P("cp", ("dp", "ep"), None),
            P(None, ("dp", "ep", "cp")),
            P(),
            P(),
            P(),
            P(),
            P("ep", None, ("dp", "cp")),
            P("ep", None, ("dp", "cp")),
            P("ep", None, ("dp", "cp")),
        ),
        check_vma=False,
    )
```
